32 devices in a mesh: seq: 8 (over y, x, core), tp: 4 (over z).
Axes of the slice: x: 2, y: 2, z: 4, core: 2. Of those that a mesh axis runs over, the one named last changes fastest.
Arguments:
- block_input: bfloat16 [4096, 1024], P('seq'), may hold values from -6 to 6
- scene_lengths: int32 [4], replicated, may hold values from 1 to 4096, as said below
- input_gain: float32 [1024], replicated, may hold values from 0.5 to 1.5
- gate_weight: bfloat16 [1024, 2048], P(None, 'tp'), may hold values from -0.1875 to 0.1875
- inner_weight: bfloat16 [1024, 2048], P(None, 'tp'), may hold values from -0.1875 to 0.1875
- state_weight: bfloat16 [1024, 256], P(None, 'tp'), may hold values from -0.1875 to 0.1875
- step_weight: bfloat16 [1024, 32], P(None, 'tp'), may hold values from -0.1875 to 0.1875
- step_bias: float32 [32], P('tp'), may hold values from -1.5 to 1
- rate_log: float32 [32], P('tp'), may hold values from -9 to -3.5
- inner_kernel: float32 [4, 2048], P(None, 'tp'), may hold values from -3 to 3
- inner_conv_bias: float32 [2048], P('tp'), may hold values from -2 to 2
- state_kernel: float32 [4, 256], P(None, 'tp'), may hold values from -3 to 3
- state_conv_bias: float32 [256], P('tp'), may hold values from -2 to 2
- skip_scale: float32 [32], P('tp'), may hold values from 1 to 8
- gate_gain: float32 [2048], P('tp'), may hold values from 0.5 to 1.5
- out_weight: bfloat16 [2048, 1024], P('tp'), may hold values from -0.125 to 0.125
- out_cotangent: bfloat16 [4096, 1024], P('seq'), may hold values from -6 to 6
Outputs:
- block_output: bfloat16 [4096, 1024], P('seq')
- input_grad: float32 [4096, 1024], P('seq')
- input_gain_grad: float32 [1024], replicated
- gate_weight_grad: float32 [1024, 2048], P('seq', 'tp')
- inner_weight_grad: float32 [1024, 2048], P('seq', 'tp')
- state_weight_grad: float32 [1024, 256], P('seq', 'tp')
- step_weight_grad: float32 [1024, 32], P('seq', 'tp')
- step_bias_grad: float32 [32], P('tp')
- rate_log_grad: float32 [32], P('tp')
- inner_kernel_grad: float32 [4, 2048], P(None, 'tp')
- inner_conv_bias_grad: float32 [2048], P('tp')
- state_kernel_grad: float32 [4, 256], P(None, 'tp')
- state_conv_bias_grad: float32 [256], P('tp')
- skip_scale_grad: float32 [32], P('tp')
- gate_gain_grad: float32 [2048], P('tp')
- out_weight_grad: float32 [2048, 1024], P('tp', 'seq')
The draws below stay inside these ranges and needn't reach their ends.
Inputs may be any that keep to these rules, and one draw needn't show every extreme that they name: `scene_lengths`: the lengths sum to 4096; one scene, which one drawn from the seed, holds all but at most 384 tokens, and every other scene holds 1 to 128.
All inputs are finite; a program needn't handle non-finite values.
Results may differ from the reference program's by a relative error of at most 0.0085.
The reference program's roundings to bfloat16 on the way count: a program that leaves them out, or rounds other values in their place, can miss the bound.
Values may be sent and summed in bfloat16 or wider, within the bound.
A program may use at most 128 MiB of HBM per device.

```python
import math
import jax
import jax.numpy as jnp
from jax import lax

D = 1024
HEADS = 32
HEAD_DIM = 64
STATE = 128
CONV = 4
BLOCK = 256
SCENES = 4
TOK_DEV = 512
INNER = 2048
TOKENS = 4096


def draw_scene_lengths(key, part):
    key = jax.random.fold_in(key, 7)
    first_key, second_key = jax.random.split(key)
    shorter = jax.random.randint(first_key, (SCENES,), 1, TOK_DEV // 4 + 1, dtype=jnp.int32)
    chosen = jax.random.randint(second_key, (), 0, SCENES, dtype=jnp.int32)
    order = jnp.arange(SCENES, dtype=jnp.int32)
    others = jnp.sum(jnp.where(order == chosen, 0, shorter)).astype(jnp.int32)
    return jnp.where(order == chosen, TOKENS - others, shorter).astype(jnp.int32)


def shard_levels(key, dims, cuts, low, high):
    factor_of = 1.0
    for dim, blocks in cuts:
        steps = jax.random.uniform(jax.random.fold_in(jax.random.fold_in(key, 6), dim), (blocks,), jnp.float32, low / len(cuts), high / len(cuts))
        factor_of = factor_of * jnp.repeat(jnp.exp(steps), dims[dim] // blocks).reshape((-1,) + (1,) * (len(dims) - 1 - dim))
    return factor_of


def noise(stream_key, dims, spread, most, cuts=(), kind=jnp.bfloat16):
    values = spread * jax.random.normal(stream_key, dims, jnp.float32)
    if cuts:
        values = values * shard_levels(stream_key, dims, cuts, -0.22, 0.18)
    return jnp.clip(values, -most, most).astype(kind)


def setup_inputs(seed: int = 0) -> dict:
    seeds = jax.random.split(jax.random.key(seed), 18)
    return {
        "block_input": noise(seeds[0], (TOKENS, D), 1.0, 6.0, ((0, 8),)),
        "scene_lengths": draw_scene_lengths(jax.random.fold_in(seeds[17], 71), 0),
        "input_gain": jnp.clip(1.0 + 0.1 * jax.random.normal(seeds[2], (D,), jnp.float32), 0.5, 1.5),
        "gate_weight": noise(seeds[3], (D, INNER), D ** -0.5, 0.1875, ((1, 4),)),
        "inner_weight": noise(seeds[4], (D, INNER), D ** -0.5, 0.1875, ((1, 4),)),
        "state_weight": noise(seeds[5], (D, 2 * STATE), D ** -0.5, 0.1875, ((1, 4),)),
        "step_weight": noise(seeds[6], (D, HEADS), D ** -0.5, 0.1875, ((1, 4),)),
        "step_bias": jnp.clip(-1.5 + 2.5 * jax.random.uniform(seeds[7], (HEADS,), jnp.float32) ** shard_levels(seeds[7], (HEADS,), ((0, 4),), -0.2, 0.2), -1.5, 1.0),
        "rate_log": jnp.clip(-9.0 + 5.5 * jax.random.uniform(seeds[8], (HEADS,), jnp.float32) ** shard_levels(seeds[8], (HEADS,), ((0, 4),), -0.2, 0.2), -9.0, -3.5),
        "inner_kernel": noise(seeds[9], (CONV, INNER), CONV ** -0.5, 3.0, ((1, 4),), jnp.float32),
        "inner_conv_bias": noise(seeds[10], (INNER,), 0.3, 2.0, ((0, 4),), jnp.float32),
        "state_kernel": noise(seeds[11], (CONV, 2 * STATE), CONV ** -0.5, 3.0, ((1, 4),), jnp.float32),
        "state_conv_bias": noise(seeds[12], (2 * STATE,), 0.3, 2.0, ((0, 4),), jnp.float32),
        "skip_scale": jnp.clip(jnp.exp(math.log(8.0) - 2.0794415 * jax.random.uniform(seeds[13], (HEADS,), jnp.float32) ** shard_levels(seeds[13], (HEADS,), ((0, 4),), -0.2, 0.2)), 1.0, 8.0),
        "gate_gain": jnp.clip(1.0 + 0.1 * jax.random.normal(seeds[14], (INNER,), jnp.float32), 0.5, 1.5),
        "out_weight": noise(seeds[15], (INNER, D), INNER ** -0.5, 0.125, ((0, 4),)),
        "out_cotangent": noise(seeds[16], (TOKENS, D), 1.0, 6.0, ((0, 8),)),
    }


epsilon = 1e-05
highest = lax.Precision.HIGHEST

@jax.custom_vjp
def low(v):
    return lax.optimization_barrier(v.astype(jnp.bfloat16)).astype(jnp.float32)

@jax.custom_vjp
def low_back(v):
    return v

def low_keep(v):
    return (low(v), None)

def low_pass(kept, grad):
    return (grad,)

def back_keep(v):
    return (v, None)

def back_low(kept, grad):
    return (low(grad),)
low.defvjp(low_keep, low_pass)
low_back.defvjp(back_keep, back_low)

def segment_ids(scene_lengths, positions):
    scene_starts = (jnp.cumsum(scene_lengths) - scene_lengths).astype(jnp.int32)
    started = (positions[:, None] >= scene_starts[None, :]).astype(jnp.int32)
    return (lax.optimization_barrier(jnp.sum(started, axis=1)) - 1).astype(jnp.int32)

def reset_flags(scene_lengths, positions):
    scene_starts = (jnp.cumsum(scene_lengths) - scene_lengths).astype(jnp.int32)
    return lax.optimization_barrier(jnp.sum((positions[:, None] == scene_starts[None, :]).astype(jnp.float32), axis=1))

def causal_conv(extended, kernel_taps, conv_bias, segment_ext, segment_now):
    length_now = segment_now.shape[0]
    result = jnp.zeros((length_now, extended.shape[1]), jnp.float32) + conv_bias[None, :]
    for offset in range(kernel_taps.shape[0]):
        window = extended[offset:offset + length_now]
        agrees = (segment_ext[offset:offset + length_now] == segment_now).astype(jnp.float32)
        result = result + kernel_taps[offset][None, :] * window * agrees[:, None]
    return result

def block_step(carried, pieces):
    values_in, keys_in, queries_in, step_in, decay_in, flag_in = pieces
    length_now = flag_in.shape[0]
    cumulative = jnp.cumsum(decay_in, axis=0)
    segment = jnp.cumsum(flag_in)
    position = jnp.arange(length_now)
    matches = ((segment[:, None] == segment[None, :]) & (position[:, None] >= position[None, :])).astype(jnp.float32)
    matches_wide = matches[:, :, None]
    difference = cumulative[:, None, :] - cumulative[None, :, :]
    decay_matrix = jnp.exp(jnp.where(matches_wide > 0.0, difference, 0.0)) * matches_wide
    scores = jnp.dot(queries_in, keys_in.T, precision=highest)
    weights = decay_matrix * scores[:, :, None] * step_in[None, :, :]
    result = jnp.einsum('ijh,jhp->ihp', weights, values_in, precision=highest)
    clean = (segment == 0.0).astype(jnp.float32)
    entering = jnp.exp(cumulative) * clean[:, None]
    result = result + entering[:, :, None] * jnp.einsum('in,hpn->ihp', queries_in, carried, precision=highest)
    tailing = (segment == segment[length_now - 1]).astype(jnp.float32)
    carry_weight = jnp.exp(cumulative[length_now - 1][None, :] - cumulative) * tailing[:, None] * step_in
    fresh = jnp.einsum('jh,jhp,jn->hpn', carry_weight, values_in, keys_in, precision=highest)
    return (entering[length_now - 1][:, None, None] * carried + fresh, result)

def forward(x_rows, input_gain, gate_weight, inner_weight, state_weight, step_weight, step_bias, rate_log, inner_kernel, inner_conv_bias, state_kernel, state_conv_bias, skip_scale, gate_gain, out_weight, segment_ext, segment_now, resets):
    inverse = lax.rsqrt(lax.optimization_barrier(jnp.mean(x_rows * x_rows, axis=1, keepdims=True)) + epsilon)
    normed = low(x_rows * inverse * input_gain)
    gate_pre = low_back(jnp.dot(normed, gate_weight, precision=highest))
    inner_pre = low_back(jnp.dot(normed, inner_weight, precision=highest))
    state_pre = low_back(jnp.dot(normed, state_weight, precision=highest))
    step_pre = low_back(jnp.dot(normed, step_weight, precision=highest))
    rim_rows = CONV - 1
    inner_ext = jnp.concatenate([jnp.zeros((rim_rows, INNER), jnp.float32), inner_pre], axis=0)
    state_ext = jnp.concatenate([jnp.zeros((rim_rows, 2 * STATE), jnp.float32), state_pre], axis=0)
    inner_act = low(jax.nn.silu(causal_conv(inner_ext, inner_kernel, inner_conv_bias, segment_ext, segment_now)))
    state_act = low(jax.nn.silu(causal_conv(state_ext, state_kernel, state_conv_bias, segment_ext, segment_now)))
    step_size = jax.nn.softplus(step_pre + step_bias)
    log_decay = step_size * -jnp.exp(rate_log)
    blocks = TOKENS // BLOCK
    pieces = (inner_act.reshape(blocks, BLOCK, HEADS, HEAD_DIM), state_act[:, :STATE].reshape(blocks, BLOCK, STATE), state_act[:, STATE:].reshape(blocks, BLOCK, STATE), step_size.reshape(blocks, BLOCK, HEADS), log_decay.reshape(blocks, BLOCK, HEADS), resets.reshape(blocks, BLOCK))
    start_state = jnp.zeros((HEADS, HEAD_DIM, STATE), jnp.float32)
    final_state, mixed_heads = lax.scan(jax.checkpoint(block_step), start_state, pieces)
    heads_out = mixed_heads.reshape(TOKENS, HEADS, HEAD_DIM) + skip_scale[None, :, None] * inner_act.reshape(TOKENS, HEADS, HEAD_DIM)
    gated = heads_out.reshape(TOKENS, INNER) * jax.nn.silu(gate_pre)
    gate_inverse = lax.rsqrt(lax.optimization_barrier(jnp.mean(gated * gated, axis=1, keepdims=True)) + epsilon)
    gated_norm = low(gated * gate_inverse * gate_gain)
    return x_rows + jnp.dot(gated_norm, out_weight, precision=highest)

def reference(block_input, scene_lengths, input_gain, gate_weight, inner_weight, state_weight, step_weight, step_bias, rate_log, inner_kernel, inner_conv_bias, state_kernel, state_conv_bias, skip_scale, gate_gain, out_weight, out_cotangent):
    positions = jnp.arange(TOKENS, dtype=jnp.int32)
    ext_positions = jnp.arange(-(CONV - 1), TOKENS, dtype=jnp.int32)
    segment_now = segment_ids(scene_lengths, positions)
    segment_ext = segment_ids(scene_lengths, ext_positions)
    resets = reset_flags(scene_lengths, positions)
    floats = tuple((array_in.astype(jnp.float32) for array_in in (block_input, input_gain, gate_weight, inner_weight, state_weight, step_weight, step_bias, rate_log, inner_kernel, inner_conv_bias, state_kernel, state_conv_bias, skip_scale, gate_gain, out_weight)))

    def forward_all(*params):
        return forward(*params, segment_ext, segment_now, resets)
    result, pullback = jax.vjp(forward_all, *floats)
    gradients = pullback(out_cotangent.astype(jnp.float32))
    return (result.astype(jnp.bfloat16), gradients[0], gradients[1], gradients[2], gradients[3], gradients[4], gradients[5], gradients[6], gradients[7], gradients[8], gradients[9], gradients[10], gradients[11], gradients[12], gradients[13], gradients[14])
```

```python
import contextlib
import functools
import types

import jax
import jax.numpy as jnp
from jax import lax
from jax.experimental import pallas as pl
from jax.experimental.pallas import tpu as pltpu
from jax.sharding import PartitionSpec as P

STATE = 128
CONV = 4
CHUNK = 256
LANES = 128
PAD = 8
ROWS = 64
epsilon = 1e-05
bf = jnp.bfloat16
f32 = jnp.float32
i32 = jnp.int32
MESH = pl.DeviceIdType.MESH


def dg(left, right, left_dim, right_dim):
    return lax.dot_general(
        left, right, (((left_dim,), (right_dim,)), ((), ())), preferred_element_type=f32
    )


def split3(v):
    high = v.astype(bf).astype(f32)
    middle = (v - high).astype(bf).astype(f32)
    return jnp.concatenate([high, middle, v - high - middle], axis=0).astype(bf)


def fold3(v):
    third = v.shape[0] // 3
    return v[:third] + v[third : 2 * third] + v[2 * third :]


def halves(v):
    high = v.astype(bf)
    return high, (v - high.astype(f32)).astype(bf)


def slope(v):
    s = jax.nn.sigmoid(v)
    return s * (1.0 + v * (1.0 - s))


def fold8(v):
    total = v[0:8]
    for i in range(1, v.shape[0] // 8):
        total = total + v[8 * i : 8 * i + 8]
    return total


def iota(shape, dim):
    return lax.broadcasted_iota(i32, shape, dim)


def kernel(sizes, names, *refs):
    r = types.SimpleNamespace(**dict(zip(names, refs)))
    n_seq, n_tp, T, D, HI, H, NS = sizes
    N = STATE
    P_ = HI // H
    Q = CHUNK
    NC = T // Q
    NP = HI // LANES
    R = HI // n_seq
    R2 = D // n_seq
    total_tokens = T * n_seq
    seq = lax.axis_index("seq")
    tp = lax.axis_index("tp")

    barrier = pltpu.get_barrier_semaphore()
    for d in range(1, n_seq):
        pl.semaphore_signal(
            barrier, inc=1, device_id=((seq + d) % n_seq, tp), device_id_type=MESH
        )
    for d in range(1, n_tp):
        pl.semaphore_signal(
            barrier, inc=1, device_id=(seq, (tp + d) % n_tp), device_id_type=MESH
        )

    waits = []
    marks = contextlib.ExitStack()

    def stage(name):
        marks.close()
        marks.enter_context(jax.named_scope(name))

    stage("norm")

    def remote(src, dst, send, recv, device):
        return pltpu.make_async_remote_copy(
            src_ref=src,
            dst_ref=dst,
            send_sem=send,
            recv_sem=recv,
            device_id=device,
            device_id_type=MESH,
        )

    def spread(axis, src_to, dst_from, send, recv):
        n = n_seq if axis == "seq" else n_tp
        me = seq if axis == "seq" else tp
        incoming = []
        for d in range(1, n):
            target = (me + d) % n
            source = (me + n - d) % n
            device = (target, tp) if axis == "seq" else (seq, target)
            out = remote(src_to(target), dst_from(me), send.at[d - 1], recv.at[d - 1], device)
            out.start()
            waits.append(out)
            incoming.append(
                remote(src_to(target), dst_from(source), send.at[d - 1], recv.at[d - 1], device)
            )

        def wait():
            for copy in incoming:
                copy.wait_recv()

        return wait

    starts = [jnp.int32(0)]
    for k in range(r.scene_lengths.shape[0] - 1):
        starts.append(starts[-1] + r.scene_lengths[k])

    def segment(position):
        found = (position >= starts[0]).astype(i32)
        for s in starts[1:]:
            found = found + (position >= s).astype(i32)
        return found

    first_token = seq * T

    def norm_rows(i, _):
        rows = pl.ds(pl.multiple_of(i * ROWS, ROWS), ROWS)
        x = r.block_input[rows, :].astype(f32)
        inverse = lax.rsqrt(jnp.mean(x * x, axis=1, keepdims=True) + epsilon)
        r.inverse[rows, :] = jnp.broadcast_to(inverse, (ROWS, LANES))
        r.normed[rows, :] = (x * inverse * r.input_gain[...].reshape(1, D)).astype(bf)
        return 0

    lax.fori_loop(0, T // ROWS, norm_rows, 0)

    stage("projections")
    r.misc_weight[...] = jnp.zeros_like(r.misc_weight)
    r.misc_weight[0:NS, :] = r.state_weight[...]
    r.misc_weight[NS : NS + H, :] = r.step_weight[...]
    normed_all = r.normed[...]
    for j in range(HI // 256):
        cols = slice(256 * j, 256 * j + 256)
        value = dg(normed_all, r.inner_weight[:, cols], 1, 0)
        r.inner_ext[2 * j, PAD : PAD + T, :] = value[:, :LANES]
        r.inner_ext[2 * j + 1, PAD : PAD + T, :] = value[:, LANES:]
    r.misc_ext[0, PAD : PAD + T, :] = dg(normed_all, r.misc_weight[...], 1, 1)

    stage("barrier")
    pl.semaphore_wait(barrier, n_seq - 1 + n_tp - 1)
    stage("gate_projection")
    right = ((seq + 1) % n_seq, tp)
    left = ((seq + n_seq - 1) % n_seq, tp)
    rim = [
        remote(
            ref.at[:, pl.ds(T, PAD)],
            ref.at[:, pl.ds(0, PAD)],
            r.rim_send.at[k],
            r.rim_recv.at[k],
            right,
        )
        for k, ref in enumerate((r.inner_ext, r.misc_ext))
    ]
    for copy in rim:
        copy.start()
    waits.extend(rim)
    for j in range(HI // 256):
        cols = slice(256 * j, 256 * j + 256)
        r.gate_pre[:, cols] = dg(normed_all, r.gate_weight[:, cols], 1, 0)

    stage("convolutions")
    def agreements(base, rows):
        position = first_token + base + iota((rows, LANES), 0)
        now = segment(position)
        return [segment(position - (CONV - 1) + k) == now for k in range(CONV - 1)]

    def conv_block(ext, taps, bias, base, lanes, masks):
        value = bias[:, lanes]
        for k in range(CONV):
            window = ext[pl.ds(base + PAD - CONV + 1 + k, ROWS), :]
            term = taps[k : k + 1, lanes] * window
            value = value + (term if k == CONV - 1 else jnp.where(masks[k], term, 0.0))
        return value

    r.misc_taps[...] = jnp.zeros_like(r.misc_taps)
    r.misc_taps[0:CONV, 0:NS] = r.state_kernel[...]
    r.misc_taps[CONV : CONV + 1, 0:NS] = r.state_conv_bias[...].reshape(1, NS)
    r.inner_bias[...] = r.inner_conv_bias[...].reshape(1, HI)
    stage("rim_wait")
    for copy in rim:
        copy.wait_recv()
    stage("conv")

    def misc_conv_rows(i, _):
        base = pl.multiple_of(i * ROWS, ROWS)
        masks = agreements(base, ROWS)
        taps = r.misc_taps[...]
        value = conv_block(
            r.misc_ext.at[0], taps, taps[CONV : CONV + 1], base, slice(0, LANES), masks
        )
        r.misc_conv[pl.ds(base, ROWS), :] = value
        return 0

    lax.fori_loop(0, T // ROWS, misc_conv_rows, 0)
    low_lanes = iota((T // 2, LANES), 1) < NS
    own = r.misc_conv[...]
    own = own * jax.nn.sigmoid(own)
    r.state_send[...] = jnp.where(
        low_lanes, own[: T // 2], pltpu.roll(own[T // 2 :], NS, 1)
    ).astype(bf)
    r.state_recv[tp] = r.state_send[...]
    state_wait = spread(
        "tp",
        lambda t: r.state_send,
        lambda t: r.state_recv.at[t],
        r.state_ss,
        r.state_rs,
    )

    def inner_conv_rows(i, _):
        base = pl.multiple_of(i * ROWS, ROWS)
        rows = pl.ds(base, ROWS)
        masks = agreements(base, ROWS)
        taps = r.inner_kernel[...]
        for g in range(NP):
            lanes = slice(g * LANES, g * LANES + LANES)
            value = conv_block(r.inner_ext.at[g], taps, r.inner_bias, base, lanes, masks)
            r.inner_conv[rows, lanes] = value
            r.act[rows, lanes] = (value * jax.nn.sigmoid(value)).astype(bf)
        return 0

    lax.fori_loop(0, T // ROWS, inner_conv_rows, 0)

    stage("decays")
    eye = iota((H, H), 0) == iota((H, H), 1)

    def column(ref):
        wide = jnp.broadcast_to(ref[...].reshape(1, H), (H, H))
        return jnp.sum(jnp.where(eye, wide, 0.0), axis=1, keepdims=True)

    step_in = r.misc_ext[0, PAD : PAD + T, :].T[NS : NS + H, :] + column(r.step_bias)
    step = jnp.maximum(step_in, 0.0) + jnp.log1p(jnp.exp(-jnp.abs(step_in)))
    rate = jnp.exp(column(r.rate_log))
    log_decay = step * -rate
    r.sigmoid_step[...] = jax.nn.sigmoid(step_in)
    r.log_decay[...] = log_decay
    r.step_rows[...] = step
    r.upto[...] = (iota((Q, Q), 0) <= iota((Q, Q), 1)).astype(f32).astype(bf)
    r.expand[...] = (iota((3 * H, HI), 0) % H == iota((3 * H, HI), 1) // P_).astype(f32).astype(bf)
    expand = r.expand[...]

    entering, tailing, chunk_decay = [], [], []
    ones_rows = jnp.ones((1, Q), f32)
    for c in range(NC):
        cols = slice(c * Q, c * Q + Q)
        cumulative = fold3(dg(split3(log_decay[:, cols]), r.upto[...], 1, 0))
        start = first_token + c * Q
        seg_row = segment(start + iota((H, Q), 1))
        seg_before = segment(start - 1)
        seg_end = segment(start + Q - 1)
        last = cumulative[:, Q - 1 : Q]
        enter = jnp.where(seg_row == seg_before, jnp.exp(cumulative), 0.0)
        tail = jnp.where(seg_row == seg_end, jnp.exp(last - cumulative), 0.0)
        entering.append(enter)
        tailing.append(tail)
        chunk_decay.append(enter[:, Q - 1 : Q])
        seg_col = segment(start + iota((Q, Q), 0))
        seg_lane = segment(start + iota((Q, Q), 1))
        keep = (seg_col == seg_lane) & (iota((Q, Q), 0) >= iota((Q, Q), 1))
        r.mask[c] = jnp.where(keep, 0.0, -1e30)
        high = cumulative.astype(bf).astype(f32)
        middle = (cumulative - high).astype(bf).astype(f32)
        rest = cumulative - high - middle
        which = iota((16, Q), 0)
        for h in range(H):
            parts = jnp.where(
                which % 3 == 0,
                high[h : h + 1],
                jnp.where(which % 3 == 1, middle[h : h + 1], rest[h : h + 1]),
            )
            first = which < 3
            second = (which >= 3) & (which < 6)
            r.cum_left[h, :, cols] = jnp.where(
                first, parts, jnp.where(second, 1.0, 0.0)
            ).astype(bf)
            r.cum_right[h, :, cols] = jnp.where(
                first, 1.0, jnp.where(second, -parts, 0.0)
            ).astype(bf)

    def wide(v):
        return dg(split3(v), expand, 0, 0)

    def wide_rows(v):
        return dg(expand, split3(jnp.broadcast_to(v, (H, LANES))), 0, 0)

    for c in range(NC):
        rows = slice(c * Q, c * Q + Q)
        r.step_wide[rows, :] = wide(step[:, rows])
        r.enter_wide[rows, :] = wide(entering[c])
        r.tail_wide[rows, :] = wide(tailing[c])
        r.decay_wide[c] = wide_rows(chunk_decay[c])
    r.skip_wide[...] = dg(split3(jnp.broadcast_to(column(r.skip_scale), (H, 8))), expand, 0, 0)

    def scaled_rows(i, _):
        rows = pl.ds(pl.multiple_of(i * ROWS, ROWS), ROWS)
        x = r.act[rows, :].astype(f32)
        r.xt[rows, :], r.xt_rest[rows, :] = halves(x * r.step_wide[rows, :] * r.tail_wide[rows, :])
        return 0

    lax.fori_loop(0, T // ROWS, scaled_rows, 0)

    stage("keys_wait")
    state_wait()
    shards = n_tp // 2
    half_low = iota((T // 2, LANES), 1) < NS
    for ref, at in ((r.keys, 0), (r.queries, shards)):
        one, two = r.state_recv[at].astype(f32), r.state_recv[at + 1].astype(f32)
        ref[0 : T // 2, :] = jnp.where(half_low, one, pltpu.roll(two, NS, 1)).astype(bf)
        ref[T // 2 : T, :] = jnp.where(half_low, pltpu.roll(one, NS, 1), two).astype(bf)

    stage("end_states")
    end_state = None
    device_decay = None
    for c in range(NC):
        rows = slice(c * Q, c * Q + Q)
        keys = r.keys[rows, :]
        fresh = dg(r.xt[rows, :], keys, 0, 0) + dg(r.xt_rest[rows, :], keys, 0, 0)
        r.fresh[c] = fresh
        end_state = fresh if c == 0 else r.decay_wide[c] * end_state + fresh
        device_decay = chunk_decay[c] if c == 0 else device_decay * chunk_decay[c]
    r.end_send[...] = end_state
    r.decay_send[...] = jnp.broadcast_to(device_decay, (H, LANES))

    def block(ref, device):
        return ref.at[pl.ds(pl.multiple_of(device * R, R), R)]

    r.end_recv[seq] = r.end_send[pl.ds(pl.multiple_of(seq * R, R), R), :]
    r.decay_recv[seq] = r.decay_send[...]
    decay_wait = spread(
        "seq", lambda d: r.decay_send, lambda d: r.decay_recv.at[d], r.decay_ss, r.decay_rs
    )
    end_wait = spread(
        "seq", lambda d: block(r.end_send, d), lambda d: r.end_recv.at[d], r.end_ss, r.end_rs
    )

    stage("inside")
    for c in range(NC):
        rows = slice(c * Q, c * Q + Q)
        r.scores[c] = dg(r.queries[rows, :], r.keys[rows, :], 1, 1)
    low = iota((Q, LANES), 1) < P_

    def inside(i, _):
        c = i // NP
        p = i % NP
        rows = pl.ds(pl.multiple_of(c * Q, Q), Q)
        lanes = pl.ds(pl.multiple_of(p * LANES, LANES), LANES)
        x = r.act[rows, lanes]
        zero = jnp.zeros_like(x)
        result = None
        for s in range(2):
            h = 2 * p + s
            difference = dg(r.cum_left[h, :, rows], r.cum_right[h, :, rows], 0, 0)
            decay = jnp.exp(difference + r.mask[c])
            r.decays[c, h] = decay
            weight, rest = halves(decay * r.scores[c] * r.step_rows[pl.ds(h, 1), rows])
            part = jnp.where(low, x, zero) if s == 0 else jnp.where(low, zero, x)
            term = dg(weight, part, 1, 0) + dg(rest, part, 1, 0)
            result = term if s == 0 else result + term
        r.mixed[rows, lanes] = result
        return 0

    lax.fori_loop(0, NC * NP, inside, 0)
    for j in range(HI // 256):
        cols = slice(256 * j, 256 * j + 256)
        r.norm_grad[:, cols] = dg(r.out_cotangent[...], r.out_weight[cols, :], 1, 1)

    stage("entering")
    head_of = (seq * R) // P_
    stage("end_wait")
    end_wait()
    decay_wait()

    def decay_of(d):
        return jnp.broadcast_to(r.decay_recv[d, pl.ds(head_of, 1), :], (R, LANES))

    running = jnp.zeros((R, N), f32)
    for d in range(n_seq):
        r.enter_send[d] = running
        running = decay_of(d) * running + r.end_recv[d]
    own_rows = pl.ds(pl.multiple_of(seq * R, R), R)
    r.enter_state[own_rows, :] = r.enter_send[seq]
    enter_wait = spread(
        "seq", lambda d: r.enter_send.at[d], lambda d: block(r.enter_state, d), r.enter_ss, r.enter_rs
    )
    stage("enter_wait")
    enter_wait()
    stage("readout")
    for c in range(NC):
        rows = slice(c * Q, c * Q + Q)
        if c == 0:
            state = r.enter_state[...]
        else:
            state = r.decay_wide[c - 1] * state + r.fresh[c - 1]
        r.state_in[c] = state
        r.state_in_low[c], r.state_in_rest[c] = halves(state)
        for j in range(HI // 256):
            cols = slice(256 * j, 256 * j + 256)
            queries = r.queries[rows, :]
            read = dg(queries, r.state_in_low[c, cols, :], 1, 1) + dg(queries, r.state_in_rest[c, cols, :], 1, 1)
            r.mixed[rows, cols] = r.mixed[rows, cols] + r.enter_wide[rows, cols] * read

    stage("gated")
    skip_row = r.skip_wide[0:1, :]
    r.gain_row[...] = r.gate_gain[...].reshape(1, HI)

    def gated_rows(i, _):
        rows = pl.ds(pl.multiple_of(i * ROWS, ROWS), ROWS)
        heads = r.mixed[rows, :] + skip_row * r.act[rows, :].astype(f32)
        gate = r.gate_pre[rows, :]
        gated = heads * (gate * jax.nn.sigmoid(gate))
        r.heads_out[rows, :] = heads
        r.gated[rows, :] = gated
        scaled = r.norm_grad[rows, :] * r.gain_row[...]
        squares = gated * gated
        products = scaled * gated

        def lane_sum(v):
            total = v[:, :LANES]
            for g in range(1, NP):
                total = total + v[:, g * LANES : g * LANES + LANES]
            return total

        r.squares[rows, :] = lane_sum(squares)
        r.products[rows, :] = lane_sum(products)
        return 0

    lax.fori_loop(0, T // ROWS, gated_rows, 0)
    square_row = jnp.sum(r.squares[...].T, axis=0, keepdims=True)
    product_row = jnp.sum(r.products[...].T, axis=0, keepdims=True)
    r.sums_send[...] = jnp.where(
        iota((8, T), 0) == 0,
        jnp.broadcast_to(square_row, (8, T)),
        jnp.broadcast_to(product_row, (8, T)),
    )
    r.sums_recv[tp] = r.sums_send[...]
    sums_wait = spread(
        "tp", lambda t: r.sums_send, lambda t: r.sums_recv.at[t], r.sums_ss, r.sums_rs
    )
    stage("sums_wait")
    sums_wait()
    stage("sums")
    sums = r.sums_recv[0]
    for t in range(1, n_tp):
        sums = sums + r.sums_recv[t]
    count = HI * n_tp
    norm_row = lax.rsqrt(sums[0:1] / count + epsilon)
    back_row = norm_row * norm_row * norm_row * (sums[1:2] / count)
    r.norm_col[...] = jnp.broadcast_to(norm_row, (LANES, T)).T
    r.back_col[...] = jnp.broadcast_to(back_row, (LANES, T)).T

    stage("back_gated")
    r.head_sum[...] = (iota((HI, LANES), 0) // P_ == iota((HI, LANES), 1)).astype(f32).astype(bf)
    r.sum_acc[...] = jnp.zeros_like(r.sum_acc)

    def tile4(v):
        return jnp.concatenate([v] * NP, axis=1)

    def summed(v, which):
        high, lowv = halves(v)
        return dg(high, which, 1, 0) + dg(lowv, which, 1, 0)

    def back_rows(i, _):
        rows = pl.ds(pl.multiple_of(i * ROWS, ROWS), ROWS)
        norm = tile4(r.norm_col[rows, :])
        back = tile4(r.back_col[rows, :])
        gated = r.gated[rows, :]
        grad = r.norm_grad[rows, :]
        gain = r.gain_row[...]
        gate = r.gate_pre[rows, :]
        sigma = jax.nn.sigmoid(gate)
        unit = gated * norm
        r.gated_norm[rows, :] = (unit * gain).astype(bf)
        r.sum_acc[0] = r.sum_acc[0] + fold8(grad * unit)
        gated_grad = norm * (grad * gain) - gated * back
        heads_grad = gated_grad * (gate * sigma)
        heads = r.heads_out[rows, :]
        r.gate_grad[rows, :] = (
            gated_grad * heads * (sigma * (1.0 + gate * (1.0 - sigma)))
        ).astype(bf)
        r.heads_grad[rows, :] = heads_grad
        x = r.act[rows, :].astype(f32)
        r.sum_acc[1] = r.sum_acc[1] + fold8(heads_grad * x)
        r.dy[rows, :], r.dy_rest[rows, :] = halves(heads_grad)
        r.dy_enter[rows, :], r.dy_enter_rest[rows, :] = halves(heads_grad * r.enter_wide[rows, :])
        r.sum_y[rows, :] = summed(heads_grad * r.mixed[rows, :], r.head_sum[...])
        return 0

    lax.fori_loop(0, T // ROWS, back_rows, 0)

    stage("grad_states")
    grad_in = None
    for c in reversed(range(NC)):
        rows = slice(c * Q, c * Q + Q)
        queries = r.queries[rows, :]
        local = dg(r.dy_enter[rows, :], queries, 0, 0) + dg(r.dy_enter_rest[rows, :], queries, 0, 0)
        r.grad_local[c] = local
        grad_in = local if grad_in is None else r.decay_wide[c] * grad_in + local
    r.grad_send[...] = grad_in
    r.grad_recv[seq] = r.grad_send[own_rows, :]
    grad_wait = spread(
        "seq", lambda d: block(r.grad_send, d), lambda d: r.grad_recv.at[d], r.grad_ss, r.grad_rs
    )
    for j in range(D // 256):
        cols = slice(256 * j, 256 * j + 256)
        r.branch[:, cols] = dg(r.gated_norm[...], r.out_weight[:, cols], 1, 0).astype(bf)

    r.score_grad[...] = jnp.zeros_like(r.score_grad)

    def inside_back(i, _):
        c = i // NP
        p = i % NP
        rows = pl.ds(pl.multiple_of(c * Q, Q), Q)
        lanes = pl.ds(pl.multiple_of(p * LANES, LANES), LANES)
        x = r.act[rows, lanes]
        dy = r.dy[rows, lanes]
        dy_rest = r.dy_rest[rows, lanes]
        zero = jnp.zeros_like(dy)
        result = None
        for s in range(2):
            h = 2 * p + s
            decay = r.decays[c, h]
            weight, rest = halves(decay * r.scores[c])

            def masked(v):
                return jnp.where(low, v, zero) if s == 0 else jnp.where(low, zero, v)

            part, part_rest = masked(dy), masked(dy_rest)
            pairs = dg(part, x, 1, 1) + dg(part_rest, x, 1, 1)
            r.score_grad[c] = r.score_grad[c] + pairs * (decay * r.step_rows[pl.ds(h, 1), rows])
            term = dg(weight, part, 0, 0) + dg(rest, part, 0, 0) + dg(weight, part_rest, 0, 0)
            result = term if s == 0 else result + term
        r.x_inside[rows, lanes] = result
        return 0

    lax.fori_loop(0, NC * NP, inside_back, 0)

    stage("grad_wait")
    grad_wait()
    stage("leave_scan")
    running = jnp.zeros((R, N), f32)
    for d in reversed(range(n_seq)):
        r.leave_send[d] = running
        running = decay_of(d) * running + r.grad_recv[d]
    r.leave_grad[own_rows, :] = r.leave_send[seq]
    leave_wait = spread(
        "seq", lambda d: r.leave_send.at[d], lambda d: block(r.leave_grad, d), r.leave_ss, r.leave_rs
    )

    stage("weights_one")
    def weight_rows(i, _):
        cols = pl.ds(pl.multiple_of(i * LANES, LANES), LANES)
        r.wg_one[cols, 0:HI] = dg(r.normed[:, cols], r.gate_grad[...], 0, 0).astype(bf)
        r.wg_one[cols, HI : 2 * HI] = dg(r.out_cotangent[:, cols], r.gated_norm[...], 0, 0).astype(bf)
        return 0

    lax.fori_loop(0, D // LANES, weight_rows, 0)

    def part_of(ref, device):
        return ref.at[pl.ds(pl.multiple_of(device * R2, R2), R2)]

    mine = pl.ds(pl.multiple_of(seq * R2, R2), R2)
    r.wg_one_recv[seq] = r.wg_one[mine, :]
    wg_one_wait = spread(
        "seq", lambda d: part_of(r.wg_one, d), lambda d: r.wg_one_recv.at[d], r.wg1_ss, r.wg1_rs
    )

    stage("leave_wait")
    leave_wait()
    stage("leave")
    carry_terms = [None] * NC
    for c in reversed(range(NC)):
        rows = slice(c * Q, c * Q + Q)
        if c == NC - 1:
            grad = r.leave_grad[...]
        else:
            grad = r.decay_wide[c + 1] * grad + r.grad_local[c + 1]
        grad_low, grad_rest = halves(grad)
        keys, queries = r.keys[rows, :], r.queries[rows, :]
        for j in range(HI // 256):
            cols = slice(256 * j, 256 * j + 256)
            read = dg(keys, grad_low[cols, :], 1, 1) + dg(keys, grad_rest[cols, :], 1, 1)
            r.x_carry[rows, cols] = r.tail_wide[rows, cols] * read
        high, lowv = halves(grad * r.state_in[c])
        pair = dg(expand[0:H], high, 1, 0) + dg(expand[0:H], lowv, 1, 0)
        carry_terms[c] = chunk_decay[c] * jnp.sum(pair, axis=1, keepdims=True)
        score_low, score_rest = halves(r.score_grad[c])
        r.query_grad[rows, :] = (
            dg(score_low, keys, 1, 0)
            + dg(score_rest, keys, 1, 0)
            + dg(r.dy_enter[rows, :], r.state_in_low[c], 1, 0)
            + dg(r.dy_enter_rest[rows, :], r.state_in_low[c], 1, 0)
            + dg(r.dy_enter[rows, :], r.state_in_rest[c], 1, 0)
        )
        r.key_grad[rows, :] = (
            dg(score_low, queries, 0, 0)
            + dg(score_rest, queries, 0, 0)
            + dg(r.xt[rows, :], grad_low, 1, 0)
            + dg(r.xt_rest[rows, :], grad_low, 1, 0)
            + dg(r.xt[rows, :], grad_rest, 1, 0)
        )

    stage("shared")
    for k, ref in enumerate((r.key_grad, r.query_grad)):
        top, bottom = ref[0 : T // 2, :], ref[T // 2 : T, :]
        r.shared_send[k * shards] = jnp.where(half_low, top, pltpu.roll(bottom, NS, 1))
        r.shared_send[k * shards + 1] = jnp.where(half_low, pltpu.roll(top, NS, 1), bottom)
    r.shared_recv[tp] = r.shared_send[tp]
    shared_wait = spread(
        "tp", lambda t: r.shared_send.at[t], lambda t: r.shared_recv.at[t], r.shared_ss, r.shared_rs
    )

    stage("x_grads")
    r.head_sum_two[...] = (
        iota((HI, LANES), 0) // P_ + H == iota((HI, LANES), 1)
    ).astype(f32).astype(bf)
    r.head_sum_three[...] = (
        iota((HI, LANES), 0) // P_ + 2 * H == iota((HI, LANES), 1)
    ).astype(f32).astype(bf)

    def x_rows(i, _):
        rows = pl.ds(pl.multiple_of(i * ROWS, ROWS), ROWS)
        x = r.act[rows, :].astype(f32)
        z = r.x_inside[rows, :]
        carried = r.x_carry[rows, :]
        both = z + carried
        step_rows = r.step_wide[rows, :]
        xs = x * step_rows
        x_grad = step_rows * both + skip_row * r.heads_grad[rows, :]
        conv_grad = x_grad * slope(r.inner_conv[rows, :])
        for g in range(NP):
            r.grad_ext[g, rows, :] = conv_grad[:, g * LANES : g * LANES + LANES]
        r.sum_x[rows, :] = (
            summed(x * both, r.head_sum[...])
            + summed(xs * carried, r.head_sum_two[...])
            + summed(xs * z, r.head_sum_three[...])
        )
        return 0

    lax.fori_loop(0, T // ROWS, x_rows, 0)
    halo_one = remote(
        r.grad_ext.at[:, pl.ds(0, PAD)],
        r.grad_ext.at[:, pl.ds(T, PAD)],
        r.halo_send.at[0],
        r.halo_recv.at[0],
        left,
    )
    halo_one.start()
    waits.append(halo_one)

    sums_y = r.sum_y[...].T
    sums_x = r.sum_x[...].T
    step_grad = sums_x[0:H]
    tail_part = sums_x[H : 2 * H]
    pair_part = sums_y[0:H] - sums_x[2 * H : 3 * H]
    decay_grads = []
    for c in range(NC):
        cols = slice(c * Q, c * Q + Q)
        suffix = fold3(dg(split3(pair_part[:, cols]), r.upto[...], 1, 1))
        before = fold3(dg(split3(tail_part[:, cols]), r.upto[...], 1, 0)) - tail_part[:, cols]
        decay_grads.append(suffix + before + carry_terms[c])
    decay_grad = jnp.concatenate(decay_grads, axis=1)
    step_total = step_grad - rate * decay_grad
    step_pre_grad = step_total * r.sigmoid_step[...]
    rate_sum = jnp.sum(r.log_decay[...] * decay_grad, axis=1, keepdims=True)
    bias_sum = jnp.sum(step_pre_grad, axis=1, keepdims=True)
    step_cols = jnp.concatenate(
        [jnp.zeros((NS, T), f32), step_pre_grad, jnp.zeros((LANES - NS - H, T), f32)], axis=0
    ).T

    stage("conv_back")
    def after_masks(base):
        position = first_token + base + iota((ROWS, LANES), 0)
        now = segment(position)
        masks = []
        for k in range(CONV - 1):
            later = position + (CONV - 1) - k
            masks.append((segment(later) == now) & (later < total_tokens))
        return masks

    def conv_back(ext, taps, base, lanes, masks):
        value = None
        for k in range(CONV):
            term = taps[k : k + 1, lanes] * ext[pl.ds(base + CONV - 1 - k, ROWS), :]
            if k < CONV - 1:
                term = jnp.where(masks[k], term, 0.0)
            value = term if value is None else value + term
        return value

    def tap_sums(ext, grad, base, masks):
        sums = []
        for k in range(CONV):
            term = grad * ext[pl.ds(base + PAD - CONV + 1 + k, ROWS), :]
            sums.append(fold8(term if k == CONV - 1 else jnp.where(masks[k], term, 0.0)))
        return sums + [fold8(grad)]

    stage("halo_one_wait")
    halo_one.wait_recv()
    stage("inner_back")

    def inner_back_rows(i, _):
        base = pl.multiple_of(i * ROWS, ROWS)
        rows = pl.ds(base, ROWS)
        masks = after_masks(base)
        before = agreements(base, ROWS)
        taps = r.inner_kernel[...]
        for g in range(NP):
            lanes = slice(g * LANES, g * LANES + LANES)
            r.inner_grad[rows, lanes] = conv_back(r.grad_ext.at[g], taps, base, lanes, masks).astype(bf)
            found = tap_sums(r.inner_ext.at[g], r.grad_ext[g, rows, :], base, before)
            for k, v in enumerate(found):
                r.sum_acc[2 + k, :, lanes] = r.sum_acc[2 + k, :, lanes] + v
        return 0

    lax.fori_loop(0, T // ROWS, inner_back_rows, 0)

    stage("shared_wait")
    shared_wait()
    stage("shared_use")
    packed = r.shared_recv[0]
    for t in range(1, n_tp):
        packed = packed + r.shared_recv[t]
    r.state_grad_ext[0 : T // 2, :] = packed * slope(r.misc_conv[0 : T // 2, :])
    r.state_grad_ext[T // 2 : T, :] = pltpu.roll(packed, NS, 1) * slope(r.misc_conv[T // 2 : T, :])
    halo_two = remote(
        r.state_grad_ext.at[pl.ds(0, PAD)],
        r.state_grad_ext.at[pl.ds(T, PAD)],
        r.halo_send.at[1],
        r.halo_recv.at[1],
        left,
    )
    halo_two.start()
    waits.append(halo_two)
    stage("halo_two_wait")
    halo_two.wait_recv()
    stage("misc_back")
    r.misc_acc[...] = jnp.zeros_like(r.misc_acc)
    r.step_cols[...] = step_cols

    def misc_back_rows(i, _):
        base = pl.multiple_of(i * ROWS, ROWS)
        rows = pl.ds(base, ROWS)
        masks = after_masks(base)
        before = agreements(base, ROWS)
        taps = r.misc_taps[...]
        lanes = slice(0, LANES)
        value = conv_back(r.state_grad_ext, taps, base, lanes, masks)
        value = jnp.where(iota((ROWS, LANES), 1) < NS, value, r.step_cols[rows, :])
        r.misc_grad[rows, :] = value.astype(bf)
        found = tap_sums(r.misc_ext.at[0], r.state_grad_ext[rows, :], base, before)
        for k, v in enumerate(found):
            r.misc_acc[k] = r.misc_acc[k] + v
        return 0

    lax.fori_loop(0, T // ROWS, misc_back_rows, 0)

    stage("normed_grad")
    for j in range(D // 256):
        cols = slice(256 * j, 256 * j + 256)
        value = (
            dg(r.gate_grad[...], r.gate_weight[cols, :], 1, 1)
            + dg(r.inner_grad[...], r.inner_weight[cols, :], 1, 1)
            + dg(r.misc_grad[...], r.misc_weight[:, cols], 1, 0)
        )
        r.normed_part[:, cols] = value.astype(bf)
        hats = r.block_input[:, cols].astype(f32) * jnp.concatenate([r.inverse[...]] * 2, axis=1)
        r.gain_part[:, cols] = fold8(value * hats)

    def weight_rows_two(i, _):
        cols = pl.ds(pl.multiple_of(i * LANES, LANES), LANES)
        r.wg_two[cols, 0:HI] = dg(r.normed[:, cols], r.inner_grad[...], 0, 0).astype(bf)
        r.wg_two[cols, HI : HI + LANES] = dg(r.normed[:, cols], r.misc_grad[...], 0, 0).astype(bf)
        return 0

    lax.fori_loop(0, D // LANES, weight_rows_two, 0)
    r.wg_two_recv[seq] = r.wg_two[mine, :]
    wg_two_wait = spread(
        "seq", lambda d: part_of(r.wg_two, d), lambda d: r.wg_two_recv.at[d], r.wg2_ss, r.wg2_rs
    )

    stage("small_sums")
    def row_of(v):
        return jnp.sum(v, axis=0, keepdims=True)

    eye_wide = iota((H, LANES), 0) == iota((H, LANES), 1)

    def lanes_of(v):
        return row_of(jnp.where(eye_wide, jnp.broadcast_to(v, (H, LANES)), 0.0))

    r.small_send[...] = jnp.zeros_like(r.small_send)
    for k in range(CONV + 1):
        r.small_send[k : k + 1, :] = row_of(r.sum_acc[2 + k])
    r.small_send[5:6, :] = row_of(r.sum_acc[0])
    r.small_send[6:7, :] = row_of(r.sum_acc[1])
    for k in range(CONV):
        r.small_send[7:8, k * LANES : k * LANES + LANES] = row_of(r.misc_acc[k])
    r.small_send[8:9, 0:LANES] = row_of(r.misc_acc[CONV])
    r.small_send[8:9, LANES : 2 * LANES] = lanes_of(bias_sum)
    r.small_send[8:9, 2 * LANES : 3 * LANES] = lanes_of(rate_sum)
    gain_rows = row_of(r.gain_part[...])
    for k in range(D // HI):
        r.small_send[9 + k : 10 + k, :] = gain_rows[:, k * HI : k * HI + HI]
    r.small_recv[seq] = r.small_send[...]
    small_wait = spread(
        "seq", lambda d: r.small_send, lambda d: r.small_recv.at[d], r.small_ss, r.small_rs
    )
    stage("small_wait")
    small_wait()
    stage("small_use")
    total = r.small_recv[0]
    for d in range(1, n_seq):
        total = total + r.small_recv[d]
    r.small_total[...] = total
    r.gain_recv[tp] = r.small_total[8:16, :]
    gain_wait = spread(
        "tp", lambda t: r.small_total.at[pl.ds(8, 8)], lambda t: r.gain_recv.at[t], r.gain_ss, r.gain_rs
    )

    stage("chains")
    pieces = r.chain_ss.shape[2]
    piece = T // (2 * pieces)
    summed_refs = ((r.branch, r.branch_hop, r.branch_sum), (r.normed_part, r.normed_hop, r.normed_sum))

    def chain_for(k):
        events = []
        for a in range(2):
            for j in range(pieces):
                for way in range(2):
                    place = k if way == 0 else n_tp - 1 - k
                    at = a * pieces + j
                    events.append((at + place * 1.0, 0, a, j, way, place))
                    if place < n_tp - 1:
                        events.append((at + (n_tp - 1) + (n_tp - 1 - place) + 0.5, 1, a, j, way, place))
        for _, back, a, j, way, place in sorted(events):
            partial, hop, final = summed_refs[a]
            rows = pl.ds((way * pieces + j) * piece, piece)
            on = (seq, k + 1) if way == 0 else (seq, k - 1)
            home = (seq, k - 1) if way == 0 else (seq, k + 1)
            sems = (a, way, j)

            def go(src, dst, send, recv, device):
                return remote(src.at[rows], dst.at[rows], send.at[sems], recv.at[sems], device)

            if not back:
                if place > 0:
                    go(hop, hop, r.chain_ss, r.chain_rs, home).wait_recv()
                    both = (partial[rows, :].astype(f32) + hop[rows, :].astype(f32)).astype(bf)
                    if place == n_tp - 1:
                        final[rows, :] = both
                    else:
                        partial[rows, :] = both
                if place < n_tp - 1:
                    go(partial, hop, r.chain_ss, r.chain_rs, on).start()
                else:
                    go(final, final, r.back_ss, r.back_rs, home).start()
            else:
                go(final, final, r.back_ss, r.back_rs, on).wait_recv()
                if place > 0:
                    go(final, final, r.back_ss, r.back_rs, home).start()
        for _, back, a, j, way, place in sorted(events):
            partial, hop, final = summed_refs[a]
            rows = pl.ds((way * pieces + j) * piece, piece)
            sems = (a, way, j)
            on = (seq, k + 1) if way == 0 else (seq, k - 1)
            home = (seq, k - 1) if way == 0 else (seq, k + 1)
            if not back:
                if place < n_tp - 1:
                    remote(partial.at[rows], hop.at[rows], r.chain_ss.at[sems], r.chain_rs.at[sems], on).wait_send()
                if place > 0:
                    remote(final.at[rows], final.at[rows], r.back_ss.at[sems], r.back_rs.at[sems], home).wait_send()

    for k in range(n_tp):
        pl.when(tp == k)(functools.partial(chain_for, k))

    stage("weights_wait")
    wg_one_wait()
    wg_two_wait()
    gain_wait()
    stage("weight_sums")

    def weight_sums(ref, recv):
        value = recv[0].astype(f32)
        for d in range(1, n_seq):
            value = value + recv[d].astype(f32)
        ref[...] = value

    weight_sums(r.sum_one, r.wg_one_recv)
    weight_sums(r.sum_two, r.wg_two_recv)
    gains = r.gain_recv[0]
    for t in range(1, n_tp):
        gains = gains + r.gain_recv[t]
    r.gain_total[...] = gains
    stage("drain")
    for copy in waits:
        copy.wait_send()
    marks.close()


def finish(sizes, names, *refs):
    r = types.SimpleNamespace(**dict(zip(names, refs)))
    T, D, HI, H, NS = sizes
    P_ = HI // H

    def final_rows(i, _):
        rows = pl.ds(pl.multiple_of(i * ROWS, ROWS), ROWS)
        x = r.block_input[rows, :].astype(f32)
        r.block_output[rows, :] = (x + r.branch_sum[rows, :].astype(f32)).astype(bf)
        inverse = lax.rsqrt(jnp.mean(x * x, axis=1, keepdims=True) + epsilon)
        hat = x * inverse
        hat_grad = r.normed_sum[rows, :].astype(f32) * r.input_gain[...].reshape(1, D)
        mean = jnp.mean(hat_grad * hat, axis=1, keepdims=True)
        r.input_grad[rows, :] = r.out_cotangent[rows, :].astype(f32) + inverse * (
            hat_grad - hat * mean
        )
        return 0

    lax.fori_loop(0, T // ROWS, final_rows, 0)
    r.gate_weight_grad[...] = r.sum_one[:, 0:HI]
    r.out_weight_grad[...] = r.sum_one[:, HI : 2 * HI].T
    r.inner_weight_grad[...] = r.sum_two[:, 0:HI]
    narrow = r.sum_two[:, HI : HI + LANES].T
    r.state_weight_grad[...] = narrow[0:NS]
    r.step_weight_grad[...] = narrow[NS : NS + H]
    small = r.small_total
    r.inner_kernel_grad[...] = small[0:CONV, :]
    r.inner_conv_bias_grad[...] = small[CONV : CONV + 1, :].reshape(HI)
    r.gate_gain_grad[...] = small[5:6, :].reshape(HI)
    head_sum = (iota((HI, LANES), 0) // P_ == iota((HI, LANES), 1)).astype(f32).astype(bf)
    skip_sums = fold3(dg(split3(jnp.broadcast_to(small[6:7, :], (8, HI))), head_sum, 1, 0))
    r.skip_scale_grad[...] = skip_sums[0:1, 0:H].reshape(H)
    for k in range(CONV):
        r.state_kernel_grad[k : k + 1, :] = small[7:8, k * LANES : k * LANES + NS]
    r.state_conv_bias_grad[...] = small[8:9, 0:NS].reshape(NS)
    r.step_bias_grad[...] = small[8:9, LANES : LANES + H].reshape(H)
    r.rate_log_grad[...] = small[8:9, 2 * LANES : 2 * LANES + H].reshape(H)
    for k in range(D // HI):
        r.input_gain_grad[k * HI : k * HI + HI] = r.gain_total[1 + k : 2 + k, :].reshape(HI)


INPUTS = (
    "block_input",
    "scene_lengths",
    "input_gain",
    "gate_weight",
    "inner_weight",
    "state_weight",
    "step_weight",
    "step_bias",
    "rate_log",
    "inner_kernel",
    "inner_conv_bias",
    "state_kernel",
    "state_conv_bias",
    "skip_scale",
    "gate_gain",
    "out_weight",
    "out_cotangent",
)
OUTPUTS = (
    "block_output",
    "input_grad",
    "input_gain_grad",
    "gate_weight_grad",
    "inner_weight_grad",
    "state_weight_grad",
    "step_weight_grad",
    "step_bias_grad",
    "rate_log_grad",
    "inner_kernel_grad",
    "inner_conv_bias_grad",
    "state_kernel_grad",
    "state_conv_bias_grad",
    "skip_scale_grad",
    "gate_gain_grad",
    "out_weight_grad",
)


SUMS = ("branch_sum", "normed_sum", "sum_one", "sum_two", "small_total", "gain_total")


def local(*args):
    given = dict(zip(INPUTS, args))
    given["state_weight"] = given["state_weight"].T
    given["step_weight"] = given["step_weight"].T
    n_seq = lax.axis_size("seq")
    n_tp = lax.axis_size("tp")
    T, D = given["block_input"].shape
    HI = given["gate_weight"].shape[1]
    H = given["step_bias"].shape[0]
    NS = given["state_weight"].shape[0]
    N = STATE
    Q = CHUNK
    NC = T // Q
    NP = HI // LANES
    R = HI // n_seq
    R2 = D // n_seq
    pieces = 4
    outs = (
        ((T, D), bf),
        ((T, D), f32),
        ((D,), f32),
        ((R2, HI), f32),
        ((R2, HI), f32),
        ((NS, R2), f32),
        ((H, R2), f32),
        ((H,), f32),
        ((H,), f32),
        ((CONV, HI), f32),
        ((HI,), f32),
        ((CONV, NS), f32),
        ((NS,), f32),
        ((H,), f32),
        ((HI,), f32),
        ((HI, R2), f32),
    )
    sums = (
        ((T, D), bf),
        ((T, D), bf),
        ((R2, 2 * HI), f32),
        ((R2, HI + LANES), f32),
        ((16, HI), f32),
        ((8, HI), f32),
    )
    scratch = dict(
        inverse=((T, LANES), f32),
        normed=((T, D), bf),
        misc_weight=((LANES, D), bf),
        inner_ext=((NP, T + PAD, LANES), f32),
        misc_ext=((1, T + PAD, LANES), f32),
        gate_pre=((T, HI), f32),
        misc_taps=((8, LANES), f32),
        inner_bias=((1, HI), f32),
        gain_row=((1, HI), f32),
        misc_conv=((T, LANES), f32),
        inner_conv=((T, HI), f32),
        act=((T, HI), bf),
        state_send=((T // 2, LANES), bf),
        state_recv=((n_tp, T // 2, LANES), bf),
        keys=((T, N), bf),
        queries=((T, N), bf),
        sigmoid_step=((H, T), f32),
        step_rows=((H, T), f32),
        log_decay=((H, T), f32),
        upto=((Q, Q), bf),
        expand=((3 * H, HI), bf),
        mask=((NC, Q, Q), f32),
        cum_left=((H, 16, T), bf),
        cum_right=((H, 16, T), bf),
        step_wide=((T, HI), f32),
        enter_wide=((T, HI), f32),
        tail_wide=((T, HI), f32),
        decay_wide=((NC, HI, LANES), f32),
        skip_wide=((8, HI), f32),
        xt=((T, HI), bf),
        xt_rest=((T, HI), bf),
        fresh=((NC, HI, N), f32),
        end_send=((HI, N), f32),
        end_recv=((n_seq, R, N), f32),
        decay_send=((H, LANES), f32),
        decay_recv=((n_seq, H, LANES), f32),
        enter_send=((n_seq, R, N), f32),
        enter_state=((HI, N), f32),
        state_in=((NC, HI, N), f32),
        state_in_low=((NC, HI, N), bf),
        state_in_rest=((NC, HI, N), bf),
        scores=((NC, Q, Q), f32),
        score_grad=((NC, Q, Q), f32),
        decays=((NC, H, Q, Q), f32),
        mixed=((T, HI), f32),
        norm_grad=((T, HI), f32),
        heads_out=((T, HI), f32),
        gated=((T, HI), f32),
        squares=((T, LANES), f32),
        products=((T, LANES), f32),
        sums_send=((8, T), f32),
        sums_recv=((n_tp, 8, T), f32),
        norm_col=((T, LANES), f32),
        back_col=((T, LANES), f32),
        head_sum=((HI, LANES), bf),
        head_sum_two=((HI, LANES), bf),
        head_sum_three=((HI, LANES), bf),
        sum_acc=((7, 8, HI), f32),
        gated_norm=((T, HI), bf),
        gate_grad=((T, HI), bf),
        heads_grad=((T, HI), f32),
        dy=((T, HI), bf),
        dy_rest=((T, HI), bf),
        dy_enter=((T, HI), bf),
        dy_enter_rest=((T, HI), bf),
        sum_y=((T, LANES), f32),
        sum_x=((T, LANES), f32),
        grad_local=((NC, HI, N), f32),
        grad_send=((HI, N), f32),
        grad_recv=((n_seq, R, N), f32),
        leave_send=((n_seq, R, N), f32),
        leave_grad=((HI, N), f32),
        x_inside=((T, HI), f32),
        x_carry=((T, HI), f32),
        wg_one=((D, 2 * HI), bf),
        wg_one_recv=((n_seq, R2, 2 * HI), bf),
        wg_two=((D, HI + LANES), bf),
        wg_two_recv=((n_seq, R2, HI + LANES), bf),
        query_grad=((T, N), f32),
        key_grad=((T, N), f32),
        shared_send=((n_tp, T // 2, LANES), f32),
        shared_recv=((n_tp, T // 2, LANES), f32),
        grad_ext=((NP, T + PAD, LANES), f32),
        state_grad_ext=((T + PAD, LANES), f32),
        inner_grad=((T, HI), bf),
        step_cols=((T, LANES), f32),
        misc_grad=((T, LANES), bf),
        misc_acc=((CONV + 1, 8, LANES), f32),
        normed_part=((T, D), bf),
        normed_hop=((T, D), bf),
        branch=((T, D), bf),
        branch_hop=((T, D), bf),
        gain_part=((8, D), f32),
        small_send=((16, HI), f32),
        small_recv=((n_seq, 16, HI), f32),
        gain_recv=((n_tp, 8, HI), f32),
    )
    semaphores = dict(
        rim_send=(2,),
        rim_recv=(2,),
        halo_send=(2,),
        halo_recv=(2,),
        chain_ss=(2, 2, pieces),
        chain_rs=(2, 2, pieces),
        back_ss=(2, 2, pieces),
        back_rs=(2, 2, pieces),
    )
    for name in ("state", "sums", "shared", "gain"):
        semaphores[name + "_ss"] = (n_tp - 1,)
        semaphores[name + "_rs"] = (n_tp - 1,)
    for name in ("decay", "end", "enter", "grad", "leave", "wg1", "wg2", "small"):
        semaphores[name + "_ss"] = (n_seq - 1,)
        semaphores[name + "_rs"] = (n_seq - 1,)
    names = INPUTS + SUMS + tuple(scratch) + tuple(semaphores)
    vmem = pl.BlockSpec(memory_space=pltpu.VMEM)
    smem = pl.BlockSpec(memory_space=pltpu.SMEM)
    totals = pl.pallas_call(
        functools.partial(kernel, (n_seq, n_tp, T, D, HI, H, NS), names),
        out_shape=tuple(jax.ShapeDtypeStruct(s, t) for s, t in sums),
        in_specs=[smem if n == "scene_lengths" else vmem for n in INPUTS],
        out_specs=tuple(vmem for _ in sums),
        scratch_shapes=[pltpu.VMEM(s, t) for s, t in scratch.values()]
        + [pltpu.SemaphoreType.DMA(s) for s in semaphores.values()],
        compiler_params=pltpu.CompilerParams(
            collective_id=0, has_side_effects=True, vmem_limit_bytes=60 * 2**20
        ),
    )(*given.values())
    needed = ("block_input", "input_gain", "out_cotangent")
    results = pl.pallas_call(
        functools.partial(finish, (T, D, HI, H, NS), needed + SUMS + OUTPUTS),
        out_shape=tuple(jax.ShapeDtypeStruct(s, t) for s, t in outs),
        in_specs=[vmem] * (len(needed) + len(SUMS)),
        out_specs=tuple(vmem for _ in outs),
        compiler_params=pltpu.CompilerParams(vmem_limit_bytes=32 * 2**20),
    )(*(given[n] for n in needed), *totals)
    results = dict(zip(OUTPUTS, results))
    results["state_weight_grad"] = results["state_weight_grad"].T
    results["step_weight_grad"] = results["step_weight_grad"].T
    return tuple(results.values())


def solution(mesh):
    rows = P("seq", None)
    cols = P(None, "tp")
    heads = P("tp")
    return jax.shard_map(
        local,
        mesh=mesh,
        in_specs=(
            rows,
            P(),
            P(),
            cols,
            cols,
            cols,
            cols,
            heads,
            heads,
            cols,
            heads,
            cols,
            heads,
            heads,
            heads,
            P("tp", None),
            rows,
        ),
        out_specs=(
            rows,
            rows,
            P(),
            P("seq", "tp"),
            P("seq", "tp"),
            P("seq", "tp"),
            P("seq", "tp"),
            heads,
            heads,
            cols,
            heads,
            cols,
            heads,
            heads,
            heads,
            P("tp", "seq"),
        ),
        check_vma=False,
    )
```

```python
import contextlib
import functools
import types

import jax
import jax.numpy as jnp
from jax import lax
from jax.experimental import pallas as pl
from jax.experimental.pallas import tpu as pltpu
from jax.sharding import PartitionSpec as P

STATE = 128
CONV = 4
CHUNK = 256
LANES = 128
PAD = 8
ROWS = 64
epsilon = 1e-05
bf = jnp.bfloat16
f32 = jnp.float32
i32 = jnp.int32
MESH = pl.DeviceIdType.MESH


def dg(left, right, left_dim, right_dim):
    return lax.dot_general(
        left, right, (((left_dim,), (right_dim,)), ((), ())), preferred_element_type=f32
    )


def split3(v):
    high = v.astype(bf).astype(f32)
    middle = (v - high).astype(bf).astype(f32)
    return jnp.concatenate([high, middle, v - high - middle], axis=0).astype(bf)


def fold3(v):
    third = v.shape[0] // 3
    return v[:third] + v[third : 2 * third] + v[2 * third :]


def halves(v):
    high = v.astype(bf)
    return high, (v - high.astype(f32)).astype(bf)


def slope(v):
    s = jax.nn.sigmoid(v)
    return s * (1.0 + v * (1.0 - s))


def fold8(v):
    total = v[0:8]
    for i in range(1, v.shape[0] // 8):
        total = total + v[8 * i : 8 * i + 8]
    return total


def iota(shape, dim):
    return lax.broadcasted_iota(i32, shape, dim)


def kernel(sizes, names, *refs):
    r = types.SimpleNamespace(**dict(zip(names, refs)))
    n_seq, n_tp, T, D, HI, H, NS = sizes
    N = STATE
    P_ = HI // H
    Q = CHUNK
    NC = T // Q
    NP = HI // LANES
    R = HI // n_seq
    R2 = D // n_seq
    total_tokens = T * n_seq
    seq = lax.axis_index("seq")
    tp = lax.axis_index("tp")

    barrier = pltpu.get_barrier_semaphore()
    for d in range(1, n_seq):
        pl.semaphore_signal(
            barrier, inc=1, device_id=((seq + d) % n_seq, tp), device_id_type=MESH
        )
    for d in range(1, n_tp):
        pl.semaphore_signal(
            barrier, inc=1, device_id=(seq, (tp + d) % n_tp), device_id_type=MESH
        )

    waits = []
    half = n_tp // 2
    inner = jnp.where(tp < half, tp + 1, tp - 1)
    outer = jnp.where(tp < half, tp - 1, tp + 1)
    is_middle = (tp == half - 1) | (tp == half)
    has_outer = (tp > 0) & (tp < n_tp - 1)
    fold_pieces = (r.branch_in.shape[0], r.normed_in.shape[0])
    fold_width = tuple(D // n for n in fold_pieces)
    fold_refs = (
        (r.branch, r.branch_in, r.branch_across, r.branch_sum),
        (r.normed_part, r.normed_in, r.normed_across, r.normed_sum),
    )

    def fold(a, j):
        partial, arrived, across, total = (
            ref.at[j] if k < 3 else ref.at[:, pl.ds(j * fold_width[a], fold_width[a])]
            for k, ref in enumerate(fold_refs[a])
        )
        return partial, arrived, across, total

    def fold_copy(a, j, leg):
        partial, arrived, across, total = fold(a, j)
        sems = leg, sum(fold_pieces[:a]) + j
        source, target, place = ((partial, arrived, inner), (partial, across, inner), (total, total, outer))[leg]
        return remote(source, target, r.fold_ss.at[sems], r.fold_rs.at[sems], (seq, place))

    def fold_start(a, j):
        pl.when(jnp.logical_not(has_outer | is_middle))(fold_copy(a, j, 0).start)

    def fold_in(a, j):
        partial, arrived, _, _ = fold(a, j)

        @pl.when(has_outer)
        def _():
            fold_copy(a, j, 0).wait_recv()
            partial[...] = (partial[...].astype(f32) + arrived[...].astype(f32)).astype(bf)

        pl.when(is_middle)(fold_copy(a, j, 1).start)
        pl.when(has_outer & jnp.logical_not(is_middle))(fold_copy(a, j, 0).start)

    def fold_middle(a, j):
        partial, _, across, total = fold(a, j)

        @pl.when(is_middle)
        def _():
            fold_copy(a, j, 1).wait_recv()
            total[...] = (partial[...].astype(f32) + across[...].astype(f32)).astype(bf)
            pl.when(has_outer)(fold_copy(a, j, 2).start)

    def fold_end(a, j):
        @pl.when(jnp.logical_not(is_middle))
        def _():
            fold_copy(a, j, 2).wait_recv()
            pl.when(has_outer)(fold_copy(a, j, 2).start)
            fold_copy(a, j, 0).wait_send()

        pl.when(has_outer)(fold_copy(a, j, 2).wait_send)
        pl.when(is_middle)(fold_copy(a, j, 1).wait_send)

    marks = contextlib.ExitStack()

    def stage(name):
        marks.close()
        marks.enter_context(jax.named_scope(name))

    stage("norm")

    def remote(src, dst, send, recv, device):
        return pltpu.make_async_remote_copy(
            src_ref=src,
            dst_ref=dst,
            send_sem=send,
            recv_sem=recv,
            device_id=device,
            device_id_type=MESH,
        )

    def spread(axis, src_to, dst_from, send, recv):
        n = n_seq if axis == "seq" else n_tp
        me = seq if axis == "seq" else tp
        incoming = []
        for d in range(1, n):
            target = (me + d) % n
            source = (me + n - d) % n
            device = (target, tp) if axis == "seq" else (seq, target)
            out = remote(src_to(target), dst_from(me), send.at[d - 1], recv.at[d - 1], device)
            out.start()
            waits.append(out)
            incoming.append(
                remote(src_to(target), dst_from(source), send.at[d - 1], recv.at[d - 1], device)
            )

        def wait():
            for copy in incoming:
                copy.wait_recv()

        return wait

    starts = [jnp.int32(0)]
    for k in range(r.scene_lengths.shape[0] - 1):
        starts.append(starts[-1] + r.scene_lengths[k])

    def segment(position):
        found = (position >= starts[0]).astype(i32)
        for s in starts[1:]:
            found = found + (position >= s).astype(i32)
        return found

    first_token = seq * T

    def norm_rows(i, _):
        rows = pl.ds(pl.multiple_of(i * ROWS, ROWS), ROWS)
        x = r.block_input[rows, :].astype(f32)
        inverse = lax.rsqrt(jnp.mean(x * x, axis=1, keepdims=True) + epsilon)
        r.inverse[rows, :] = jnp.broadcast_to(inverse, (ROWS, LANES))
        r.normed[rows, :] = (x * inverse * r.input_gain[...].reshape(1, D)).astype(bf)
        return 0

    lax.fori_loop(0, T // ROWS, norm_rows, 0)

    stage("projections")
    r.misc_weight[...] = jnp.zeros_like(r.misc_weight)
    r.misc_weight[0:NS, :] = r.state_weight[...]
    r.misc_weight[NS : NS + H, :] = r.step_weight[...]
    normed_all = r.normed[...]
    for j in range(HI // 256):
        cols = slice(256 * j, 256 * j + 256)
        value = dg(normed_all, r.inner_weight[:, cols], 1, 0)
        r.inner_ext[2 * j, PAD : PAD + T, :] = value[:, :LANES]
        r.inner_ext[2 * j + 1, PAD : PAD + T, :] = value[:, LANES:]
    r.misc_ext[0, PAD : PAD + T, :] = dg(normed_all, r.misc_weight[...], 1, 1)

    stage("barrier")
    pl.semaphore_wait(barrier, n_seq - 1 + n_tp - 1)
    stage("gate_projection")
    right = ((seq + 1) % n_seq, tp)
    left = ((seq + n_seq - 1) % n_seq, tp)
    rim = [
        remote(
            ref.at[:, pl.ds(T, PAD)],
            ref.at[:, pl.ds(0, PAD)],
            r.rim_send.at[k],
            r.rim_recv.at[k],
            right,
        )
        for k, ref in enumerate((r.inner_ext, r.misc_ext))
    ]
    for copy in rim:
        copy.start()
    waits.extend(rim)
    for j in range(HI // 256):
        cols = slice(256 * j, 256 * j + 256)
        r.gate_pre[:, cols] = dg(normed_all, r.gate_weight[:, cols], 1, 0)

    stage("convolutions")
    def agreements(base, rows):
        position = first_token + base + iota((rows, LANES), 0)
        now = segment(position)
        return [segment(position - (CONV - 1) + k) == now for k in range(CONV - 1)]

    def conv_block(ext, taps, bias, base, lanes, masks):
        value = bias[:, lanes]
        for k in range(CONV):
            window = ext[pl.ds(base + PAD - CONV + 1 + k, ROWS), :]
            term = taps[k : k + 1, lanes] * window
            value = value + (term if k == CONV - 1 else jnp.where(masks[k], term, 0.0))
        return value

    r.misc_taps[...] = jnp.zeros_like(r.misc_taps)
    r.misc_taps[0:CONV, 0:NS] = r.state_kernel[...]
    r.misc_taps[CONV : CONV + 1, 0:NS] = r.state_conv_bias[...].reshape(1, NS)
    r.inner_bias[...] = r.inner_conv_bias[...].reshape(1, HI)
    stage("rim_wait")
    for copy in rim:
        copy.wait_recv()
    stage("conv")

    def misc_conv_rows(i, _):
        base = pl.multiple_of(i * ROWS, ROWS)
        masks = agreements(base, ROWS)
        taps = r.misc_taps[...]
        value = conv_block(
            r.misc_ext.at[0], taps, taps[CONV : CONV + 1], base, slice(0, LANES), masks
        )
        r.misc_conv[pl.ds(base, ROWS), :] = value
        return 0

    lax.fori_loop(0, T // ROWS, misc_conv_rows, 0)
    low_lanes = iota((T // 2, LANES), 1) < NS
    own = r.misc_conv[...]
    own = own * jax.nn.sigmoid(own)
    r.state_send[...] = jnp.where(
        low_lanes, own[: T // 2], pltpu.roll(own[T // 2 :], NS, 1)
    ).astype(bf)
    r.state_recv[tp] = r.state_send[...]
    state_wait = spread(
        "tp",
        lambda t: r.state_send,
        lambda t: r.state_recv.at[t],
        r.state_ss,
        r.state_rs,
    )

    def inner_conv_rows(i, _):
        base = pl.multiple_of(i * ROWS, ROWS)
        rows = pl.ds(base, ROWS)
        masks = agreements(base, ROWS)
        taps = r.inner_kernel[...]
        for g in range(NP):
            lanes = slice(g * LANES, g * LANES + LANES)
            value = conv_block(r.inner_ext.at[g], taps, r.inner_bias, base, lanes, masks)
            r.inner_conv[rows, lanes] = value
            r.act[rows, lanes] = (value * jax.nn.sigmoid(value)).astype(bf)
        return 0

    lax.fori_loop(0, T // ROWS, inner_conv_rows, 0)

    stage("decays")
    eye = iota((H, H), 0) == iota((H, H), 1)

    def column(ref):
        wide = jnp.broadcast_to(ref[...].reshape(1, H), (H, H))
        return jnp.sum(jnp.where(eye, wide, 0.0), axis=1, keepdims=True)

    step_in = r.misc_ext[0, PAD : PAD + T, :].T[NS : NS + H, :] + column(r.step_bias)
    step = jnp.maximum(step_in, 0.0) + jnp.log1p(jnp.exp(-jnp.abs(step_in)))
    rate = jnp.exp(column(r.rate_log))
    log_decay = step * -rate
    r.sigmoid_step[...] = jax.nn.sigmoid(step_in)
    r.log_decay[...] = log_decay
    r.step_rows[...] = step
    r.upto[...] = (iota((Q, Q), 0) <= iota((Q, Q), 1)).astype(f32).astype(bf)
    r.expand[...] = (iota((3 * H, HI), 0) % H == iota((3 * H, HI), 1) // P_).astype(f32).astype(bf)
    expand = r.expand[...]

    entering, tailing, chunk_decay = [], [], []
    ones_rows = jnp.ones((1, Q), f32)
    for c in range(NC):
        cols = slice(c * Q, c * Q + Q)
        cumulative = fold3(dg(split3(log_decay[:, cols]), r.upto[...], 1, 0))
        start = first_token + c * Q
        seg_row = segment(start + iota((H, Q), 1))
        seg_before = segment(start - 1)
        seg_end = segment(start + Q - 1)
        last = cumulative[:, Q - 1 : Q]
        enter = jnp.where(seg_row == seg_before, jnp.exp(cumulative), 0.0)
        tail = jnp.where(seg_row == seg_end, jnp.exp(last - cumulative), 0.0)
        entering.append(enter)
        tailing.append(tail)
        chunk_decay.append(enter[:, Q - 1 : Q])
        seg_col = segment(start + iota((Q, Q), 0))
        seg_lane = segment(start + iota((Q, Q), 1))
        keep = (seg_col == seg_lane) & (iota((Q, Q), 0) >= iota((Q, Q), 1))
        r.mask[c] = jnp.where(keep, 0.0, -1e30)
        high = cumulative.astype(bf).astype(f32)
        middle = (cumulative - high).astype(bf).astype(f32)
        rest = cumulative - high - middle
        which = iota((16, Q), 0)
        for h in range(H):
            parts = jnp.where(
                which % 3 == 0,
                high[h : h + 1],
                jnp.where(which % 3 == 1, middle[h : h + 1], rest[h : h + 1]),
            )
            first = which < 3
            second = (which >= 3) & (which < 6)
            r.cum_left[h, :, cols] = jnp.where(
                first, parts, jnp.where(second, 1.0, 0.0)
            ).astype(bf)
            r.cum_right[h, :, cols] = jnp.where(
                first, 1.0, jnp.where(second, -parts, 0.0)
            ).astype(bf)

    def wide(v):
        return dg(split3(v), expand, 0, 0)

    def wide_rows(v):
        return dg(expand, split3(jnp.broadcast_to(v, (H, LANES))), 0, 0)

    for c in range(NC):
        rows = slice(c * Q, c * Q + Q)
        r.step_wide[rows, :] = wide(step[:, rows])
        r.enter_wide[rows, :] = wide(entering[c])
        r.tail_wide[rows, :] = wide(tailing[c])
        r.decay_wide[c] = wide_rows(chunk_decay[c])
    r.skip_wide[...] = dg(split3(jnp.broadcast_to(column(r.skip_scale), (H, 8))), expand, 0, 0)

    def scaled_rows(i, _):
        rows = pl.ds(pl.multiple_of(i * ROWS, ROWS), ROWS)
        x = r.act[rows, :].astype(f32)
        r.xt[rows, :], r.xt_rest[rows, :] = halves(x * r.step_wide[rows, :] * r.tail_wide[rows, :])
        return 0

    lax.fori_loop(0, T // ROWS, scaled_rows, 0)

    stage("keys_wait")
    state_wait()
    shards = n_tp // 2
    half_low = iota((T // 2, LANES), 1) < NS
    for ref, at in ((r.keys, 0), (r.queries, shards)):
        one, two = r.state_recv[at].astype(f32), r.state_recv[at + 1].astype(f32)
        ref[0 : T // 2, :] = jnp.where(half_low, one, pltpu.roll(two, NS, 1)).astype(bf)
        ref[T // 2 : T, :] = jnp.where(half_low, pltpu.roll(one, NS, 1), two).astype(bf)

    stage("end_states")
    end_state = None
    device_decay = None
    for c in range(NC):
        rows = slice(c * Q, c * Q + Q)
        keys = r.keys[rows, :]
        fresh = dg(r.xt[rows, :], keys, 0, 0) + dg(r.xt_rest[rows, :], keys, 0, 0)
        r.fresh[c] = fresh
        end_state = fresh if c == 0 else r.decay_wide[c] * end_state + fresh
        device_decay = chunk_decay[c] if c == 0 else device_decay * chunk_decay[c]
    r.end_send[...] = end_state
    r.decay_send[...] = jnp.broadcast_to(device_decay, (H, LANES))

    def block(ref, device):
        return ref.at[pl.ds(pl.multiple_of(device * R, R), R)]

    r.end_recv[seq] = r.end_send[pl.ds(pl.multiple_of(seq * R, R), R), :]
    r.decay_recv[seq] = r.decay_send[...]
    decay_wait = spread(
        "seq", lambda d: r.decay_send, lambda d: r.decay_recv.at[d], r.decay_ss, r.decay_rs
    )
    end_wait = spread(
        "seq", lambda d: block(r.end_send, d), lambda d: r.end_recv.at[d], r.end_ss, r.end_rs
    )

    stage("inside")
    for c in range(NC):
        rows = slice(c * Q, c * Q + Q)
        r.scores[c] = dg(r.queries[rows, :], r.keys[rows, :], 1, 1)
    low = iota((Q, LANES), 1) < P_

    def inside(i, _):
        c = i // NP
        p = i % NP
        rows = pl.ds(pl.multiple_of(c * Q, Q), Q)
        lanes = pl.ds(pl.multiple_of(p * LANES, LANES), LANES)
        x = r.act[rows, lanes]
        zero = jnp.zeros_like(x)
        result = None
        for s in range(2):
            h = 2 * p + s
            difference = dg(r.cum_left[h, :, rows], r.cum_right[h, :, rows], 0, 0)
            decay = jnp.exp(difference + r.mask[c])
            r.decays[c, h] = decay
            weight, rest = halves(decay * r.scores[c] * r.step_rows[pl.ds(h, 1), rows])
            part = jnp.where(low, x, zero) if s == 0 else jnp.where(low, zero, x)
            term = dg(weight, part, 1, 0) + dg(rest, part, 1, 0)
            result = term if s == 0 else result + term
        r.mixed[rows, lanes] = result
        return 0

    lax.fori_loop(0, NC * NP, inside, 0)
    for j in range(HI // 256):
        cols = slice(256 * j, 256 * j + 256)
        r.norm_grad[:, cols] = dg(r.out_cotangent[...], r.out_weight[cols, :], 1, 1)

    stage("entering")
    head_of = (seq * R) // P_
    stage("end_wait")
    end_wait()
    decay_wait()

    def decay_of(d):
        return jnp.broadcast_to(r.decay_recv[d, pl.ds(head_of, 1), :], (R, LANES))

    running = jnp.zeros((R, N), f32)
    for d in range(n_seq):
        r.enter_send[d] = running
        running = decay_of(d) * running + r.end_recv[d]
    own_rows = pl.ds(pl.multiple_of(seq * R, R), R)
    r.enter_state[own_rows, :] = r.enter_send[seq]
    enter_wait = spread(
        "seq", lambda d: r.enter_send.at[d], lambda d: block(r.enter_state, d), r.enter_ss, r.enter_rs
    )
    stage("enter_wait")
    enter_wait()
    stage("readout")
    for c in range(NC):
        rows = slice(c * Q, c * Q + Q)
        if c == 0:
            state = r.enter_state[...]
        else:
            state = r.decay_wide[c - 1] * state + r.fresh[c - 1]
        r.state_in[c] = state
        r.state_in_low[c], r.state_in_rest[c] = halves(state)
        for j in range(HI // 256):
            cols = slice(256 * j, 256 * j + 256)
            queries = r.queries[rows, :]
            read = dg(queries, r.state_in_low[c, cols, :], 1, 1) + dg(queries, r.state_in_rest[c, cols, :], 1, 1)
            r.mixed[rows, cols] = r.mixed[rows, cols] + r.enter_wide[rows, cols] * read

    stage("gated")
    skip_row = r.skip_wide[0:1, :]
    r.gain_row[...] = r.gate_gain[...].reshape(1, HI)

    def gated_rows(i, _):
        rows = pl.ds(pl.multiple_of(i * ROWS, ROWS), ROWS)
        heads = r.mixed[rows, :] + skip_row * r.act[rows, :].astype(f32)
        gate = r.gate_pre[rows, :]
        gated = heads * (gate * jax.nn.sigmoid(gate))
        r.heads_out[rows, :] = heads
        r.gated[rows, :] = gated
        scaled = r.norm_grad[rows, :] * r.gain_row[...]
        squares = gated * gated
        products = scaled * gated

        def lane_sum(v):
            total = v[:, :LANES]
            for g in range(1, NP):
                total = total + v[:, g * LANES : g * LANES + LANES]
            return total

        r.squares[rows, :] = lane_sum(squares)
        r.products[rows, :] = lane_sum(products)
        return 0

    lax.fori_loop(0, T // ROWS, gated_rows, 0)
    square_row = jnp.sum(r.squares[...].T, axis=0, keepdims=True)
    product_row = jnp.sum(r.products[...].T, axis=0, keepdims=True)
    r.sums_send[...] = jnp.where(
        iota((8, T), 0) == 0,
        jnp.broadcast_to(square_row, (8, T)),
        jnp.broadcast_to(product_row, (8, T)),
    )
    r.sums_recv[tp] = r.sums_send[...]
    sums_wait = spread(
        "tp", lambda t: r.sums_send, lambda t: r.sums_recv.at[t], r.sums_ss, r.sums_rs
    )
    stage("sums_wait")
    sums_wait()
    stage("sums")
    sums = r.sums_recv[0]
    for t in range(1, n_tp):
        sums = sums + r.sums_recv[t]
    count = HI * n_tp
    norm_row = lax.rsqrt(sums[0:1] / count + epsilon)
    back_row = norm_row * norm_row * norm_row * (sums[1:2] / count)
    r.norm_col[...] = jnp.broadcast_to(norm_row, (LANES, T)).T
    r.back_col[...] = jnp.broadcast_to(back_row, (LANES, T)).T

    stage("back_gated")
    r.head_sum[...] = (iota((HI, LANES), 0) // P_ == iota((HI, LANES), 1)).astype(f32).astype(bf)
    r.sum_acc[...] = jnp.zeros_like(r.sum_acc)

    def tile4(v):
        return jnp.concatenate([v] * NP, axis=1)

    def summed(v, which):
        high, lowv = halves(v)
        return dg(high, which, 1, 0) + dg(lowv, which, 1, 0)

    def back_rows(i, _):
        rows = pl.ds(pl.multiple_of(i * ROWS, ROWS), ROWS)
        norm = tile4(r.norm_col[rows, :])
        back = tile4(r.back_col[rows, :])
        gated = r.gated[rows, :]
        grad = r.norm_grad[rows, :]
        gain = r.gain_row[...]
        gate = r.gate_pre[rows, :]
        sigma = jax.nn.sigmoid(gate)
        unit = gated * norm
        r.gated_norm[rows, :] = (unit * gain).astype(bf)
        r.sum_acc[0] = r.sum_acc[0] + fold8(grad * unit)
        gated_grad = norm * (grad * gain) - gated * back
        heads_grad = gated_grad * (gate * sigma)
        heads = r.heads_out[rows, :]
        r.gate_grad[rows, :] = (
            gated_grad * heads * (sigma * (1.0 + gate * (1.0 - sigma)))
        ).astype(bf)
        r.heads_grad[rows, :] = heads_grad
        x = r.act[rows, :].astype(f32)
        r.sum_acc[1] = r.sum_acc[1] + fold8(heads_grad * x)
        r.dy[rows, :], r.dy_rest[rows, :] = halves(heads_grad)
        r.dy_enter[rows, :], r.dy_enter_rest[rows, :] = halves(heads_grad * r.enter_wide[rows, :])
        r.sum_y[rows, :] = summed(heads_grad * r.mixed[rows, :], r.head_sum[...])
        return 0

    lax.fori_loop(0, T // ROWS, back_rows, 0)

    stage("grad_states")
    grad_in = None
    for c in reversed(range(NC)):
        rows = slice(c * Q, c * Q + Q)
        queries = r.queries[rows, :]
        local = dg(r.dy_enter[rows, :], queries, 0, 0) + dg(r.dy_enter_rest[rows, :], queries, 0, 0)
        r.grad_local[c] = local
        grad_in = local if grad_in is None else r.decay_wide[c] * grad_in + local
    r.grad_send[...] = grad_in
    r.grad_recv[seq] = r.grad_send[own_rows, :]
    grad_wait = spread(
        "seq", lambda d: block(r.grad_send, d), lambda d: r.grad_recv.at[d], r.grad_ss, r.grad_rs
    )
    stage("out_projection")
    for j in range(fold_pieces[0]):
        cols = slice(fold_width[0] * j, fold_width[0] * (j + 1))
        r.branch[j] = dg(r.gated_norm[...], r.out_weight[:, cols], 1, 0).astype(bf)
        fold_start(0, j)
    stage("inside_back")
    r.score_grad[...] = jnp.zeros_like(r.score_grad)

    def inside_back(i, _):
        c = i // NP
        p = i % NP
        rows = pl.ds(pl.multiple_of(c * Q, Q), Q)
        lanes = pl.ds(pl.multiple_of(p * LANES, LANES), LANES)
        x = r.act[rows, lanes]
        dy = r.dy[rows, lanes]
        dy_rest = r.dy_rest[rows, lanes]
        zero = jnp.zeros_like(dy)
        result = None
        for s in range(2):
            h = 2 * p + s
            decay = r.decays[c, h]
            weight, rest = halves(decay * r.scores[c])

            def masked(v):
                return jnp.where(low, v, zero) if s == 0 else jnp.where(low, zero, v)

            part, part_rest = masked(dy), masked(dy_rest)
            pairs = dg(part, x, 1, 1) + dg(part_rest, x, 1, 1)
            r.score_grad[c] = r.score_grad[c] + pairs * (decay * r.step_rows[pl.ds(h, 1), rows])
            term = dg(weight, part, 0, 0) + dg(rest, part, 0, 0) + dg(weight, part_rest, 0, 0)
            result = term if s == 0 else result + term
        r.x_inside[rows, lanes] = result
        return 0

    lax.fori_loop(0, NC * NP, inside_back, 0)

    stage("query_grad")
    for c in range(NC):
        rows = slice(c * Q, c * Q + Q)
        score_low = r.score_grad[c].astype(bf)
        r.query_grad[rows, :] = (
            dg(score_low, r.keys[rows, :], 1, 0)
            + dg(r.dy_enter[rows, :], r.state_in_low[c], 1, 0)
            + dg(r.dy_enter_rest[rows, :], r.state_in_low[c], 1, 0)
            + dg(r.dy_enter[rows, :], r.state_in_rest[c], 1, 0)
        )

    def shared_copy(d, arriving=False):
        target = (tp + d) % n_tp
        slot = (tp + n_tp - d) % n_tp if arriving else tp
        sems = (r.shared_ss.at[d - 1], r.shared_rs.at[d - 1])
        return remote(r.shared_send.at[target], r.shared_recv.at[slot], *sems, (seq, target))

    def pack_shared(ref, group):
        top, bottom = ref[0 : T // 2, :], ref[T // 2 : T, :]
        at = group * shards
        r.shared_send[at] = jnp.where(half_low, top, pltpu.roll(bottom, NS, 1)).astype(bf)
        r.shared_send[at + 1] = jnp.where(half_low, pltpu.roll(top, NS, 1), bottom).astype(bf)

        @pl.when(tp // shards == group)
        def _():
            r.shared_recv[tp] = r.shared_send[tp]

        for d in range(1, n_tp):
            pl.when((tp + d) % n_tp // shards == group)(shared_copy(d).start)

    pack_shared(r.query_grad, 1)
    stage("grad_wait")
    grad_wait()
    stage("leave_scan")
    running = jnp.zeros((R, N), f32)
    for d in reversed(range(n_seq)):
        r.leave_send[d] = running
        running = decay_of(d) * running + r.grad_recv[d]
    r.leave_grad[own_rows, :] = r.leave_send[seq]
    leave_wait = spread(
        "seq", lambda d: r.leave_send.at[d], lambda d: block(r.leave_grad, d), r.leave_ss, r.leave_rs
    )

    stage("weights_one")
    def weight_rows(i, _):
        cols = pl.ds(pl.multiple_of(i * LANES, LANES), LANES)
        r.wg_one[cols, 0:HI] = dg(r.normed[:, cols], r.gate_grad[...], 0, 0).astype(bf)
        r.wg_one[cols, HI : 2 * HI] = dg(r.out_cotangent[:, cols], r.gated_norm[...], 0, 0).astype(bf)
        return 0

    lax.fori_loop(0, D // LANES, weight_rows, 0)

    stage("poll_one")
    fold_in(0, 0)
    fold_in(0, 1)
    stage("leave_wait")
    leave_wait()
    stage("leave")
    def part_of(ref, device):
        return ref.at[pl.ds(pl.multiple_of(device * R2, R2), R2)]

    mine = pl.ds(pl.multiple_of(seq * R2, R2), R2)
    r.wg_one_recv[seq] = r.wg_one[mine, :]
    wg_one_wait = spread(
        "seq", lambda d: part_of(r.wg_one, d), lambda d: r.wg_one_recv.at[d], r.wg1_ss, r.wg1_rs
    )

    carry_terms = [None] * NC
    for c in reversed(range(NC)):
        rows = slice(c * Q, c * Q + Q)
        if c == NC - 1:
            grad = r.leave_grad[...]
        else:
            grad = r.decay_wide[c + 1] * grad + r.grad_local[c + 1]
        grad_low, grad_rest = halves(grad)
        keys, queries = r.keys[rows, :], r.queries[rows, :]
        for j in range(HI // 256):
            cols = slice(256 * j, 256 * j + 256)
            read = dg(keys, grad_low[cols, :], 1, 1) + dg(keys, grad_rest[cols, :], 1, 1)
            r.x_carry[rows, cols] = r.tail_wide[rows, cols] * read
        high, lowv = halves(grad * r.state_in[c])
        pair = dg(expand[0:H], high, 1, 0) + dg(expand[0:H], lowv, 1, 0)
        carry_terms[c] = chunk_decay[c] * jnp.sum(pair, axis=1, keepdims=True)
        score_low = r.score_grad[c].astype(bf)
        r.key_grad[rows, :] = (
            dg(score_low, queries, 0, 0)
            + dg(r.xt[rows, :], grad_low, 1, 0)
            + dg(r.xt_rest[rows, :], grad_low, 1, 0)
            + dg(r.xt[rows, :], grad_rest, 1, 0)
        )

    pack_shared(r.key_grad, 0)
    stage("x_grads")
    r.head_sum_two[...] = (
        iota((HI, LANES), 0) // P_ + H == iota((HI, LANES), 1)
    ).astype(f32).astype(bf)
    r.head_sum_three[...] = (
        iota((HI, LANES), 0) // P_ + 2 * H == iota((HI, LANES), 1)
    ).astype(f32).astype(bf)

    def x_rows(i, _):
        rows = pl.ds(pl.multiple_of(i * ROWS, ROWS), ROWS)
        x = r.act[rows, :].astype(f32)
        z = r.x_inside[rows, :]
        carried = r.x_carry[rows, :]
        both = z + carried
        step_rows = r.step_wide[rows, :]
        xs = x * step_rows
        x_grad = step_rows * both + skip_row * r.heads_grad[rows, :]
        conv_grad = x_grad * slope(r.inner_conv[rows, :])
        for g in range(NP):
            r.grad_ext[g, rows, :] = conv_grad[:, g * LANES : g * LANES + LANES]
        r.sum_x[rows, :] = (
            summed(x * both, r.head_sum[...])
            + summed(xs * carried, r.head_sum_two[...])
            + summed(xs * z, r.head_sum_three[...])
        )
        return 0

    lax.fori_loop(0, T // ROWS, x_rows, 0)
    halo_one = remote(
        r.grad_ext.at[:, pl.ds(0, PAD)],
        r.grad_ext.at[:, pl.ds(T, PAD)],
        r.halo_send.at[0],
        r.halo_recv.at[0],
        left,
    )
    halo_one.start()
    waits.append(halo_one)

    sums_y = r.sum_y[...].T
    sums_x = r.sum_x[...].T
    step_grad = sums_x[0:H]
    tail_part = sums_x[H : 2 * H]
    pair_part = sums_y[0:H] - sums_x[2 * H : 3 * H]
    decay_grads = []
    for c in range(NC):
        cols = slice(c * Q, c * Q + Q)
        suffix = fold3(dg(split3(pair_part[:, cols]), r.upto[...], 1, 1))
        before = fold3(dg(split3(tail_part[:, cols]), r.upto[...], 1, 0)) - tail_part[:, cols]
        decay_grads.append(suffix + before + carry_terms[c])
    decay_grad = jnp.concatenate(decay_grads, axis=1)
    step_total = step_grad - rate * decay_grad
    step_pre_grad = step_total * r.sigmoid_step[...]
    rate_sum = jnp.sum(r.log_decay[...] * decay_grad, axis=1, keepdims=True)
    bias_sum = jnp.sum(step_pre_grad, axis=1, keepdims=True)
    step_cols = jnp.concatenate(
        [jnp.zeros((NS, T), f32), step_pre_grad, jnp.zeros((LANES - NS - H, T), f32)], axis=0
    ).T

    stage("conv_back")
    def after_masks(base):
        position = first_token + base + iota((ROWS, LANES), 0)
        now = segment(position)
        masks = []
        for k in range(CONV - 1):
            later = position + (CONV - 1) - k
            masks.append((segment(later) == now) & (later < total_tokens))
        return masks

    def conv_back(ext, taps, base, lanes, masks):
        value = None
        for k in range(CONV):
            term = taps[k : k + 1, lanes] * ext[pl.ds(base + CONV - 1 - k, ROWS), :]
            if k < CONV - 1:
                term = jnp.where(masks[k], term, 0.0)
            value = term if value is None else value + term
        return value

    def tap_sums(ext, grad, base, masks):
        sums = []
        for k in range(CONV):
            term = grad * ext[pl.ds(base + PAD - CONV + 1 + k, ROWS), :]
            sums.append(fold8(term if k == CONV - 1 else jnp.where(masks[k], term, 0.0)))
        return sums + [fold8(grad)]

    stage("poll_two")
    fold_in(0, 2)
    fold_middle(0, 0)
    stage("halo_one_wait")
    halo_one.wait_recv()
    stage("inner_back")

    def inner_back_rows(i, _):
        base = pl.multiple_of(i * ROWS, ROWS)
        rows = pl.ds(base, ROWS)
        masks = after_masks(base)
        before = agreements(base, ROWS)
        taps = r.inner_kernel[...]
        for g in range(NP):
            lanes = slice(g * LANES, g * LANES + LANES)
            r.inner_grad[rows, lanes] = conv_back(r.grad_ext.at[g], taps, base, lanes, masks).astype(bf)
            found = tap_sums(r.inner_ext.at[g], r.grad_ext[g, rows, :], base, before)
            for k, v in enumerate(found):
                r.sum_acc[2 + k, :, lanes] = r.sum_acc[2 + k, :, lanes] + v
        return 0

    lax.fori_loop(0, T // ROWS, inner_back_rows, 0)

    stage("poll_three")
    fold_in(0, 3)
    fold_middle(0, 1)
    stage("shared_wait")
    for d in range(1, n_tp):
        shared_copy(d, True).wait_recv()
    stage("shared_use")
    packed = r.shared_recv[0].astype(f32)
    for t in range(1, n_tp):
        packed = packed + r.shared_recv[t].astype(f32)
    r.state_grad_ext[0 : T // 2, :] = packed * slope(r.misc_conv[0 : T // 2, :])
    r.state_grad_ext[T // 2 : T, :] = pltpu.roll(packed, NS, 1) * slope(r.misc_conv[T // 2 : T, :])
    halo_two = remote(
        r.state_grad_ext.at[pl.ds(0, PAD)],
        r.state_grad_ext.at[pl.ds(T, PAD)],
        r.halo_send.at[1],
        r.halo_recv.at[1],
        left,
    )
    halo_two.start()
    waits.append(halo_two)
    stage("halo_two_wait")
    halo_two.wait_recv()
    stage("misc_back")
    r.misc_acc[...] = jnp.zeros_like(r.misc_acc)
    r.step_cols[...] = step_cols

    def misc_back_rows(i, _):
        base = pl.multiple_of(i * ROWS, ROWS)
        rows = pl.ds(base, ROWS)
        masks = after_masks(base)
        before = agreements(base, ROWS)
        taps = r.misc_taps[...]
        lanes = slice(0, LANES)
        value = conv_back(r.state_grad_ext, taps, base, lanes, masks)
        value = jnp.where(iota((ROWS, LANES), 1) < NS, value, r.step_cols[rows, :])
        r.misc_grad[rows, :] = value.astype(bf)
        found = tap_sums(r.misc_ext.at[0], r.state_grad_ext[rows, :], base, before)
        for k, v in enumerate(found):
            r.misc_acc[k] = r.misc_acc[k] + v
        return 0

    lax.fori_loop(0, T // ROWS, misc_back_rows, 0)

    stage("normed_grad")
    width = fold_width[1]
    for j in range(fold_pieces[1]):
        cols = slice(width * j, width * (j + 1))
        value = (
            dg(r.gate_grad[...], r.gate_weight[cols, :], 1, 1)
            + dg(r.inner_grad[...], r.inner_weight[cols, :], 1, 1)
            + dg(r.misc_grad[...], r.misc_weight[:, cols], 1, 0)
        )
        r.normed_part[j] = value.astype(bf)
        fold_start(1, j)
        hats = r.block_input[:, cols].astype(f32) * jnp.concatenate(
            [r.inverse[...]] * (width // LANES), axis=1
        )
        r.gain_part[:, cols] = fold8(value * hats)

    stage("small_sums")

    def row_of(v):
        return jnp.sum(v, axis=0, keepdims=True)

    eye_wide = iota((H, LANES), 0) == iota((H, LANES), 1)

    def lanes_of(v):
        return row_of(jnp.where(eye_wide, jnp.broadcast_to(v, (H, LANES)), 0.0))

    r.small_send[...] = jnp.zeros_like(r.small_send)
    for k in range(CONV + 1):
        r.small_send[k : k + 1, :] = row_of(r.sum_acc[2 + k])
    r.small_send[5:6, :] = row_of(r.sum_acc[0])
    r.small_send[6:7, :] = row_of(r.sum_acc[1])
    for k in range(CONV):
        r.small_send[7:8, k * LANES : k * LANES + LANES] = row_of(r.misc_acc[k])
    r.small_send[8:9, 0:LANES] = row_of(r.misc_acc[CONV])
    r.small_send[8:9, LANES : 2 * LANES] = lanes_of(bias_sum)
    r.small_send[8:9, 2 * LANES : 3 * LANES] = lanes_of(rate_sum)
    gain_rows = row_of(r.gain_part[...])
    for k in range(D // HI):
        r.small_send[9 + k : 10 + k, :] = gain_rows[:, k * HI : k * HI + HI]
    r.small_recv[seq] = r.small_send[...]
    small_wait = spread(
        "seq", lambda d: r.small_send, lambda d: r.small_recv.at[d], r.small_ss, r.small_rs
    )
    stage("poll_four")
    fold_middle(0, 2)
    fold_middle(0, 3)
    stage("weights_two")

    def weight_rows_two(i, _):
        cols = pl.ds(pl.multiple_of(i * LANES, LANES), LANES)
        r.wg_two[cols, 0:HI] = dg(r.normed[:, cols], r.inner_grad[...], 0, 0).astype(bf)
        r.wg_two[cols, HI : HI + LANES] = dg(r.normed[:, cols], r.misc_grad[...], 0, 0).astype(bf)
        return 0

    lax.fori_loop(0, D // LANES, weight_rows_two, 0)
    r.wg_two_recv[seq] = r.wg_two[mine, :]
    wg_two_wait = spread(
        "seq", lambda d: part_of(r.wg_two, d), lambda d: r.wg_two_recv.at[d], r.wg2_ss, r.wg2_rs
    )
    stage("small_wait")
    small_wait()
    total = r.small_recv[0]
    for d in range(1, n_seq):
        total = total + r.small_recv[d]
    r.small_total[...] = total
    r.gain_recv[tp] = r.small_total[8:16, :]
    gain_wait = spread(
        "tp", lambda t: r.small_total.at[pl.ds(8, 8)], lambda t: r.gain_recv.at[t], r.gain_ss, r.gain_rs
    )

    stage("folds")
    for j in range(fold_pieces[1] + 1):
        if j < fold_pieces[1]:
            fold_in(1, j)
        if j > 0:
            fold_middle(1, j - 1)
    for j in range(fold_pieces[0]):
        fold_end(0, j)
    for j in range(fold_pieces[1]):
        fold_end(1, j)

    stage("weights_wait")
    wg_one_wait()
    wg_two_wait()
    gain_wait()
    stage("weight_sums")

    def weight_sums(ref, recv):
        value = recv[0].astype(f32)
        for d in range(1, n_seq):
            value = value + recv[d].astype(f32)
        ref[...] = value

    weight_sums(r.sum_one, r.wg_one_recv)
    weight_sums(r.sum_two, r.wg_two_recv)
    gains = r.gain_recv[0]
    for t in range(1, n_tp):
        gains = gains + r.gain_recv[t]
    r.gain_total[...] = gains
    stage("drain")
    for d in range(1, n_tp):
        shared_copy(d).wait_send()
    for copy in waits:
        copy.wait_send()
    marks.close()


def finish(sizes, names, *refs):
    r = types.SimpleNamespace(**dict(zip(names, refs)))
    T, D, HI, H, NS = sizes
    P_ = HI // H

    def final_rows(i, _):
        rows = pl.ds(pl.multiple_of(i * ROWS, ROWS), ROWS)
        x = r.block_input[rows, :].astype(f32)
        r.block_output[rows, :] = (x + r.branch_sum[rows, :].astype(f32)).astype(bf)
        inverse = lax.rsqrt(jnp.mean(x * x, axis=1, keepdims=True) + epsilon)
        hat = x * inverse
        hat_grad = r.normed_sum[rows, :].astype(f32) * r.input_gain[...].reshape(1, D)
        mean = jnp.mean(hat_grad * hat, axis=1, keepdims=True)
        r.input_grad[rows, :] = r.out_cotangent[rows, :].astype(f32) + inverse * (
            hat_grad - hat * mean
        )
        return 0

    lax.fori_loop(0, T // ROWS, final_rows, 0)
    r.gate_weight_grad[...] = r.sum_one[:, 0:HI]
    r.out_weight_grad[...] = r.sum_one[:, HI : 2 * HI].T
    r.inner_weight_grad[...] = r.sum_two[:, 0:HI]
    narrow = r.sum_two[:, HI : HI + LANES].T
    r.state_weight_grad[...] = narrow[0:NS]
    r.step_weight_grad[...] = narrow[NS : NS + H]
    small = r.small_total
    r.inner_kernel_grad[...] = small[0:CONV, :]
    r.inner_conv_bias_grad[...] = small[CONV : CONV + 1, :].reshape(HI)
    r.gate_gain_grad[...] = small[5:6, :].reshape(HI)
    head_sum = (iota((HI, LANES), 0) // P_ == iota((HI, LANES), 1)).astype(f32).astype(bf)
    skip_sums = fold3(dg(split3(jnp.broadcast_to(small[6:7, :], (8, HI))), head_sum, 1, 0))
    r.skip_scale_grad[...] = skip_sums[0:1, 0:H].reshape(H)
    for k in range(CONV):
        r.state_kernel_grad[k : k + 1, :] = small[7:8, k * LANES : k * LANES + NS]
    r.state_conv_bias_grad[...] = small[8:9, 0:NS].reshape(NS)
    r.step_bias_grad[...] = small[8:9, LANES : LANES + H].reshape(H)
    r.rate_log_grad[...] = small[8:9, 2 * LANES : 2 * LANES + H].reshape(H)
    for k in range(D // HI):
        r.input_gain_grad[k * HI : k * HI + HI] = r.gain_total[1 + k : 2 + k, :].reshape(HI)


INPUTS = (
    "block_input",
    "scene_lengths",
    "input_gain",
    "gate_weight",
    "inner_weight",
    "state_weight",
    "step_weight",
    "step_bias",
    "rate_log",
    "inner_kernel",
    "inner_conv_bias",
    "state_kernel",
    "state_conv_bias",
    "skip_scale",
    "gate_gain",
    "out_weight",
    "out_cotangent",
)
OUTPUTS = (
    "block_output",
    "input_grad",
    "input_gain_grad",
    "gate_weight_grad",
    "inner_weight_grad",
    "state_weight_grad",
    "step_weight_grad",
    "step_bias_grad",
    "rate_log_grad",
    "inner_kernel_grad",
    "inner_conv_bias_grad",
    "state_kernel_grad",
    "state_conv_bias_grad",
    "skip_scale_grad",
    "gate_gain_grad",
    "out_weight_grad",
)


SUMS = ("branch_sum", "normed_sum", "sum_one", "sum_two", "small_total", "gain_total")


def local(*args):
    given = dict(zip(INPUTS, args))
    given["state_weight"] = given["state_weight"].T
    given["step_weight"] = given["step_weight"].T
    n_seq = lax.axis_size("seq")
    n_tp = lax.axis_size("tp")
    T, D = given["block_input"].shape
    HI = given["gate_weight"].shape[1]
    H = given["step_bias"].shape[0]
    NS = given["state_weight"].shape[0]
    N = STATE
    Q = CHUNK
    NC = T // Q
    NP = HI // LANES
    R = HI // n_seq
    R2 = D // n_seq
    outs = (
        ((T, D), bf),
        ((T, D), f32),
        ((D,), f32),
        ((R2, HI), f32),
        ((R2, HI), f32),
        ((NS, R2), f32),
        ((H, R2), f32),
        ((H,), f32),
        ((H,), f32),
        ((CONV, HI), f32),
        ((HI,), f32),
        ((CONV, NS), f32),
        ((NS,), f32),
        ((H,), f32),
        ((HI,), f32),
        ((HI, R2), f32),
    )
    sums = (
        ((T, D), bf),
        ((T, D), bf),
        ((R2, 2 * HI), f32),
        ((R2, HI + LANES), f32),
        ((16, HI), f32),
        ((8, HI), f32),
    )
    scratch = dict(
        inverse=((T, LANES), f32),
        normed=((T, D), bf),
        misc_weight=((LANES, D), bf),
        inner_ext=((NP, T + PAD, LANES), f32),
        misc_ext=((1, T + PAD, LANES), f32),
        gate_pre=((T, HI), f32),
        misc_taps=((8, LANES), f32),
        inner_bias=((1, HI), f32),
        gain_row=((1, HI), f32),
        misc_conv=((T, LANES), f32),
        inner_conv=((T, HI), f32),
        act=((T, HI), bf),
        state_send=((T // 2, LANES), bf),
        state_recv=((n_tp, T // 2, LANES), bf),
        keys=((T, N), bf),
        queries=((T, N), bf),
        sigmoid_step=((H, T), f32),
        step_rows=((H, T), f32),
        log_decay=((H, T), f32),
        upto=((Q, Q), bf),
        expand=((3 * H, HI), bf),
        mask=((NC, Q, Q), f32),
        cum_left=((H, 16, T), bf),
        cum_right=((H, 16, T), bf),
        step_wide=((T, HI), f32),
        enter_wide=((T, HI), f32),
        tail_wide=((T, HI), f32),
        decay_wide=((NC, HI, LANES), f32),
        skip_wide=((8, HI), f32),
        xt=((T, HI), bf),
        xt_rest=((T, HI), bf),
        fresh=((NC, HI, N), f32),
        end_send=((HI, N), f32),
        end_recv=((n_seq, R, N), f32),
        decay_send=((H, LANES), f32),
        decay_recv=((n_seq, H, LANES), f32),
        enter_send=((n_seq, R, N), f32),
        enter_state=((HI, N), f32),
        state_in=((NC, HI, N), f32),
        state_in_low=((NC, HI, N), bf),
        state_in_rest=((NC, HI, N), bf),
        scores=((NC, Q, Q), f32),
        score_grad=((NC, Q, Q), f32),
        decays=((NC, H, Q, Q), f32),
        mixed=((T, HI), f32),
        norm_grad=((T, HI), f32),
        heads_out=((T, HI), f32),
        gated=((T, HI), f32),
        squares=((T, LANES), f32),
        products=((T, LANES), f32),
        sums_send=((8, T), f32),
        sums_recv=((n_tp, 8, T), f32),
        norm_col=((T, LANES), f32),
        back_col=((T, LANES), f32),
        head_sum=((HI, LANES), bf),
        head_sum_two=((HI, LANES), bf),
        head_sum_three=((HI, LANES), bf),
        sum_acc=((7, 8, HI), f32),
        gated_norm=((T, HI), bf),
        gate_grad=((T, HI), bf),
        heads_grad=((T, HI), f32),
        dy=((T, HI), bf),
        dy_rest=((T, HI), bf),
        dy_enter=((T, HI), bf),
        dy_enter_rest=((T, HI), bf),
        sum_y=((T, LANES), f32),
        sum_x=((T, LANES), f32),
        grad_local=((NC, HI, N), f32),
        grad_send=((HI, N), f32),
        grad_recv=((n_seq, R, N), f32),
        leave_send=((n_seq, R, N), f32),
        leave_grad=((HI, N), f32),
        x_inside=((T, HI), f32),
        x_carry=((T, HI), f32),
        wg_one=((D, 2 * HI), bf),
        wg_one_recv=((n_seq, R2, 2 * HI), bf),
        wg_two=((D, HI + LANES), bf),
        wg_two_recv=((n_seq, R2, HI + LANES), bf),
        query_grad=((T, N), f32),
        key_grad=((T, N), f32),
        shared_send=((n_tp, T // 2, LANES), bf),
        shared_recv=((n_tp, T // 2, LANES), bf),
        grad_ext=((NP, T + PAD, LANES), f32),
        state_grad_ext=((T + PAD, LANES), f32),
        inner_grad=((T, HI), bf),
        step_cols=((T, LANES), f32),
        misc_grad=((T, LANES), bf),
        misc_acc=((CONV + 1, 8, LANES), f32),
        normed_part=((8, T, D // 8), bf),
        normed_in=((8, T, D // 8), bf),
        normed_across=((8, T, D // 8), bf),
        branch=((4, T, D // 4), bf),
        branch_in=((4, T, D // 4), bf),
        branch_across=((4, T, D // 4), bf),
        gain_part=((8, D), f32),
        small_send=((16, HI), f32),
        small_recv=((n_seq, 16, HI), f32),
        gain_recv=((n_tp, 8, HI), f32),
    )
    semaphores = dict(
        rim_send=(2,),
        rim_recv=(2,),
        halo_send=(2,),
        halo_recv=(2,),
        fold_ss=(3, 12),
        fold_rs=(3, 12),
    )
    for name in ("state", "sums", "shared", "gain"):
        semaphores[name + "_ss"] = (n_tp - 1,)
        semaphores[name + "_rs"] = (n_tp - 1,)
    for name in ("decay", "end", "enter", "grad", "leave", "wg1", "wg2", "small"):
        semaphores[name + "_ss"] = (n_seq - 1,)
        semaphores[name + "_rs"] = (n_seq - 1,)
    names = INPUTS + SUMS + tuple(scratch) + tuple(semaphores)
    vmem = pl.BlockSpec(memory_space=pltpu.VMEM)
    smem = pl.BlockSpec(memory_space=pltpu.SMEM)
    totals = pl.pallas_call(
        functools.partial(kernel, (n_seq, n_tp, T, D, HI, H, NS), names),
        out_shape=tuple(jax.ShapeDtypeStruct(s, t) for s, t in sums),
        in_specs=[smem if n == "scene_lengths" else vmem for n in INPUTS],
        out_specs=tuple(vmem for _ in sums),
        scratch_shapes=[pltpu.VMEM(s, t) for s, t in scratch.values()]
        + [pltpu.SemaphoreType.DMA(s) for s in semaphores.values()],
        compiler_params=pltpu.CompilerParams(
            collective_id=0, has_side_effects=True, vmem_limit_bytes=60 * 2**20
        ),
    )(*given.values())
    needed = ("block_input", "input_gain", "out_cotangent")
    results = pl.pallas_call(
        functools.partial(finish, (T, D, HI, H, NS), needed + SUMS + OUTPUTS),
        out_shape=tuple(jax.ShapeDtypeStruct(s, t) for s, t in outs),
        in_specs=[vmem] * (len(needed) + len(SUMS)),
        out_specs=tuple(vmem for _ in outs),
        compiler_params=pltpu.CompilerParams(vmem_limit_bytes=60 * 2**20),
    )(*(given[n] for n in needed), *totals)
    results = dict(zip(OUTPUTS, results))
    results["state_weight_grad"] = results["state_weight_grad"].T
    results["step_weight_grad"] = results["step_weight_grad"].T
    return tuple(results.values())


def solution(mesh):
    rows = P("seq", None)
    cols = P(None, "tp")
    heads = P("tp")
    return jax.shard_map(
        local,
        mesh=mesh,
        in_specs=(
            rows,
            P(),
            P(),
            cols,
            cols,
            cols,
            cols,
            heads,
            heads,
            cols,
            heads,
            cols,
            heads,
            heads,
            heads,
            P("tp", None),
            rows,
        ),
        out_specs=(
            rows,
            rows,
            P(),
            P("seq", "tp"),
            P("seq", "tp"),
            P("seq", "tp"),
            P("seq", "tp"),
            heads,
            heads,
            cols,
            heads,
            cols,
            heads,
            heads,
            heads,
            P("tp", "seq"),
        ),
        check_vma=False,
    )
```

```python
import contextlib
import functools
import types

import jax
import jax.numpy as jnp
from jax import lax
from jax.experimental import pallas as pl
from jax.experimental.pallas import tpu as pltpu
from jax.sharding import PartitionSpec as P

STATE = 128
CONV = 4
CHUNK = 256
LANES = 128
PAD = 8
ROWS = 64
epsilon = 1e-05
bf = jnp.bfloat16
f32 = jnp.float32
i32 = jnp.int32
MESH = pl.DeviceIdType.MESH


def dg(left, right, left_dim, right_dim):
    return lax.dot_general(
        left, right, (((left_dim,), (right_dim,)), ((), ())), preferred_element_type=f32
    )


def split3(v):
    high = v.astype(bf).astype(f32)
    middle = (v - high).astype(bf).astype(f32)
    return jnp.concatenate([high, middle, v - high - middle], axis=0).astype(bf)


def fold3(v):
    third = v.shape[0] // 3
    return v[:third] + v[third : 2 * third] + v[2 * third :]


def halves(v):
    high = v.astype(bf)
    return high, (v - high.astype(f32)).astype(bf)


def slope(v):
    s = jax.nn.sigmoid(v)
    return s * (1.0 + v * (1.0 - s))


def fold8(v):
    total = v[0:8]
    for i in range(1, v.shape[0] // 8):
        total = total + v[8 * i : 8 * i + 8]
    return total


def iota(shape, dim):
    return lax.broadcasted_iota(i32, shape, dim)


def kernel(sizes, names, *refs):
    r = types.SimpleNamespace(**dict(zip(names, refs)))
    n_seq, n_tp, T, D, HI, H, NS = sizes
    N = STATE
    P_ = HI // H
    Q = CHUNK
    NC = T // Q
    NP = HI // LANES
    R = HI // n_seq
    R2 = D // n_seq
    total_tokens = T * n_seq
    seq = lax.axis_index("seq")
    tp = lax.axis_index("tp")

    barrier = pltpu.get_barrier_semaphore()
    for d in range(1, n_seq):
        pl.semaphore_signal(
            barrier, inc=1, device_id=((seq + d) % n_seq, tp), device_id_type=MESH
        )
    for d in range(1, n_tp):
        pl.semaphore_signal(
            barrier, inc=1, device_id=(seq, (tp + d) % n_tp), device_id_type=MESH
        )

    waits = []
    half = n_tp // 2
    inner = jnp.where(tp < half, tp + 1, tp - 1)
    outer = jnp.where(tp < half, tp - 1, tp + 1)
    is_middle = (tp == half - 1) | (tp == half)
    has_outer = (tp > 0) & (tp < n_tp - 1)
    fold_pieces = (r.branch_in.shape[0], r.normed_in.shape[0])
    fold_width = tuple(D // n for n in fold_pieces)
    fold_refs = (
        (r.branch, r.branch_in, r.branch_across, r.branch_sum),
        (r.normed_part, r.normed_in, r.normed_across, r.normed_sum),
    )

    def fold(a, j):
        partial, arrived, across, total = (
            ref.at[j] if k < 3 else ref.at[:, pl.ds(j * fold_width[a], fold_width[a])]
            for k, ref in enumerate(fold_refs[a])
        )
        return partial, arrived, across, total

    def fold_copy(a, j, leg):
        partial, arrived, across, total = fold(a, j)
        sems = leg, sum(fold_pieces[:a]) + j
        source, target, place = ((partial, arrived, inner), (partial, across, inner), (total, total, outer))[leg]
        return remote(source, target, r.fold_ss.at[sems], r.fold_rs.at[sems], (seq, place))

    def fold_start(a, j):
        pl.when(jnp.logical_not(has_outer | is_middle))(fold_copy(a, j, 0).start)

    def fold_in(a, j):
        partial, arrived, _, _ = fold(a, j)

        @pl.when(has_outer)
        def _():
            fold_copy(a, j, 0).wait_recv()
            partial[...] = (partial[...].astype(f32) + arrived[...].astype(f32)).astype(bf)

        pl.when(is_middle)(fold_copy(a, j, 1).start)
        pl.when(has_outer & jnp.logical_not(is_middle))(fold_copy(a, j, 0).start)

    def fold_middle(a, j):
        partial, _, across, total = fold(a, j)

        @pl.when(is_middle)
        def _():
            fold_copy(a, j, 1).wait_recv()
            total[...] = (partial[...].astype(f32) + across[...].astype(f32)).astype(bf)
            pl.when(has_outer)(fold_copy(a, j, 2).start)

    def fold_end(a, j):
        @pl.when(jnp.logical_not(is_middle))
        def _():
            fold_copy(a, j, 2).wait_recv()
            pl.when(has_outer)(fold_copy(a, j, 2).start)
            fold_copy(a, j, 0).wait_send()

        pl.when(has_outer)(fold_copy(a, j, 2).wait_send)
        pl.when(is_middle)(fold_copy(a, j, 1).wait_send)

    marks = contextlib.ExitStack()

    def stage(name):
        marks.close()
        marks.enter_context(jax.named_scope(name))

    stage("norm")

    def remote(src, dst, send, recv, device):
        return pltpu.make_async_remote_copy(
            src_ref=src,
            dst_ref=dst,
            send_sem=send,
            recv_sem=recv,
            device_id=device,
            device_id_type=MESH,
        )

    def spread(axis, src_to, dst_from, send, recv):
        n = n_seq if axis == "seq" else n_tp
        me = seq if axis == "seq" else tp
        incoming = []
        for d in range(1, n):
            target = (me + d) % n
            source = (me + n - d) % n
            device = (target, tp) if axis == "seq" else (seq, target)
            out = remote(src_to(target), dst_from(me), send.at[d - 1], recv.at[d - 1], device)
            out.start()
            waits.append(out)
            incoming.append(
                remote(src_to(target), dst_from(source), send.at[d - 1], recv.at[d - 1], device)
            )

        def wait():
            for copy in incoming:
                copy.wait_recv()

        return wait

    starts = [jnp.int32(0)]
    for k in range(r.scene_lengths.shape[0] - 1):
        starts.append(starts[-1] + r.scene_lengths[k])

    def segment(position):
        found = (position >= starts[0]).astype(i32)
        for s in starts[1:]:
            found = found + (position >= s).astype(i32)
        return found

    first_token = seq * T

    def norm_rows(i, _):
        rows = pl.ds(pl.multiple_of(i * ROWS, ROWS), ROWS)
        x = r.block_input[rows, :].astype(f32)
        inverse = lax.rsqrt(jnp.mean(x * x, axis=1, keepdims=True) + epsilon)
        r.inverse[rows, :] = jnp.broadcast_to(inverse, (ROWS, LANES))
        r.normed[rows, :] = (x * inverse * r.input_gain[...].reshape(1, D)).astype(bf)
        return 0

    lax.fori_loop(0, T // ROWS, norm_rows, 0)

    stage("projections")
    r.misc_weight[...] = jnp.zeros_like(r.misc_weight)
    r.misc_weight[0:NS, :] = r.state_weight[...]
    r.misc_weight[NS : NS + H, :] = r.step_weight[...]
    normed_all = r.normed[...]
    for j in range(HI // 256):
        cols = slice(256 * j, 256 * j + 256)
        value = dg(normed_all, r.inner_weight[:, cols], 1, 0)
        r.inner_ext[2 * j, PAD : PAD + T, :] = value[:, :LANES]
        r.inner_ext[2 * j + 1, PAD : PAD + T, :] = value[:, LANES:]
    r.misc_ext[0, PAD : PAD + T, :] = dg(normed_all, r.misc_weight[...], 1, 1)

    stage("barrier")
    pl.semaphore_wait(barrier, n_seq - 1 + n_tp - 1)
    stage("gate_projection")
    right = ((seq + 1) % n_seq, tp)
    left = ((seq + n_seq - 1) % n_seq, tp)
    rim = [
        remote(
            ref.at[:, pl.ds(T, PAD)],
            ref.at[:, pl.ds(0, PAD)],
            r.rim_send.at[k],
            r.rim_recv.at[k],
            right,
        )
        for k, ref in enumerate((r.inner_ext, r.misc_ext))
    ]
    for copy in rim:
        copy.start()
    waits.extend(rim)
    for j in range(HI // 256):
        cols = slice(256 * j, 256 * j + 256)
        r.gate_pre[:, cols] = dg(normed_all, r.gate_weight[:, cols], 1, 0)

    stage("convolutions")
    def agreements(base, rows):
        position = first_token + base + iota((rows, LANES), 0)
        now = segment(position)
        return [segment(position - (CONV - 1) + k) == now for k in range(CONV - 1)]

    def conv_block(ext, taps, bias, base, lanes, masks):
        value = bias[:, lanes]
        for k in range(CONV):
            window = ext[pl.ds(base + PAD - CONV + 1 + k, ROWS), :]
            term = taps[k : k + 1, lanes] * window
            value = value + (term if k == CONV - 1 else jnp.where(masks[k], term, 0.0))
        return value

    r.misc_taps[...] = jnp.zeros_like(r.misc_taps)
    r.misc_taps[0:CONV, 0:NS] = r.state_kernel[...]
    r.misc_taps[CONV : CONV + 1, 0:NS] = r.state_conv_bias[...].reshape(1, NS)
    r.inner_bias[...] = r.inner_conv_bias[...].reshape(1, HI)
    stage("rim_wait")
    for copy in rim:
        copy.wait_recv()
    stage("conv")

    def misc_conv_rows(i, _):
        base = pl.multiple_of(i * ROWS, ROWS)
        masks = agreements(base, ROWS)
        taps = r.misc_taps[...]
        value = conv_block(
            r.misc_ext.at[0], taps, taps[CONV : CONV + 1], base, slice(0, LANES), masks
        )
        r.misc_conv[pl.ds(base, ROWS), :] = value
        return 0

    lax.fori_loop(0, T // ROWS, misc_conv_rows, 0)
    low_lanes = iota((T // 2, LANES), 1) < NS
    own = r.misc_conv[...]
    own = own * jax.nn.sigmoid(own)
    r.state_send[...] = jnp.where(
        low_lanes, own[: T // 2], pltpu.roll(own[T // 2 :], NS, 1)
    ).astype(bf)
    r.state_recv[tp] = r.state_send[...]
    state_wait = spread(
        "tp",
        lambda t: r.state_send,
        lambda t: r.state_recv.at[t],
        r.state_ss,
        r.state_rs,
    )

    def inner_conv_rows(i, _):
        base = pl.multiple_of(i * ROWS, ROWS)
        rows = pl.ds(base, ROWS)
        masks = agreements(base, ROWS)
        taps = r.inner_kernel[...]
        for g in range(NP):
            lanes = slice(g * LANES, g * LANES + LANES)
            value = conv_block(r.inner_ext.at[g], taps, r.inner_bias, base, lanes, masks)
            r.inner_conv[rows, lanes] = value
            r.act[rows, lanes] = (value * jax.nn.sigmoid(value)).astype(bf)
        return 0

    lax.fori_loop(0, T // ROWS, inner_conv_rows, 0)

    stage("decays")
    eye = iota((H, H), 0) == iota((H, H), 1)

    def column(ref):
        wide = jnp.broadcast_to(ref[...].reshape(1, H), (H, H))
        return jnp.sum(jnp.where(eye, wide, 0.0), axis=1, keepdims=True)

    step_in = r.misc_ext[0, PAD : PAD + T, :].T[NS : NS + H, :] + column(r.step_bias)
    step = jnp.maximum(step_in, 0.0) + jnp.log1p(jnp.exp(-jnp.abs(step_in)))
    rate = jnp.exp(column(r.rate_log))
    log_decay = step * -rate
    r.sigmoid_step[...] = jax.nn.sigmoid(step_in)
    r.log_decay[...] = log_decay
    r.step_rows[...] = step
    r.upto[...] = (iota((Q, Q), 0) <= iota((Q, Q), 1)).astype(f32).astype(bf)
    r.expand[...] = (iota((3 * H, HI), 0) % H == iota((3 * H, HI), 1) // P_).astype(f32).astype(bf)
    expand = r.expand[...]

    entering, tailing, chunk_decay = [], [], []
    ones_rows = jnp.ones((1, Q), f32)
    for c in range(NC):
        cols = slice(c * Q, c * Q + Q)
        cumulative = fold3(dg(split3(log_decay[:, cols]), r.upto[...], 1, 0))
        start = first_token + c * Q
        seg_row = segment(start + iota((H, Q), 1))
        seg_before = segment(start - 1)
        seg_end = segment(start + Q - 1)
        last = cumulative[:, Q - 1 : Q]
        enter = jnp.where(seg_row == seg_before, jnp.exp(cumulative), 0.0)
        tail = jnp.where(seg_row == seg_end, jnp.exp(last - cumulative), 0.0)
        entering.append(enter)
        tailing.append(tail)
        chunk_decay.append(enter[:, Q - 1 : Q])
        seg_col = segment(start + iota((Q, Q), 0))
        seg_lane = segment(start + iota((Q, Q), 1))
        keep = (seg_col == seg_lane) & (iota((Q, Q), 0) >= iota((Q, Q), 1))
        r.mask[c] = jnp.where(keep, 0.0, -1e30)
        high = cumulative.astype(bf).astype(f32)
        middle = (cumulative - high).astype(bf).astype(f32)
        rest = cumulative - high - middle
        which = iota((16, Q), 0)
        for h in range(H):
            parts = jnp.where(
                which % 3 == 0,
                high[h : h + 1],
                jnp.where(which % 3 == 1, middle[h : h + 1], rest[h : h + 1]),
            )
            first = which < 3
            second = (which >= 3) & (which < 6)
            r.cum_left[h, :, cols] = jnp.where(
                first, parts, jnp.where(second, 1.0, 0.0)
            ).astype(bf)
            r.cum_right[h, :, cols] = jnp.where(
                first, 1.0, jnp.where(second, -parts, 0.0)
            ).astype(bf)

    def wide(v):
        return dg(split3(v), expand, 0, 0)

    def wide_rows(v):
        return dg(expand, split3(jnp.broadcast_to(v, (H, LANES))), 0, 0)

    for c in range(NC):
        rows = slice(c * Q, c * Q + Q)
        r.step_wide[rows, :] = wide(step[:, rows])
        r.enter_wide[rows, :] = wide(entering[c])
        r.tail_wide[rows, :] = wide(tailing[c])
        r.decay_wide[c] = wide_rows(chunk_decay[c])
    r.skip_wide[...] = dg(split3(jnp.broadcast_to(column(r.skip_scale), (H, 8))), expand, 0, 0)

    def scaled_rows(i, _):
        rows = pl.ds(pl.multiple_of(i * ROWS, ROWS), ROWS)
        x = r.act[rows, :].astype(f32)
        r.xt[rows, :], r.xt_rest[rows, :] = halves(x * r.step_wide[rows, :] * r.tail_wide[rows, :])
        return 0

    lax.fori_loop(0, T // ROWS, scaled_rows, 0)

    stage("decay_matrices")

    def decay_matrix(i, _):
        c = i // H
        h = i % H
        rows = pl.ds(pl.multiple_of(c * Q, Q), Q)
        difference = dg(r.cum_left[h, :, rows], r.cum_right[h, :, rows], 0, 0)
        r.decays[c, h] = jnp.exp(difference + r.mask[c])
        return 0

    lax.fori_loop(0, NC * H, decay_matrix, 0)

    stage("keys_wait")
    state_wait()
    shards = n_tp // 2
    half_low = iota((T // 2, LANES), 1) < NS
    for ref, at in ((r.keys, 0), (r.queries, shards)):
        one, two = r.state_recv[at].astype(f32), r.state_recv[at + 1].astype(f32)
        ref[0 : T // 2, :] = jnp.where(half_low, one, pltpu.roll(two, NS, 1)).astype(bf)
        ref[T // 2 : T, :] = jnp.where(half_low, pltpu.roll(one, NS, 1), two).astype(bf)

    stage("end_states")
    end_state = None
    device_decay = None
    for c in range(NC):
        rows = slice(c * Q, c * Q + Q)
        keys = r.keys[rows, :]
        fresh = dg(r.xt[rows, :], keys, 0, 0) + dg(r.xt_rest[rows, :], keys, 0, 0)
        r.fresh[c] = fresh
        end_state = fresh if c == 0 else r.decay_wide[c] * end_state + fresh
        device_decay = chunk_decay[c] if c == 0 else device_decay * chunk_decay[c]
    r.end_send[...] = end_state
    r.decay_send[...] = jnp.broadcast_to(device_decay, (H, LANES))

    def block(ref, device):
        return ref.at[pl.ds(pl.multiple_of(device * R, R), R)]

    r.end_recv[seq] = r.end_send[pl.ds(pl.multiple_of(seq * R, R), R), :]
    r.decay_recv[seq] = r.decay_send[...]
    decay_wait = spread(
        "seq", lambda d: r.decay_send, lambda d: r.decay_recv.at[d], r.decay_ss, r.decay_rs
    )
    end_wait = spread(
        "seq", lambda d: block(r.end_send, d), lambda d: r.end_recv.at[d], r.end_ss, r.end_rs
    )

    stage("inside")
    for c in range(NC):
        rows = slice(c * Q, c * Q + Q)
        r.scores[c] = dg(r.queries[rows, :], r.keys[rows, :], 1, 1)
    low = iota((Q, LANES), 1) < P_

    def inside(i, _):
        c = i // NP
        p = i % NP
        rows = pl.ds(pl.multiple_of(c * Q, Q), Q)
        lanes = pl.ds(pl.multiple_of(p * LANES, LANES), LANES)
        x = r.act[rows, lanes]
        zero = jnp.zeros_like(x)
        result = None
        for s in range(2):
            h = 2 * p + s
            weight, rest = halves(r.decays[c, h] * r.scores[c] * r.step_rows[pl.ds(h, 1), rows])
            part = jnp.where(low, x, zero) if s == 0 else jnp.where(low, zero, x)
            term = dg(weight, part, 1, 0) + dg(rest, part, 1, 0)
            result = term if s == 0 else result + term
        r.mixed[rows, lanes] = result
        return 0

    lax.fori_loop(0, NC * NP, inside, 0)
    for j in range(HI // 256):
        cols = slice(256 * j, 256 * j + 256)
        r.norm_grad[:, cols] = dg(r.out_cotangent[...], r.out_weight[cols, :], 1, 1)

    stage("entering")
    head_of = (seq * R) // P_
    stage("end_wait")
    end_wait()
    decay_wait()

    def decay_of(d):
        return jnp.broadcast_to(r.decay_recv[d, pl.ds(head_of, 1), :], (R, LANES))

    running = jnp.zeros((R, N), f32)
    for d in range(n_seq):
        r.enter_send[d] = running
        running = decay_of(d) * running + r.end_recv[d]
    own_rows = pl.ds(pl.multiple_of(seq * R, R), R)
    r.enter_state[own_rows, :] = r.enter_send[seq]
    enter_wait = spread(
        "seq", lambda d: r.enter_send.at[d], lambda d: block(r.enter_state, d), r.enter_ss, r.enter_rs
    )
    stage("enter_wait")
    enter_wait()
    stage("readout")
    for c in range(NC):
        rows = slice(c * Q, c * Q + Q)
        if c == 0:
            state = r.enter_state[...]
        else:
            state = r.decay_wide[c - 1] * state + r.fresh[c - 1]
        r.state_in[c] = state
        r.state_in_low[c], r.state_in_rest[c] = halves(state)
        for j in range(HI // 256):
            cols = slice(256 * j, 256 * j + 256)
            queries = r.queries[rows, :]
            read = dg(queries, r.state_in_low[c, cols, :], 1, 1) + dg(queries, r.state_in_rest[c, cols, :], 1, 1)
            r.mixed[rows, cols] = r.mixed[rows, cols] + r.enter_wide[rows, cols] * read

    stage("gated")
    skip_row = r.skip_wide[0:1, :]
    r.gain_row[...] = r.gate_gain[...].reshape(1, HI)

    def gated_rows(i, _):
        rows = pl.ds(pl.multiple_of(i * ROWS, ROWS), ROWS)
        heads = r.mixed[rows, :] + skip_row * r.act[rows, :].astype(f32)
        gate = r.gate_pre[rows, :]
        gated = heads * (gate * jax.nn.sigmoid(gate))
        r.heads_out[rows, :] = heads
        r.gated[rows, :] = gated
        scaled = r.norm_grad[rows, :] * r.gain_row[...]
        squares = gated * gated
        products = scaled * gated

        def lane_sum(v):
            total = v[:, :LANES]
            for g in range(1, NP):
                total = total + v[:, g * LANES : g * LANES + LANES]
            return total

        r.squares[rows, :] = lane_sum(squares)
        r.products[rows, :] = lane_sum(products)
        return 0

    lax.fori_loop(0, T // ROWS, gated_rows, 0)
    square_row = jnp.sum(r.squares[...].T, axis=0, keepdims=True)
    product_row = jnp.sum(r.products[...].T, axis=0, keepdims=True)
    r.sums_send[...] = jnp.where(
        iota((8, T), 0) == 0,
        jnp.broadcast_to(square_row, (8, T)),
        jnp.broadcast_to(product_row, (8, T)),
    )
    r.sums_recv[tp] = r.sums_send[...]
    sums_wait = spread(
        "tp", lambda t: r.sums_send, lambda t: r.sums_recv.at[t], r.sums_ss, r.sums_rs
    )
    stage("sums_wait")
    sums_wait()
    stage("sums")
    sums = r.sums_recv[0]
    for t in range(1, n_tp):
        sums = sums + r.sums_recv[t]
    count = HI * n_tp
    norm_row = lax.rsqrt(sums[0:1] / count + epsilon)
    back_row = norm_row * norm_row * norm_row * (sums[1:2] / count)
    r.norm_col[...] = jnp.broadcast_to(norm_row, (LANES, T)).T
    r.back_col[...] = jnp.broadcast_to(back_row, (LANES, T)).T

    stage("back_gated")
    r.head_sum[...] = (iota((HI, LANES), 0) // P_ == iota((HI, LANES), 1)).astype(f32).astype(bf)
    r.sum_acc[...] = jnp.zeros_like(r.sum_acc)

    def tile4(v):
        return jnp.concatenate([v] * NP, axis=1)

    def summed(v, which):
        high, lowv = halves(v)
        return dg(high, which, 1, 0) + dg(lowv, which, 1, 0)

    def back_rows(i, _):
        rows = pl.ds(pl.multiple_of(i * ROWS, ROWS), ROWS)
        norm = tile4(r.norm_col[rows, :])
        back = tile4(r.back_col[rows, :])
        gated = r.gated[rows, :]
        grad = r.norm_grad[rows, :]
        gain = r.gain_row[...]
        gate = r.gate_pre[rows, :]
        sigma = jax.nn.sigmoid(gate)
        unit = gated * norm
        r.gated_norm[rows, :] = (unit * gain).astype(bf)
        r.sum_acc[0] = r.sum_acc[0] + fold8(grad * unit)
        gated_grad = norm * (grad * gain) - gated * back
        heads_grad = gated_grad * (gate * sigma)
        heads = r.heads_out[rows, :]
        r.gate_grad[rows, :] = (
            gated_grad * heads * (sigma * (1.0 + gate * (1.0 - sigma)))
        ).astype(bf)
        r.heads_grad[rows, :] = heads_grad
        x = r.act[rows, :].astype(f32)
        r.sum_acc[1] = r.sum_acc[1] + fold8(heads_grad * x)
        r.dy[rows, :], r.dy_rest[rows, :] = halves(heads_grad)
        r.dy_enter[rows, :], r.dy_enter_rest[rows, :] = halves(heads_grad * r.enter_wide[rows, :])
        r.sum_y[rows, :] = summed(heads_grad * r.mixed[rows, :], r.head_sum[...])
        return 0

    lax.fori_loop(0, T // ROWS, back_rows, 0)

    stage("grad_states")
    grad_in = None
    for c in reversed(range(NC)):
        rows = slice(c * Q, c * Q + Q)
        queries = r.queries[rows, :]
        local = dg(r.dy_enter[rows, :], queries, 0, 0) + dg(r.dy_enter_rest[rows, :], queries, 0, 0)
        r.grad_local[c] = local
        grad_in = local if grad_in is None else r.decay_wide[c] * grad_in + local
    r.grad_send[...] = grad_in
    r.grad_recv[seq] = r.grad_send[own_rows, :]
    grad_wait = spread(
        "seq", lambda d: block(r.grad_send, d), lambda d: r.grad_recv.at[d], r.grad_ss, r.grad_rs
    )
    stage("out_projection")
    for j in range(fold_pieces[0]):
        cols = slice(fold_width[0] * j, fold_width[0] * (j + 1))
        r.branch[j] = dg(r.gated_norm[...], r.out_weight[:, cols], 1, 0).astype(bf)
        fold_start(0, j)
    stage("inside_back")
    r.score_grad[...] = jnp.zeros_like(r.score_grad)

    def inside_back(i, _):
        c = i // NP
        p = i % NP
        rows = pl.ds(pl.multiple_of(c * Q, Q), Q)
        lanes = pl.ds(pl.multiple_of(p * LANES, LANES), LANES)
        x = r.act[rows, lanes]
        dy = r.dy[rows, lanes]
        dy_rest = r.dy_rest[rows, lanes]
        zero = jnp.zeros_like(dy)
        result = None
        for s in range(2):
            h = 2 * p + s
            decay = r.decays[c, h]
            weight, rest = halves(decay * r.scores[c])

            def masked(v):
                return jnp.where(low, v, zero) if s == 0 else jnp.where(low, zero, v)

            part, part_rest = masked(dy), masked(dy_rest)
            pairs = dg(part, x, 1, 1) + dg(part_rest, x, 1, 1)
            r.score_grad[c] = r.score_grad[c] + pairs * (decay * r.step_rows[pl.ds(h, 1), rows])
            term = dg(weight, part, 0, 0) + dg(rest, part, 0, 0) + dg(weight, part_rest, 0, 0)
            result = term if s == 0 else result + term
        r.x_inside[rows, lanes] = result
        return 0

    lax.fori_loop(0, NC * NP, inside_back, 0)

    stage("query_grad")
    for c in range(NC):
        rows = slice(c * Q, c * Q + Q)
        score_low = r.score_grad[c].astype(bf)
        r.query_grad[rows, :] = (
            dg(score_low, r.keys[rows, :], 1, 0)
            + dg(r.dy_enter[rows, :], r.state_in_low[c], 1, 0)
            + dg(r.dy_enter_rest[rows, :], r.state_in_low[c], 1, 0)
            + dg(r.dy_enter[rows, :], r.state_in_rest[c], 1, 0)
        )

    def shared_copy(d, arriving=False):
        target = (tp + d) % n_tp
        slot = (tp + n_tp - d) % n_tp if arriving else tp
        sems = (r.shared_ss.at[d - 1], r.shared_rs.at[d - 1])
        return remote(r.shared_send.at[target], r.shared_recv.at[slot], *sems, (seq, target))

    def pack_shared(ref, group):
        top, bottom = ref[0 : T // 2, :], ref[T // 2 : T, :]
        at = group * shards
        r.shared_send[at] = jnp.where(half_low, top, pltpu.roll(bottom, NS, 1)).astype(bf)
        r.shared_send[at + 1] = jnp.where(half_low, pltpu.roll(top, NS, 1), bottom).astype(bf)

        @pl.when(tp // shards == group)
        def _():
            r.shared_recv[tp] = r.shared_send[tp]

        for d in range(1, n_tp):
            pl.when((tp + d) % n_tp // shards == group)(shared_copy(d).start)

    pack_shared(r.query_grad, 1)
    stage("grad_wait")
    grad_wait()
    stage("leave_scan")
    running = jnp.zeros((R, N), f32)
    for d in reversed(range(n_seq)):
        r.leave_send[d] = running
        running = decay_of(d) * running + r.grad_recv[d]
    r.leave_grad[own_rows, :] = r.leave_send[seq]
    leave_wait = spread(
        "seq", lambda d: r.leave_send.at[d], lambda d: block(r.leave_grad, d), r.leave_ss, r.leave_rs
    )

    stage("weights_one")
    def weight_rows(i, _):
        cols = pl.ds(pl.multiple_of(i * LANES, LANES), LANES)
        r.wg_one[cols, 0:HI] = dg(r.normed[:, cols], r.gate_grad[...], 0, 0).astype(bf)
        r.wg_one[cols, HI : 2 * HI] = dg(r.out_cotangent[:, cols], r.gated_norm[...], 0, 0).astype(bf)
        return 0

    lax.fori_loop(0, D // LANES, weight_rows, 0)

    chips = n_seq // 2
    core = seq % 2
    chip = seq // 2
    sibling = seq + 1 - 2 * core

    def pair_copy(k, q):
        rows = pl.ds(pl.multiple_of((2 * q + 1 - core) * R2, R2), R2)
        source, target = ((r.wg_one, r.pair_one), (r.wg_two, r.pair_two))[k]
        return remote(
            source.at[rows], target.at[q], r.pair_ss.at[k, q], r.pair_rs.at[k, q], (sibling, tp)
        )

    def chip_copy(k, d, arriving=False):
        to = (chip + d) % chips
        slot = (chip + chips - d) % chips if arriving else chip
        source, target = ((r.chip_one_send, r.chip_one), (r.chip_two_send, r.chip_two))[k]
        return remote(
            source.at[to],
            target.at[slot],
            r.chip_ss.at[k, d - 1],
            r.chip_rs.at[k, d - 1],
            (2 * to + core, tp),
        )

    def pair_start(k):
        for q in range(chips):
            pair_copy(k, q).start()

    def chip_start(k):
        own, pair, send, kept = (
            (r.wg_one, r.pair_one, r.chip_one_send, r.chip_one),
            (r.wg_two, r.pair_two, r.chip_two_send, r.chip_two),
        )[k]
        for q in range(chips):
            rows = pl.ds(pl.multiple_of((2 * q + core) * R2, R2), R2)
            pair_copy(k, q).wait_recv()
            send[q] = (own[rows, :].astype(f32) + pair[q].astype(f32)).astype(bf)
        for d in range(1, chips):
            chip_copy(k, d).start()
        kept[chip] = send[chip]

    def chip_sum(k):
        kept = (r.chip_one, r.chip_two)[k]
        for d in range(1, chips):
            chip_copy(k, d, True).wait_recv()
        value = kept[0].astype(f32)
        for q in range(1, chips):
            value = value + kept[q].astype(f32)
        for q in range(chips):
            pair_copy(k, q).wait_send()
        for d in range(1, chips):
            chip_copy(k, d).wait_send()
        return value

    pair_start(0)
    stage("poll_one")
    fold_in(0, 0)
    fold_in(0, 1)
    stage("leave_wait")
    leave_wait()
    stage("leave")
    carry_terms = [None] * NC
    for c in reversed(range(NC)):
        rows = slice(c * Q, c * Q + Q)
        if c == NC - 1:
            grad = r.leave_grad[...]
        else:
            grad = r.decay_wide[c + 1] * grad + r.grad_local[c + 1]
        grad_low, grad_rest = halves(grad)
        keys, queries = r.keys[rows, :], r.queries[rows, :]
        for j in range(HI // 256):
            cols = slice(256 * j, 256 * j + 256)
            read = dg(keys, grad_low[cols, :], 1, 1) + dg(keys, grad_rest[cols, :], 1, 1)
            r.x_carry[rows, cols] = r.tail_wide[rows, cols] * read
        high, lowv = halves(grad * r.state_in[c])
        pair = dg(expand[0:H], high, 1, 0) + dg(expand[0:H], lowv, 1, 0)
        carry_terms[c] = chunk_decay[c] * jnp.sum(pair, axis=1, keepdims=True)
        score_low = r.score_grad[c].astype(bf)
        r.key_grad[rows, :] = (
            dg(score_low, queries, 0, 0)
            + dg(r.xt[rows, :], grad_low, 1, 0)
            + dg(r.xt_rest[rows, :], grad_low, 1, 0)
            + dg(r.xt[rows, :], grad_rest, 1, 0)
        )

    pack_shared(r.key_grad, 0)
    stage("chip_one")
    chip_start(0)
    stage("x_grads")
    r.head_sum_two[...] = (
        iota((HI, LANES), 0) // P_ + H == iota((HI, LANES), 1)
    ).astype(f32).astype(bf)
    r.head_sum_three[...] = (
        iota((HI, LANES), 0) // P_ + 2 * H == iota((HI, LANES), 1)
    ).astype(f32).astype(bf)

    def x_rows(i, _):
        rows = pl.ds(pl.multiple_of(i * ROWS, ROWS), ROWS)
        x = r.act[rows, :].astype(f32)
        z = r.x_inside[rows, :]
        carried = r.x_carry[rows, :]
        both = z + carried
        step_rows = r.step_wide[rows, :]
        xs = x * step_rows
        x_grad = step_rows * both + skip_row * r.heads_grad[rows, :]
        conv_grad = x_grad * slope(r.inner_conv[rows, :])
        for g in range(NP):
            r.grad_ext[g, rows, :] = conv_grad[:, g * LANES : g * LANES + LANES]
        r.sum_x[rows, :] = (
            summed(x * both, r.head_sum[...])
            + summed(xs * carried, r.head_sum_two[...])
            + summed(xs * z, r.head_sum_three[...])
        )
        return 0

    lax.fori_loop(0, T // ROWS, x_rows, 0)
    halo_one = remote(
        r.grad_ext.at[:, pl.ds(0, PAD)],
        r.grad_ext.at[:, pl.ds(T, PAD)],
        r.halo_send.at[0],
        r.halo_recv.at[0],
        left,
    )
    halo_one.start()
    waits.append(halo_one)

    sums_y = r.sum_y[...].T
    sums_x = r.sum_x[...].T
    step_grad = sums_x[0:H]
    tail_part = sums_x[H : 2 * H]
    pair_part = sums_y[0:H] - sums_x[2 * H : 3 * H]
    decay_grads = []
    for c in range(NC):
        cols = slice(c * Q, c * Q + Q)
        suffix = fold3(dg(split3(pair_part[:, cols]), r.upto[...], 1, 1))
        before = fold3(dg(split3(tail_part[:, cols]), r.upto[...], 1, 0)) - tail_part[:, cols]
        decay_grads.append(suffix + before + carry_terms[c])
    decay_grad = jnp.concatenate(decay_grads, axis=1)
    step_total = step_grad - rate * decay_grad
    step_pre_grad = step_total * r.sigmoid_step[...]
    rate_sum = jnp.sum(r.log_decay[...] * decay_grad, axis=1, keepdims=True)
    bias_sum = jnp.sum(step_pre_grad, axis=1, keepdims=True)
    step_cols = jnp.concatenate(
        [jnp.zeros((NS, T), f32), step_pre_grad, jnp.zeros((LANES - NS - H, T), f32)], axis=0
    ).T

    stage("conv_back")
    def after_masks(base):
        position = first_token + base + iota((ROWS, LANES), 0)
        now = segment(position)
        masks = []
        for k in range(CONV - 1):
            later = position + (CONV - 1) - k
            masks.append((segment(later) == now) & (later < total_tokens))
        return masks

    def conv_back(ext, taps, base, lanes, masks):
        value = None
        for k in range(CONV):
            term = taps[k : k + 1, lanes] * ext[pl.ds(base + CONV - 1 - k, ROWS), :]
            if k < CONV - 1:
                term = jnp.where(masks[k], term, 0.0)
            value = term if value is None else value + term
        return value

    def tap_sums(ext, grad, base, masks):
        sums = []
        for k in range(CONV):
            term = grad * ext[pl.ds(base + PAD - CONV + 1 + k, ROWS), :]
            sums.append(fold8(term if k == CONV - 1 else jnp.where(masks[k], term, 0.0)))
        return sums + [fold8(grad)]

    stage("inner_back")

    def inner_back_rows(i, _):
        base = pl.multiple_of(i * ROWS, ROWS)
        rows = pl.ds(base, ROWS)
        masks = after_masks(base)
        before = agreements(base, ROWS)
        taps = r.inner_kernel[...]
        for g in range(NP):
            lanes = slice(g * LANES, g * LANES + LANES)
            r.inner_grad[rows, lanes] = conv_back(r.grad_ext.at[g], taps, base, lanes, masks).astype(bf)
            found = tap_sums(r.inner_ext.at[g], r.grad_ext[g, rows, :], base, before)
            for k, v in enumerate(found):
                r.sum_acc[2 + k, :, lanes] = r.sum_acc[2 + k, :, lanes] + v
        return 0

    lax.fori_loop(0, T // ROWS - 1, inner_back_rows, 0)
    stage("poll_two")
    fold_in(0, 2)
    fold_middle(0, 0)
    stage("halo_one_wait")
    halo_one.wait_recv()
    stage("inner_back_last")
    inner_back_rows(T // ROWS - 1, 0)

    stage("poll_three")
    fold_in(0, 3)
    fold_middle(0, 1)
    stage("shared_wait")
    for d in range(1, n_tp):
        shared_copy(d, True).wait_recv()
    stage("shared_use")
    packed = r.shared_recv[0].astype(f32)
    for t in range(1, n_tp):
        packed = packed + r.shared_recv[t].astype(f32)
    r.state_grad_ext[0 : T // 2, :] = packed * slope(r.misc_conv[0 : T // 2, :])
    r.state_grad_ext[T // 2 : T, :] = pltpu.roll(packed, NS, 1) * slope(r.misc_conv[T // 2 : T, :])
    halo_two = remote(
        r.state_grad_ext.at[pl.ds(0, PAD)],
        r.state_grad_ext.at[pl.ds(T, PAD)],
        r.halo_send.at[1],
        r.halo_recv.at[1],
        left,
    )
    halo_two.start()
    waits.append(halo_two)
    stage("misc_back")
    r.misc_acc[...] = jnp.zeros_like(r.misc_acc)
    r.step_cols[...] = step_cols

    def misc_back_rows(i, _):
        base = pl.multiple_of(i * ROWS, ROWS)
        rows = pl.ds(base, ROWS)
        masks = after_masks(base)
        before = agreements(base, ROWS)
        taps = r.misc_taps[...]
        lanes = slice(0, LANES)
        value = conv_back(r.state_grad_ext, taps, base, lanes, masks)
        value = jnp.where(iota((ROWS, LANES), 1) < NS, value, r.step_cols[rows, :])
        r.misc_grad[rows, :] = value.astype(bf)
        found = tap_sums(r.misc_ext.at[0], r.state_grad_ext[rows, :], base, before)
        for k, v in enumerate(found):
            r.misc_acc[k] = r.misc_acc[k] + v
        return 0

    lax.fori_loop(0, T // ROWS - 1, misc_back_rows, 0)
    stage("halo_two_wait")
    halo_two.wait_recv()
    stage("misc_back_last")
    misc_back_rows(T // ROWS - 1, 0)

    stage("normed_grad")
    width = fold_width[1]
    for j in range(D // 256):
        cols = slice(256 * j, 256 * (j + 1))
        value = (
            dg(r.gate_grad[...], r.gate_weight[cols, :], 1, 1)
            + dg(r.inner_grad[...], r.inner_weight[cols, :], 1, 1)
            + dg(r.misc_grad[...], r.misc_weight[:, cols], 1, 0)
        )
        for k in range(256 // width):
            at = j * (256 // width) + k
            r.normed_part[at] = value[:, k * width : k * width + width].astype(bf)
            fold_start(1, at)
        hats = r.block_input[:, cols].astype(f32) * jnp.concatenate([r.inverse[...]] * 2, axis=1)
        r.gain_part[:, cols] = fold8(value * hats)

    stage("small_sums")

    def row_of(v):
        return jnp.sum(v, axis=0, keepdims=True)

    eye_wide = iota((H, LANES), 0) == iota((H, LANES), 1)

    def lanes_of(v):
        return row_of(jnp.where(eye_wide, jnp.broadcast_to(v, (H, LANES)), 0.0))

    r.small_send[...] = jnp.zeros_like(r.small_send)
    for k in range(CONV + 1):
        r.small_send[k : k + 1, :] = row_of(r.sum_acc[2 + k])
    r.small_send[5:6, :] = row_of(r.sum_acc[0])
    r.small_send[6:7, :] = row_of(r.sum_acc[1])
    for k in range(CONV):
        r.small_send[7:8, k * LANES : k * LANES + LANES] = row_of(r.misc_acc[k])
    r.small_send[8:9, 0:LANES] = row_of(r.misc_acc[CONV])
    r.small_send[8:9, LANES : 2 * LANES] = lanes_of(bias_sum)
    r.small_send[8:9, 2 * LANES : 3 * LANES] = lanes_of(rate_sum)
    gain_rows = row_of(r.gain_part[...])
    for k in range(D // HI):
        r.small_send[9 + k : 10 + k, :] = gain_rows[:, k * HI : k * HI + HI]
    r.small_recv[seq] = r.small_send[...]
    small_wait = spread(
        "seq", lambda d: r.small_send, lambda d: r.small_recv.at[d], r.small_ss, r.small_rs
    )
    stage("poll_four")
    fold_middle(0, 2)
    fold_middle(0, 3)
    stage("weights_two")

    def weight_rows_two(i, _):
        cols = pl.ds(pl.multiple_of(i * LANES, LANES), LANES)
        r.wg_two[cols, 0:HI] = dg(r.normed[:, cols], r.inner_grad[...], 0, 0).astype(bf)
        r.wg_two[cols, HI : HI + LANES] = dg(r.normed[:, cols], r.misc_grad[...], 0, 0).astype(bf)
        return 0

    lax.fori_loop(0, D // LANES, weight_rows_two, 0)
    pair_start(1)
    stage("folds")
    last = fold_pieces[1]
    for j in range(last + 1):
        if j < last:
            fold_in(1, j)
        if j > 0:
            fold_middle(1, j - 1)
        if j == 0:
            chip_start(1)
        if j == 1:
            small_wait()
            total = r.small_recv[0]
            for d in range(1, n_seq):
                total = total + r.small_recv[d]
            r.small_total[...] = total
            r.gain_recv[tp] = r.small_total[8:16, :]
            gain_wait = spread(
                "tp",
                lambda t: r.small_total.at[pl.ds(8, 8)],
                lambda t: r.gain_recv.at[t],
                r.gain_ss,
                r.gain_rs,
            )
        if j == last - 1:
            stage("weight_sums")
            r.sum_one[...] = chip_sum(0)
            r.sum_two[...] = chip_sum(1)
            gain_wait()
            gains = r.gain_recv[0]
            for t in range(1, n_tp):
                gains = gains + r.gain_recv[t]
            r.gain_total[...] = gains
            stage("folds_last")
    for j in range(fold_pieces[0]):
        fold_end(0, j)
    for j in range(fold_pieces[1]):
        fold_end(1, j)
    stage("drain")
    for d in range(1, n_tp):
        shared_copy(d).wait_send()
    for copy in waits:
        copy.wait_send()
    marks.close()


def finish(sizes, names, *refs):
    r = types.SimpleNamespace(**dict(zip(names, refs)))
    T, D, HI, H, NS = sizes
    P_ = HI // H
    T = r.block_input.shape[0]

    def final_rows(i, _):
        rows = pl.ds(pl.multiple_of(i * ROWS, ROWS), ROWS)
        x = r.block_input[rows, :].astype(f32)
        r.block_output[rows, :] = (x + r.branch_sum[rows, :].astype(f32)).astype(bf)
        inverse = lax.rsqrt(jnp.mean(x * x, axis=1, keepdims=True) + epsilon)
        hat = x * inverse
        hat_grad = r.normed_sum[rows, :].astype(f32) * r.input_gain[...].reshape(1, D)
        mean = jnp.mean(hat_grad * hat, axis=1, keepdims=True)
        r.input_grad[rows, :] = r.out_cotangent[rows, :].astype(f32) + inverse * (
            hat_grad - hat * mean
        )
        return 0

    lax.fori_loop(0, T // ROWS, final_rows, 0)
    @pl.when(pl.program_id(0) == 0)
    def _():
        r.gate_weight_grad[...] = r.sum_one[:, 0:HI]
        r.out_weight_grad[...] = r.sum_one[:, HI : 2 * HI].T
        r.inner_weight_grad[...] = r.sum_two[:, 0:HI]
        narrow = r.sum_two[:, HI : HI + LANES].T
        r.state_weight_grad[...] = narrow[0:NS]
        r.step_weight_grad[...] = narrow[NS : NS + H]
        small = r.small_total
        r.inner_kernel_grad[...] = small[0:CONV, :]
        r.inner_conv_bias_grad[...] = small[CONV : CONV + 1, :].reshape(HI)
        r.gate_gain_grad[...] = small[5:6, :].reshape(HI)
        head_sum = (iota((HI, LANES), 0) // P_ == iota((HI, LANES), 1)).astype(f32).astype(bf)
        skip_sums = fold3(dg(split3(jnp.broadcast_to(small[6:7, :], (8, HI))), head_sum, 1, 0))
        r.skip_scale_grad[...] = skip_sums[0:1, 0:H].reshape(H)
        for k in range(CONV):
            r.state_kernel_grad[k : k + 1, :] = small[7:8, k * LANES : k * LANES + NS]
        r.state_conv_bias_grad[...] = small[8:9, 0:NS].reshape(NS)
        r.step_bias_grad[...] = small[8:9, LANES : LANES + H].reshape(H)
        r.rate_log_grad[...] = small[8:9, 2 * LANES : 2 * LANES + H].reshape(H)
        for k in range(D // HI):
            r.input_gain_grad[k * HI : k * HI + HI] = r.gain_total[1 + k : 2 + k, :].reshape(HI)


INPUTS = (
    "block_input",
    "scene_lengths",
    "input_gain",
    "gate_weight",
    "inner_weight",
    "state_weight",
    "step_weight",
    "step_bias",
    "rate_log",
    "inner_kernel",
    "inner_conv_bias",
    "state_kernel",
    "state_conv_bias",
    "skip_scale",
    "gate_gain",
    "out_weight",
    "out_cotangent",
)
OUTPUTS = (
    "block_output",
    "input_grad",
    "input_gain_grad",
    "gate_weight_grad",
    "inner_weight_grad",
    "state_weight_grad",
    "step_weight_grad",
    "step_bias_grad",
    "rate_log_grad",
    "inner_kernel_grad",
    "inner_conv_bias_grad",
    "state_kernel_grad",
    "state_conv_bias_grad",
    "skip_scale_grad",
    "gate_gain_grad",
    "out_weight_grad",
)


SUMS = ("branch_sum", "normed_sum", "sum_one", "sum_two", "small_total", "gain_total")


def local(*args):
    given = dict(zip(INPUTS, args))
    given["state_weight"] = given["state_weight"].T
    given["step_weight"] = given["step_weight"].T
    n_seq = lax.axis_size("seq")
    n_tp = lax.axis_size("tp")
    T, D = given["block_input"].shape
    HI = given["gate_weight"].shape[1]
    H = given["step_bias"].shape[0]
    NS = given["state_weight"].shape[0]
    N = STATE
    Q = CHUNK
    NC = T // Q
    NP = HI // LANES
    R = HI // n_seq
    R2 = D // n_seq
    outs = (
        ((T, D), bf),
        ((T, D), f32),
        ((D,), f32),
        ((R2, HI), f32),
        ((R2, HI), f32),
        ((NS, R2), f32),
        ((H, R2), f32),
        ((H,), f32),
        ((H,), f32),
        ((CONV, HI), f32),
        ((HI,), f32),
        ((CONV, NS), f32),
        ((NS,), f32),
        ((H,), f32),
        ((HI,), f32),
        ((HI, R2), f32),
    )
    sums = (
        ((T, D), bf),
        ((T, D), bf),
        ((R2, 2 * HI), f32),
        ((R2, HI + LANES), f32),
        ((16, HI), f32),
        ((8, HI), f32),
    )
    scratch = dict(
        inverse=((T, LANES), f32),
        normed=((T, D), bf),
        misc_weight=((LANES, D), bf),
        inner_ext=((NP, T + PAD, LANES), f32),
        misc_ext=((1, T + PAD, LANES), f32),
        gate_pre=((T, HI), f32),
        misc_taps=((8, LANES), f32),
        inner_bias=((1, HI), f32),
        gain_row=((1, HI), f32),
        misc_conv=((T, LANES), f32),
        inner_conv=((T, HI), f32),
        act=((T, HI), bf),
        state_send=((T // 2, LANES), bf),
        state_recv=((n_tp, T // 2, LANES), bf),
        keys=((T, N), bf),
        queries=((T, N), bf),
        sigmoid_step=((H, T), f32),
        step_rows=((H, T), f32),
        log_decay=((H, T), f32),
        upto=((Q, Q), bf),
        expand=((3 * H, HI), bf),
        mask=((NC, Q, Q), f32),
        cum_left=((H, 16, T), bf),
        cum_right=((H, 16, T), bf),
        step_wide=((T, HI), f32),
        enter_wide=((T, HI), f32),
        tail_wide=((T, HI), f32),
        decay_wide=((NC, HI, LANES), f32),
        skip_wide=((8, HI), f32),
        xt=((T, HI), bf),
        xt_rest=((T, HI), bf),
        fresh=((NC, HI, N), f32),
        end_send=((HI, N), f32),
        end_recv=((n_seq, R, N), f32),
        decay_send=((H, LANES), f32),
        decay_recv=((n_seq, H, LANES), f32),
        enter_send=((n_seq, R, N), f32),
        enter_state=((HI, N), f32),
        state_in=((NC, HI, N), f32),
        state_in_low=((NC, HI, N), bf),
        state_in_rest=((NC, HI, N), bf),
        scores=((NC, Q, Q), f32),
        score_grad=((NC, Q, Q), f32),
        decays=((NC, H, Q, Q), f32),
        mixed=((T, HI), f32),
        norm_grad=((T, HI), f32),
        heads_out=((T, HI), f32),
        gated=((T, HI), f32),
        squares=((T, LANES), f32),
        products=((T, LANES), f32),
        sums_send=((8, T), f32),
        sums_recv=((n_tp, 8, T), f32),
        norm_col=((T, LANES), f32),
        back_col=((T, LANES), f32),
        head_sum=((HI, LANES), bf),
        head_sum_two=((HI, LANES), bf),
        head_sum_three=((HI, LANES), bf),
        sum_acc=((7, 8, HI), f32),
        gated_norm=((T, HI), bf),
        gate_grad=((T, HI), bf),
        heads_grad=((T, HI), f32),
        dy=((T, HI), bf),
        dy_rest=((T, HI), bf),
        dy_enter=((T, HI), bf),
        dy_enter_rest=((T, HI), bf),
        sum_y=((T, LANES), f32),
        sum_x=((T, LANES), f32),
        grad_local=((NC, HI, N), f32),
        grad_send=((HI, N), f32),
        grad_recv=((n_seq, R, N), f32),
        leave_send=((n_seq, R, N), f32),
        leave_grad=((HI, N), f32),
        x_inside=((T, HI), f32),
        x_carry=((T, HI), f32),
        wg_one=((D, 2 * HI), bf),
        pair_one=((n_seq // 2, R2, 2 * HI), bf),
        chip_one_send=((n_seq // 2, R2, 2 * HI), bf),
        chip_one=((n_seq // 2, R2, 2 * HI), bf),
        wg_two=((D, HI + LANES), bf),
        pair_two=((n_seq // 2, R2, HI + LANES), bf),
        chip_two_send=((n_seq // 2, R2, HI + LANES), bf),
        chip_two=((n_seq // 2, R2, HI + LANES), bf),
        query_grad=((T, N), f32),
        key_grad=((T, N), f32),
        shared_send=((n_tp, T // 2, LANES), bf),
        shared_recv=((n_tp, T // 2, LANES), bf),
        grad_ext=((NP, T + PAD, LANES), f32),
        state_grad_ext=((T + PAD, LANES), f32),
        inner_grad=((T, HI), bf),
        step_cols=((T, LANES), f32),
        misc_grad=((T, LANES), bf),
        misc_acc=((CONV + 1, 8, LANES), f32),
        normed_part=((8, T, D // 8), bf),
        normed_in=((8, T, D // 8), bf),
        normed_across=((8, T, D // 8), bf),
        branch=((4, T, D // 4), bf),
        branch_in=((4, T, D // 4), bf),
        branch_across=((4, T, D // 4), bf),
        gain_part=((8, D), f32),
        small_send=((16, HI), f32),
        small_recv=((n_seq, 16, HI), f32),
        gain_recv=((n_tp, 8, HI), f32),
    )
    semaphores = dict(
        rim_send=(2,),
        rim_recv=(2,),
        halo_send=(2,),
        halo_recv=(2,),
        pair_ss=(2, n_seq // 2),
        pair_rs=(2, n_seq // 2),
        chip_ss=(2, n_seq // 2 - 1),
        chip_rs=(2, n_seq // 2 - 1),
        fold_ss=(3, 12),
        fold_rs=(3, 12),
    )
    for name in ("state", "sums", "shared", "gain"):
        semaphores[name + "_ss"] = (n_tp - 1,)
        semaphores[name + "_rs"] = (n_tp - 1,)
    for name in ("decay", "end", "enter", "grad", "leave", "small"):
        semaphores[name + "_ss"] = (n_seq - 1,)
        semaphores[name + "_rs"] = (n_seq - 1,)
    names = INPUTS + SUMS + tuple(scratch) + tuple(semaphores)
    vmem = pl.BlockSpec(memory_space=pltpu.VMEM)
    smem = pl.BlockSpec(memory_space=pltpu.SMEM)
    totals = pl.pallas_call(
        functools.partial(kernel, (n_seq, n_tp, T, D, HI, H, NS), names),
        out_shape=tuple(jax.ShapeDtypeStruct(s, t) for s, t in sums),
        in_specs=[smem if n == "scene_lengths" else vmem for n in INPUTS],
        out_specs=tuple(vmem for _ in sums),
        scratch_shapes=[pltpu.VMEM(s, t) for s, t in scratch.values()]
        + [pltpu.SemaphoreType.DMA(s) for s in semaphores.values()],
        compiler_params=pltpu.CompilerParams(
            collective_id=0, has_side_effects=True, vmem_limit_bytes=60 * 2**20
        ),
    )(*given.values())
    tall = ("block_input", "out_cotangent", "branch_sum", "normed_sum", "block_output", "input_grad")
    steps = 4
    by_rows = pl.BlockSpec((T // steps, D), lambda i: (i, 0))

    def whole(shape):
        return pl.BlockSpec(shape, lambda i: (0,) * len(shape))

    needed = ("block_input", "input_gain", "out_cotangent")
    results = pl.pallas_call(
        functools.partial(finish, (T, D, HI, H, NS), needed + SUMS + OUTPUTS),
        out_shape=tuple(jax.ShapeDtypeStruct(s, t) for s, t in outs),
        grid=(steps,),
        in_specs=[by_rows if n in tall else whole(given[n].shape) for n in needed]
        + [by_rows if n in tall else whole(s) for n, (s, _) in zip(SUMS, sums)],
        out_specs=tuple(by_rows if n in tall else whole(s) for n, (s, _) in zip(OUTPUTS, outs)),
        compiler_params=pltpu.CompilerParams(vmem_limit_bytes=60 * 2**20),
    )(*(given[n] for n in needed), *totals)
    results = dict(zip(OUTPUTS, results))
    results["state_weight_grad"] = results["state_weight_grad"].T
    results["step_weight_grad"] = results["step_weight_grad"].T
    return tuple(results.values())


def solution(mesh):
    rows = P("seq", None)
    cols = P(None, "tp")
    heads = P("tp")
    return jax.shard_map(
        local,
        mesh=mesh,
        in_specs=(
            rows,
            P(),
            P(),
            cols,
            cols,
            cols,
            cols,
            heads,
            heads,
            cols,
            heads,
            cols,
            heads,
            heads,
            heads,
            P("tp", None),
            rows,
        ),
        out_specs=(
            rows,
            rows,
            P(),
            P("seq", "tp"),
            P("seq", "tp"),
            P("seq", "tp"),
            P("seq", "tp"),
            heads,
            heads,
            cols,
            heads,
            cols,
            heads,
            heads,
            heads,
            P("tp", "seq"),
        ),
        check_vma=False,
    )
```

```python
import contextlib
import functools
import types

import jax
import jax.numpy as jnp
from jax import lax
from jax.experimental import pallas as pl
from jax.experimental.pallas import tpu as pltpu
from jax.sharding import PartitionSpec as P

STATE = 128
CONV = 4
CHUNK = 256
LANES = 128
PAD = 8
ROWS = 64
epsilon = 1e-05
bf = jnp.bfloat16
f32 = jnp.float32
i32 = jnp.int32
MESH = pl.DeviceIdType.MESH


def dg(left, right, left_dim, right_dim):
    return lax.dot_general(
        left, right, (((left_dim,), (right_dim,)), ((), ())), preferred_element_type=f32
    )


def split3(v):
    high = v.astype(bf).astype(f32)
    middle = (v - high).astype(bf).astype(f32)
    return jnp.concatenate([high, middle, v - high - middle], axis=0).astype(bf)


def fold3(v):
    third = v.shape[0] // 3
    return v[:third] + v[third : 2 * third] + v[2 * third :]


def halves(v):
    high = v.astype(bf)
    return high, (v - high.astype(f32)).astype(bf)


def slope(v):
    s = jax.nn.sigmoid(v)
    return s * (1.0 + v * (1.0 - s))


def fold8(v):
    total = v[0:8]
    for i in range(1, v.shape[0] // 8):
        total = total + v[8 * i : 8 * i + 8]
    return total


def iota(shape, dim):
    return lax.broadcasted_iota(i32, shape, dim)


def kernel(sizes, names, *refs):
    r = types.SimpleNamespace(**dict(zip(names, refs)))
    n_seq, n_tp, T, D, HI, H, NS = sizes
    N = STATE
    P_ = HI // H
    Q = CHUNK
    NC = T // Q
    NP = HI // LANES
    R = HI // n_seq
    R2 = D // n_seq
    total_tokens = T * n_seq
    seq = lax.axis_index("seq")
    tp = lax.axis_index("tp")

    barrier = pltpu.get_barrier_semaphore()
    for d in range(1, n_seq):
        pl.semaphore_signal(
            barrier, inc=1, device_id=((seq + d) % n_seq, tp), device_id_type=MESH
        )
    for d in range(1, n_tp):
        pl.semaphore_signal(
            barrier, inc=1, device_id=(seq, (tp + d) % n_tp), device_id_type=MESH
        )

    waits = []
    half = n_tp // 2
    inner = jnp.where(tp < half, tp + 1, tp - 1)
    outer = jnp.where(tp < half, tp - 1, tp + 1)
    is_middle = (tp == half - 1) | (tp == half)
    has_outer = (tp > 0) & (tp < n_tp - 1)
    fold_pieces = (r.branch_in.shape[0], r.normed_in.shape[0])
    fold_width = D // fold_pieces[0], LANES
    fold_rows = T, T * D // LANES // fold_pieces[1]
    fold_refs = (
        (r.branch, r.branch_in, r.branch_across, r.branch_sum),
        (r.normed_part, r.normed_in, r.normed_across, r.normed_sum),
    )

    def fold(a, j):
        high = T // fold_rows[a]
        place = (
            pl.ds(j % high * fold_rows[a], fold_rows[a]),
            pl.ds(j // high * fold_width[a], fold_width[a]),
        )
        partial, arrived, across, total = (
            ref.at[j] if k < 3 else ref.at[place]
            for k, ref in enumerate(fold_refs[a])
        )
        return partial, arrived, across, total

    def fold_copy(a, j, leg):
        partial, arrived, across, total = fold(a, j)
        sems = leg, sum(fold_pieces[:a]) + j
        source, target, place = ((partial, arrived, inner), (partial, across, inner), (total, total, outer))[leg]
        return remote(source, target, r.fold_ss.at[sems], r.fold_rs.at[sems], (seq, place))

    def fold_start(a, j):
        pl.when(jnp.logical_not(has_outer | is_middle))(fold_copy(a, j, 0).start)

    def fold_in(a, j):
        partial, arrived, _, _ = fold(a, j)

        @pl.when(has_outer)
        def _():
            fold_copy(a, j, 0).wait_recv()
            partial[...] = (partial[...].astype(f32) + arrived[...].astype(f32)).astype(bf)

        pl.when(is_middle)(fold_copy(a, j, 1).start)
        pl.when(has_outer & jnp.logical_not(is_middle))(fold_copy(a, j, 0).start)

    def fold_middle(a, j):
        partial, _, across, total = fold(a, j)

        @pl.when(is_middle)
        def _():
            fold_copy(a, j, 1).wait_recv()
            total[...] = (partial[...].astype(f32) + across[...].astype(f32)).astype(bf)
            pl.when(has_outer)(fold_copy(a, j, 2).start)

    def fold_end(a, j):
        @pl.when(jnp.logical_not(is_middle))
        def _():
            fold_copy(a, j, 2).wait_recv()
            pl.when(has_outer)(fold_copy(a, j, 2).start)
            fold_copy(a, j, 0).wait_send()

        pl.when(has_outer)(fold_copy(a, j, 2).wait_send)
        pl.when(is_middle)(fold_copy(a, j, 1).wait_send)

    marks = contextlib.ExitStack()

    def stage(name):
        marks.close()
        marks.enter_context(jax.named_scope(name))

    stage("norm")

    def remote(src, dst, send, recv, device):
        return pltpu.make_async_remote_copy(
            src_ref=src,
            dst_ref=dst,
            send_sem=send,
            recv_sem=recv,
            device_id=device,
            device_id_type=MESH,
        )

    def spread(axis, src_to, dst_from, send, recv):
        n = n_seq if axis == "seq" else n_tp
        me = seq if axis == "seq" else tp
        incoming = []
        for d in range(1, n):
            target = (me + d) % n
            source = (me + n - d) % n
            device = (target, tp) if axis == "seq" else (seq, target)
            out = remote(src_to(target), dst_from(me), send.at[d - 1], recv.at[d - 1], device)
            out.start()
            waits.append(out)
            incoming.append(
                remote(src_to(target), dst_from(source), send.at[d - 1], recv.at[d - 1], device)
            )

        def wait():
            for copy in incoming:
                copy.wait_recv()

        return wait

    starts = [jnp.int32(0)]
    for k in range(r.scene_lengths.shape[0] - 1):
        starts.append(starts[-1] + r.scene_lengths[k])

    def segment(position):
        found = (position >= starts[0]).astype(i32)
        for s in starts[1:]:
            found = found + (position >= s).astype(i32)
        return found

    first_token = seq * T

    def norm_rows(i, _):
        rows = pl.ds(pl.multiple_of(i * ROWS, ROWS), ROWS)
        x = r.block_input[rows, :].astype(f32)
        inverse = lax.rsqrt(jnp.mean(x * x, axis=1, keepdims=True) + epsilon)
        r.inverse[rows, :] = jnp.broadcast_to(inverse, (ROWS, LANES))
        r.normed[rows, :] = (x * inverse * r.input_gain[...].reshape(1, D)).astype(bf)
        return 0

    lax.fori_loop(0, T // ROWS, norm_rows, 0)

    stage("projections")
    r.misc_weight[...] = jnp.zeros_like(r.misc_weight)
    r.misc_weight[0:NS, :] = r.state_weight[...]
    r.misc_weight[NS : NS + H, :] = r.step_weight[...]
    normed_all = r.normed[...]
    r.misc_ext[0, PAD : PAD + T, :] = dg(normed_all, r.misc_weight[...], 1, 1)
    stage("barrier")
    pl.semaphore_wait(barrier, n_seq - 1 + n_tp - 1)
    stage("inner_projection")
    right = ((seq + 1) % n_seq, tp)
    left = ((seq + n_seq - 1) % n_seq, tp)
    misc_rim, inner_rim = [
        remote(
            ref.at[:, pl.ds(T, PAD)],
            ref.at[:, pl.ds(0, PAD)],
            r.rim_send.at[k],
            r.rim_recv.at[k],
            right,
        )
        for k, ref in enumerate((r.misc_ext, r.inner_ext))
    ]
    waits.extend((misc_rim, inner_rim))
    misc_rim.start()
    for j in range(HI // 256):
        cols = slice(256 * j, 256 * j + 256)
        value = dg(normed_all, r.inner_weight[:, cols], 1, 0)
        r.inner_ext[2 * j, PAD : PAD + T, :] = value[:, :LANES]
        r.inner_ext[2 * j + 1, PAD : PAD + T, :] = value[:, LANES:]
    inner_rim.start()
    stage("gate_projection")
    for j in range(HI // 256):
        cols = slice(256 * j, 256 * j + 256)
        r.gate_pre[:, cols] = dg(normed_all, r.gate_weight[:, cols], 1, 0)

    stage("convolutions")
    def agreements(base, rows):
        position = first_token + base + iota((rows, LANES), 0)
        now = segment(position)
        return [segment(position - (CONV - 1) + k) == now for k in range(CONV - 1)]

    def conv_block(ext, taps, bias, base, lanes, masks):
        value = bias[:, lanes]
        for k in range(CONV):
            window = ext[pl.ds(base + PAD - CONV + 1 + k, ROWS), :]
            term = taps[k : k + 1, lanes] * window
            value = value + (term if k == CONV - 1 else jnp.where(masks[k], term, 0.0))
        return value

    r.misc_taps[...] = jnp.zeros_like(r.misc_taps)
    r.misc_taps[0:CONV, 0:NS] = r.state_kernel[...]
    r.misc_taps[CONV : CONV + 1, 0:NS] = r.state_conv_bias[...].reshape(1, NS)
    r.inner_bias[...] = r.inner_conv_bias[...].reshape(1, HI)
    stage("rim_wait")
    misc_rim.wait_recv()
    stage("conv")

    def misc_conv_rows(i, _):
        base = pl.multiple_of(i * ROWS, ROWS)
        masks = agreements(base, ROWS)
        taps = r.misc_taps[...]
        value = conv_block(
            r.misc_ext.at[0], taps, taps[CONV : CONV + 1], base, slice(0, LANES), masks
        )
        r.misc_conv[pl.ds(base, ROWS), :] = value
        return 0

    lax.fori_loop(0, T // ROWS, misc_conv_rows, 0)
    low_lanes = iota((T // 2, LANES), 1) < NS
    own = r.misc_conv[...]
    own = own * jax.nn.sigmoid(own)
    r.state_send[...] = jnp.where(
        low_lanes, own[: T // 2], pltpu.roll(own[T // 2 :], NS, 1)
    ).astype(bf)
    r.state_recv[tp] = r.state_send[...]
    state_wait = spread(
        "tp",
        lambda t: r.state_send,
        lambda t: r.state_recv.at[t],
        r.state_ss,
        r.state_rs,
    )

    def inner_conv_rows(i, _):
        base = pl.multiple_of(i * ROWS, ROWS)
        rows = pl.ds(base, ROWS)
        masks = agreements(base, ROWS)
        taps = r.inner_kernel[...]
        for g in range(NP):
            lanes = slice(g * LANES, g * LANES + LANES)
            value = conv_block(r.inner_ext.at[g], taps, r.inner_bias, base, lanes, masks)
            r.inner_conv[rows, lanes] = value
            r.act[rows, lanes] = (value * jax.nn.sigmoid(value)).astype(bf)
        return 0

    inner_rim.wait_recv()
    lax.fori_loop(0, T // ROWS, inner_conv_rows, 0)

    stage("decays")
    eye = iota((H, H), 0) == iota((H, H), 1)

    def column(ref):
        wide = jnp.broadcast_to(ref[...].reshape(1, H), (H, H))
        return jnp.sum(jnp.where(eye, wide, 0.0), axis=1, keepdims=True)

    step_in = r.misc_ext[0, PAD : PAD + T, :].T[NS : NS + H, :] + column(r.step_bias)
    step = jnp.maximum(step_in, 0.0) + jnp.log1p(jnp.exp(-jnp.abs(step_in)))
    rate = jnp.exp(column(r.rate_log))
    log_decay = step * -rate
    r.sigmoid_step[...] = jax.nn.sigmoid(step_in)
    r.log_decay[...] = log_decay
    r.step_rows[...] = step
    r.upto[...] = (iota((Q, Q), 0) <= iota((Q, Q), 1)).astype(f32).astype(bf)
    r.expand[...] = (iota((3 * H, HI), 0) % H == iota((3 * H, HI), 1) // P_).astype(f32).astype(bf)
    expand = r.expand[...]

    entering, tailing, chunk_decay = [], [], []
    ones_rows = jnp.ones((1, Q), f32)
    for c in range(NC):
        cols = slice(c * Q, c * Q + Q)
        cumulative = fold3(dg(split3(log_decay[:, cols]), r.upto[...], 1, 0))
        start = first_token + c * Q
        seg_row = segment(start + iota((H, Q), 1))
        seg_before = segment(start - 1)
        seg_end = segment(start + Q - 1)
        last = cumulative[:, Q - 1 : Q]
        enter = jnp.where(seg_row == seg_before, jnp.exp(cumulative), 0.0)
        tail = jnp.where(seg_row == seg_end, jnp.exp(last - cumulative), 0.0)
        entering.append(enter)
        tailing.append(tail)
        chunk_decay.append(enter[:, Q - 1 : Q])
        seg_col = segment(start + iota((Q, Q), 0))
        seg_lane = segment(start + iota((Q, Q), 1))
        keep = (seg_col == seg_lane) & (iota((Q, Q), 0) >= iota((Q, Q), 1))
        r.mask[c] = jnp.where(keep, 0.0, -1e30)
        high = cumulative.astype(bf).astype(f32)
        middle = (cumulative - high).astype(bf).astype(f32)
        rest = cumulative - high - middle
        which = iota((16, Q), 0)
        for h in range(H):
            parts = jnp.where(
                which % 3 == 0,
                high[h : h + 1],
                jnp.where(which % 3 == 1, middle[h : h + 1], rest[h : h + 1]),
            )
            first = which < 3
            second = (which >= 3) & (which < 6)
            r.cum_left[h, :, cols] = jnp.where(
                first, parts, jnp.where(second, 1.0, 0.0)
            ).astype(bf)
            r.cum_right[h, :, cols] = jnp.where(
                first, 1.0, jnp.where(second, -parts, 0.0)
            ).astype(bf)

    def wide(v):
        return dg(split3(v), expand, 0, 0)

    def wide_rows(v):
        return dg(expand, split3(jnp.broadcast_to(v, (H, LANES))), 0, 0)

    for c in range(NC):
        rows = slice(c * Q, c * Q + Q)
        r.step_wide[rows, :] = wide(step[:, rows])
        r.enter_wide[rows, :] = wide(entering[c])
        r.tail_wide[rows, :] = wide(tailing[c])
        r.decay_wide[c] = wide_rows(chunk_decay[c])
    r.skip_wide[...] = dg(split3(jnp.broadcast_to(column(r.skip_scale), (H, 8))), expand, 0, 0)

    def scaled_rows(i, _):
        rows = pl.ds(pl.multiple_of(i * ROWS, ROWS), ROWS)
        x = r.act[rows, :].astype(f32)
        r.xt[rows, :], r.xt_rest[rows, :] = halves(x * r.step_wide[rows, :] * r.tail_wide[rows, :])
        return 0

    lax.fori_loop(0, T // ROWS, scaled_rows, 0)

    stage("decay_matrices")

    def decay_matrix(i, _):
        c = i // H
        h = i % H
        rows = pl.ds(pl.multiple_of(c * Q, Q), Q)
        difference = dg(r.cum_left[h, :, rows], r.cum_right[h, :, rows], 0, 0)
        r.decays[c, h] = jnp.exp(difference + r.mask[c])
        return 0

    lax.fori_loop(0, NC * H, decay_matrix, 0)

    stage("keys_wait")
    state_wait()
    shards = n_tp // 2
    half_low = iota((T // 2, LANES), 1) < NS
    for ref, at in ((r.keys, 0), (r.queries, shards)):
        one, two = r.state_recv[at].astype(f32), r.state_recv[at + 1].astype(f32)
        ref[0 : T // 2, :] = jnp.where(half_low, one, pltpu.roll(two, NS, 1)).astype(bf)
        ref[T // 2 : T, :] = jnp.where(half_low, pltpu.roll(one, NS, 1), two).astype(bf)

    stage("end_states")
    end_state = None
    device_decay = None
    for c in range(NC):
        rows = slice(c * Q, c * Q + Q)
        keys = r.keys[rows, :]
        fresh = dg(r.xt[rows, :], keys, 0, 0) + dg(r.xt_rest[rows, :], keys, 0, 0)
        r.fresh[c] = fresh
        end_state = fresh if c == 0 else r.decay_wide[c] * end_state + fresh
        device_decay = chunk_decay[c] if c == 0 else device_decay * chunk_decay[c]
    r.end_send[...] = end_state
    r.decay_send[...] = jnp.broadcast_to(device_decay, (H, LANES))

    def block(ref, device):
        return ref.at[pl.ds(pl.multiple_of(device * R, R), R)]

    r.end_recv[seq] = r.end_send[pl.ds(pl.multiple_of(seq * R, R), R), :]
    r.decay_recv[seq] = r.decay_send[...]
    decay_wait = spread(
        "seq", lambda d: r.decay_send, lambda d: r.decay_recv.at[d], r.decay_ss, r.decay_rs
    )
    end_wait = spread(
        "seq", lambda d: block(r.end_send, d), lambda d: r.end_recv.at[d], r.end_ss, r.end_rs
    )

    stage("inside")
    for c in range(NC):
        rows = slice(c * Q, c * Q + Q)
        r.scores[c] = dg(r.queries[rows, :], r.keys[rows, :], 1, 1)
    low = iota((Q, LANES), 1) < P_

    def inside(i, _):
        c = i // NP
        p = i % NP
        rows = pl.ds(pl.multiple_of(c * Q, Q), Q)
        lanes = pl.ds(pl.multiple_of(p * LANES, LANES), LANES)
        x = r.act[rows, lanes]
        zero = jnp.zeros_like(x)
        result = None
        for s in range(2):
            h = 2 * p + s
            stepped = r.decays[c, h] * r.step_rows[pl.ds(h, 1), rows]
            weight, rest = halves(stepped * r.scores[c])
            part = jnp.where(low, x, zero) if s == 0 else jnp.where(low, zero, x)
            term = dg(weight, part, 1, 0) + dg(rest, part, 1, 0)
            result = term if s == 0 else result + term
        r.mixed[rows, lanes] = result
        return 0

    lax.fori_loop(0, NC * NP, inside, 0)
    for j in range(HI // 256):
        cols = slice(256 * j, 256 * j + 256)
        r.norm_grad[:, cols] = dg(r.out_cotangent[...], r.out_weight[cols, :], 1, 1)

    stage("entering")
    head_of = (seq * R) // P_
    stage("end_wait")
    end_wait()
    decay_wait()

    def decay_of(d):
        return jnp.broadcast_to(r.decay_recv[d, pl.ds(head_of, 1), :], (R, LANES))

    running = jnp.zeros((R, N), f32)
    for d in range(n_seq):
        r.enter_send[d] = running
        running = decay_of(d) * running + r.end_recv[d]
    own_rows = pl.ds(pl.multiple_of(seq * R, R), R)
    r.enter_state[own_rows, :] = r.enter_send[seq]
    enter_wait = spread(
        "seq", lambda d: r.enter_send.at[d], lambda d: block(r.enter_state, d), r.enter_ss, r.enter_rs
    )
    stage("turned_weights")

    def turned_weight(i, _):
        c = i // H
        h = i % H
        r.turned[c, h] = (r.decays[c, h] * r.scores[c]).T.astype(bf)
        return 0

    lax.fori_loop(0, NC * H, turned_weight, 0)
    stage("enter_wait")
    enter_wait()
    stage("readout")
    for c in range(NC):
        rows = slice(c * Q, c * Q + Q)
        if c == 0:
            state = r.enter_state[...]
        else:
            state = r.decay_wide[c - 1] * state + r.fresh[c - 1]
        r.state_in[c] = state
        r.state_in_low[c], r.state_in_rest[c] = halves(state)
        for j in range(HI // 256):
            cols = slice(256 * j, 256 * j + 256)
            queries = r.queries[rows, :]
            read = dg(queries, r.state_in_low[c, cols, :], 1, 1) + dg(queries, r.state_in_rest[c, cols, :], 1, 1)
            r.mixed[rows, cols] = r.mixed[rows, cols] + r.enter_wide[rows, cols] * read

    stage("gated")
    skip_row = r.skip_wide[0:1, :]
    r.gain_row[...] = r.gate_gain[...].reshape(1, HI)

    def gated_rows(i, _):
        rows = pl.ds(pl.multiple_of(i * ROWS, ROWS), ROWS)
        heads = r.mixed[rows, :] + skip_row * r.act[rows, :].astype(f32)
        gate = r.gate_pre[rows, :]
        gated = heads * (gate * jax.nn.sigmoid(gate))
        r.gated[rows, :] = gated
        scaled = r.norm_grad[rows, :] * r.gain_row[...]
        squares = gated * gated
        products = scaled * gated

        def lane_sum(v):
            total = v[:, :LANES]
            for g in range(1, NP):
                total = total + v[:, g * LANES : g * LANES + LANES]
            return total

        r.squares[rows, :] = lane_sum(squares)
        r.products[rows, :] = lane_sum(products)
        return 0

    lax.fori_loop(0, T // ROWS, gated_rows, 0)
    square_row = jnp.sum(r.squares[...].T, axis=0, keepdims=True)
    product_row = jnp.sum(r.products[...].T, axis=0, keepdims=True)
    r.sums_send[...] = jnp.where(
        iota((8, T), 0) == 0,
        jnp.broadcast_to(square_row, (8, T)),
        jnp.broadcast_to(product_row, (8, T)),
    )
    r.sums_recv[tp] = r.sums_send[...]
    sums_wait = spread(
        "tp", lambda t: r.sums_send, lambda t: r.sums_recv.at[t], r.sums_ss, r.sums_rs
    )
    stage("sums_wait")
    sums_wait()
    stage("sums")
    sums = r.sums_recv[0]
    for t in range(1, n_tp):
        sums = sums + r.sums_recv[t]
    count = HI * n_tp
    norm_row = lax.rsqrt(sums[0:1] / count + epsilon)
    back_row = norm_row * norm_row * norm_row * (sums[1:2] / count)
    r.norm_col[...] = jnp.broadcast_to(norm_row, (LANES, T)).T
    r.back_col[...] = jnp.broadcast_to(back_row, (LANES, T)).T

    stage("back_gated")
    r.head_sum[...] = (iota((HI, LANES), 0) // P_ == iota((HI, LANES), 1)).astype(f32).astype(bf)
    r.sum_acc[...] = jnp.zeros_like(r.sum_acc)

    def tile4(v):
        return jnp.concatenate([v] * NP, axis=1)

    def summed(v, which):
        high, lowv = halves(v)
        return dg(high, which, 1, 0) + dg(lowv, which, 1, 0)

    def back_rows(i, _):
        rows = pl.ds(pl.multiple_of(i * ROWS, ROWS), ROWS)
        norm = tile4(r.norm_col[rows, :])
        back = tile4(r.back_col[rows, :])
        gated = r.gated[rows, :]
        grad = r.norm_grad[rows, :]
        gain = r.gain_row[...]
        gate = r.gate_pre[rows, :]
        sigma = jax.nn.sigmoid(gate)
        unit = gated * norm
        r.gated_norm[rows, :] = (unit * gain).astype(bf)
        r.sum_acc[0] = r.sum_acc[0] + fold8(grad * unit)
        gated_grad = norm * (grad * gain) - gated * back
        heads_grad = gated_grad * (gate * sigma)
        heads = r.mixed[rows, :] + skip_row * r.act[rows, :].astype(f32)
        r.gate_grad[rows, :] = (
            gated_grad * heads * (sigma * (1.0 + gate * (1.0 - sigma)))
        ).astype(bf)
        r.heads_grad[rows, :] = heads_grad
        x = r.act[rows, :].astype(f32)
        r.sum_acc[1] = r.sum_acc[1] + fold8(heads_grad * x)
        r.dy[rows, :], r.dy_rest[rows, :] = halves(heads_grad)
        r.dy_enter[rows, :], r.dy_enter_rest[rows, :] = halves(heads_grad * r.enter_wide[rows, :])
        r.sum_y[rows, :] = summed(heads_grad * r.mixed[rows, :], r.head_sum[...])
        return 0

    lax.fori_loop(0, T // ROWS, back_rows, 0)

    stage("grad_states")
    grad_in = None
    for c in reversed(range(NC)):
        rows = slice(c * Q, c * Q + Q)
        queries = r.queries[rows, :]
        local = dg(r.dy_enter[rows, :], queries, 0, 0) + dg(r.dy_enter_rest[rows, :], queries, 0, 0)
        r.grad_local[c] = local
        grad_in = local if grad_in is None else r.decay_wide[c] * grad_in + local
    r.grad_send[...] = grad_in
    r.grad_recv[seq] = r.grad_send[own_rows, :]
    grad_wait = spread(
        "seq", lambda d: block(r.grad_send, d), lambda d: r.grad_recv.at[d], r.grad_ss, r.grad_rs
    )
    stage("out_projection")
    for j in range(D // 256):
        value = dg(r.gated_norm[...], r.out_weight[:, 256 * j : 256 * j + 256], 1, 0).astype(bf)
        for k in range(256 // fold_width[0]):
            at = j * (256 // fold_width[0]) + k
            r.branch[at] = value[:, k * fold_width[0] : (k + 1) * fold_width[0]]
            fold_start(0, at)
    stage("inside_back")
    r.score_grad[...] = jnp.zeros_like(r.score_grad)

    def inside_back(i, _):
        c = i // NP
        p = i % NP
        rows = pl.ds(pl.multiple_of(c * Q, Q), Q)
        lanes = pl.ds(pl.multiple_of(p * LANES, LANES), LANES)
        x = r.act[rows, lanes]
        dy = r.dy[rows, lanes]
        dy_rest = r.dy_rest[rows, lanes]
        zero = jnp.zeros_like(dy)
        x_turned, dy_turned = pltpu.roll(x, P_, 1), pltpu.roll(dy_rest, P_, 1)
        result = None
        for s in range(2):
            h = 2 * p + s
            ours = low if s == 0 else jnp.logical_not(low)
            pairs = dg(jnp.where(ours, dy, dy_turned), jnp.where(ours, x, x_turned), 1, 1)
            r.score_grad[c] = r.score_grad[c] + pairs * (r.decays[c, h] * r.step_rows[pl.ds(h, 1), rows])
            term = dg(r.turned[c, h], jnp.where(ours, dy, zero), 1, 0)
            result = term if s == 0 else result + term
        r.x_inside[rows, lanes] = result
        return 0

    lax.fori_loop(0, NC * NP, inside_back, 0)

    stage("poll_at_grad_wait")
    fold_in(0, 0)
    stage("grad_wait")
    grad_wait()
    stage("leave_scan")
    running = jnp.zeros((R, N), f32)
    for d in reversed(range(n_seq)):
        r.leave_send[d] = running
        running = decay_of(d) * running + r.grad_recv[d]
    r.leave_grad[own_rows, :] = r.leave_send[seq]
    leave_wait = spread(
        "seq", lambda d: r.leave_send.at[d], lambda d: block(r.leave_grad, d), r.leave_ss, r.leave_rs
    )

    stage("query_grad")
    for c in range(NC):
        rows = slice(c * Q, c * Q + Q)
        score_low = r.score_grad[c].astype(bf)
        r.query_grad[rows, :] = (
            dg(score_low, r.keys[rows, :], 1, 0)
            + dg(r.dy_enter[rows, :], r.state_in_low[c], 1, 0)
            + dg(r.dy_enter_rest[rows, :], r.state_in_low[c], 1, 0)
            + dg(r.dy_enter[rows, :], r.state_in_rest[c], 1, 0)
        )

    def shared_copy(d, arriving=False):
        target = (tp + d) % n_tp
        slot = (tp + n_tp - d) % n_tp if arriving else tp
        sems = (r.shared_ss.at[d - 1], r.shared_rs.at[d - 1])
        return remote(r.shared_send.at[target], r.shared_recv.at[slot], *sems, (seq, target))

    def pack_shared(ref, group):
        top, bottom = ref[0 : T // 2, :], ref[T // 2 : T, :]
        at = group * shards
        r.shared_send[at] = jnp.where(half_low, top, pltpu.roll(bottom, NS, 1)).astype(bf)
        r.shared_send[at + 1] = jnp.where(half_low, pltpu.roll(top, NS, 1), bottom).astype(bf)

        @pl.when(tp // shards == group)
        def _():
            r.shared_recv[tp] = r.shared_send[tp]

        for d in range(1, n_tp):
            pl.when((tp + d) % n_tp // shards == group)(shared_copy(d).start)

    pack_shared(r.query_grad, 1)
    stage("poll_at_weights_one")
    fold_in(0, 1)
    stage("weights_one")
    def weight_rows(i, _):
        cols = pl.ds(pl.multiple_of(i * LANES, LANES), LANES)
        r.wg_one[cols, 0:HI] = dg(r.normed[:, cols], r.gate_grad[...], 0, 0).astype(bf)
        r.wg_one[cols, HI : 2 * HI] = dg(r.out_cotangent[:, cols], r.gated_norm[...], 0, 0).astype(bf)
        return 0

    lax.fori_loop(0, D // LANES, weight_rows, 0)

    chips = n_seq // 2
    core = seq % 2
    chip = seq // 2
    sibling = seq + 1 - 2 * core

    def pair_copy(k, q):
        rows = pl.ds(pl.multiple_of((2 * q + 1 - core) * R2, R2), R2)
        source, target = ((r.wg_one, r.pair_one), (r.wg_two, r.pair_two))[k]
        return remote(
            source.at[rows], target.at[q], r.pair_ss.at[k, q], r.pair_rs.at[k, q], (sibling, tp)
        )

    def chip_copy(k, d, arriving=False):
        to = (chip + d) % chips
        slot = (chip + chips - d) % chips if arriving else chip
        source, target = ((r.chip_one_send, r.chip_one), (r.chip_two_send, r.chip_two))[k]
        return remote(
            source.at[to],
            target.at[slot],
            r.chip_ss.at[k, d - 1],
            r.chip_rs.at[k, d - 1],
            (2 * to + core, tp),
        )

    def pair_start(k):
        for q in range(chips):
            pair_copy(k, q).start()

    def chip_start(k):
        own, pair, send, kept = (
            (r.wg_one, r.pair_one, r.chip_one_send, r.chip_one),
            (r.wg_two, r.pair_two, r.chip_two_send, r.chip_two),
        )[k]
        for q in range(chips):
            rows = pl.ds(pl.multiple_of((2 * q + core) * R2, R2), R2)
            pair_copy(k, q).wait_recv()
            send[q] = (own[rows, :].astype(f32) + pair[q].astype(f32)).astype(bf)
        for d in range(1, chips):
            chip_copy(k, d).start()
        kept[chip] = send[chip]

    def chip_sum(k):
        kept = (r.chip_one, r.chip_two)[k]
        for d in range(1, chips):
            chip_copy(k, d, True).wait_recv()
        value = kept[0].astype(f32)
        for q in range(1, chips):
            value = value + kept[q].astype(f32)
        for q in range(chips):
            pair_copy(k, q).wait_send()
        for d in range(1, chips):
            chip_copy(k, d).wait_send()
        return value

    pair_start(0)
    stage("poll_at_leave_wait")
    fold_in(0, 2)
    fold_middle(0, 0)
    stage("leave_wait")
    leave_wait()
    stage("leave")
    carry_terms = [None] * NC
    for c in reversed(range(NC)):
        rows = slice(c * Q, c * Q + Q)
        if c == NC - 1:
            grad = r.leave_grad[...]
        else:
            grad = r.decay_wide[c + 1] * grad + r.grad_local[c + 1]
        grad_low, grad_rest = halves(grad)
        keys, queries = r.keys[rows, :], r.queries[rows, :]
        for j in range(HI // 256):
            cols = slice(256 * j, 256 * j + 256)
            read = dg(keys, grad_low[cols, :], 1, 1) + dg(keys, grad_rest[cols, :], 1, 1)
            r.x_carry[rows, cols] = r.tail_wide[rows, cols] * read
        high, lowv = halves(grad * r.state_in[c])
        pair = dg(expand[0:H], high, 1, 0) + dg(expand[0:H], lowv, 1, 0)
        carry_terms[c] = chunk_decay[c] * jnp.sum(pair, axis=1, keepdims=True)
        score_low = r.score_grad[c].astype(bf)
        r.key_grad[rows, :] = (
            dg(score_low, queries, 0, 0)
            + dg(r.xt[rows, :], grad_low, 1, 0)
            + dg(r.xt_rest[rows, :], grad_low, 1, 0)
            + dg(r.xt[rows, :], grad_rest, 1, 0)
        )

    pack_shared(r.key_grad, 0)
    stage("poll_at_chip_one")
    fold_in(0, 3)
    fold_middle(0, 1)
    stage("chip_one")
    chip_start(0)
    stage("poll_at_x_grads")
    fold_in(0, 4)
    fold_middle(0, 2)
    stage("x_grads")
    r.head_sum_two[...] = (
        iota((HI, LANES), 0) // P_ + H == iota((HI, LANES), 1)
    ).astype(f32).astype(bf)
    r.head_sum_three[...] = (
        iota((HI, LANES), 0) // P_ + 2 * H == iota((HI, LANES), 1)
    ).astype(f32).astype(bf)

    def x_rows(i, _):
        rows = pl.ds(pl.multiple_of(i * ROWS, ROWS), ROWS)
        x = r.act[rows, :].astype(f32)
        z = r.x_inside[rows, :]
        carried = r.x_carry[rows, :]
        both = z + carried
        step_rows = r.step_wide[rows, :]
        xs = x * step_rows
        x_grad = step_rows * both + skip_row * r.heads_grad[rows, :]
        conv_grad = x_grad * slope(r.inner_conv[rows, :])
        for g in range(NP):
            r.grad_ext[g, rows, :] = conv_grad[:, g * LANES : g * LANES + LANES]
        r.sum_x[rows, :] = (
            summed(x * both, r.head_sum[...])
            + summed(xs * carried, r.head_sum_two[...])
            + summed(xs * z, r.head_sum_three[...])
        )
        return 0

    lax.fori_loop(0, T // ROWS, x_rows, 0)
    halo_one = remote(
        r.grad_ext.at[:, pl.ds(0, PAD)],
        r.grad_ext.at[:, pl.ds(T, PAD)],
        r.halo_send.at[0],
        r.halo_recv.at[0],
        left,
    )
    halo_one.start()
    waits.append(halo_one)

    sums_y = r.sum_y[...].T
    sums_x = r.sum_x[...].T
    step_grad = sums_x[0:H]
    tail_part = sums_x[H : 2 * H]
    pair_part = sums_y[0:H] - sums_x[2 * H : 3 * H]
    decay_grads = []
    for c in range(NC):
        cols = slice(c * Q, c * Q + Q)
        suffix = fold3(dg(split3(pair_part[:, cols]), r.upto[...], 1, 1))
        before = fold3(dg(split3(tail_part[:, cols]), r.upto[...], 1, 0)) - tail_part[:, cols]
        decay_grads.append(suffix + before + carry_terms[c])
    decay_grad = jnp.concatenate(decay_grads, axis=1)
    step_total = step_grad - rate * decay_grad
    step_pre_grad = step_total * r.sigmoid_step[...]
    rate_sum = jnp.sum(r.log_decay[...] * decay_grad, axis=1, keepdims=True)
    bias_sum = jnp.sum(step_pre_grad, axis=1, keepdims=True)
    step_cols = jnp.concatenate(
        [jnp.zeros((NS, T), f32), step_pre_grad, jnp.zeros((LANES - NS - H, T), f32)], axis=0
    ).T

    stage("poll_at_conv_back")
    fold_in(0, 5)
    fold_middle(0, 3)
    stage("conv_back")
    def after_masks(base):
        position = first_token + base + iota((ROWS, LANES), 0)
        now = segment(position)
        masks = []
        for k in range(CONV - 1):
            later = position + (CONV - 1) - k
            masks.append((segment(later) == now) & (later < total_tokens))
        return masks

    def conv_back(ext, taps, base, lanes, masks):
        value = None
        for k in range(CONV):
            term = taps[k : k + 1, lanes] * ext[pl.ds(base + CONV - 1 - k, ROWS), :]
            if k < CONV - 1:
                term = jnp.where(masks[k], term, 0.0)
            value = term if value is None else value + term
        return value

    def tap_sums(ext, grad, base, masks):
        sums = []
        for k in range(CONV):
            term = grad * ext[pl.ds(base + PAD - CONV + 1 + k, ROWS), :]
            sums.append(fold8(term if k == CONV - 1 else jnp.where(masks[k], term, 0.0)))
        return sums + [fold8(grad)]

    stage("inner_back")

    def inner_back_rows(i, _):
        base = pl.multiple_of(i * ROWS, ROWS)
        rows = pl.ds(base, ROWS)
        masks = after_masks(base)
        before = agreements(base, ROWS)
        taps = r.inner_kernel[...]
        for g in range(NP):
            lanes = slice(g * LANES, g * LANES + LANES)
            r.inner_grad[rows, lanes] = conv_back(r.grad_ext.at[g], taps, base, lanes, masks).astype(bf)
            found = tap_sums(r.inner_ext.at[g], r.grad_ext[g, rows, :], base, before)
            for k, v in enumerate(found):
                r.sum_acc[2 + k, :, lanes] = r.sum_acc[2 + k, :, lanes] + v
        return 0

    lax.fori_loop(0, T // ROWS - 1, inner_back_rows, 0)
    stage("poll_at_halo_one_wait")
    fold_in(0, 6)
    fold_middle(0, 4)
    stage("halo_one_wait")
    halo_one.wait_recv()
    stage("inner_back_last")
    inner_back_rows(T // ROWS - 1, 0)

    stage("poll_at_shared_wait")
    fold_middle(0, 5)
    stage("shared_wait")
    for d in range(1, n_tp):
        shared_copy(d, True).wait_recv()
    stage("shared_use")
    packed = r.shared_recv[0].astype(f32)
    for t in range(1, n_tp):
        packed = packed + r.shared_recv[t].astype(f32)
    r.state_grad_ext[0 : T // 2, :] = packed * slope(r.misc_conv[0 : T // 2, :])
    r.state_grad_ext[T // 2 : T, :] = pltpu.roll(packed, NS, 1) * slope(r.misc_conv[T // 2 : T, :])
    halo_two = remote(
        r.state_grad_ext.at[pl.ds(0, PAD)],
        r.state_grad_ext.at[pl.ds(T, PAD)],
        r.halo_send.at[1],
        r.halo_recv.at[1],
        left,
    )
    halo_two.start()
    waits.append(halo_two)
    stage("poll_at_misc_back")
    fold_in(0, 7)
    stage("misc_back")
    r.misc_acc[...] = jnp.zeros_like(r.misc_acc)
    r.step_cols[...] = step_cols

    def misc_back_rows(i, _):
        base = pl.multiple_of(i * ROWS, ROWS)
        rows = pl.ds(base, ROWS)
        masks = after_masks(base)
        before = agreements(base, ROWS)
        taps = r.misc_taps[...]
        lanes = slice(0, LANES)
        value = conv_back(r.state_grad_ext, taps, base, lanes, masks)
        value = jnp.where(iota((ROWS, LANES), 1) < NS, value, r.step_cols[rows, :])
        r.misc_grad[rows, :] = value.astype(bf)
        found = tap_sums(r.misc_ext.at[0], r.state_grad_ext[rows, :], base, before)
        for k, v in enumerate(found):
            r.misc_acc[k] = r.misc_acc[k] + v
        return 0

    lax.fori_loop(0, T // ROWS - 1, misc_back_rows, 0)
    stage("halo_two_wait")
    halo_two.wait_recv()
    stage("misc_back_last")
    misc_back_rows(T // ROWS - 1, 0)

    stage("poll_at_normed_grad")
    fold_middle(0, 6)
    stage("normed_grad")
    width, tall = fold_width[1], fold_rows[1]
    for j in range(D // 256):
        cols = slice(256 * j, 256 * (j + 1))
        value = (
            dg(r.gate_grad[...], r.gate_weight[cols, :], 1, 1)
            + dg(r.inner_grad[...], r.inner_weight[cols, :], 1, 1)
            + dg(r.misc_grad[...], r.misc_weight[:, cols], 1, 0)
        )
        value_low = value.astype(bf)
        for k in range(256 // width):
            for m in range(T // tall):
                at = (j * (256 // width) + k) * (T // tall) + m
                r.normed_part[at] = value_low[m * tall : m * tall + tall, k * width : k * width + width]
                fold_start(1, at)
        hats = r.block_input[:, cols].astype(f32) * jnp.concatenate([r.inverse[...]] * 2, axis=1)
        r.gain_part[:, cols] = fold8(value * hats)

    stage("poll_at_small_sums")
    fold_middle(0, 7)
    stage("small_sums")

    def row_of(v):
        return jnp.sum(v, axis=0, keepdims=True)

    eye_wide = iota((H, LANES), 0) == iota((H, LANES), 1)

    def lanes_of(v):
        return row_of(jnp.where(eye_wide, jnp.broadcast_to(v, (H, LANES)), 0.0))

    r.small_send[...] = jnp.zeros_like(r.small_send)
    for k in range(CONV + 1):
        r.small_send[k : k + 1, :] = row_of(r.sum_acc[2 + k])
    r.small_send[5:6, :] = row_of(r.sum_acc[0])
    r.small_send[6:7, :] = row_of(r.sum_acc[1])
    for k in range(CONV):
        r.small_send[7:8, k * LANES : k * LANES + LANES] = row_of(r.misc_acc[k])
    r.small_send[8:9, 0:LANES] = row_of(r.misc_acc[CONV])
    r.small_send[8:9, LANES : 2 * LANES] = lanes_of(bias_sum)
    r.small_send[8:9, 2 * LANES : 3 * LANES] = lanes_of(rate_sum)
    gain_rows = row_of(r.gain_part[...])
    for k in range(D // HI):
        r.small_send[9 + k : 10 + k, :] = gain_rows[:, k * HI : k * HI + HI]
    r.small_recv[seq] = r.small_send[...]
    small_wait = spread(
        "seq", lambda d: r.small_send, lambda d: r.small_recv.at[d], r.small_ss, r.small_rs
    )
    stage("weights_two")

    def weight_rows_two(i, _):
        cols = pl.ds(pl.multiple_of(i * LANES, LANES), LANES)
        r.wg_two[cols, 0:HI] = dg(r.normed[:, cols], r.inner_grad[...], 0, 0).astype(bf)
        r.wg_two[cols, HI : HI + LANES] = dg(r.normed[:, cols], r.misc_grad[...], 0, 0).astype(bf)
        return 0

    lax.fori_loop(0, D // LANES // 2, weight_rows_two, 0)
    fold_in(1, 0)
    lax.fori_loop(D // LANES // 2, D // LANES, weight_rows_two, 0)
    pair_start(1)
    stage("folds")
    last = fold_pieces[1]
    for j in range(last + 2):
        if 0 < j < last:
            fold_in(1, j)
        if j > 1:
            fold_middle(1, j - 2)
        if j == 2:
            chip_start(1)
        if j == 4:
            small_wait()
            total = r.small_recv[0]
            for d in range(1, n_seq):
                total = total + r.small_recv[d]
            r.small_total[...] = total
            r.gain_recv[tp] = r.small_total[8:16, :]
            gain_wait = spread(
                "tp",
                lambda t: r.small_total.at[pl.ds(8, 8)],
                lambda t: r.gain_recv.at[t],
                r.gain_ss,
                r.gain_rs,
            )
    for j in range(fold_pieces[0]):
        fold_end(0, j)
    stage("weight_sums")
    r.sum_one[...] = chip_sum(0)
    r.sum_two[...] = chip_sum(1)
    gain_wait()
    gains = r.gain_recv[0]
    for t in range(1, n_tp):
        gains = gains + r.gain_recv[t]
    r.gain_total[...] = gains
    stage("folds_last")
    for j in range(fold_pieces[1]):
        fold_end(1, j)
    stage("drain")
    for d in range(1, n_tp):
        shared_copy(d).wait_send()
    for copy in waits:
        copy.wait_send()
    marks.close()


def finish(sizes, names, *refs):
    r = types.SimpleNamespace(**dict(zip(names, refs)))
    T, D, HI, H, NS = sizes
    P_ = HI // H
    T = r.block_input.shape[0]

    def final_rows(i, _):
        rows = pl.ds(pl.multiple_of(i * ROWS, ROWS), ROWS)
        x = r.block_input[rows, :].astype(f32)
        r.block_output[rows, :] = (x + r.branch_sum[rows, :].astype(f32)).astype(bf)
        inverse = lax.rsqrt(jnp.mean(x * x, axis=1, keepdims=True) + epsilon)
        hat = x * inverse
        hat_grad = r.normed_sum[rows, :].astype(f32) * r.input_gain[...].reshape(1, D)
        mean = jnp.mean(hat_grad * hat, axis=1, keepdims=True)
        r.input_grad[rows, :] = r.out_cotangent[rows, :].astype(f32) + inverse * (
            hat_grad - hat * mean
        )
        return 0

    lax.fori_loop(0, T // ROWS, final_rows, 0)
    @pl.when(pl.program_id(0) == 0)
    def _():
        r.gate_weight_grad[...] = r.sum_one[:, 0:HI]
        r.out_weight_grad[...] = r.sum_one[:, HI : 2 * HI].T
        r.inner_weight_grad[...] = r.sum_two[:, 0:HI]
        narrow = r.sum_two[:, HI : HI + LANES].T
        r.state_weight_grad[...] = narrow[0:NS]
        r.step_weight_grad[...] = narrow[NS : NS + H]
        small = r.small_total
        r.inner_kernel_grad[...] = small[0:CONV, :]
        r.inner_conv_bias_grad[...] = small[CONV : CONV + 1, :].reshape(HI)
        r.gate_gain_grad[...] = small[5:6, :].reshape(HI)
        head_sum = (iota((HI, LANES), 0) // P_ == iota((HI, LANES), 1)).astype(f32).astype(bf)
        skip_sums = fold3(dg(split3(jnp.broadcast_to(small[6:7, :], (8, HI))), head_sum, 1, 0))
        r.skip_scale_grad[...] = skip_sums[0:1, 0:H].reshape(H)
        for k in range(CONV):
            r.state_kernel_grad[k : k + 1, :] = small[7:8, k * LANES : k * LANES + NS]
        r.state_conv_bias_grad[...] = small[8:9, 0:NS].reshape(NS)
        r.step_bias_grad[...] = small[8:9, LANES : LANES + H].reshape(H)
        r.rate_log_grad[...] = small[8:9, 2 * LANES : 2 * LANES + H].reshape(H)
        for k in range(D // HI):
            r.input_gain_grad[k * HI : k * HI + HI] = r.gain_total[1 + k : 2 + k, :].reshape(HI)


INPUTS = (
    "block_input",
    "scene_lengths",
    "input_gain",
    "gate_weight",
    "inner_weight",
    "state_weight",
    "step_weight",
    "step_bias",
    "rate_log",
    "inner_kernel",
    "inner_conv_bias",
    "state_kernel",
    "state_conv_bias",
    "skip_scale",
    "gate_gain",
    "out_weight",
    "out_cotangent",
)
OUTPUTS = (
    "block_output",
    "input_grad",
    "input_gain_grad",
    "gate_weight_grad",
    "inner_weight_grad",
    "state_weight_grad",
    "step_weight_grad",
    "step_bias_grad",
    "rate_log_grad",
    "inner_kernel_grad",
    "inner_conv_bias_grad",
    "state_kernel_grad",
    "state_conv_bias_grad",
    "skip_scale_grad",
    "gate_gain_grad",
    "out_weight_grad",
)


SUMS = ("branch_sum", "normed_sum", "sum_one", "sum_two", "small_total", "gain_total")


def local(*args):
    given = dict(zip(INPUTS, args))
    given["state_weight"] = given["state_weight"].T
    given["step_weight"] = given["step_weight"].T
    n_seq = lax.axis_size("seq")
    n_tp = lax.axis_size("tp")
    T, D = given["block_input"].shape
    HI = given["gate_weight"].shape[1]
    H = given["step_bias"].shape[0]
    NS = given["state_weight"].shape[0]
    N = STATE
    Q = CHUNK
    NC = T // Q
    NP = HI // LANES
    R = HI // n_seq
    R2 = D // n_seq
    outs = (
        ((T, D), bf),
        ((T, D), f32),
        ((D,), f32),
        ((R2, HI), f32),
        ((R2, HI), f32),
        ((NS, R2), f32),
        ((H, R2), f32),
        ((H,), f32),
        ((H,), f32),
        ((CONV, HI), f32),
        ((HI,), f32),
        ((CONV, NS), f32),
        ((NS,), f32),
        ((H,), f32),
        ((HI,), f32),
        ((HI, R2), f32),
    )
    sums = (
        ((T, D), bf),
        ((T, D), bf),
        ((R2, 2 * HI), f32),
        ((R2, HI + LANES), f32),
        ((16, HI), f32),
        ((8, HI), f32),
    )
    scratch = dict(
        inverse=((T, LANES), f32),
        normed=((T, D), bf),
        misc_weight=((LANES, D), bf),
        inner_ext=((NP, T + PAD, LANES), f32),
        misc_ext=((1, T + PAD, LANES), f32),
        gate_pre=((T, HI), f32),
        misc_taps=((8, LANES), f32),
        inner_bias=((1, HI), f32),
        gain_row=((1, HI), f32),
        misc_conv=((T, LANES), f32),
        inner_conv=((T, HI), f32),
        act=((T, HI), bf),
        state_send=((T // 2, LANES), bf),
        state_recv=((n_tp, T // 2, LANES), bf),
        keys=((T, N), bf),
        queries=((T, N), bf),
        sigmoid_step=((H, T), f32),
        step_rows=((H, T), f32),
        log_decay=((H, T), f32),
        upto=((Q, Q), bf),
        expand=((3 * H, HI), bf),
        mask=((NC, Q, Q), f32),
        cum_left=((H, 16, T), bf),
        cum_right=((H, 16, T), bf),
        step_wide=((T, HI), f32),
        enter_wide=((T, HI), f32),
        tail_wide=((T, HI), f32),
        decay_wide=((NC, HI, LANES), f32),
        skip_wide=((8, HI), f32),
        xt=((T, HI), bf),
        xt_rest=((T, HI), bf),
        fresh=((NC, HI, N), f32),
        end_send=((HI, N), f32),
        end_recv=((n_seq, R, N), f32),
        decay_send=((H, LANES), f32),
        decay_recv=((n_seq, H, LANES), f32),
        enter_send=((n_seq, R, N), f32),
        enter_state=((HI, N), f32),
        state_in=((NC, HI, N), f32),
        state_in_low=((NC, HI, N), bf),
        state_in_rest=((NC, HI, N), bf),
        scores=((NC, Q, Q), f32),
        score_grad=((NC, Q, Q), f32),
        decays=((NC, H, Q, Q), f32),
        turned=((NC, H, Q, Q), bf),
        mixed=((T, HI), f32),
        norm_grad=((T, HI), f32),
        gated=((T, HI), f32),
        squares=((T, LANES), f32),
        products=((T, LANES), f32),
        sums_send=((8, T), f32),
        sums_recv=((n_tp, 8, T), f32),
        norm_col=((T, LANES), f32),
        back_col=((T, LANES), f32),
        head_sum=((HI, LANES), bf),
        head_sum_two=((HI, LANES), bf),
        head_sum_three=((HI, LANES), bf),
        sum_acc=((7, 8, HI), f32),
        gated_norm=((T, HI), bf),
        gate_grad=((T, HI), bf),
        heads_grad=((T, HI), f32),
        dy=((T, HI), bf),
        dy_rest=((T, HI), bf),
        dy_enter=((T, HI), bf),
        dy_enter_rest=((T, HI), bf),
        sum_y=((T, LANES), f32),
        sum_x=((T, LANES), f32),
        grad_local=((NC, HI, N), f32),
        grad_send=((HI, N), f32),
        grad_recv=((n_seq, R, N), f32),
        leave_send=((n_seq, R, N), f32),
        leave_grad=((HI, N), f32),
        x_inside=((T, HI), f32),
        x_carry=((T, HI), f32),
        wg_one=((D, 2 * HI), bf),
        pair_one=((n_seq // 2, R2, 2 * HI), bf),
        chip_one_send=((n_seq // 2, R2, 2 * HI), bf),
        chip_one=((n_seq // 2, R2, 2 * HI), bf),
        wg_two=((D, HI + LANES), bf),
        pair_two=((n_seq // 2, R2, HI + LANES), bf),
        chip_two_send=((n_seq // 2, R2, HI + LANES), bf),
        chip_two=((n_seq // 2, R2, HI + LANES), bf),
        query_grad=((T, N), f32),
        key_grad=((T, N), f32),
        shared_send=((n_tp, T // 2, LANES), bf),
        shared_recv=((n_tp, T // 2, LANES), bf),
        grad_ext=((NP, T + PAD, LANES), f32),
        state_grad_ext=((T + PAD, LANES), f32),
        inner_grad=((T, HI), bf),
        step_cols=((T, LANES), f32),
        misc_grad=((T, LANES), bf),
        misc_acc=((CONV + 1, 8, LANES), f32),
        normed_part=((16, T // 2, D // 8), bf),
        normed_in=((16, T // 2, D // 8), bf),
        normed_across=((16, T // 2, D // 8), bf),
        branch=((8, T, D // 8), bf),
        branch_in=((8, T, D // 8), bf),
        branch_across=((8, T, D // 8), bf),
        gain_part=((8, D), f32),
        small_send=((16, HI), f32),
        small_recv=((n_seq, 16, HI), f32),
        gain_recv=((n_tp, 8, HI), f32),
    )
    semaphores = dict(
        rim_send=(2,),
        rim_recv=(2,),
        halo_send=(2,),
        halo_recv=(2,),
        pair_ss=(2, n_seq // 2),
        pair_rs=(2, n_seq // 2),
        chip_ss=(2, n_seq // 2 - 1),
        chip_rs=(2, n_seq // 2 - 1),
        fold_ss=(3, 24),
        fold_rs=(3, 24),
    )
    for name in ("state", "sums", "shared", "gain"):
        semaphores[name + "_ss"] = (n_tp - 1,)
        semaphores[name + "_rs"] = (n_tp - 1,)
    for name in ("decay", "end", "enter", "grad", "leave", "small"):
        semaphores[name + "_ss"] = (n_seq - 1,)
        semaphores[name + "_rs"] = (n_seq - 1,)
    names = INPUTS + SUMS + tuple(scratch) + tuple(semaphores)
    vmem = pl.BlockSpec(memory_space=pltpu.VMEM)
    smem = pl.BlockSpec(memory_space=pltpu.SMEM)
    totals = pl.pallas_call(
        functools.partial(kernel, (n_seq, n_tp, T, D, HI, H, NS), names),
        out_shape=tuple(jax.ShapeDtypeStruct(s, t) for s, t in sums),
        in_specs=[smem if n == "scene_lengths" else vmem for n in INPUTS],
        out_specs=tuple(vmem for _ in sums),
        scratch_shapes=[pltpu.VMEM(s, t) for s, t in scratch.values()]
        + [pltpu.SemaphoreType.DMA(s) for s in semaphores.values()],
        compiler_params=pltpu.CompilerParams(
            collective_id=0, has_side_effects=True, vmem_limit_bytes=61 * 2**20
        ),
    )(*given.values())
    tall = ("block_input", "out_cotangent", "branch_sum", "normed_sum", "block_output", "input_grad")
    steps = 4
    by_rows = pl.BlockSpec((T // steps, D), lambda i: (i, 0))

    def whole(shape):
        return pl.BlockSpec(shape, lambda i: (0,) * len(shape))

    needed = ("block_input", "input_gain", "out_cotangent")
    results = pl.pallas_call(
        functools.partial(finish, (T, D, HI, H, NS), needed + SUMS + OUTPUTS),
        out_shape=tuple(jax.ShapeDtypeStruct(s, t) for s, t in outs),
        grid=(steps,),
        in_specs=[by_rows if n in tall else whole(given[n].shape) for n in needed]
        + [by_rows if n in tall else whole(s) for n, (s, _) in zip(SUMS, sums)],
        out_specs=tuple(by_rows if n in tall else whole(s) for n, (s, _) in zip(OUTPUTS, outs)),
        compiler_params=pltpu.CompilerParams(vmem_limit_bytes=60 * 2**20),
    )(*(given[n] for n in needed), *totals)
    results = dict(zip(OUTPUTS, results))
    results["state_weight_grad"] = results["state_weight_grad"].T
    results["step_weight_grad"] = results["step_weight_grad"].T
    return tuple(results.values())


def solution(mesh):
    rows = P("seq", None)
    cols = P(None, "tp")
    heads = P("tp")
    return jax.shard_map(
        local,
        mesh=mesh,
        in_specs=(
            rows,
            P(),
            P(),
            cols,
            cols,
            cols,
            cols,
            heads,
            heads,
            cols,
            heads,
            cols,
            heads,
            heads,
            heads,
            P("tp", None),
            rows,
        ),
        out_specs=(
            rows,
            rows,
            P(),
            P("seq", "tp"),
            P("seq", "tp"),
            P("seq", "tp"),
            P("seq", "tp"),
            heads,
            heads,
            cols,
            heads,
            cols,
            heads,
            heads,
            heads,
            P("tp", "seq"),
        ),
        check_vma=False,
    )
```

```python
import contextlib
import functools
import types

import jax
import jax.numpy as jnp
from jax import lax
from jax.experimental import pallas as pl
from jax.experimental.pallas import tpu as pltpu
from jax.sharding import PartitionSpec as P

STATE = 128
CONV = 4
CHUNK = 256
LANES = 128
PAD = 8
ROWS = 64
epsilon = 1e-05
bf = jnp.bfloat16
f32 = jnp.float32
i32 = jnp.int32
MESH = pl.DeviceIdType.MESH


def dg(left, right, left_dim, right_dim):
    return lax.dot_general(
        left, right, (((left_dim,), (right_dim,)), ((), ())), preferred_element_type=f32
    )


def split3(v):
    high = v.astype(bf).astype(f32)
    middle = (v - high).astype(bf).astype(f32)
    return jnp.concatenate([high, middle, v - high - middle], axis=0).astype(bf)


def fold3(v):
    third = v.shape[0] // 3
    return v[:third] + v[third : 2 * third] + v[2 * third :]


def halves(v):
    high = v.astype(bf)
    return high, (v - high.astype(f32)).astype(bf)


def slope(v):
    s = jax.nn.sigmoid(v)
    return s * (1.0 + v * (1.0 - s))


def fold8(v):
    total = v[0:8]
    for i in range(1, v.shape[0] // 8):
        total = total + v[8 * i : 8 * i + 8]
    return total


def iota(shape, dim):
    return lax.broadcasted_iota(i32, shape, dim)


LOADED = ("inner_weight", "gate_weight", "out_weight", "out_cotangent")


def kernel(sizes, names, *refs):
    r = types.SimpleNamespace(**dict(zip(names, refs)))
    n_seq, n_tp, T, D, HI, H, NS = sizes
    N = STATE
    P_ = HI // H
    Q = CHUNK
    NC = T // Q
    NP = HI // LANES
    R = HI // n_seq
    R2 = D // n_seq
    total_tokens = T * n_seq
    seq = lax.axis_index("seq")
    tp = lax.axis_index("tp")

    barrier = pltpu.get_barrier_semaphore()
    for d in range(1, n_seq):
        pl.semaphore_signal(
            barrier, inc=1, device_id=((seq + d) % n_seq, tp), device_id_type=MESH
        )
    for d in range(1, n_tp):
        pl.semaphore_signal(
            barrier, inc=1, device_id=(seq, (tp + d) % n_tp), device_id_type=MESH
        )

    waits = []
    loads = {}
    for k, n in enumerate(LOADED):
        loads[n] = pltpu.make_async_copy(getattr(r, n + "_hbm"), getattr(r, n), r.load_sems.at[k])
        loads[n].start()
    half = n_tp // 2
    inner = jnp.where(tp < half, tp + 1, tp - 1)
    outer = jnp.where(tp < half, tp - 1, tp + 1)
    is_middle = (tp == half - 1) | (tp == half)
    has_outer = (tp > 0) & (tp < n_tp - 1)
    fold_pieces = (r.branch_in.shape[0], r.normed_in.shape[0])
    fold_width = D // fold_pieces[0], LANES
    fold_rows = T, T * D // LANES // fold_pieces[1]
    fold_refs = (
        (r.branch, r.branch_in, r.branch_across, r.branch_sum),
        (r.normed_part, r.normed_in, r.normed_across, r.normed_sum),
    )

    def fold(a, j):
        high = T // fold_rows[a]
        place = (
            pl.ds(j % high * fold_rows[a], fold_rows[a]),
            pl.ds(j // high * fold_width[a], fold_width[a]),
        )
        partial, arrived, across, total = (
            ref.at[j] if k < 3 else ref.at[place]
            for k, ref in enumerate(fold_refs[a])
        )
        return partial, arrived, across, total

    def fold_copy(a, j, leg):
        partial, arrived, across, total = fold(a, j)
        sems = leg, sum(fold_pieces[:a]) + j
        source, target, place = ((partial, arrived, inner), (partial, across, inner), (total, total, outer))[leg]
        return remote(source, target, r.fold_ss.at[sems], r.fold_rs.at[sems], (seq, place))

    def fold_start(a, j):
        pl.when(jnp.logical_not(has_outer | is_middle))(fold_copy(a, j, 0).start)

    def fold_in(a, j):
        partial, arrived, _, _ = fold(a, j)

        @pl.when(has_outer)
        def _():
            fold_copy(a, j, 0).wait_recv()
            partial[...] = (partial[...].astype(f32) + arrived[...].astype(f32)).astype(bf)

        pl.when(is_middle)(fold_copy(a, j, 1).start)
        pl.when(has_outer & jnp.logical_not(is_middle))(fold_copy(a, j, 0).start)

    def fold_middle(a, j):
        partial, _, across, total = fold(a, j)

        @pl.when(is_middle)
        def _():
            fold_copy(a, j, 1).wait_recv()
            total[...] = (partial[...].astype(f32) + across[...].astype(f32)).astype(bf)
            pl.when(has_outer)(fold_copy(a, j, 2).start)

    def fold_end(a, j):
        @pl.when(jnp.logical_not(is_middle))
        def _():
            fold_copy(a, j, 2).wait_recv()
            pl.when(has_outer)(fold_copy(a, j, 2).start)
            fold_copy(a, j, 0).wait_send()

        pl.when(has_outer)(fold_copy(a, j, 2).wait_send)
        pl.when(is_middle)(fold_copy(a, j, 1).wait_send)

    marks = contextlib.ExitStack()

    def stage(name):
        marks.close()
        marks.enter_context(jax.named_scope(name))

    stage("norm")

    def remote(src, dst, send, recv, device):
        return pltpu.make_async_remote_copy(
            src_ref=src,
            dst_ref=dst,
            send_sem=send,
            recv_sem=recv,
            device_id=device,
            device_id_type=MESH,
        )

    def spread(axis, src_to, dst_from, send, recv):
        n = n_seq if axis == "seq" else n_tp
        me = seq if axis == "seq" else tp
        incoming = []
        for d in range(1, n):
            target = (me + d) % n
            source = (me + n - d) % n
            device = (target, tp) if axis == "seq" else (seq, target)
            out = remote(src_to(target), dst_from(me), send.at[d - 1], recv.at[d - 1], device)
            out.start()
            waits.append(out)
            incoming.append(
                remote(src_to(target), dst_from(source), send.at[d - 1], recv.at[d - 1], device)
            )

        def wait():
            for copy in incoming:
                copy.wait_recv()

        return wait

    starts = [jnp.int32(0)]
    for k in range(r.scene_lengths.shape[0] - 1):
        starts.append(starts[-1] + r.scene_lengths[k])

    def segment(position):
        found = (position >= starts[0]).astype(i32)
        for s in starts[1:]:
            found = found + (position >= s).astype(i32)
        return found

    first_token = seq * T

    def norm_rows(i, _):
        rows = pl.ds(pl.multiple_of(i * ROWS, ROWS), ROWS)
        x = r.block_input[rows, :].astype(f32)
        inverse = lax.rsqrt(jnp.mean(x * x, axis=1, keepdims=True) + epsilon)
        r.inverse[rows, :] = jnp.broadcast_to(inverse, (ROWS, LANES))
        r.normed[rows, :] = (x * inverse * r.input_gain[...].reshape(1, D)).astype(bf)
        return 0

    lax.fori_loop(0, T // ROWS, norm_rows, 0)

    stage("projections")
    r.misc_weight[...] = jnp.zeros_like(r.misc_weight)
    r.misc_weight[0:NS, :] = r.state_weight[...]
    r.misc_weight[NS : NS + H, :] = r.step_weight[...]
    normed_all = r.normed[...]
    r.misc_ext[0, PAD : PAD + T, :] = dg(normed_all, r.misc_weight[...], 1, 1)
    stage("barrier")
    pl.semaphore_wait(barrier, n_seq - 1 + n_tp - 1)
    stage("inner_projection")
    right = ((seq + 1) % n_seq, tp)
    left = ((seq + n_seq - 1) % n_seq, tp)
    misc_rim, inner_rim = [
        remote(
            ref.at[:, pl.ds(T, PAD)],
            ref.at[:, pl.ds(0, PAD)],
            r.rim_send.at[k],
            r.rim_recv.at[k],
            right,
        )
        for k, ref in enumerate((r.misc_ext, r.inner_ext))
    ]
    waits.extend((misc_rim, inner_rim))
    misc_rim.start()
    for j in range(HI // 256):
        cols = slice(256 * j, 256 * j + 256)
        if j == 0:
            loads["inner_weight"].wait()
        value = dg(normed_all, r.inner_weight[:, cols], 1, 0)
        r.inner_ext[2 * j, PAD : PAD + T, :] = value[:, :LANES]
        r.inner_ext[2 * j + 1, PAD : PAD + T, :] = value[:, LANES:]
    inner_rim.start()
    stage("gate_projection")
    for j in range(HI // 256):
        cols = slice(256 * j, 256 * j + 256)
        if j == 0:
            loads["gate_weight"].wait()
        r.gate_pre[:, cols] = dg(normed_all, r.gate_weight[:, cols], 1, 0)

    stage("convolutions")
    def agreements(base, rows):
        position = first_token + base + iota((rows, LANES), 0)
        now = segment(position)
        return [segment(position - (CONV - 1) + k) == now for k in range(CONV - 1)]

    def conv_block(ext, taps, bias, base, lanes, masks):
        value = bias[:, lanes]
        for k in range(CONV):
            window = ext[pl.ds(base + PAD - CONV + 1 + k, ROWS), :]
            term = taps[k : k + 1, lanes] * window
            value = value + (term if k == CONV - 1 else jnp.where(masks[k], term, 0.0))
        return value

    r.misc_taps[...] = jnp.zeros_like(r.misc_taps)
    r.misc_taps[0:CONV, 0:NS] = r.state_kernel[...]
    r.misc_taps[CONV : CONV + 1, 0:NS] = r.state_conv_bias[...].reshape(1, NS)
    r.inner_bias[...] = r.inner_conv_bias[...].reshape(1, HI)
    stage("rim_wait")
    misc_rim.wait_recv()
    stage("conv")

    def misc_conv_rows(i, _):
        base = pl.multiple_of(i * ROWS, ROWS)
        masks = agreements(base, ROWS)
        taps = r.misc_taps[...]
        value = conv_block(
            r.misc_ext.at[0], taps, taps[CONV : CONV + 1], base, slice(0, LANES), masks
        )
        r.misc_conv[pl.ds(base, ROWS), :] = value
        return 0

    lax.fori_loop(0, T // ROWS, misc_conv_rows, 0)
    low_lanes = iota((T // 2, LANES), 1) < NS
    own = r.misc_conv[...]
    own = own * jax.nn.sigmoid(own)
    r.state_send[...] = jnp.where(
        low_lanes, own[: T // 2], pltpu.roll(own[T // 2 :], NS, 1)
    ).astype(bf)
    r.state_recv[tp] = r.state_send[...]
    state_wait = spread(
        "tp",
        lambda t: r.state_send,
        lambda t: r.state_recv.at[t],
        r.state_ss,
        r.state_rs,
    )

    def inner_conv_rows(i, _):
        base = pl.multiple_of(i * ROWS, ROWS)
        rows = pl.ds(base, ROWS)
        masks = agreements(base, ROWS)
        taps = r.inner_kernel[...]
        for g in range(NP):
            lanes = slice(g * LANES, g * LANES + LANES)
            value = conv_block(r.inner_ext.at[g], taps, r.inner_bias, base, lanes, masks)
            r.inner_conv[rows, lanes] = value
            r.act[rows, lanes] = (value * jax.nn.sigmoid(value)).astype(bf)
        return 0

    inner_rim.wait_recv()
    lax.fori_loop(0, T // ROWS, inner_conv_rows, 0)

    stage("decays")
    eye = iota((H, H), 0) == iota((H, H), 1)

    def column(ref):
        wide = jnp.broadcast_to(ref[...].reshape(1, H), (H, H))
        return jnp.sum(jnp.where(eye, wide, 0.0), axis=1, keepdims=True)

    step_in = r.misc_ext[0, PAD : PAD + T, :].T[NS : NS + H, :] + column(r.step_bias)
    step = jnp.maximum(step_in, 0.0) + jnp.log1p(jnp.exp(-jnp.abs(step_in)))
    rate = jnp.exp(column(r.rate_log))
    log_decay = step * -rate
    r.sigmoid_step[...] = jax.nn.sigmoid(step_in)
    r.log_decay[...] = log_decay
    r.step_rows[...] = step
    r.upto[...] = (iota((Q, Q), 0) <= iota((Q, Q), 1)).astype(f32).astype(bf)
    r.expand[...] = (iota((3 * H, HI), 0) % H == iota((3 * H, HI), 1) // P_).astype(f32).astype(bf)
    expand = r.expand[...]

    entering, tailing, chunk_decay = [], [], []
    ones_rows = jnp.ones((1, Q), f32)
    for c in range(NC):
        cols = slice(c * Q, c * Q + Q)
        cumulative = fold3(dg(split3(log_decay[:, cols]), r.upto[...], 1, 0))
        start = first_token + c * Q
        seg_row = segment(start + iota((H, Q), 1))
        seg_before = segment(start - 1)
        seg_end = segment(start + Q - 1)
        last = cumulative[:, Q - 1 : Q]
        enter = jnp.where(seg_row == seg_before, jnp.exp(cumulative), 0.0)
        tail = jnp.where(seg_row == seg_end, jnp.exp(last - cumulative), 0.0)
        entering.append(enter)
        tailing.append(tail)
        chunk_decay.append(enter[:, Q - 1 : Q])
        seg_col = segment(start + iota((Q, Q), 0))
        seg_lane = segment(start + iota((Q, Q), 1))
        keep = (seg_col == seg_lane) & (iota((Q, Q), 0) >= iota((Q, Q), 1))
        r.mask[c] = jnp.where(keep, 0.0, -1e30)
        high = cumulative.astype(bf).astype(f32)
        middle = (cumulative - high).astype(bf).astype(f32)
        rest = cumulative - high - middle
        which = iota((16, Q), 0)
        for h in range(H):
            parts = jnp.where(
                which % 3 == 0,
                high[h : h + 1],
                jnp.where(which % 3 == 1, middle[h : h + 1], rest[h : h + 1]),
            )
            first = which < 3
            second = (which >= 3) & (which < 6)
            r.cum_left[h, :, cols] = jnp.where(
                first, parts, jnp.where(second, 1.0, 0.0)
            ).astype(bf)
            r.cum_right[h, :, cols] = jnp.where(
                first, 1.0, jnp.where(second, -parts, 0.0)
            ).astype(bf)

    def wide(v):
        return dg(split3(v), expand, 0, 0)

    def wide_rows(v):
        return dg(expand, split3(jnp.broadcast_to(v, (H, LANES))), 0, 0)

    for c in range(NC):
        rows = slice(c * Q, c * Q + Q)
        r.step_wide[rows, :] = wide(step[:, rows])
        r.enter_wide[rows, :] = wide(entering[c])
        r.tail_wide[rows, :] = wide(tailing[c])
        r.decay_wide[c] = wide_rows(chunk_decay[c])
    r.skip_wide[...] = dg(split3(jnp.broadcast_to(column(r.skip_scale), (H, 8))), expand, 0, 0)

    def scaled_rows(i, _):
        rows = pl.ds(pl.multiple_of(i * ROWS, ROWS), ROWS)
        x = r.act[rows, :].astype(f32)
        r.xt[rows, :], r.xt_rest[rows, :] = halves(x * r.step_wide[rows, :] * r.tail_wide[rows, :])
        return 0

    lax.fori_loop(0, T // ROWS, scaled_rows, 0)

    stage("decay_matrices")

    def decay_matrix(i, _):
        c = i // H
        h = i % H
        rows = pl.ds(pl.multiple_of(c * Q, Q), Q)
        difference = dg(r.cum_left[h, :, rows], r.cum_right[h, :, rows], 0, 0)
        r.decays[c, h] = jnp.exp(difference + r.mask[c])
        return 0

    lax.fori_loop(0, NC * H, decay_matrix, 0)

    stage("keys_wait")
    state_wait()
    shards = n_tp // 2
    half_low = iota((T // 2, LANES), 1) < NS
    for ref, at in ((r.keys, 0), (r.queries, shards)):
        one, two = r.state_recv[at].astype(f32), r.state_recv[at + 1].astype(f32)
        ref[0 : T // 2, :] = jnp.where(half_low, one, pltpu.roll(two, NS, 1)).astype(bf)
        ref[T // 2 : T, :] = jnp.where(half_low, pltpu.roll(one, NS, 1), two).astype(bf)

    stage("end_states")
    end_state = None
    device_decay = None
    for c in range(NC):
        rows = slice(c * Q, c * Q + Q)
        keys = r.keys[rows, :]
        fresh = dg(r.xt[rows, :], keys, 0, 0) + dg(r.xt_rest[rows, :], keys, 0, 0)
        r.fresh[c] = fresh
        end_state = fresh if c == 0 else r.decay_wide[c] * end_state + fresh
        device_decay = chunk_decay[c] if c == 0 else device_decay * chunk_decay[c]
    r.end_send[...] = end_state
    r.decay_send[...] = jnp.broadcast_to(device_decay, (H, LANES))

    def block(ref, device):
        return ref.at[pl.ds(pl.multiple_of(device * R, R), R)]

    r.end_recv[seq] = r.end_send[pl.ds(pl.multiple_of(seq * R, R), R), :]
    r.decay_recv[seq] = r.decay_send[...]
    decay_wait = spread(
        "seq", lambda d: r.decay_send, lambda d: r.decay_recv.at[d], r.decay_ss, r.decay_rs
    )
    end_wait = spread(
        "seq", lambda d: block(r.end_send, d), lambda d: r.end_recv.at[d], r.end_ss, r.end_rs
    )

    stage("inside")
    for c in range(NC):
        rows = slice(c * Q, c * Q + Q)
        r.scores[c] = dg(r.queries[rows, :], r.keys[rows, :], 1, 1)
    low = iota((Q, LANES), 1) < P_

    def inside(i, _):
        c = i // NP
        p = i % NP
        rows = pl.ds(pl.multiple_of(c * Q, Q), Q)
        lanes = pl.ds(pl.multiple_of(p * LANES, LANES), LANES)
        x = r.act[rows, lanes]
        zero = jnp.zeros_like(x)
        result = None
        for s in range(2):
            h = 2 * p + s
            stepped = r.decays[c, h] * r.step_rows[pl.ds(h, 1), rows]
            weight, rest = halves(stepped * r.scores[c])
            part = jnp.where(low, x, zero) if s == 0 else jnp.where(low, zero, x)
            term = dg(weight, part, 1, 0) + dg(rest, part, 1, 0)
            result = term if s == 0 else result + term
        r.mixed[rows, lanes] = result
        return 0

    lax.fori_loop(0, NC * NP, inside, 0)
    for j in range(HI // 256):
        cols = slice(256 * j, 256 * j + 256)
        if j == 0:
            loads["out_weight"].wait()
            loads["out_cotangent"].wait()
        r.norm_grad[:, cols] = dg(r.out_cotangent[...], r.out_weight[cols, :], 1, 1)

    stage("entering")
    head_of = (seq * R) // P_
    stage("end_wait")
    end_wait()
    decay_wait()

    def decay_of(d):
        return jnp.broadcast_to(r.decay_recv[d, pl.ds(head_of, 1), :], (R, LANES))

    running = jnp.zeros((R, N), f32)
    for d in range(n_seq):
        r.enter_send[d] = running
        running = decay_of(d) * running + r.end_recv[d]
    own_rows = pl.ds(pl.multiple_of(seq * R, R), R)
    r.enter_state[own_rows, :] = r.enter_send[seq]
    enter_wait = spread(
        "seq", lambda d: r.enter_send.at[d], lambda d: block(r.enter_state, d), r.enter_ss, r.enter_rs
    )
    stage("turned_weights")

    def turned_weight(i, _):
        c = i // H
        h = i % H
        r.turned[c, h] = (r.decays[c, h] * r.scores[c]).T.astype(bf)
        return 0

    lax.fori_loop(0, NC * H, turned_weight, 0)
    stage("enter_wait")
    enter_wait()
    stage("readout")
    for c in range(NC):
        rows = slice(c * Q, c * Q + Q)
        if c == 0:
            state = r.enter_state[...]
        else:
            state = r.decay_wide[c - 1] * state + r.fresh[c - 1]
        r.state_in[c] = state
        r.state_in_low[c], r.state_in_rest[c] = halves(state)
        for j in range(HI // 256):
            cols = slice(256 * j, 256 * j + 256)
            queries = r.queries[rows, :]
            read = dg(queries, r.state_in_low[c, cols, :], 1, 1) + dg(queries, r.state_in_rest[c, cols, :], 1, 1)
            r.mixed[rows, cols] = r.mixed[rows, cols] + r.enter_wide[rows, cols] * read

    stage("gated")
    skip_row = r.skip_wide[0:1, :]
    r.gain_row[...] = r.gate_gain[...].reshape(1, HI)

    def gated_rows(i, _):
        rows = pl.ds(pl.multiple_of(i * ROWS, ROWS), ROWS)
        heads = r.mixed[rows, :] + skip_row * r.act[rows, :].astype(f32)
        gate = r.gate_pre[rows, :]
        gated = heads * (gate * jax.nn.sigmoid(gate))
        r.gated[rows, :] = gated
        scaled = r.norm_grad[rows, :] * r.gain_row[...]
        squares = gated * gated
        products = scaled * gated

        def lane_sum(v):
            total = v[:, :LANES]
            for g in range(1, NP):
                total = total + v[:, g * LANES : g * LANES + LANES]
            return total

        r.squares[rows, :] = lane_sum(squares)
        r.products[rows, :] = lane_sum(products)
        return 0

    lax.fori_loop(0, T // ROWS, gated_rows, 0)
    square_row = jnp.sum(r.squares[...].T, axis=0, keepdims=True)
    product_row = jnp.sum(r.products[...].T, axis=0, keepdims=True)
    r.sums_send[...] = jnp.where(
        iota((8, T), 0) == 0,
        jnp.broadcast_to(square_row, (8, T)),
        jnp.broadcast_to(product_row, (8, T)),
    )
    r.sums_recv[tp] = r.sums_send[...]
    sums_wait = spread(
        "tp", lambda t: r.sums_send, lambda t: r.sums_recv.at[t], r.sums_ss, r.sums_rs
    )
    stage("sums_wait")
    sums_wait()
    stage("sums")
    sums = r.sums_recv[0]
    for t in range(1, n_tp):
        sums = sums + r.sums_recv[t]
    count = HI * n_tp
    norm_row = lax.rsqrt(sums[0:1] / count + epsilon)
    back_row = norm_row * norm_row * norm_row * (sums[1:2] / count)
    r.norm_col[...] = jnp.broadcast_to(norm_row, (LANES, T)).T
    r.back_col[...] = jnp.broadcast_to(back_row, (LANES, T)).T

    stage("back_gated")
    r.head_sum[...] = (iota((HI, LANES), 0) // P_ == iota((HI, LANES), 1)).astype(f32).astype(bf)
    r.sum_acc[...] = jnp.zeros_like(r.sum_acc)

    def tile4(v):
        return jnp.concatenate([v] * NP, axis=1)

    def summed(v, which):
        high, lowv = halves(v)
        return dg(high, which, 1, 0) + dg(lowv, which, 1, 0)

    def gated_norm_rows(i, _):
        rows = pl.ds(pl.multiple_of(i * ROWS, ROWS), ROWS)
        unit = r.gated[rows, :] * tile4(r.norm_col[rows, :])
        r.gated_norm[rows, :] = (unit * r.gain_row[...]).astype(bf)
        return 0

    lax.fori_loop(0, T // ROWS, gated_norm_rows, 0)
    stage("out_projection")
    for j in range(D // 256):
        value = dg(r.gated_norm[...], r.out_weight[:, 256 * j : 256 * j + 256], 1, 0).astype(bf)
        for k in range(256 // fold_width[0]):
            at = j * (256 // fold_width[0]) + k
            r.branch[at] = value[:, k * fold_width[0] : (k + 1) * fold_width[0]]
            fold_start(0, at)
    stage("back_rows")

    def back_rows(i, _):
        rows = pl.ds(pl.multiple_of(i * ROWS, ROWS), ROWS)
        norm = tile4(r.norm_col[rows, :])
        back = tile4(r.back_col[rows, :])
        gated = r.gated[rows, :]
        grad = r.norm_grad[rows, :]
        gain = r.gain_row[...]
        gate = r.gate_pre[rows, :]
        sigma = jax.nn.sigmoid(gate)
        unit = gated * norm
        r.sum_acc[0] = r.sum_acc[0] + fold8(grad * unit)
        gated_grad = norm * (grad * gain) - gated * back
        heads_grad = gated_grad * (gate * sigma)
        heads = r.mixed[rows, :] + skip_row * r.act[rows, :].astype(f32)
        r.gate_grad[rows, :] = (
            gated_grad * heads * (sigma * (1.0 + gate * (1.0 - sigma)))
        ).astype(bf)
        r.heads_grad[rows, :] = heads_grad
        x = r.act[rows, :].astype(f32)
        r.sum_acc[1] = r.sum_acc[1] + fold8(heads_grad * x)
        r.dy[rows, :], r.dy_rest[rows, :] = halves(heads_grad)
        r.dy_enter[rows, :], r.dy_enter_rest[rows, :] = halves(heads_grad * r.enter_wide[rows, :])
        r.sum_y[rows, :] = summed(heads_grad * r.mixed[rows, :], r.head_sum[...])
        return 0

    lax.fori_loop(0, T // ROWS, back_rows, 0)

    stage("grad_states")
    grad_in = None
    for c in reversed(range(NC)):
        rows = slice(c * Q, c * Q + Q)
        queries = r.queries[rows, :]
        local = dg(r.dy_enter[rows, :], queries, 0, 0) + dg(r.dy_enter_rest[rows, :], queries, 0, 0)
        r.grad_local[c] = local
        grad_in = local if grad_in is None else r.decay_wide[c] * grad_in + local
    r.grad_send[...] = grad_in
    r.grad_recv[seq] = r.grad_send[own_rows, :]
    grad_wait = spread(
        "seq", lambda d: block(r.grad_send, d), lambda d: r.grad_recv.at[d], r.grad_ss, r.grad_rs
    )
    stage("inside_back")
    r.score_grad[...] = jnp.zeros_like(r.score_grad)

    def inside_back(i, _):
        c = i // NP
        p = i % NP
        rows = pl.ds(pl.multiple_of(c * Q, Q), Q)
        lanes = pl.ds(pl.multiple_of(p * LANES, LANES), LANES)
        x = r.act[rows, lanes]
        dy = r.dy[rows, lanes]
        dy_rest = r.dy_rest[rows, lanes]
        zero = jnp.zeros_like(dy)
        x_turned, dy_turned = pltpu.roll(x, P_, 1), pltpu.roll(dy_rest, P_, 1)
        result = None
        for s in range(2):
            h = 2 * p + s
            ours = low if s == 0 else jnp.logical_not(low)
            pairs = dg(jnp.where(ours, dy, dy_turned), jnp.where(ours, x, x_turned), 1, 1)
            r.score_grad[c] = r.score_grad[c] + pairs * (r.decays[c, h] * r.step_rows[pl.ds(h, 1), rows])
            term = dg(r.turned[c, h], jnp.where(ours, dy, zero), 1, 0)
            result = term if s == 0 else result + term
        r.x_inside[rows, lanes] = result
        return 0

    lax.fori_loop(0, NC * NP, inside_back, 0)

    stage("poll_at_grad_wait")
    fold_in(0, 0)
    stage("grad_wait")
    grad_wait()
    stage("leave_scan")
    running = jnp.zeros((R, N), f32)
    for d in reversed(range(n_seq)):
        r.leave_send[d] = running
        running = decay_of(d) * running + r.grad_recv[d]
    r.leave_grad[own_rows, :] = r.leave_send[seq]
    leave_wait = spread(
        "seq", lambda d: r.leave_send.at[d], lambda d: block(r.leave_grad, d), r.leave_ss, r.leave_rs
    )

    stage("query_grad")
    for c in range(NC):
        rows = slice(c * Q, c * Q + Q)
        score_low = r.score_grad[c].astype(bf)
        r.query_grad[rows, :] = (
            dg(score_low, r.keys[rows, :], 1, 0)
            + dg(r.dy_enter[rows, :], r.state_in_low[c], 1, 0)
            + dg(r.dy_enter_rest[rows, :], r.state_in_low[c], 1, 0)
            + dg(r.dy_enter[rows, :], r.state_in_rest[c], 1, 0)
        )

    def shared_copy(d, arriving=False):
        target = (tp + d) % n_tp
        slot = (tp + n_tp - d) % n_tp if arriving else tp
        sems = (r.shared_ss.at[d - 1], r.shared_rs.at[d - 1])
        return remote(r.shared_send.at[target], r.shared_recv.at[slot], *sems, (seq, target))

    def pack_shared(ref, group):
        top, bottom = ref[0 : T // 2, :], ref[T // 2 : T, :]
        at = group * shards
        r.shared_send[at] = jnp.where(half_low, top, pltpu.roll(bottom, NS, 1)).astype(bf)
        r.shared_send[at + 1] = jnp.where(half_low, pltpu.roll(top, NS, 1), bottom).astype(bf)

        @pl.when(tp // shards == group)
        def _():
            r.shared_recv[tp] = r.shared_send[tp]

        for d in range(1, n_tp):
            pl.when((tp + d) % n_tp // shards == group)(shared_copy(d).start)

    pack_shared(r.query_grad, 1)
    stage("poll_at_weights_one")
    fold_in(0, 1)
    stage("weights_one")
    def weight_rows(i, _):
        cols = pl.ds(pl.multiple_of(i * LANES, LANES), LANES)
        r.wg_one[cols, 0:HI] = dg(r.normed[:, cols], r.gate_grad[...], 0, 0).astype(bf)
        r.wg_one[cols, HI : 2 * HI] = dg(r.out_cotangent[:, cols], r.gated_norm[...], 0, 0).astype(bf)
        return 0

    lax.fori_loop(0, D // LANES, weight_rows, 0)

    chips = n_seq // 2
    core = seq % 2
    chip = seq // 2
    sibling = seq + 1 - 2 * core

    def pair_copy(k, q):
        rows = pl.ds(pl.multiple_of((2 * q + 1 - core) * R2, R2), R2)
        source, target = ((r.wg_one, r.pair_one), (r.wg_two, r.pair_two))[k]
        return remote(
            source.at[rows], target.at[q], r.pair_ss.at[k, q], r.pair_rs.at[k, q], (sibling, tp)
        )

    def chip_copy(k, d, arriving=False):
        to = (chip + d) % chips
        slot = (chip + chips - d) % chips if arriving else chip
        source, target = ((r.chip_one_send, r.chip_one), (r.chip_two_send, r.chip_two))[k]
        return remote(
            source.at[to],
            target.at[slot],
            r.chip_ss.at[k, d - 1],
            r.chip_rs.at[k, d - 1],
            (2 * to + core, tp),
        )

    def pair_start(k):
        for q in range(chips):
            pair_copy(k, q).start()

    def chip_start(k):
        own, pair, send, kept = (
            (r.wg_one, r.pair_one, r.chip_one_send, r.chip_one),
            (r.wg_two, r.pair_two, r.chip_two_send, r.chip_two),
        )[k]
        for q in range(chips):
            rows = pl.ds(pl.multiple_of((2 * q + core) * R2, R2), R2)
            pair_copy(k, q).wait_recv()
            send[q] = (own[rows, :].astype(f32) + pair[q].astype(f32)).astype(bf)
        for d in range(1, chips):
            chip_copy(k, d).start()
        kept[chip] = send[chip]

    def chip_sum(k):
        kept = (r.chip_one, r.chip_two)[k]
        for d in range(1, chips):
            chip_copy(k, d, True).wait_recv()
        value = kept[0].astype(f32)
        for q in range(1, chips):
            value = value + kept[q].astype(f32)
        for q in range(chips):
            pair_copy(k, q).wait_send()
        for d in range(1, chips):
            chip_copy(k, d).wait_send()
        return value

    pair_start(0)
    stage("poll_at_leave_wait")
    fold_in(0, 2)
    fold_middle(0, 0)
    stage("leave_wait")
    leave_wait()
    stage("leave")
    carry_terms = [None] * NC
    for c in reversed(range(NC)):
        rows = slice(c * Q, c * Q + Q)
        if c == NC - 1:
            grad = r.leave_grad[...]
        else:
            grad = r.decay_wide[c + 1] * grad + r.grad_local[c + 1]
        grad_low, grad_rest = halves(grad)
        keys, queries = r.keys[rows, :], r.queries[rows, :]
        for j in range(HI // 256):
            cols = slice(256 * j, 256 * j + 256)
            read = dg(keys, grad_low[cols, :], 1, 1) + dg(keys, grad_rest[cols, :], 1, 1)
            r.x_carry[rows, cols] = r.tail_wide[rows, cols] * read
        high, lowv = halves(grad * r.state_in[c])
        pair = dg(expand[0:H], high, 1, 0) + dg(expand[0:H], lowv, 1, 0)
        carry_terms[c] = chunk_decay[c] * jnp.sum(pair, axis=1, keepdims=True)
        score_low = r.score_grad[c].astype(bf)
        r.key_grad[rows, :] = (
            dg(score_low, queries, 0, 0)
            + dg(r.xt[rows, :], grad_low, 1, 0)
            + dg(r.xt_rest[rows, :], grad_low, 1, 0)
            + dg(r.xt[rows, :], grad_rest, 1, 0)
        )

    pack_shared(r.key_grad, 0)
    stage("poll_at_chip_one")
    fold_in(0, 3)
    fold_middle(0, 1)
    stage("after_keys")
    stage("poll_at_x_grads")
    fold_in(0, 4)
    fold_middle(0, 2)
    stage("x_grads")
    r.head_sum_two[...] = (
        iota((HI, LANES), 0) // P_ + H == iota((HI, LANES), 1)
    ).astype(f32).astype(bf)
    r.head_sum_three[...] = (
        iota((HI, LANES), 0) // P_ + 2 * H == iota((HI, LANES), 1)
    ).astype(f32).astype(bf)

    def x_rows(i, _):
        rows = pl.ds(pl.multiple_of(i * ROWS, ROWS), ROWS)
        x = r.act[rows, :].astype(f32)
        z = r.x_inside[rows, :]
        carried = r.x_carry[rows, :]
        both = z + carried
        step_rows = r.step_wide[rows, :]
        xs = x * step_rows
        x_grad = step_rows * both + skip_row * r.heads_grad[rows, :]
        conv_grad = x_grad * slope(r.inner_conv[rows, :])
        for g in range(NP):
            r.grad_ext[g, rows, :] = conv_grad[:, g * LANES : g * LANES + LANES]
        r.sum_x[rows, :] = (
            summed(x * both, r.head_sum[...])
            + summed(xs * carried, r.head_sum_two[...])
            + summed(xs * z, r.head_sum_three[...])
        )
        return 0

    lax.fori_loop(0, T // ROWS, x_rows, 0)
    halo_one = remote(
        r.grad_ext.at[:, pl.ds(0, PAD)],
        r.grad_ext.at[:, pl.ds(T, PAD)],
        r.halo_send.at[0],
        r.halo_recv.at[0],
        left,
    )
    halo_one.start()
    waits.append(halo_one)

    sums_y = r.sum_y[...].T
    sums_x = r.sum_x[...].T
    step_grad = sums_x[0:H]
    tail_part = sums_x[H : 2 * H]
    pair_part = sums_y[0:H] - sums_x[2 * H : 3 * H]
    decay_grads = []
    for c in range(NC):
        cols = slice(c * Q, c * Q + Q)
        suffix = fold3(dg(split3(pair_part[:, cols]), r.upto[...], 1, 1))
        before = fold3(dg(split3(tail_part[:, cols]), r.upto[...], 1, 0)) - tail_part[:, cols]
        decay_grads.append(suffix + before + carry_terms[c])
    decay_grad = jnp.concatenate(decay_grads, axis=1)
    step_total = step_grad - rate * decay_grad
    step_pre_grad = step_total * r.sigmoid_step[...]
    rate_sum = jnp.sum(r.log_decay[...] * decay_grad, axis=1, keepdims=True)
    bias_sum = jnp.sum(step_pre_grad, axis=1, keepdims=True)
    step_cols = jnp.concatenate(
        [jnp.zeros((NS, T), f32), step_pre_grad, jnp.zeros((LANES - NS - H, T), f32)], axis=0
    ).T

    stage("poll_at_conv_back")
    fold_in(0, 5)
    fold_middle(0, 3)
    stage("conv_back")
    def after_masks(base):
        position = first_token + base + iota((ROWS, LANES), 0)
        now = segment(position)
        masks = []
        for k in range(CONV - 1):
            later = position + (CONV - 1) - k
            masks.append((segment(later) == now) & (later < total_tokens))
        return masks

    def conv_back(ext, taps, base, lanes, masks):
        value = None
        for k in range(CONV):
            term = taps[k : k + 1, lanes] * ext[pl.ds(base + CONV - 1 - k, ROWS), :]
            if k < CONV - 1:
                term = jnp.where(masks[k], term, 0.0)
            value = term if value is None else value + term
        return value

    def tap_sums(ext, grad, base, masks):
        sums = []
        for k in range(CONV):
            term = grad * ext[pl.ds(base + PAD - CONV + 1 + k, ROWS), :]
            sums.append(fold8(term if k == CONV - 1 else jnp.where(masks[k], term, 0.0)))
        return sums + [fold8(grad)]

    stage("inner_back")

    def inner_back_rows(i, _):
        base = pl.multiple_of(i * ROWS, ROWS)
        rows = pl.ds(base, ROWS)
        masks = after_masks(base)
        before = agreements(base, ROWS)
        taps = r.inner_kernel[...]
        for g in range(NP):
            lanes = slice(g * LANES, g * LANES + LANES)
            r.inner_grad[rows, lanes] = conv_back(r.grad_ext.at[g], taps, base, lanes, masks).astype(bf)
            found = tap_sums(r.inner_ext.at[g], r.grad_ext[g, rows, :], base, before)
            for k, v in enumerate(found):
                r.sum_acc[2 + k, :, lanes] = r.sum_acc[2 + k, :, lanes] + v
        return 0

    lax.fori_loop(0, T // ROWS - 1, inner_back_rows, 0)
    stage("poll_at_halo_one_wait")
    fold_in(0, 6)
    fold_middle(0, 4)
    stage("halo_one_wait")
    halo_one.wait_recv()
    stage("inner_back_last")
    inner_back_rows(T // ROWS - 1, 0)

    stage("poll_at_shared_wait")
    fold_middle(0, 5)
    stage("shared_wait")
    for d in range(1, n_tp):
        shared_copy(d, True).wait_recv()
    stage("shared_use")
    packed = r.shared_recv[0].astype(f32)
    for t in range(1, n_tp):
        packed = packed + r.shared_recv[t].astype(f32)
    r.state_grad_ext[0 : T // 2, :] = packed * slope(r.misc_conv[0 : T // 2, :])
    r.state_grad_ext[T // 2 : T, :] = pltpu.roll(packed, NS, 1) * slope(r.misc_conv[T // 2 : T, :])
    halo_two = remote(
        r.state_grad_ext.at[pl.ds(0, PAD)],
        r.state_grad_ext.at[pl.ds(T, PAD)],
        r.halo_send.at[1],
        r.halo_recv.at[1],
        left,
    )
    halo_two.start()
    waits.append(halo_two)
    stage("chip_one")
    chip_start(0)
    stage("poll_at_misc_back")
    fold_in(0, 7)
    stage("misc_back")
    r.misc_acc[...] = jnp.zeros_like(r.misc_acc)
    r.step_cols[...] = step_cols

    def misc_back_rows(i, _):
        base = pl.multiple_of(i * ROWS, ROWS)
        rows = pl.ds(base, ROWS)
        masks = after_masks(base)
        before = agreements(base, ROWS)
        taps = r.misc_taps[...]
        lanes = slice(0, LANES)
        value = conv_back(r.state_grad_ext, taps, base, lanes, masks)
        value = jnp.where(iota((ROWS, LANES), 1) < NS, value, r.step_cols[rows, :])
        r.misc_grad[rows, :] = value.astype(bf)
        found = tap_sums(r.misc_ext.at[0], r.state_grad_ext[rows, :], base, before)
        for k, v in enumerate(found):
            r.misc_acc[k] = r.misc_acc[k] + v
        return 0

    lax.fori_loop(0, T // ROWS - 1, misc_back_rows, 0)
    stage("halo_two_wait")
    halo_two.wait_recv()
    stage("misc_back_last")
    misc_back_rows(T // ROWS - 1, 0)

    stage("poll_at_normed_grad")
    fold_middle(0, 6)
    stage("normed_grad")
    width, tall = fold_width[1], fold_rows[1]
    for j in range(D // 256):
        cols = slice(256 * j, 256 * (j + 1))
        value = (
            dg(r.gate_grad[...], r.gate_weight[cols, :], 1, 1)
            + dg(r.inner_grad[...], r.inner_weight[cols, :], 1, 1)
            + dg(r.misc_grad[...], r.misc_weight[:, cols], 1, 0)
        )
        value_low = value.astype(bf)
        for k in range(256 // width):
            for m in range(T // tall):
                at = (j * (256 // width) + k) * (T // tall) + m
                r.normed_part[at] = value_low[m * tall : m * tall + tall, k * width : k * width + width]
                fold_start(1, at)
        hats = r.block_input[:, cols].astype(f32) * jnp.concatenate([r.inverse[...]] * 2, axis=1)
        r.gain_part[:, cols] = fold8(value * hats)

    stage("poll_at_small_sums")
    fold_middle(0, 7)
    stage("small_sums")

    def row_of(v):
        return jnp.sum(v, axis=0, keepdims=True)

    eye_wide = iota((H, LANES), 0) == iota((H, LANES), 1)

    def lanes_of(v):
        return row_of(jnp.where(eye_wide, jnp.broadcast_to(v, (H, LANES)), 0.0))

    r.small_send[...] = jnp.zeros_like(r.small_send)
    for k in range(CONV + 1):
        r.small_send[k : k + 1, :] = row_of(r.sum_acc[2 + k])
    r.small_send[5:6, :] = row_of(r.sum_acc[0])
    r.small_send[6:7, :] = row_of(r.sum_acc[1])
    for k in range(CONV):
        r.small_send[7:8, k * LANES : k * LANES + LANES] = row_of(r.misc_acc[k])
    r.small_send[8:9, 0:LANES] = row_of(r.misc_acc[CONV])
    r.small_send[8:9, LANES : 2 * LANES] = lanes_of(bias_sum)
    r.small_send[8:9, 2 * LANES : 3 * LANES] = lanes_of(rate_sum)
    gain_rows = row_of(r.gain_part[...])
    for k in range(D // HI):
        r.small_send[9 + k : 10 + k, :] = gain_rows[:, k * HI : k * HI + HI]
    r.small_recv[seq] = r.small_send[...]
    small_wait = spread(
        "seq", lambda d: r.small_send, lambda d: r.small_recv.at[d], r.small_ss, r.small_rs
    )
    stage("weights_two")

    def weight_rows_two(i, _):
        cols = pl.ds(pl.multiple_of(i * LANES, LANES), LANES)
        r.wg_two[cols, 0:HI] = dg(r.normed[:, cols], r.inner_grad[...], 0, 0).astype(bf)
        r.wg_two[cols, HI : HI + LANES] = dg(r.normed[:, cols], r.misc_grad[...], 0, 0).astype(bf)
        return 0

    lax.fori_loop(0, D // LANES // 2, weight_rows_two, 0)
    fold_in(1, 0)
    lax.fori_loop(D // LANES // 2, D // LANES, weight_rows_two, 0)
    pair_start(1)
    stage("folds")
    last = fold_pieces[1]
    for j in range(last + 2):
        if 0 < j < last:
            fold_in(1, j)
        if j > 1:
            fold_middle(1, j - 2)
        if j == 2:
            chip_start(1)
        if j == 10:
            small_wait()
            total = r.small_recv[0]
            for d in range(1, n_seq):
                total = total + r.small_recv[d]
            r.small_total[...] = total
            r.gain_recv[tp] = r.small_total[8:16, :]
            gain_wait = spread(
                "tp",
                lambda t: r.small_total.at[pl.ds(8, 8)],
                lambda t: r.gain_recv.at[t],
                r.gain_ss,
                r.gain_rs,
            )
    for j in range(fold_pieces[0]):
        fold_end(0, j)
    stage("weight_sums")
    r.sum_one[...] = chip_sum(0)
    r.sum_two[...] = chip_sum(1)
    gain_wait()
    gains = r.gain_recv[0]
    for t in range(1, n_tp):
        gains = gains + r.gain_recv[t]
    r.gain_total[...] = gains
    stage("folds_last")
    for j in range(fold_pieces[1]):
        fold_end(1, j)
    stage("drain")
    for d in range(1, n_tp):
        shared_copy(d).wait_send()
    for copy in waits:
        copy.wait_send()
    marks.close()


def finish(sizes, names, *refs):
    r = types.SimpleNamespace(**dict(zip(names, refs)))
    T, D, HI, H, NS = sizes
    P_ = HI // H
    T = r.block_input.shape[0]

    def final_rows(i, _):
        rows = pl.ds(pl.multiple_of(i * ROWS, ROWS), ROWS)
        x = r.block_input[rows, :].astype(f32)
        r.block_output[rows, :] = (x + r.branch_sum[rows, :].astype(f32)).astype(bf)
        inverse = lax.rsqrt(jnp.mean(x * x, axis=1, keepdims=True) + epsilon)
        hat = x * inverse
        hat_grad = r.normed_sum[rows, :].astype(f32) * r.input_gain[...].reshape(1, D)
        mean = jnp.mean(hat_grad * hat, axis=1, keepdims=True)
        r.input_grad[rows, :] = r.out_cotangent[rows, :].astype(f32) + inverse * (
            hat_grad - hat * mean
        )
        return 0

    lax.fori_loop(0, T // ROWS, final_rows, 0)
    @pl.when(pl.program_id(0) == 0)
    def _():
        r.gate_weight_grad[...] = r.sum_one[:, 0:HI]
        r.out_weight_grad[...] = r.sum_one[:, HI : 2 * HI].T
        r.inner_weight_grad[...] = r.sum_two[:, 0:HI]
        narrow = r.sum_two[:, HI : HI + LANES].T
        r.state_weight_grad[...] = narrow[0:NS]
        r.step_weight_grad[...] = narrow[NS : NS + H]
        small = r.small_total
        r.inner_kernel_grad[...] = small[0:CONV, :]
        r.inner_conv_bias_grad[...] = small[CONV : CONV + 1, :].reshape(HI)
        r.gate_gain_grad[...] = small[5:6, :].reshape(HI)
        head_sum = (iota((HI, LANES), 0) // P_ == iota((HI, LANES), 1)).astype(f32).astype(bf)
        skip_sums = fold3(dg(split3(jnp.broadcast_to(small[6:7, :], (8, HI))), head_sum, 1, 0))
        r.skip_scale_grad[...] = skip_sums[0:1, 0:H].reshape(H)
        for k in range(CONV):
            r.state_kernel_grad[k : k + 1, :] = small[7:8, k * LANES : k * LANES + NS]
        r.state_conv_bias_grad[...] = small[8:9, 0:NS].reshape(NS)
        r.step_bias_grad[...] = small[8:9, LANES : LANES + H].reshape(H)
        r.rate_log_grad[...] = small[8:9, 2 * LANES : 2 * LANES + H].reshape(H)
        for k in range(D // HI):
            r.input_gain_grad[k * HI : k * HI + HI] = r.gain_total[1 + k : 2 + k, :].reshape(HI)


INPUTS = (
    "block_input",
    "scene_lengths",
    "input_gain",
    "gate_weight",
    "inner_weight",
    "state_weight",
    "step_weight",
    "step_bias",
    "rate_log",
    "inner_kernel",
    "inner_conv_bias",
    "state_kernel",
    "state_conv_bias",
    "skip_scale",
    "gate_gain",
    "out_weight",
    "out_cotangent",
)
OUTPUTS = (
    "block_output",
    "input_grad",
    "input_gain_grad",
    "gate_weight_grad",
    "inner_weight_grad",
    "state_weight_grad",
    "step_weight_grad",
    "step_bias_grad",
    "rate_log_grad",
    "inner_kernel_grad",
    "inner_conv_bias_grad",
    "state_kernel_grad",
    "state_conv_bias_grad",
    "skip_scale_grad",
    "gate_gain_grad",
    "out_weight_grad",
)


SUMS = ("branch_sum", "normed_sum", "sum_one", "sum_two", "small_total", "gain_total")


def local(*args):
    given = dict(zip(INPUTS, args))
    given["state_weight"] = given["state_weight"].T
    given["step_weight"] = given["step_weight"].T
    n_seq = lax.axis_size("seq")
    n_tp = lax.axis_size("tp")
    T, D = given["block_input"].shape
    HI = given["gate_weight"].shape[1]
    H = given["step_bias"].shape[0]
    NS = given["state_weight"].shape[0]
    N = STATE
    Q = CHUNK
    NC = T // Q
    NP = HI // LANES
    R = HI // n_seq
    R2 = D // n_seq
    outs = (
        ((T, D), bf),
        ((T, D), f32),
        ((D,), f32),
        ((R2, HI), f32),
        ((R2, HI), f32),
        ((NS, R2), f32),
        ((H, R2), f32),
        ((H,), f32),
        ((H,), f32),
        ((CONV, HI), f32),
        ((HI,), f32),
        ((CONV, NS), f32),
        ((NS,), f32),
        ((H,), f32),
        ((HI,), f32),
        ((HI, R2), f32),
    )
    sums = (
        ((T, D), bf),
        ((T, D), bf),
        ((R2, 2 * HI), f32),
        ((R2, HI + LANES), f32),
        ((16, HI), f32),
        ((8, HI), f32),
    )
    scratch = dict(
        inverse=((T, LANES), f32),
        normed=((T, D), bf),
        misc_weight=((LANES, D), bf),
        inner_ext=((NP, T + PAD, LANES), f32),
        misc_ext=((1, T + PAD, LANES), f32),
        gate_pre=((T, HI), f32),
        misc_taps=((8, LANES), f32),
        inner_bias=((1, HI), f32),
        gain_row=((1, HI), f32),
        misc_conv=((T, LANES), f32),
        inner_conv=((T, HI), f32),
        act=((T, HI), bf),
        state_send=((T // 2, LANES), bf),
        state_recv=((n_tp, T // 2, LANES), bf),
        keys=((T, N), bf),
        queries=((T, N), bf),
        sigmoid_step=((H, T), f32),
        step_rows=((H, T), f32),
        log_decay=((H, T), f32),
        upto=((Q, Q), bf),
        expand=((3 * H, HI), bf),
        mask=((NC, Q, Q), f32),
        cum_left=((H, 16, T), bf),
        cum_right=((H, 16, T), bf),
        step_wide=((T, HI), f32),
        enter_wide=((T, HI), f32),
        tail_wide=((T, HI), f32),
        decay_wide=((NC, HI, LANES), f32),
        skip_wide=((8, HI), f32),
        xt=((T, HI), bf),
        xt_rest=((T, HI), bf),
        fresh=((NC, HI, N), f32),
        end_send=((HI, N), f32),
        end_recv=((n_seq, R, N), f32),
        decay_send=((H, LANES), f32),
        decay_recv=((n_seq, H, LANES), f32),
        enter_send=((n_seq, R, N), f32),
        enter_state=((HI, N), f32),
        state_in=((NC, HI, N), f32),
        state_in_low=((NC, HI, N), bf),
        state_in_rest=((NC, HI, N), bf),
        scores=((NC, Q, Q), f32),
        score_grad=((NC, Q, Q), f32),
        decays=((NC, H, Q, Q), f32),
        turned=((NC, H, Q, Q), bf),
        mixed=((T, HI), f32),
        norm_grad=((T, HI), f32),
        gated=((T, HI), f32),
        squares=((T, LANES), f32),
        products=((T, LANES), f32),
        sums_send=((8, T), f32),
        sums_recv=((n_tp, 8, T), f32),
        norm_col=((T, LANES), f32),
        back_col=((T, LANES), f32),
        head_sum=((HI, LANES), bf),
        head_sum_two=((HI, LANES), bf),
        head_sum_three=((HI, LANES), bf),
        sum_acc=((7, 8, HI), f32),
        gated_norm=((T, HI), bf),
        gate_grad=((T, HI), bf),
        heads_grad=((T, HI), f32),
        dy=((T, HI), bf),
        dy_rest=((T, HI), bf),
        dy_enter=((T, HI), bf),
        dy_enter_rest=((T, HI), bf),
        sum_y=((T, LANES), f32),
        sum_x=((T, LANES), f32),
        grad_local=((NC, HI, N), f32),
        grad_send=((HI, N), f32),
        grad_recv=((n_seq, R, N), f32),
        leave_send=((n_seq, R, N), f32),
        leave_grad=((HI, N), f32),
        x_inside=((T, HI), f32),
        x_carry=((T, HI), f32),
        wg_one=((D, 2 * HI), bf),
        pair_one=((n_seq // 2, R2, 2 * HI), bf),
        chip_one_send=((n_seq // 2, R2, 2 * HI), bf),
        chip_one=((n_seq // 2, R2, 2 * HI), bf),
        wg_two=((D, HI + LANES), bf),
        pair_two=((n_seq // 2, R2, HI + LANES), bf),
        chip_two_send=((n_seq // 2, R2, HI + LANES), bf),
        chip_two=((n_seq // 2, R2, HI + LANES), bf),
        query_grad=((T, N), f32),
        key_grad=((T, N), f32),
        shared_send=((n_tp, T // 2, LANES), bf),
        shared_recv=((n_tp, T // 2, LANES), bf),
        grad_ext=((NP, T + PAD, LANES), f32),
        state_grad_ext=((T + PAD, LANES), f32),
        inner_grad=((T, HI), bf),
        step_cols=((T, LANES), f32),
        misc_grad=((T, LANES), bf),
        misc_acc=((CONV + 1, 8, LANES), f32),
        normed_part=((16, T // 2, D // 8), bf),
        normed_in=((16, T // 2, D // 8), bf),
        normed_across=((16, T // 2, D // 8), bf),
        branch=((8, T, D // 8), bf),
        branch_in=((8, T, D // 8), bf),
        branch_across=((8, T, D // 8), bf),
        gain_part=((8, D), f32),
        small_send=((16, HI), f32),
        small_recv=((n_seq, 16, HI), f32),
        gain_recv=((n_tp, 8, HI), f32),
    )
    semaphores = dict(
        rim_send=(2,),
        rim_recv=(2,),
        halo_send=(2,),
        halo_recv=(2,),
        pair_ss=(2, n_seq // 2),
        pair_rs=(2, n_seq // 2),
        chip_ss=(2, n_seq // 2 - 1),
        chip_rs=(2, n_seq // 2 - 1),
        fold_ss=(3, 24),
        fold_rs=(3, 24),
    )
    for name in ("state", "sums", "shared", "gain"):
        semaphores[name + "_ss"] = (n_tp - 1,)
        semaphores[name + "_rs"] = (n_tp - 1,)
    for name in ("decay", "end", "enter", "grad", "leave", "small"):
        semaphores[name + "_ss"] = (n_seq - 1,)
        semaphores[name + "_rs"] = (n_seq - 1,)
    scratch.update({n: (given[n].shape, bf) for n in LOADED})
    semaphores["load_sems"] = (len(LOADED),)
    names = tuple(n + "_hbm" if n in LOADED else n for n in INPUTS) + SUMS + tuple(scratch) + tuple(semaphores)
    vmem = pl.BlockSpec(memory_space=pltpu.VMEM)
    smem = pl.BlockSpec(memory_space=pltpu.SMEM)
    totals = pl.pallas_call(
        functools.partial(kernel, (n_seq, n_tp, T, D, HI, H, NS), names),
        out_shape=tuple(jax.ShapeDtypeStruct(s, t) for s, t in sums),
        in_specs=[
            smem if n == "scene_lengths" else pl.BlockSpec(memory_space=pl.ANY) if n in LOADED else vmem
            for n in INPUTS
        ],
        out_specs=tuple(vmem for _ in sums),
        scratch_shapes=[pltpu.VMEM(s, t) for s, t in scratch.values()]
        + [pltpu.SemaphoreType.DMA(s) for s in semaphores.values()],
        compiler_params=pltpu.CompilerParams(
            collective_id=0, has_side_effects=True, vmem_limit_bytes=61 * 2**20
        ),
    )(*given.values())
    tall = ("block_input", "out_cotangent", "branch_sum", "normed_sum", "block_output", "input_grad")
    steps = 2
    by_rows = pl.BlockSpec((T // steps, D), lambda i: (i, 0))

    def whole(shape):
        return pl.BlockSpec(shape, lambda i: (0,) * len(shape))

    needed = ("block_input", "input_gain", "out_cotangent")
    results = pl.pallas_call(
        functools.partial(finish, (T, D, HI, H, NS), needed + SUMS + OUTPUTS),
        out_shape=tuple(jax.ShapeDtypeStruct(s, t) for s, t in outs),
        grid=(steps,),
        in_specs=[by_rows if n in tall else whole(given[n].shape) for n in needed]
        + [by_rows if n in tall else whole(s) for n, (s, _) in zip(SUMS, sums)],
        out_specs=tuple(by_rows if n in tall else whole(s) for n, (s, _) in zip(OUTPUTS, outs)),
        compiler_params=pltpu.CompilerParams(vmem_limit_bytes=60 * 2**20),
    )(*(given[n] for n in needed), *totals)
    results = dict(zip(OUTPUTS, results))
    results["state_weight_grad"] = results["state_weight_grad"].T
    results["step_weight_grad"] = results["step_weight_grad"].T
    return tuple(results.values())


def solution(mesh):
    rows = P("seq", None)
    cols = P(None, "tp")
    heads = P("tp")
    return jax.shard_map(
        local,
        mesh=mesh,
        in_specs=(
            rows,
            P(),
            P(),
            cols,
            cols,
            cols,
            cols,
            heads,
            heads,
            cols,
            heads,
            cols,
            heads,
            heads,
            heads,
            P("tp", None),
            rows,
        ),
        out_specs=(
            rows,
            rows,
            P(),
            P("seq", "tp"),
            P("seq", "tp"),
            P("seq", "tp"),
            P("seq", "tp"),
            heads,
            heads,
            cols,
            heads,
            cols,
            heads,
            heads,
            heads,
            P("tp", "seq"),
        ),
        check_vma=False,
    )
```

```python
import contextlib
import functools
import types

import jax
import jax.numpy as jnp
from jax import lax
from jax.experimental import pallas as pl
from jax.experimental.pallas import tpu as pltpu
from jax.sharding import PartitionSpec as P

STATE = 128
CONV = 4
CHUNK = 256
LANES = 128
PAD = 8
ROWS = 64
epsilon = 1e-05
bf = jnp.bfloat16
f32 = jnp.float32
i32 = jnp.int32
MESH = pl.DeviceIdType.MESH


def dg(left, right, left_dim, right_dim):
    return lax.dot_general(
        left, right, (((left_dim,), (right_dim,)), ((), ())), preferred_element_type=f32
    )


def split3(v):
    high = v.astype(bf).astype(f32)
    middle = (v - high).astype(bf).astype(f32)
    return jnp.concatenate([high, middle, v - high - middle], axis=0).astype(bf)


def fold3(v):
    third = v.shape[0] // 3
    return v[:third] + v[third : 2 * third] + v[2 * third :]


def halves(v):
    high = v.astype(bf)
    return high, (v - high.astype(f32)).astype(bf)


def slope(v):
    s = jax.nn.sigmoid(v)
    return s * (1.0 + v * (1.0 - s))


def fold8(v):
    total = v[0:8]
    for i in range(1, v.shape[0] // 8):
        total = total + v[8 * i : 8 * i + 8]
    return total


def iota(shape, dim):
    return lax.broadcasted_iota(i32, shape, dim)


LOADED = ("inner_weight", "gate_weight", "out_weight", "out_cotangent")


def kernel(sizes, names, *refs):
    r = types.SimpleNamespace(**dict(zip(names, refs)))
    n_seq, n_tp, T, D, HI, H, NS = sizes
    N = STATE
    P_ = HI // H
    Q = CHUNK
    NC = T // Q
    NP = HI // LANES
    R = HI // n_seq
    R2 = D // n_seq
    total_tokens = T * n_seq
    seq = lax.axis_index("seq")
    tp = lax.axis_index("tp")

    barrier = pltpu.get_barrier_semaphore()
    for d in range(1, n_seq):
        pl.semaphore_signal(
            barrier, inc=1, device_id=((seq + d) % n_seq, tp), device_id_type=MESH
        )
    for d in range(1, n_tp):
        pl.semaphore_signal(
            barrier, inc=1, device_id=(seq, (tp + d) % n_tp), device_id_type=MESH
        )

    waits = []
    loads = {}
    for k, n in enumerate(LOADED):
        loads[n] = pltpu.make_async_copy(getattr(r, n + "_hbm"), getattr(r, n), r.load_sems.at[k])
        loads[n].start()
    half = n_tp // 2
    inner = jnp.where(tp < half, tp + 1, tp - 1)
    outer = jnp.where(tp < half, tp - 1, tp + 1)
    is_middle = (tp == half - 1) | (tp == half)
    has_outer = (tp > 0) & (tp < n_tp - 1)
    fold_pieces = (r.branch_in.shape[0], r.normed_in.shape[0])
    fold_width = D // fold_pieces[0], LANES
    fold_rows = T, T * D // LANES // fold_pieces[1]
    fold_refs = (
        (r.branch, r.branch_in, r.branch_across, r.branch_sum),
        (r.normed_part, r.normed_in, r.normed_across, r.normed_sum),
    )

    def fold(a, j):
        high = T // fold_rows[a]
        place = (
            pl.ds(j % high * fold_rows[a], fold_rows[a]),
            pl.ds(j // high * fold_width[a], fold_width[a]),
        )
        partial, arrived, across, total = (
            ref.at[j] if k < 3 else ref.at[place]
            for k, ref in enumerate(fold_refs[a])
        )
        return partial, arrived, across, total

    def fold_copy(a, j, leg):
        partial, arrived, across, total = fold(a, j)
        sems = leg, sum(fold_pieces[:a]) + j
        source, target, place = ((partial, arrived, inner), (partial, across, inner), (total, total, outer))[leg]
        return remote(source, target, r.fold_ss.at[sems], r.fold_rs.at[sems], (seq, place))

    def fold_start(a, j):
        pl.when(jnp.logical_not(has_outer | is_middle))(fold_copy(a, j, 0).start)

    def fold_in(a, j):
        partial, arrived, _, _ = fold(a, j)

        @pl.when(has_outer)
        def _():
            fold_copy(a, j, 0).wait_recv()
            partial[...] = (partial[...].astype(f32) + arrived[...].astype(f32)).astype(bf)

        pl.when(is_middle)(fold_copy(a, j, 1).start)
        pl.when(has_outer & jnp.logical_not(is_middle))(fold_copy(a, j, 0).start)

    def fold_middle(a, j):
        partial, _, across, total = fold(a, j)

        @pl.when(is_middle)
        def _():
            fold_copy(a, j, 1).wait_recv()
            total[...] = (partial[...].astype(f32) + across[...].astype(f32)).astype(bf)
            pl.when(has_outer)(fold_copy(a, j, 2).start)

    def fold_end(a, j):
        @pl.when(jnp.logical_not(is_middle))
        def _():
            fold_copy(a, j, 2).wait_recv()
            pl.when(has_outer)(fold_copy(a, j, 2).start)
            fold_copy(a, j, 0).wait_send()

        pl.when(has_outer)(fold_copy(a, j, 2).wait_send)
        pl.when(is_middle)(fold_copy(a, j, 1).wait_send)

    marks = contextlib.ExitStack()

    def stage(name):
        marks.close()
        marks.enter_context(jax.named_scope(name))

    stage("norm")

    def remote(src, dst, send, recv, device):
        return pltpu.make_async_remote_copy(
            src_ref=src,
            dst_ref=dst,
            send_sem=send,
            recv_sem=recv,
            device_id=device,
            device_id_type=MESH,
        )

    def spread(axis, src_to, dst_from, send, recv):
        n = n_seq if axis == "seq" else n_tp
        me = seq if axis == "seq" else tp
        incoming = []
        for d in range(1, n):
            target = (me + d) % n
            source = (me + n - d) % n
            device = (target, tp) if axis == "seq" else (seq, target)
            out = remote(src_to(target), dst_from(me), send.at[d - 1], recv.at[d - 1], device)
            out.start()
            waits.append(out)
            incoming.append(
                remote(src_to(target), dst_from(source), send.at[d - 1], recv.at[d - 1], device)
            )

        def wait():
            for copy in incoming:
                copy.wait_recv()

        return wait

    starts = [jnp.int32(0)]
    for k in range(r.scene_lengths.shape[0] - 1):
        starts.append(starts[-1] + r.scene_lengths[k])

    def segment(position):
        found = (position >= starts[0]).astype(i32)
        for s in starts[1:]:
            found = found + (position >= s).astype(i32)
        return found

    first_token = seq * T

    def norm_rows(i, _):
        rows = pl.ds(pl.multiple_of(i * ROWS, ROWS), ROWS)
        x = r.block_input[rows, :].astype(f32)
        inverse = lax.rsqrt(jnp.mean(x * x, axis=1, keepdims=True) + epsilon)
        r.inverse[rows, :] = jnp.broadcast_to(inverse, (ROWS, LANES))
        r.normed[rows, :] = (x * inverse * r.input_gain[...].reshape(1, D)).astype(bf)
        return 0

    lax.fori_loop(0, T // ROWS, norm_rows, 0)

    stage("projections")
    r.misc_weight[...] = jnp.zeros_like(r.misc_weight)
    r.misc_weight[0:NS, :] = r.state_weight[...]
    r.misc_weight[NS : NS + H, :] = r.step_weight[...]
    normed_all = r.normed[...]
    r.misc_ext[0, PAD : PAD + T, :] = dg(normed_all, r.misc_weight[...], 1, 1)
    stage("barrier")
    pl.semaphore_wait(barrier, n_seq - 1 + n_tp - 1)
    stage("inner_projection")
    right = ((seq + 1) % n_seq, tp)
    left = ((seq + n_seq - 1) % n_seq, tp)
    misc_rim, inner_rim = [
        remote(
            ref.at[:, pl.ds(T, PAD)],
            ref.at[:, pl.ds(0, PAD)],
            r.rim_send.at[k],
            r.rim_recv.at[k],
            right,
        )
        for k, ref in enumerate((r.misc_ext, r.inner_ext))
    ]
    waits.extend((misc_rim, inner_rim))
    misc_rim.start()
    for j in range(HI // 256):
        cols = slice(256 * j, 256 * j + 256)
        if j == 0:
            loads["inner_weight"].wait()
        value = dg(normed_all, r.inner_weight[:, cols], 1, 0)
        r.inner_ext[2 * j, PAD : PAD + T, :] = value[:, :LANES]
        r.inner_ext[2 * j + 1, PAD : PAD + T, :] = value[:, LANES:]
    inner_rim.start()
    stage("gate_projection")
    for j in range(HI // 256):
        cols = slice(256 * j, 256 * j + 256)
        if j == 0:
            loads["gate_weight"].wait()
        r.gate_pre[:, cols] = dg(normed_all, r.gate_weight[:, cols], 1, 0)

    stage("convolutions")
    def agreements(base, rows):
        position = first_token + base + iota((rows, LANES), 0)
        now = segment(position)
        return [segment(position - (CONV - 1) + k) == now for k in range(CONV - 1)]

    def conv_block(ext, taps, bias, base, lanes, masks):
        value = bias[:, lanes]
        for k in range(CONV):
            window = ext[pl.ds(base + PAD - CONV + 1 + k, ROWS), :]
            term = taps[k : k + 1, lanes] * window
            value = value + (term if k == CONV - 1 else jnp.where(masks[k], term, 0.0))
        return value

    r.misc_taps[...] = jnp.zeros_like(r.misc_taps)
    r.misc_taps[0:CONV, 0:NS] = r.state_kernel[...]
    r.misc_taps[CONV : CONV + 1, 0:NS] = r.state_conv_bias[...].reshape(1, NS)
    r.inner_bias[...] = r.inner_conv_bias[...].reshape(1, HI)
    stage("rim_wait")
    misc_rim.wait_recv()
    stage("conv")

    def misc_conv_rows(i, _):
        base = pl.multiple_of(i * ROWS, ROWS)
        masks = agreements(base, ROWS)
        taps = r.misc_taps[...]
        value = conv_block(
            r.misc_ext.at[0], taps, taps[CONV : CONV + 1], base, slice(0, LANES), masks
        )
        r.misc_conv[pl.ds(base, ROWS), :] = value
        return 0

    lax.fori_loop(0, T // ROWS, misc_conv_rows, 0)
    low_lanes = iota((T // 2, LANES), 1) < NS
    own = r.misc_conv[...]
    own = own * jax.nn.sigmoid(own)
    r.state_send[...] = jnp.where(
        low_lanes, own[: T // 2], pltpu.roll(own[T // 2 :], NS, 1)
    ).astype(bf)
    r.state_recv[tp] = r.state_send[...]
    state_wait = spread(
        "tp",
        lambda t: r.state_send,
        lambda t: r.state_recv.at[t],
        r.state_ss,
        r.state_rs,
    )

    def inner_conv_rows(i, _):
        base = pl.multiple_of(i * ROWS, ROWS)
        rows = pl.ds(base, ROWS)
        masks = agreements(base, ROWS)
        taps = r.inner_kernel[...]
        for g in range(NP):
            lanes = slice(g * LANES, g * LANES + LANES)
            value = conv_block(r.inner_ext.at[g], taps, r.inner_bias, base, lanes, masks)
            r.inner_conv[rows, lanes] = value
            r.act[rows, lanes] = (value * jax.nn.sigmoid(value)).astype(bf)
        return 0

    inner_rim.wait_recv()
    lax.fori_loop(0, T // ROWS, inner_conv_rows, 0)

    stage("decays")
    eye = iota((H, H), 0) == iota((H, H), 1)

    def column(ref):
        wide = jnp.broadcast_to(ref[...].reshape(1, H), (H, H))
        return jnp.sum(jnp.where(eye, wide, 0.0), axis=1, keepdims=True)

    step_in = r.misc_ext[0, PAD : PAD + T, :].T[NS : NS + H, :] + column(r.step_bias)
    step = jnp.maximum(step_in, 0.0) + jnp.log1p(jnp.exp(-jnp.abs(step_in)))
    rate = jnp.exp(column(r.rate_log))
    log_decay = step * -rate
    r.sigmoid_step[...] = jax.nn.sigmoid(step_in)
    r.log_decay[...] = log_decay
    r.step_rows[...] = step
    r.upto[...] = (iota((Q, Q), 0) <= iota((Q, Q), 1)).astype(f32).astype(bf)
    r.expand[...] = (iota((3 * H, HI), 0) % H == iota((3 * H, HI), 1) // P_).astype(f32).astype(bf)
    expand = r.expand[...]

    entering, tailing, chunk_decay = [], [], []
    ones_rows = jnp.ones((1, Q), f32)
    for c in range(NC):
        cols = slice(c * Q, c * Q + Q)
        cumulative = fold3(dg(split3(log_decay[:, cols]), r.upto[...], 1, 0))
        start = first_token + c * Q
        seg_row = segment(start + iota((H, Q), 1))
        seg_before = segment(start - 1)
        seg_end = segment(start + Q - 1)
        last = cumulative[:, Q - 1 : Q]
        enter = jnp.where(seg_row == seg_before, jnp.exp(cumulative), 0.0)
        tail = jnp.where(seg_row == seg_end, jnp.exp(last - cumulative), 0.0)
        entering.append(enter)
        tailing.append(tail)
        chunk_decay.append(enter[:, Q - 1 : Q])
        seg_col = segment(start + iota((Q, Q), 0))
        seg_lane = segment(start + iota((Q, Q), 1))
        keep = (seg_col == seg_lane) & (iota((Q, Q), 0) >= iota((Q, Q), 1))
        r.mask[c] = jnp.where(keep, 0.0, -1e30)
        high = cumulative.astype(bf).astype(f32)
        middle = (cumulative - high).astype(bf).astype(f32)
        rest = cumulative - high - middle
        which = iota((16, Q), 0)
        for h in range(H):
            parts = jnp.where(
                which % 3 == 0,
                high[h : h + 1],
                jnp.where(which % 3 == 1, middle[h : h + 1], rest[h : h + 1]),
            )
            first = which < 3
            second = (which >= 3) & (which < 6)
            r.cum_left[h, :, cols] = jnp.where(
                first, parts, jnp.where(second, 1.0, 0.0)
            ).astype(bf)
            r.cum_right[h, :, cols] = jnp.where(
                first, 1.0, jnp.where(second, -parts, 0.0)
            ).astype(bf)

    def wide(v):
        return dg(split3(v), expand, 0, 0)

    def wide_rows(v):
        return dg(expand, split3(jnp.broadcast_to(v, (H, LANES))), 0, 0)

    for c in range(NC):
        rows = slice(c * Q, c * Q + Q)
        r.step_wide[rows, :] = wide(step[:, rows])
        r.enter_wide[rows, :] = wide(entering[c])
        r.tail_wide[rows, :] = wide(tailing[c])
        r.decay_wide[c] = wide_rows(chunk_decay[c])
    r.skip_wide[...] = dg(split3(jnp.broadcast_to(column(r.skip_scale), (H, 8))), expand, 0, 0)

    def scaled_rows(i, _):
        rows = pl.ds(pl.multiple_of(i * ROWS, ROWS), ROWS)
        x = r.act[rows, :].astype(f32)
        r.xt[rows, :], r.xt_rest[rows, :] = halves(x * r.step_wide[rows, :] * r.tail_wide[rows, :])
        return 0

    lax.fori_loop(0, T // ROWS, scaled_rows, 0)

    stage("decay_matrices")

    def decay_matrix(i, _):
        c = i // H
        h = i % H
        rows = pl.ds(pl.multiple_of(c * Q, Q), Q)
        difference = dg(r.cum_left[h, :, rows], r.cum_right[h, :, rows], 0, 0)
        r.decays[c, h] = jnp.exp(difference + r.mask[c])
        return 0

    lax.fori_loop(0, NC * H, decay_matrix, 0)

    stage("keys_wait")
    state_wait()
    shards = n_tp // 2
    half_low = iota((T // 2, LANES), 1) < NS
    for ref, at in ((r.keys, 0), (r.queries, shards)):
        one, two = r.state_recv[at].astype(f32), r.state_recv[at + 1].astype(f32)
        ref[0 : T // 2, :] = jnp.where(half_low, one, pltpu.roll(two, NS, 1)).astype(bf)
        ref[T // 2 : T, :] = jnp.where(half_low, pltpu.roll(one, NS, 1), two).astype(bf)

    stage("end_states")
    end_state = None
    device_decay = None
    for c in range(NC):
        rows = slice(c * Q, c * Q + Q)
        keys = r.keys[rows, :]
        fresh = dg(r.xt[rows, :], keys, 0, 0) + dg(r.xt_rest[rows, :], keys, 0, 0)
        r.fresh[c] = fresh
        end_state = fresh if c == 0 else r.decay_wide[c] * end_state + fresh
        device_decay = chunk_decay[c] if c == 0 else device_decay * chunk_decay[c]
    r.end_send[...] = end_state
    r.decay_send[...] = jnp.broadcast_to(device_decay, (H, LANES))

    def block(ref, device):
        return ref.at[pl.ds(pl.multiple_of(device * R, R), R)]

    r.end_recv[seq] = r.end_send[pl.ds(pl.multiple_of(seq * R, R), R), :]
    r.decay_recv[seq] = r.decay_send[...]
    decay_wait = spread(
        "seq", lambda d: r.decay_send, lambda d: r.decay_recv.at[d], r.decay_ss, r.decay_rs
    )
    end_wait = spread(
        "seq", lambda d: block(r.end_send, d), lambda d: r.end_recv.at[d], r.end_ss, r.end_rs
    )

    stage("inside")
    for c in range(NC):
        rows = slice(c * Q, c * Q + Q)
        r.scores[c] = dg(r.queries[rows, :], r.keys[rows, :], 1, 1)
    low = iota((Q, LANES), 1) < P_

    def inside(i, _):
        c = i // NP
        p = i % NP
        rows = pl.ds(pl.multiple_of(c * Q, Q), Q)
        lanes = pl.ds(pl.multiple_of(p * LANES, LANES), LANES)
        x = r.act[rows, lanes]
        zero = jnp.zeros_like(x)
        result = None
        for s in range(2):
            h = 2 * p + s
            stepped = r.decays[c, h] * r.step_rows[pl.ds(h, 1), rows]
            weight, rest = halves(stepped * r.scores[c])
            part = jnp.where(low, x, zero) if s == 0 else jnp.where(low, zero, x)
            term = dg(weight, part, 1, 0) + dg(rest, part, 1, 0)
            result = term if s == 0 else result + term
        r.mixed[rows, lanes] = result
        return 0

    lax.fori_loop(0, NC * NP, inside, 0)
    for j in range(HI // 256):
        cols = slice(256 * j, 256 * j + 256)
        if j == 0:
            loads["out_weight"].wait()
            loads["out_cotangent"].wait()
        r.norm_grad[:, cols] = dg(r.out_cotangent[...], r.out_weight[cols, :], 1, 1)

    stage("entering")
    head_of = (seq * R) // P_
    stage("end_wait")
    end_wait()
    decay_wait()

    def decay_of(d):
        return jnp.broadcast_to(r.decay_recv[d, pl.ds(head_of, 1), :], (R, LANES))

    running = jnp.zeros((R, N), f32)
    for d in range(n_seq):
        r.enter_send[d] = running
        running = decay_of(d) * running + r.end_recv[d]
    own_rows = pl.ds(pl.multiple_of(seq * R, R), R)
    r.enter_state[own_rows, :] = r.enter_send[seq]
    enter_wait = spread(
        "seq", lambda d: r.enter_send.at[d], lambda d: block(r.enter_state, d), r.enter_ss, r.enter_rs
    )
    stage("turned_weights")

    def turned_weight(i, _):
        c = i // H
        h = i % H
        r.turned[c, h] = (r.decays[c, h] * r.scores[c]).T.astype(bf)
        return 0

    lax.fori_loop(0, NC * H, turned_weight, 0)
    stage("enter_wait")
    enter_wait()
    stage("readout")
    for c in range(NC):
        rows = slice(c * Q, c * Q + Q)
        if c == 0:
            state = r.enter_state[...]
        else:
            state = r.decay_wide[c - 1] * state + r.fresh[c - 1]
        r.state_in[c] = state
        r.state_in_low[c], r.state_in_rest[c] = halves(state)
        for j in range(HI // 256):
            cols = slice(256 * j, 256 * j + 256)
            queries = r.queries[rows, :]
            read = dg(queries, r.state_in_low[c, cols, :], 1, 1) + dg(queries, r.state_in_rest[c, cols, :], 1, 1)
            r.mixed[rows, cols] = r.mixed[rows, cols] + r.enter_wide[rows, cols] * read

    stage("gated")
    skip_row = r.skip_wide[0:1, :]
    r.gain_row[...] = r.gate_gain[...].reshape(1, HI)

    def gated_rows(i, _):
        rows = pl.ds(pl.multiple_of(i * ROWS, ROWS), ROWS)
        heads = r.mixed[rows, :] + skip_row * r.act[rows, :].astype(f32)
        gate = r.gate_pre[rows, :]
        gated = heads * (gate * jax.nn.sigmoid(gate))
        r.gated[rows, :] = gated
        scaled = r.norm_grad[rows, :] * r.gain_row[...]
        squares = gated * gated
        products = scaled * gated

        def lane_sum(v):
            total = v[:, :LANES]
            for g in range(1, NP):
                total = total + v[:, g * LANES : g * LANES + LANES]
            return total

        r.squares[rows, :] = lane_sum(squares)
        r.products[rows, :] = lane_sum(products)
        return 0

    lax.fori_loop(0, T // ROWS, gated_rows, 0)
    square_row = jnp.sum(r.squares[...].T, axis=0, keepdims=True)
    product_row = jnp.sum(r.products[...].T, axis=0, keepdims=True)
    r.sums_send[...] = jnp.where(
        iota((8, T), 0) == 0,
        jnp.broadcast_to(square_row, (8, T)),
        jnp.broadcast_to(product_row, (8, T)),
    )
    r.sums_recv[tp] = r.sums_send[...]
    sums_wait = spread(
        "tp", lambda t: r.sums_send, lambda t: r.sums_recv.at[t], r.sums_ss, r.sums_rs
    )
    stage("sums_wait")
    sums_wait()
    stage("sums")
    sums = r.sums_recv[0]
    for t in range(1, n_tp):
        sums = sums + r.sums_recv[t]
    count = HI * n_tp
    norm_row = lax.rsqrt(sums[0:1] / count + epsilon)
    back_row = norm_row * norm_row * norm_row * (sums[1:2] / count)
    r.norm_col[...] = jnp.broadcast_to(norm_row, (LANES, T)).T
    r.back_col[...] = jnp.broadcast_to(back_row, (LANES, T)).T

    stage("back_gated")
    r.head_sum[...] = (iota((HI, LANES), 0) // P_ == iota((HI, LANES), 1)).astype(f32).astype(bf)
    r.sum_acc[...] = jnp.zeros_like(r.sum_acc)

    def tile4(v):
        return jnp.concatenate([v] * NP, axis=1)

    def summed(v, which):
        high, lowv = halves(v)
        return dg(high, which, 1, 0) + dg(lowv, which, 1, 0)

    def gated_norm_rows(i, _):
        rows = pl.ds(pl.multiple_of(i * ROWS, ROWS), ROWS)
        unit = r.gated[rows, :] * tile4(r.norm_col[rows, :])
        r.gated_norm[rows, :] = (unit * r.gain_row[...]).astype(bf)
        return 0

    lax.fori_loop(0, T // ROWS, gated_norm_rows, 0)
    stage("out_projection")
    for j in range(D // 256):
        value = dg(r.gated_norm[...], r.out_weight[:, 256 * j : 256 * j + 256], 1, 0).astype(bf)
        for k in range(256 // fold_width[0]):
            at = j * (256 // fold_width[0]) + k
            r.branch[at] = value[:, k * fold_width[0] : (k + 1) * fold_width[0]]
            fold_start(0, at)
    stage("back_rows")

    def back_rows(i, _):
        rows = pl.ds(pl.multiple_of(i * ROWS, ROWS), ROWS)
        norm = tile4(r.norm_col[rows, :])
        back = tile4(r.back_col[rows, :])
        gated = r.gated[rows, :]
        grad = r.norm_grad[rows, :]
        gain = r.gain_row[...]
        gate = r.gate_pre[rows, :]
        sigma = jax.nn.sigmoid(gate)
        unit = gated * norm
        r.sum_acc[0] = r.sum_acc[0] + fold8(grad * unit)
        gated_grad = norm * (grad * gain) - gated * back
        heads_grad = gated_grad * (gate * sigma)
        heads = r.mixed[rows, :] + skip_row * r.act[rows, :].astype(f32)
        r.gate_grad[rows, :] = (
            gated_grad * heads * (sigma * (1.0 + gate * (1.0 - sigma)))
        ).astype(bf)
        r.heads_grad[rows, :] = heads_grad
        x = r.act[rows, :].astype(f32)
        r.sum_acc[1] = r.sum_acc[1] + fold8(heads_grad * x)
        r.dy[rows, :], r.dy_rest[rows, :] = halves(heads_grad)
        r.dy_enter[rows, :], r.dy_enter_rest[rows, :] = halves(heads_grad * r.enter_wide[rows, :])
        r.sum_y[rows, :] = summed(heads_grad * r.mixed[rows, :], r.head_sum[...])
        return 0

    lax.fori_loop(0, T // ROWS, back_rows, 0)

    stage("grad_states")
    grad_in = None
    for c in reversed(range(NC)):
        rows = slice(c * Q, c * Q + Q)
        queries = r.queries[rows, :]
        local = dg(r.dy_enter[rows, :], queries, 0, 0) + dg(r.dy_enter_rest[rows, :], queries, 0, 0)
        r.grad_local[c] = local
        grad_in = local if grad_in is None else r.decay_wide[c] * grad_in + local
    r.grad_send[...] = grad_in
    r.grad_recv[seq] = r.grad_send[own_rows, :]
    grad_wait = spread(
        "seq", lambda d: block(r.grad_send, d), lambda d: r.grad_recv.at[d], r.grad_ss, r.grad_rs
    )
    stage("inside_back")
    r.score_grad[...] = jnp.zeros_like(r.score_grad)

    def inside_back(i, _):
        c = i // NP
        p = i % NP
        rows = pl.ds(pl.multiple_of(c * Q, Q), Q)
        lanes = pl.ds(pl.multiple_of(p * LANES, LANES), LANES)
        x = r.act[rows, lanes]
        dy = r.dy[rows, lanes]
        dy_rest = r.dy_rest[rows, lanes]
        zero = jnp.zeros_like(dy)
        x_turned, dy_turned = pltpu.roll(x, P_, 1), pltpu.roll(dy_rest, P_, 1)
        result = None
        for s in range(2):
            h = 2 * p + s
            ours = low if s == 0 else jnp.logical_not(low)
            pairs = dg(jnp.where(ours, dy, dy_turned), jnp.where(ours, x, x_turned), 1, 1)
            r.score_grad[c] = r.score_grad[c] + pairs * (r.decays[c, h] * r.step_rows[pl.ds(h, 1), rows])
            term = dg(r.turned[c, h], jnp.where(ours, dy, zero), 1, 0)
            result = term if s == 0 else result + term
        r.x_inside[rows, lanes] = result
        return 0

    lax.fori_loop(0, 4, inside_back, 0)
    fold_in(0, 0)
    lax.fori_loop(4, 7, inside_back, 0)
    fold_in(0, 1)
    lax.fori_loop(7, NC * NP, inside_back, 0)

    stage("poll_at_grad_wait")
    stage("grad_wait")
    grad_wait()
    stage("leave_scan")
    running = jnp.zeros((R, N), f32)
    for d in reversed(range(n_seq)):
        r.leave_send[d] = running
        running = decay_of(d) * running + r.grad_recv[d]
    r.leave_grad[own_rows, :] = r.leave_send[seq]
    leave_wait = spread(
        "seq", lambda d: r.leave_send.at[d], lambda d: block(r.leave_grad, d), r.leave_ss, r.leave_rs
    )

    stage("query_grad")
    for c in range(NC):
        rows = slice(c * Q, c * Q + Q)
        score_low, score_rest = halves(r.score_grad[c])
        r.query_grad[rows, :] = (
            dg(score_low, r.keys[rows, :], 1, 0)
            + dg(score_rest, r.keys[rows, :], 1, 0)
            + dg(r.dy_enter[rows, :], r.state_in_low[c], 1, 0)
            + dg(r.dy_enter_rest[rows, :], r.state_in_low[c], 1, 0)
            + dg(r.dy_enter[rows, :], r.state_in_rest[c], 1, 0)
        )

    def shared_copy(d, arriving=False):
        target = (tp + d) % n_tp
        slot = (tp + n_tp - d) % n_tp if arriving else tp
        sems = (r.shared_ss.at[d - 1], r.shared_rs.at[d - 1])
        return remote(r.shared_send.at[target], r.shared_recv.at[slot], *sems, (seq, target))

    def pack_shared(ref, group):
        top, bottom = ref[0 : T // 2, :], ref[T // 2 : T, :]
        at = group * shards
        r.shared_send[at] = jnp.where(half_low, top, pltpu.roll(bottom, NS, 1)).astype(bf)
        r.shared_send[at + 1] = jnp.where(half_low, pltpu.roll(top, NS, 1), bottom).astype(bf)

        @pl.when(tp // shards == group)
        def _():
            r.shared_recv[tp] = r.shared_send[tp]

        for d in range(1, n_tp):
            pl.when((tp + d) % n_tp // shards == group)(shared_copy(d).start)

    pack_shared(r.query_grad, 1)
    stage("poll_at_weights_one")
    fold_in(0, 2)
    stage("weights_one")
    def weight_rows(i, _):
        cols = pl.ds(pl.multiple_of(i * LANES, LANES), LANES)
        r.wg_one[cols, 0:HI] = dg(r.normed[:, cols], r.gate_grad[...], 0, 0).astype(bf)
        r.wg_one[cols, HI : 2 * HI] = dg(r.out_cotangent[:, cols], r.gated_norm[...], 0, 0).astype(bf)
        return 0

    lax.fori_loop(0, D // LANES, weight_rows, 0)

    chips = n_seq // 2
    core = seq % 2
    chip = seq // 2
    sibling = seq + 1 - 2 * core

    def pair_copy(k, q):
        rows = pl.ds(pl.multiple_of((2 * q + 1 - core) * R2, R2), R2)
        source, target = ((r.wg_one, r.pair_one), (r.wg_two, r.pair_two))[k]
        return remote(
            source.at[rows], target.at[q], r.pair_ss.at[k, q], r.pair_rs.at[k, q], (sibling, tp)
        )

    def chip_copy(k, d, arriving=False):
        to = (chip + d) % chips
        slot = (chip + chips - d) % chips if arriving else chip
        source, target = ((r.chip_one_send, r.chip_one), (r.chip_two_send, r.chip_two))[k]
        return remote(
            source.at[to],
            target.at[slot],
            r.chip_ss.at[k, d - 1],
            r.chip_rs.at[k, d - 1],
            (2 * to + core, tp),
        )

    def pair_start(k):
        for q in range(chips):
            pair_copy(k, q).start()

    def chip_start(k):
        own, pair, send, kept = (
            (r.wg_one, r.pair_one, r.chip_one_send, r.chip_one),
            (r.wg_two, r.pair_two, r.chip_two_send, r.chip_two),
        )[k]
        for q in range(chips):
            rows = pl.ds(pl.multiple_of((2 * q + core) * R2, R2), R2)
            pair_copy(k, q).wait_recv()
            send[q] = (own[rows, :].astype(f32) + pair[q].astype(f32)).astype(bf)
        for d in range(1, chips):
            chip_copy(k, d).start()
        kept[chip] = send[chip]

    def chip_sum(k):
        kept = (r.chip_one, r.chip_two)[k]
        for d in range(1, chips):
            chip_copy(k, d, True).wait_recv()
        value = kept[0].astype(f32)
        for q in range(1, chips):
            value = value + kept[q].astype(f32)
        for q in range(chips):
            pair_copy(k, q).wait_send()
        for d in range(1, chips):
            chip_copy(k, d).wait_send()
        return value

    pair_start(0)
    stage("poll_at_leave_wait")
    fold_middle(0, 0)
    fold_in(0, 3)
    stage("leave_wait")
    leave_wait()
    stage("leave")
    carry_terms = [None] * NC
    for c in reversed(range(NC)):
        rows = slice(c * Q, c * Q + Q)
        if c == NC - 1:
            grad = r.leave_grad[...]
        else:
            grad = r.decay_wide[c + 1] * grad + r.grad_local[c + 1]
        grad_low, grad_rest = halves(grad)
        keys, queries = r.keys[rows, :], r.queries[rows, :]
        for j in range(HI // 256):
            cols = slice(256 * j, 256 * j + 256)
            read = dg(keys, grad_low[cols, :], 1, 1) + dg(keys, grad_rest[cols, :], 1, 1)
            r.x_carry[rows, cols] = r.tail_wide[rows, cols] * read
        high, lowv = halves(grad * r.state_in[c])
        pair = dg(expand[0:H], high, 1, 0) + dg(expand[0:H], lowv, 1, 0)
        carry_terms[c] = chunk_decay[c] * jnp.sum(pair, axis=1, keepdims=True)
        score_low, score_rest = halves(r.score_grad[c])
        r.key_grad[rows, :] = (
            dg(score_low, queries, 0, 0)
            + dg(score_rest, queries, 0, 0)
            + dg(r.xt[rows, :], grad_low, 1, 0)
            + dg(r.xt_rest[rows, :], grad_low, 1, 0)
            + dg(r.xt[rows, :], grad_rest, 1, 0)
        )

    pack_shared(r.key_grad, 0)
    stage("poll_at_chip_one")
    fold_middle(0, 1)
    stage("after_keys")
    stage("poll_at_x_grads")
    fold_in(0, 4)
    fold_middle(0, 2)
    stage("x_grads")
    r.head_sum_two[...] = (
        iota((HI, LANES), 0) // P_ + H == iota((HI, LANES), 1)
    ).astype(f32).astype(bf)
    r.head_sum_three[...] = (
        iota((HI, LANES), 0) // P_ + 2 * H == iota((HI, LANES), 1)
    ).astype(f32).astype(bf)

    def x_rows(i, _):
        rows = pl.ds(pl.multiple_of(i * ROWS, ROWS), ROWS)
        x = r.act[rows, :].astype(f32)
        z = r.x_inside[rows, :]
        carried = r.x_carry[rows, :]
        both = z + carried
        step_rows = r.step_wide[rows, :]
        xs = x * step_rows
        x_grad = step_rows * both + skip_row * r.heads_grad[rows, :]
        conv_grad = x_grad * slope(r.inner_conv[rows, :])
        for g in range(NP):
            r.grad_ext[g, rows, :] = conv_grad[:, g * LANES : g * LANES + LANES]
        r.sum_x[rows, :] = (
            summed(x * both, r.head_sum[...])
            + summed(xs * carried, r.head_sum_two[...])
            + summed(xs * z, r.head_sum_three[...])
        )
        return 0

    lax.fori_loop(0, T // ROWS, x_rows, 0)
    halo_one = remote(
        r.grad_ext.at[:, pl.ds(0, PAD)],
        r.grad_ext.at[:, pl.ds(T, PAD)],
        r.halo_send.at[0],
        r.halo_recv.at[0],
        left,
    )
    halo_one.start()
    waits.append(halo_one)

    sums_y = r.sum_y[...].T
    sums_x = r.sum_x[...].T
    step_grad = sums_x[0:H]
    tail_part = sums_x[H : 2 * H]
    pair_part = sums_y[0:H] - sums_x[2 * H : 3 * H]
    decay_grads = []
    for c in range(NC):
        cols = slice(c * Q, c * Q + Q)
        suffix = fold3(dg(split3(pair_part[:, cols]), r.upto[...], 1, 1))
        before = fold3(dg(split3(tail_part[:, cols]), r.upto[...], 1, 0)) - tail_part[:, cols]
        decay_grads.append(suffix + before + carry_terms[c])
    decay_grad = jnp.concatenate(decay_grads, axis=1)
    step_total = step_grad - rate * decay_grad
    step_pre_grad = step_total * r.sigmoid_step[...]
    rate_sum = jnp.sum(r.log_decay[...] * decay_grad, axis=1, keepdims=True)
    bias_sum = jnp.sum(step_pre_grad, axis=1, keepdims=True)
    step_cols = jnp.concatenate(
        [jnp.zeros((NS, T), f32), step_pre_grad, jnp.zeros((LANES - NS - H, T), f32)], axis=0
    ).T

    stage("poll_at_conv_back")
    fold_in(0, 5)
    fold_middle(0, 3)
    stage("conv_back")
    def after_masks(base):
        position = first_token + base + iota((ROWS, LANES), 0)
        now = segment(position)
        masks = []
        for k in range(CONV - 1):
            later = position + (CONV - 1) - k
            masks.append((segment(later) == now) & (later < total_tokens))
        return masks

    def conv_back(ext, taps, base, lanes, masks):
        value = None
        for k in range(CONV):
            term = taps[k : k + 1, lanes] * ext[pl.ds(base + CONV - 1 - k, ROWS), :]
            if k < CONV - 1:
                term = jnp.where(masks[k], term, 0.0)
            value = term if value is None else value + term
        return value

    def tap_sums(ext, grad, base, masks):
        sums = []
        for k in range(CONV):
            term = grad * ext[pl.ds(base + PAD - CONV + 1 + k, ROWS), :]
            sums.append(fold8(term if k == CONV - 1 else jnp.where(masks[k], term, 0.0)))
        return sums + [fold8(grad)]

    stage("inner_back")

    def inner_back_rows(i, _):
        base = pl.multiple_of(i * ROWS, ROWS)
        rows = pl.ds(base, ROWS)
        masks = after_masks(base)
        before = agreements(base, ROWS)
        taps = r.inner_kernel[...]
        for g in range(NP):
            lanes = slice(g * LANES, g * LANES + LANES)
            r.inner_grad[rows, lanes] = conv_back(r.grad_ext.at[g], taps, base, lanes, masks).astype(bf)
            found = tap_sums(r.inner_ext.at[g], r.grad_ext[g, rows, :], base, before)
            for k, v in enumerate(found):
                r.sum_acc[2 + k, :, lanes] = r.sum_acc[2 + k, :, lanes] + v
        return 0

    lax.fori_loop(0, T // ROWS - 1, inner_back_rows, 0)
    stage("poll_at_halo_one_wait")
    fold_in(0, 6)
    fold_middle(0, 4)
    stage("halo_one_wait")
    halo_one.wait_recv()
    stage("inner_back_last")
    inner_back_rows(T // ROWS - 1, 0)

    stage("poll_at_shared_wait")
    fold_middle(0, 5)
    fold_in(0, 7)
    stage("shared_wait")
    for d in range(1, n_tp):
        shared_copy(d, True).wait_recv()
    stage("shared_use")
    packed = r.shared_recv[0].astype(f32)
    for t in range(1, n_tp):
        packed = packed + r.shared_recv[t].astype(f32)
    r.state_grad_ext[0 : T // 2, :] = packed * slope(r.misc_conv[0 : T // 2, :])
    r.state_grad_ext[T // 2 : T, :] = pltpu.roll(packed, NS, 1) * slope(r.misc_conv[T // 2 : T, :])
    halo_two = remote(
        r.state_grad_ext.at[pl.ds(0, PAD)],
        r.state_grad_ext.at[pl.ds(T, PAD)],
        r.halo_send.at[1],
        r.halo_recv.at[1],
        left,
    )
    halo_two.start()
    waits.append(halo_two)
    stage("chip_one")
    chip_start(0)
    stage("poll_at_misc_back")
    fold_middle(0, 6)
    stage("misc_back")
    r.misc_acc[...] = jnp.zeros_like(r.misc_acc)
    r.step_cols[...] = step_cols

    def misc_back_rows(i, _):
        base = pl.multiple_of(i * ROWS, ROWS)
        rows = pl.ds(base, ROWS)
        masks = after_masks(base)
        before = agreements(base, ROWS)
        taps = r.misc_taps[...]
        lanes = slice(0, LANES)
        value = conv_back(r.state_grad_ext, taps, base, lanes, masks)
        value = jnp.where(iota((ROWS, LANES), 1) < NS, value, r.step_cols[rows, :])
        r.misc_grad[rows, :] = value.astype(bf)
        found = tap_sums(r.misc_ext.at[0], r.state_grad_ext[rows, :], base, before)
        for k, v in enumerate(found):
            r.misc_acc[k] = r.misc_acc[k] + v
        return 0

    lax.fori_loop(0, T // ROWS - 1, misc_back_rows, 0)
    stage("halo_two_wait")
    halo_two.wait_recv()
    stage("misc_back_last")
    misc_back_rows(T // ROWS - 1, 0)

    stage("poll_at_normed_grad")
    stage("normed_grad")
    width, tall = fold_width[1], fold_rows[1]
    for j in range(D // 256):
        cols = slice(256 * j, 256 * (j + 1))
        value = (
            dg(r.gate_grad[...], r.gate_weight[cols, :], 1, 1)
            + dg(r.inner_grad[...], r.inner_weight[cols, :], 1, 1)
            + dg(r.misc_grad[...], r.misc_weight[:, cols], 1, 0)
        )
        value_low = value.astype(bf)
        for k in range(256 // width):
            for m in range(T // tall):
                at = (j * (256 // width) + k) * (T // tall) + m
                r.normed_part[at] = value_low[m * tall : m * tall + tall, k * width : k * width + width]
                fold_start(1, at)
        hats = r.block_input[:, cols].astype(f32) * jnp.concatenate([r.inverse[...]] * 2, axis=1)
        r.gain_part[:, cols] = fold8(value * hats)

    stage("poll_at_small_sums")
    fold_middle(0, 7)
    stage("small_sums")

    def row_of(v):
        return jnp.sum(v, axis=0, keepdims=True)

    eye_wide = iota((H, LANES), 0) == iota((H, LANES), 1)

    def lanes_of(v):
        return row_of(jnp.where(eye_wide, jnp.broadcast_to(v, (H, LANES)), 0.0))

    r.small_send[...] = jnp.zeros_like(r.small_send)
    for k in range(CONV + 1):
        r.small_send[k : k + 1, :] = row_of(r.sum_acc[2 + k])
    r.small_send[5:6, :] = row_of(r.sum_acc[0])
    r.small_send[6:7, :] = row_of(r.sum_acc[1])
    for k in range(CONV):
        r.small_send[7:8, k * LANES : k * LANES + LANES] = row_of(r.misc_acc[k])
    r.small_send[8:9, 0:LANES] = row_of(r.misc_acc[CONV])
    r.small_send[8:9, LANES : 2 * LANES] = lanes_of(bias_sum)
    r.small_send[8:9, 2 * LANES : 3 * LANES] = lanes_of(rate_sum)
    gain_rows = row_of(r.gain_part[...])
    for k in range(D // HI):
        r.small_send[9 + k : 10 + k, :] = gain_rows[:, k * HI : k * HI + HI]
    r.small_recv[seq] = r.small_send[...]
    small_wait = spread(
        "seq", lambda d: r.small_send, lambda d: r.small_recv.at[d], r.small_ss, r.small_rs
    )
    stage("weights_two")

    def weight_rows_two(i, _):
        cols = pl.ds(pl.multiple_of(i * LANES, LANES), LANES)
        r.wg_two[cols, 0:HI] = dg(r.normed[:, cols], r.inner_grad[...], 0, 0).astype(bf)
        r.wg_two[cols, HI : HI + LANES] = dg(r.normed[:, cols], r.misc_grad[...], 0, 0).astype(bf)
        return 0

    lax.fori_loop(0, D // LANES // 2, weight_rows_two, 0)
    fold_in(1, 0)
    lax.fori_loop(D // LANES // 2, D // LANES, weight_rows_two, 0)
    pair_start(1)
    stage("folds")
    last = fold_pieces[1]
    for j in range(last + 2):
        if 0 < j < last:
            fold_in(1, j)
        if j > 1:
            fold_middle(1, j - 2)
        if j == 2:
            chip_start(1)
        if j == 10:
            small_wait()
            total = r.small_recv[0]
            for d in range(1, n_seq):
                total = total + r.small_recv[d]
            r.small_total[...] = total
            r.gain_recv[tp] = r.small_total[8:16, :]
            gain_wait = spread(
                "tp",
                lambda t: r.small_total.at[pl.ds(8, 8)],
                lambda t: r.gain_recv.at[t],
                r.gain_ss,
                r.gain_rs,
            )
    for j in range(fold_pieces[0]):
        fold_end(0, j)
    stage("weight_sums")
    r.sum_one[...] = chip_sum(0)
    r.sum_two[...] = chip_sum(1)
    gain_wait()
    gains = r.gain_recv[0]
    for t in range(1, n_tp):
        gains = gains + r.gain_recv[t]
    r.gain_total[...] = gains
    stage("folds_last")
    for j in range(fold_pieces[1]):
        fold_end(1, j)
    stage("drain")
    for d in range(1, n_tp):
        shared_copy(d).wait_send()
    for copy in waits:
        copy.wait_send()
    marks.close()


def finish(sizes, names, *refs):
    r = types.SimpleNamespace(**dict(zip(names, refs)))
    T, D, HI, H, NS = sizes
    P_ = HI // H
    T = r.block_input.shape[0]

    def final_rows(i, _):
        rows = pl.ds(pl.multiple_of(i * ROWS, ROWS), ROWS)
        x = r.block_input[rows, :].astype(f32)
        r.block_output[rows, :] = (x + r.branch_sum[rows, :].astype(f32)).astype(bf)
        inverse = lax.rsqrt(jnp.mean(x * x, axis=1, keepdims=True) + epsilon)
        hat = x * inverse
        hat_grad = r.normed_sum[rows, :].astype(f32) * r.input_gain[...].reshape(1, D)
        mean = jnp.mean(hat_grad * hat, axis=1, keepdims=True)
        r.input_grad[rows, :] = r.out_cotangent[rows, :].astype(f32) + inverse * (
            hat_grad - hat * mean
        )
        return 0

    lax.fori_loop(0, T // ROWS, final_rows, 0)
    @pl.when(pl.program_id(0) == 0)
    def _():
        r.gate_weight_grad[...] = r.sum_one[:, 0:HI]
        r.out_weight_grad[...] = r.sum_one[:, HI : 2 * HI].T
        r.inner_weight_grad[...] = r.sum_two[:, 0:HI]
        narrow = r.sum_two[:, HI : HI + LANES].T
        r.state_weight_grad[...] = narrow[0:NS]
        r.step_weight_grad[...] = narrow[NS : NS + H]
        small = r.small_total
        r.inner_kernel_grad[...] = small[0:CONV, :]
        r.inner_conv_bias_grad[...] = small[CONV : CONV + 1, :].reshape(HI)
        r.gate_gain_grad[...] = small[5:6, :].reshape(HI)
        head_sum = (iota((HI, LANES), 0) // P_ == iota((HI, LANES), 1)).astype(f32).astype(bf)
        skip_sums = fold3(dg(split3(jnp.broadcast_to(small[6:7, :], (8, HI))), head_sum, 1, 0))
        r.skip_scale_grad[...] = skip_sums[0:1, 0:H].reshape(H)
        for k in range(CONV):
            r.state_kernel_grad[k : k + 1, :] = small[7:8, k * LANES : k * LANES + NS]
        r.state_conv_bias_grad[...] = small[8:9, 0:NS].reshape(NS)
        r.step_bias_grad[...] = small[8:9, LANES : LANES + H].reshape(H)
        r.rate_log_grad[...] = small[8:9, 2 * LANES : 2 * LANES + H].reshape(H)
        for k in range(D // HI):
            r.input_gain_grad[k * HI : k * HI + HI] = r.gain_total[1 + k : 2 + k, :].reshape(HI)


INPUTS = (
    "block_input",
    "scene_lengths",
    "input_gain",
    "gate_weight",
    "inner_weight",
    "state_weight",
    "step_weight",
    "step_bias",
    "rate_log",
    "inner_kernel",
    "inner_conv_bias",
    "state_kernel",
    "state_conv_bias",
    "skip_scale",
    "gate_gain",
    "out_weight",
    "out_cotangent",
)
OUTPUTS = (
    "block_output",
    "input_grad",
    "input_gain_grad",
    "gate_weight_grad",
    "inner_weight_grad",
    "state_weight_grad",
    "step_weight_grad",
    "step_bias_grad",
    "rate_log_grad",
    "inner_kernel_grad",
    "inner_conv_bias_grad",
    "state_kernel_grad",
    "state_conv_bias_grad",
    "skip_scale_grad",
    "gate_gain_grad",
    "out_weight_grad",
)


SUMS = ("branch_sum", "normed_sum", "sum_one", "sum_two", "small_total", "gain_total")


def local(*args):
    given = dict(zip(INPUTS, args))
    given["state_weight"] = given["state_weight"].T
    given["step_weight"] = given["step_weight"].T
    n_seq = lax.axis_size("seq")
    n_tp = lax.axis_size("tp")
    T, D = given["block_input"].shape
    HI = given["gate_weight"].shape[1]
    H = given["step_bias"].shape[0]
    NS = given["state_weight"].shape[0]
    N = STATE
    Q = CHUNK
    NC = T // Q
    NP = HI // LANES
    R = HI // n_seq
    R2 = D // n_seq
    outs = (
        ((T, D), bf),
        ((T, D), f32),
        ((D,), f32),
        ((R2, HI), f32),
        ((R2, HI), f32),
        ((NS, R2), f32),
        ((H, R2), f32),
        ((H,), f32),
        ((H,), f32),
        ((CONV, HI), f32),
        ((HI,), f32),
        ((CONV, NS), f32),
        ((NS,), f32),
        ((H,), f32),
        ((HI,), f32),
        ((HI, R2), f32),
    )
    sums = (
        ((T, D), bf),
        ((T, D), bf),
        ((R2, 2 * HI), f32),
        ((R2, HI + LANES), f32),
        ((16, HI), f32),
        ((8, HI), f32),
    )
    scratch = dict(
        inverse=((T, LANES), f32),
        normed=((T, D), bf),
        misc_weight=((LANES, D), bf),
        inner_ext=((NP, T + PAD, LANES), f32),
        misc_ext=((1, T + PAD, LANES), f32),
        gate_pre=((T, HI), f32),
        misc_taps=((8, LANES), f32),
        inner_bias=((1, HI), f32),
        gain_row=((1, HI), f32),
        misc_conv=((T, LANES), f32),
        inner_conv=((T, HI), f32),
        act=((T, HI), bf),
        state_send=((T // 2, LANES), bf),
        state_recv=((n_tp, T // 2, LANES), bf),
        keys=((T, N), bf),
        queries=((T, N), bf),
        sigmoid_step=((H, T), f32),
        step_rows=((H, T), f32),
        log_decay=((H, T), f32),
        upto=((Q, Q), bf),
        expand=((3 * H, HI), bf),
        mask=((NC, Q, Q), f32),
        cum_left=((H, 16, T), bf),
        cum_right=((H, 16, T), bf),
        step_wide=((T, HI), f32),
        enter_wide=((T, HI), f32),
        tail_wide=((T, HI), f32),
        decay_wide=((NC, HI, LANES), f32),
        skip_wide=((8, HI), f32),
        xt=((T, HI), bf),
        xt_rest=((T, HI), bf),
        fresh=((NC, HI, N), f32),
        end_send=((HI, N), f32),
        end_recv=((n_seq, R, N), f32),
        decay_send=((H, LANES), f32),
        decay_recv=((n_seq, H, LANES), f32),
        enter_send=((n_seq, R, N), f32),
        enter_state=((HI, N), f32),
        state_in=((NC, HI, N), f32),
        state_in_low=((NC, HI, N), bf),
        state_in_rest=((NC, HI, N), bf),
        scores=((NC, Q, Q), f32),
        score_grad=((NC, Q, Q), f32),
        decays=((NC, H, Q, Q), f32),
        turned=((NC, H, Q, Q), bf),
        mixed=((T, HI), f32),
        norm_grad=((T, HI), f32),
        gated=((T, HI), f32),
        squares=((T, LANES), f32),
        products=((T, LANES), f32),
        sums_send=((8, T), f32),
        sums_recv=((n_tp, 8, T), f32),
        norm_col=((T, LANES), f32),
        back_col=((T, LANES), f32),
        head_sum=((HI, LANES), bf),
        head_sum_two=((HI, LANES), bf),
        head_sum_three=((HI, LANES), bf),
        sum_acc=((7, 8, HI), f32),
        gated_norm=((T, HI), bf),
        gate_grad=((T, HI), bf),
        heads_grad=((T, HI), f32),
        dy=((T, HI), bf),
        dy_rest=((T, HI), bf),
        dy_enter=((T, HI), bf),
        dy_enter_rest=((T, HI), bf),
        sum_y=((T, LANES), f32),
        sum_x=((T, LANES), f32),
        grad_local=((NC, HI, N), f32),
        grad_send=((HI, N), f32),
        grad_recv=((n_seq, R, N), f32),
        leave_send=((n_seq, R, N), f32),
        leave_grad=((HI, N), f32),
        x_inside=((T, HI), f32),
        x_carry=((T, HI), f32),
        wg_one=((D, 2 * HI), bf),
        pair_one=((n_seq // 2, R2, 2 * HI), bf),
        chip_one_send=((n_seq // 2, R2, 2 * HI), bf),
        chip_one=((n_seq // 2, R2, 2 * HI), bf),
        wg_two=((D, HI + LANES), bf),
        pair_two=((n_seq // 2, R2, HI + LANES), bf),
        chip_two_send=((n_seq // 2, R2, HI + LANES), bf),
        chip_two=((n_seq // 2, R2, HI + LANES), bf),
        query_grad=((T, N), f32),
        key_grad=((T, N), f32),
        shared_send=((n_tp, T // 2, LANES), bf),
        shared_recv=((n_tp, T // 2, LANES), bf),
        grad_ext=((NP, T + PAD, LANES), f32),
        state_grad_ext=((T + PAD, LANES), f32),
        inner_grad=((T, HI), bf),
        step_cols=((T, LANES), f32),
        misc_grad=((T, LANES), bf),
        misc_acc=((CONV + 1, 8, LANES), f32),
        normed_part=((16, T // 2, D // 8), bf),
        normed_in=((16, T // 2, D // 8), bf),
        normed_across=((16, T // 2, D // 8), bf),
        branch=((8, T, D // 8), bf),
        branch_in=((8, T, D // 8), bf),
        branch_across=((8, T, D // 8), bf),
        gain_part=((8, D), f32),
        small_send=((16, HI), f32),
        small_recv=((n_seq, 16, HI), f32),
        gain_recv=((n_tp, 8, HI), f32),
    )
    semaphores = dict(
        rim_send=(2,),
        rim_recv=(2,),
        halo_send=(2,),
        halo_recv=(2,),
        pair_ss=(2, n_seq // 2),
        pair_rs=(2, n_seq // 2),
        chip_ss=(2, n_seq // 2 - 1),
        chip_rs=(2, n_seq // 2 - 1),
        fold_ss=(3, 24),
        fold_rs=(3, 24),
    )
    for name in ("state", "sums", "shared", "gain"):
        semaphores[name + "_ss"] = (n_tp - 1,)
        semaphores[name + "_rs"] = (n_tp - 1,)
    for name in ("decay", "end", "enter", "grad", "leave", "small"):
        semaphores[name + "_ss"] = (n_seq - 1,)
        semaphores[name + "_rs"] = (n_seq - 1,)
    scratch.update({n: (given[n].shape, bf) for n in LOADED})
    semaphores["load_sems"] = (len(LOADED),)
    names = tuple(n + "_hbm" if n in LOADED else n for n in INPUTS) + SUMS + tuple(scratch) + tuple(semaphores)
    vmem = pl.BlockSpec(memory_space=pltpu.VMEM)
    smem = pl.BlockSpec(memory_space=pltpu.SMEM)
    totals = pl.pallas_call(
        functools.partial(kernel, (n_seq, n_tp, T, D, HI, H, NS), names),
        out_shape=tuple(jax.ShapeDtypeStruct(s, t) for s, t in sums),
        in_specs=[
            smem if n == "scene_lengths" else pl.BlockSpec(memory_space=pl.ANY) if n in LOADED else vmem
            for n in INPUTS
        ],
        out_specs=tuple(vmem for _ in sums),
        scratch_shapes=[pltpu.VMEM(s, t) for s, t in scratch.values()]
        + [pltpu.SemaphoreType.DMA(s) for s in semaphores.values()],
        compiler_params=pltpu.CompilerParams(
            collective_id=0, has_side_effects=True, vmem_limit_bytes=61 * 2**20
        ),
    )(*given.values())
    tall = ("block_input", "out_cotangent", "branch_sum", "normed_sum", "block_output", "input_grad")
    steps = 2
    by_rows = pl.BlockSpec((T // steps, D), lambda i: (i, 0))

    def whole(shape):
        return pl.BlockSpec(shape, lambda i: (0,) * len(shape))

    needed = ("block_input", "input_gain", "out_cotangent")
    results = pl.pallas_call(
        functools.partial(finish, (T, D, HI, H, NS), needed + SUMS + OUTPUTS),
        out_shape=tuple(jax.ShapeDtypeStruct(s, t) for s, t in outs),
        grid=(steps,),
        in_specs=[by_rows if n in tall else whole(given[n].shape) for n in needed]
        + [by_rows if n in tall else whole(s) for n, (s, _) in zip(SUMS, sums)],
        out_specs=tuple(by_rows if n in tall else whole(s) for n, (s, _) in zip(OUTPUTS, outs)),
        compiler_params=pltpu.CompilerParams(vmem_limit_bytes=60 * 2**20),
    )(*(given[n] for n in needed), *totals)
    results = dict(zip(OUTPUTS, results))
    results["state_weight_grad"] = results["state_weight_grad"].T
    results["step_weight_grad"] = results["step_weight_grad"].T
    return tuple(results.values())


def solution(mesh):
    rows = P("seq", None)
    cols = P(None, "tp")
    heads = P("tp")
    return jax.shard_map(
        local,
        mesh=mesh,
        in_specs=(
            rows,
            P(),
            P(),
            cols,
            cols,
            cols,
            cols,
            heads,
            heads,
            cols,
            heads,
            cols,
            heads,
            heads,
            heads,
            P("tp", None),
            rows,
        ),
        out_specs=(
            rows,
            rows,
            P(),
            P("seq", "tp"),
            P("seq", "tp"),
            P("seq", "tp"),
            P("seq", "tp"),
            heads,
            heads,
            cols,
            heads,
            cols,
            heads,
            heads,
            heads,
            P("tp", "seq"),
        ),
        check_vma=False,
    )
```

```python
import contextlib
import functools
import types

import jax
import jax.numpy as jnp
from jax import lax
from jax.experimental import pallas as pl
from jax.experimental.pallas import tpu as pltpu
from jax.sharding import PartitionSpec as P

STATE = 128
CONV = 4
CHUNK = 256
LANES = 128
PAD = 8
ROWS = 64
epsilon = 1e-05
bf = jnp.bfloat16
f32 = jnp.float32
i32 = jnp.int32
MESH = pl.DeviceIdType.MESH


def dg(left, right, left_dim, right_dim):
    return lax.dot_general(
        left, right, (((left_dim,), (right_dim,)), ((), ())), preferred_element_type=f32
    )


def split3(v):
    high = v.astype(bf).astype(f32)
    middle = (v - high).astype(bf).astype(f32)
    return jnp.concatenate([high, middle, v - high - middle], axis=0).astype(bf)


def fold3(v):
    third = v.shape[0] // 3
    return v[:third] + v[third : 2 * third] + v[2 * third :]


def halves(v):
    high = v.astype(bf)
    return high, (v - high.astype(f32)).astype(bf)


def slope(v):
    s = jax.nn.sigmoid(v)
    return s * (1.0 + v * (1.0 - s))


def fold8(v):
    total = v[0:8]
    for i in range(1, v.shape[0] // 8):
        total = total + v[8 * i : 8 * i + 8]
    return total


def iota(shape, dim):
    return lax.broadcasted_iota(i32, shape, dim)


LOADED = ("inner_weight", "gate_weight", "out_weight", "out_cotangent")


def kernel(sizes, names, *refs):
    r = types.SimpleNamespace(**dict(zip(names, refs)))
    n_seq, n_tp, T, D, HI, H, NS = sizes
    N = STATE
    P_ = HI // H
    Q = CHUNK
    NC = T // Q
    NP = HI // LANES
    R = HI // n_seq
    R2 = D // n_seq
    total_tokens = T * n_seq
    seq = lax.axis_index("seq")
    tp = lax.axis_index("tp")

    barrier = pltpu.get_barrier_semaphore()
    for d in range(1, n_seq):
        pl.semaphore_signal(
            barrier, inc=1, device_id=((seq + d) % n_seq, tp), device_id_type=MESH
        )
    for d in range(1, n_tp):
        pl.semaphore_signal(
            barrier, inc=1, device_id=(seq, (tp + d) % n_tp), device_id_type=MESH
        )

    waits = []
    loads = {}
    for k, n in enumerate(LOADED):
        loads[n] = pltpu.make_async_copy(getattr(r, n + "_hbm"), getattr(r, n), r.load_sems.at[k])
        loads[n].start()
    half = n_tp // 2
    inner = jnp.where(tp < half, tp + 1, tp - 1)
    outer = jnp.where(tp < half, tp - 1, tp + 1)
    is_middle = (tp == half - 1) | (tp == half)
    has_outer = (tp > 0) & (tp < n_tp - 1)
    fold_pieces = (r.branch_in.shape[0], r.normed_in.shape[0])
    fold_width = D // fold_pieces[0], LANES
    fold_rows = T, T * D // LANES // fold_pieces[1]
    fold_refs = (
        (r.branch, r.branch_in, r.branch_across, r.branch_sum),
        (r.normed_part, r.normed_in, r.normed_across, r.normed_sum),
    )

    def fold(a, j):
        high = T // fold_rows[a]
        place = (
            pl.ds(j % high * fold_rows[a], fold_rows[a]),
            pl.ds(j // high * fold_width[a], fold_width[a]),
        )
        partial, arrived, across, total = (
            ref.at[j] if k < 3 else ref.at[place]
            for k, ref in enumerate(fold_refs[a])
        )
        return partial, arrived, across, total

    def fold_copy(a, j, leg):
        partial, arrived, across, total = fold(a, j)
        sems = leg, sum(fold_pieces[:a]) + j
        source, target, place = ((partial, arrived, inner), (partial, across, inner), (total, total, outer))[leg]
        return remote(source, target, r.fold_ss.at[sems], r.fold_rs.at[sems], (seq, place))

    def fold_start(a, j):
        pl.when(jnp.logical_not(has_outer | is_middle))(fold_copy(a, j, 0).start)

    def fold_in(a, j):
        partial, arrived, _, _ = fold(a, j)

        @pl.when(has_outer)
        def _():
            fold_copy(a, j, 0).wait_recv()
            partial[...] = (partial[...].astype(f32) + arrived[...].astype(f32)).astype(bf)

        pl.when(is_middle)(fold_copy(a, j, 1).start)
        pl.when(has_outer & jnp.logical_not(is_middle))(fold_copy(a, j, 0).start)

    def fold_middle(a, j):
        partial, _, across, total = fold(a, j)

        @pl.when(is_middle)
        def _():
            fold_copy(a, j, 1).wait_recv()
            total[...] = (partial[...].astype(f32) + across[...].astype(f32)).astype(bf)
            pl.when(has_outer)(fold_copy(a, j, 2).start)

    def fold_end(a, j):
        @pl.when(jnp.logical_not(is_middle))
        def _():
            fold_copy(a, j, 2).wait_recv()
            pl.when(has_outer)(fold_copy(a, j, 2).start)
            fold_copy(a, j, 0).wait_send()

        pl.when(has_outer)(fold_copy(a, j, 2).wait_send)
        pl.when(is_middle)(fold_copy(a, j, 1).wait_send)

    marks = contextlib.ExitStack()

    def stage(name):
        marks.close()
        marks.enter_context(jax.named_scope(name))

    stage("norm")

    def remote(src, dst, send, recv, device):
        return pltpu.make_async_remote_copy(
            src_ref=src,
            dst_ref=dst,
            send_sem=send,
            recv_sem=recv,
            device_id=device,
            device_id_type=MESH,
        )

    def spread(axis, src_to, dst_from, send, recv):
        n = n_seq if axis == "seq" else n_tp
        me = seq if axis == "seq" else tp
        incoming = []
        for d in range(1, n):
            target = (me + d) % n
            source = (me + n - d) % n
            device = (target, tp) if axis == "seq" else (seq, target)
            out = remote(src_to(target), dst_from(me), send.at[d - 1], recv.at[d - 1], device)
            out.start()
            waits.append(out)
            incoming.append(
                remote(src_to(target), dst_from(source), send.at[d - 1], recv.at[d - 1], device)
            )

        def wait():
            for copy in incoming:
                copy.wait_recv()

        return wait

    starts = [jnp.int32(0)]
    for k in range(r.scene_lengths.shape[0] - 1):
        starts.append(starts[-1] + r.scene_lengths[k])

    def segment(position):
        found = (position >= starts[0]).astype(i32)
        for s in starts[1:]:
            found = found + (position >= s).astype(i32)
        return found

    first_token = seq * T

    def norm_rows(i, _):
        rows = pl.ds(pl.multiple_of(i * ROWS, ROWS), ROWS)
        x = r.block_input[rows, :].astype(f32)
        inverse = lax.rsqrt(jnp.mean(x * x, axis=1, keepdims=True) + epsilon)
        r.inverse[rows, :] = jnp.broadcast_to(inverse, (ROWS, LANES))
        r.normed[rows, :] = (x * inverse * r.input_gain[...].reshape(1, D)).astype(bf)
        return 0

    lax.fori_loop(0, T // ROWS, norm_rows, 0)

    stage("projections")
    r.misc_weight[...] = jnp.zeros_like(r.misc_weight)
    r.misc_weight[0:NS, :] = r.state_weight[...]
    r.misc_weight[NS : NS + H, :] = r.step_weight[...]
    normed_all = r.normed[...]
    r.misc_ext[0, PAD : PAD + T, :] = dg(normed_all, r.misc_weight[...], 1, 1)
    stage("barrier")
    pl.semaphore_wait(barrier, n_seq - 1 + n_tp - 1)
    stage("inner_projection")
    right = ((seq + 1) % n_seq, tp)
    left = ((seq + n_seq - 1) % n_seq, tp)
    misc_rim, inner_rim = [
        remote(
            ref.at[:, pl.ds(T, PAD)],
            ref.at[:, pl.ds(0, PAD)],
            r.rim_send.at[k],
            r.rim_recv.at[k],
            right,
        )
        for k, ref in enumerate((r.misc_ext, r.inner_ext))
    ]
    waits.extend((misc_rim, inner_rim))
    misc_rim.start()
    for j in range(HI // 256):
        cols = slice(256 * j, 256 * j + 256)
        if j == 0:
            loads["inner_weight"].wait()
        value = dg(normed_all, r.inner_weight[:, cols], 1, 0)
        r.inner_ext[2 * j, PAD : PAD + T, :] = value[:, :LANES]
        r.inner_ext[2 * j + 1, PAD : PAD + T, :] = value[:, LANES:]
    inner_rim.start()
    stage("gate_projection")
    for j in range(HI // 256):
        cols = slice(256 * j, 256 * j + 256)
        if j == 0:
            loads["gate_weight"].wait()
        r.gate_pre[:, cols] = dg(normed_all, r.gate_weight[:, cols], 1, 0)

    stage("convolutions")
    def agreements(base, rows):
        position = first_token + base + iota((rows, LANES), 0)
        now = segment(position)
        return [segment(position - (CONV - 1) + k) == now for k in range(CONV - 1)]

    def conv_block(ext, taps, bias, base, lanes, masks):
        value = bias[:, lanes]
        for k in range(CONV):
            window = ext[pl.ds(base + PAD - CONV + 1 + k, ROWS), :]
            term = taps[k : k + 1, lanes] * window
            value = value + (term if k == CONV - 1 else jnp.where(masks[k], term, 0.0))
        return value

    r.misc_taps[...] = jnp.zeros_like(r.misc_taps)
    r.misc_taps[0:CONV, 0:NS] = r.state_kernel[...]
    r.misc_taps[CONV : CONV + 1, 0:NS] = r.state_conv_bias[...].reshape(1, NS)
    r.inner_bias[...] = r.inner_conv_bias[...].reshape(1, HI)
    stage("rim_wait")
    misc_rim.wait_recv()
    stage("conv")

    def misc_conv_rows(i, _):
        base = pl.multiple_of(i * ROWS, ROWS)
        masks = agreements(base, ROWS)
        taps = r.misc_taps[...]
        value = conv_block(
            r.misc_ext.at[0], taps, taps[CONV : CONV + 1], base, slice(0, LANES), masks
        )
        r.misc_conv[pl.ds(base, ROWS), :] = value
        return 0

    lax.fori_loop(0, T // ROWS, misc_conv_rows, 0)
    low_lanes = iota((T // 2, LANES), 1) < NS
    own = r.misc_conv[...]
    own = own * jax.nn.sigmoid(own)
    r.state_send[...] = jnp.where(
        low_lanes, own[: T // 2], pltpu.roll(own[T // 2 :], NS, 1)
    ).astype(bf)
    r.state_recv[tp] = r.state_send[...]
    state_wait = spread(
        "tp",
        lambda t: r.state_send,
        lambda t: r.state_recv.at[t],
        r.state_ss,
        r.state_rs,
    )

    def inner_conv_rows(i, _):
        base = pl.multiple_of(i * ROWS, ROWS)
        rows = pl.ds(base, ROWS)
        masks = agreements(base, ROWS)
        taps = r.inner_kernel[...]
        for g in range(NP):
            lanes = slice(g * LANES, g * LANES + LANES)
            value = conv_block(r.inner_ext.at[g], taps, r.inner_bias, base, lanes, masks)
            r.inner_conv[rows, lanes] = value
            r.act[rows, lanes] = (value * jax.nn.sigmoid(value)).astype(bf)
        return 0

    inner_rim.wait_recv()
    lax.fori_loop(0, T // ROWS, inner_conv_rows, 0)

    stage("decays")
    eye = iota((H, H), 0) == iota((H, H), 1)

    def column(ref):
        wide = jnp.broadcast_to(ref[...].reshape(1, H), (H, H))
        return jnp.sum(jnp.where(eye, wide, 0.0), axis=1, keepdims=True)

    step_in = r.misc_ext[0, PAD : PAD + T, :].T[NS : NS + H, :] + column(r.step_bias)
    step = jnp.maximum(step_in, 0.0) + jnp.log1p(jnp.exp(-jnp.abs(step_in)))
    rate = jnp.exp(column(r.rate_log))
    log_decay = step * -rate
    r.sigmoid_step[...] = jax.nn.sigmoid(step_in)
    r.log_decay[...] = log_decay
    r.step_rows[...] = step
    r.upto[...] = (iota((Q, Q), 0) <= iota((Q, Q), 1)).astype(f32).astype(bf)
    r.expand[...] = (iota((3 * H, HI), 0) % H == iota((3 * H, HI), 1) // P_).astype(f32).astype(bf)
    expand = r.expand[...]

    entering, tailing, chunk_decay = [], [], []
    ones_rows = jnp.ones((1, Q), f32)
    for c in range(NC):
        cols = slice(c * Q, c * Q + Q)
        cumulative = fold3(dg(split3(log_decay[:, cols]), r.upto[...], 1, 0))
        start = first_token + c * Q
        seg_row = segment(start + iota((H, Q), 1))
        seg_before = segment(start - 1)
        seg_end = segment(start + Q - 1)
        last = cumulative[:, Q - 1 : Q]
        enter = jnp.where(seg_row == seg_before, jnp.exp(cumulative), 0.0)
        tail = jnp.where(seg_row == seg_end, jnp.exp(last - cumulative), 0.0)
        entering.append(enter)
        tailing.append(tail)
        chunk_decay.append(enter[:, Q - 1 : Q])
        seg_col = segment(start + iota((Q, Q), 0))
        seg_lane = segment(start + iota((Q, Q), 1))
        keep = (seg_col == seg_lane) & (iota((Q, Q), 0) >= iota((Q, Q), 1))
        r.mask[c] = jnp.where(keep, 0.0, -1e30)
        high = cumulative.astype(bf).astype(f32)
        middle = (cumulative - high).astype(bf).astype(f32)
        rest = cumulative - high - middle
        which = iota((16, Q), 0)
        for h in range(H):
            parts = jnp.where(
                which % 3 == 0,
                high[h : h + 1],
                jnp.where(which % 3 == 1, middle[h : h + 1], rest[h : h + 1]),
            )
            first = which < 3
            second = (which >= 3) & (which < 6)
            r.cum_left[h, :, cols] = jnp.where(
                first, parts, jnp.where(second, 1.0, 0.0)
            ).astype(bf)
            r.cum_right[h, :, cols] = jnp.where(
                first, 1.0, jnp.where(second, -parts, 0.0)
            ).astype(bf)

    def wide(v):
        return dg(split3(v), expand, 0, 0)

    def wide_rows(v):
        return dg(expand, split3(jnp.broadcast_to(v, (H, LANES))), 0, 0)

    for c in range(NC):
        rows = slice(c * Q, c * Q + Q)
        r.step_wide[rows, :] = wide(step[:, rows])
        r.enter_wide[rows, :] = wide(entering[c])
        r.tail_wide[rows, :] = wide(tailing[c])
        r.decay_wide[c] = wide_rows(chunk_decay[c])
    r.skip_wide[...] = dg(split3(jnp.broadcast_to(column(r.skip_scale), (H, 8))), expand, 0, 0)

    def scaled_rows(i, _):
        rows = pl.ds(pl.multiple_of(i * ROWS, ROWS), ROWS)
        x = r.act[rows, :].astype(f32)
        r.xt[rows, :], r.xt_rest[rows, :] = halves(x * r.step_wide[rows, :] * r.tail_wide[rows, :])
        return 0

    lax.fori_loop(0, T // ROWS, scaled_rows, 0)

    stage("decay_matrices")

    def decay_matrix(i, _):
        c = i // H
        h = i % H
        rows = pl.ds(pl.multiple_of(c * Q, Q), Q)
        difference = dg(r.cum_left[h, :, rows], r.cum_right[h, :, rows], 0, 0)
        r.decays[c, h] = jnp.exp(difference + r.mask[c])
        return 0

    lax.fori_loop(0, NC * H, decay_matrix, 0)

    stage("keys_wait")
    state_wait()
    shards = n_tp // 2
    half_low = iota((T // 2, LANES), 1) < NS
    for ref, at in ((r.keys, 0), (r.queries, shards)):
        one, two = r.state_recv[at].astype(f32), r.state_recv[at + 1].astype(f32)
        ref[0 : T // 2, :] = jnp.where(half_low, one, pltpu.roll(two, NS, 1)).astype(bf)
        ref[T // 2 : T, :] = jnp.where(half_low, pltpu.roll(one, NS, 1), two).astype(bf)

    stage("end_states")
    end_state = None
    device_decay = None
    for c in range(NC):
        rows = slice(c * Q, c * Q + Q)
        keys = r.keys[rows, :]
        fresh = dg(r.xt[rows, :], keys, 0, 0) + dg(r.xt_rest[rows, :], keys, 0, 0)
        r.fresh[c] = fresh
        end_state = fresh if c == 0 else r.decay_wide[c] * end_state + fresh
        device_decay = chunk_decay[c] if c == 0 else device_decay * chunk_decay[c]
    r.end_send[...] = end_state
    r.decay_send[...] = jnp.broadcast_to(device_decay, (H, LANES))

    def block(ref, device):
        return ref.at[pl.ds(pl.multiple_of(device * R, R), R)]

    r.end_recv[seq] = r.end_send[pl.ds(pl.multiple_of(seq * R, R), R), :]
    r.decay_recv[seq] = r.decay_send[...]
    decay_wait = spread(
        "seq", lambda d: r.decay_send, lambda d: r.decay_recv.at[d], r.decay_ss, r.decay_rs
    )
    end_wait = spread(
        "seq", lambda d: block(r.end_send, d), lambda d: r.end_recv.at[d], r.end_ss, r.end_rs
    )

    stage("inside")
    for c in range(NC):
        rows = slice(c * Q, c * Q + Q)
        r.scores[c] = dg(r.queries[rows, :], r.keys[rows, :], 1, 1)
    low = iota((Q, LANES), 1) < P_

    def inside(i, _):
        c = i // NP
        p = i % NP
        rows = pl.ds(pl.multiple_of(c * Q, Q), Q)
        lanes = pl.ds(pl.multiple_of(p * LANES, LANES), LANES)
        x = r.act[rows, lanes]
        zero = jnp.zeros_like(x)
        result = None
        for s in range(2):
            h = 2 * p + s
            stepped = r.decays[c, h] * r.step_rows[pl.ds(h, 1), rows]
            weight, rest = halves(stepped * r.scores[c])
            part = jnp.where(low, x, zero) if s == 0 else jnp.where(low, zero, x)
            term = dg(weight, part, 1, 0) + dg(rest, part, 1, 0)
            result = term if s == 0 else result + term
        r.mixed[rows, lanes] = result
        return 0

    lax.fori_loop(0, NC * NP, inside, 0)
    for j in range(HI // 256):
        cols = slice(256 * j, 256 * j + 256)
        if j == 0:
            loads["out_weight"].wait()
            loads["out_cotangent"].wait()
        r.norm_grad[:, cols] = dg(r.out_cotangent[...], r.out_weight[cols, :], 1, 1)

    stage("entering")
    head_of = (seq * R) // P_
    stage("end_wait")
    end_wait()
    decay_wait()

    def decay_of(d):
        return jnp.broadcast_to(r.decay_recv[d, pl.ds(head_of, 1), :], (R, LANES))

    running = jnp.zeros((R, N), f32)
    for d in range(n_seq):
        r.enter_send[d] = running
        running = decay_of(d) * running + r.end_recv[d]
    own_rows = pl.ds(pl.multiple_of(seq * R, R), R)
    r.enter_state[own_rows, :] = r.enter_send[seq]
    enter_wait = spread(
        "seq", lambda d: r.enter_send.at[d], lambda d: block(r.enter_state, d), r.enter_ss, r.enter_rs
    )
    stage("turned_weights")

    def turned_weight(i, _):
        c = i // H
        h = i % H
        r.turned[c, h] = (r.decays[c, h] * r.scores[c]).T.astype(bf)
        return 0

    lax.fori_loop(0, NC * H, turned_weight, 0)
    stage("enter_wait")
    enter_wait()
    stage("readout")
    for c in range(NC):
        rows = slice(c * Q, c * Q + Q)
        if c == 0:
            state = r.enter_state[...]
        else:
            state = r.decay_wide[c - 1] * state + r.fresh[c - 1]
        r.state_in[c] = state
        r.state_in_low[c], r.state_in_rest[c] = halves(state)
        for j in range(HI // 256):
            cols = slice(256 * j, 256 * j + 256)
            queries = r.queries[rows, :]
            read = dg(queries, r.state_in_low[c, cols, :], 1, 1) + dg(queries, r.state_in_rest[c, cols, :], 1, 1)
            r.mixed[rows, cols] = r.mixed[rows, cols] + r.enter_wide[rows, cols] * read

    stage("gated")
    skip_row = r.skip_wide[0:1, :]
    r.gain_row[...] = r.gate_gain[...].reshape(1, HI)

    def gated_rows(i, _):
        rows = pl.ds(pl.multiple_of(i * ROWS, ROWS), ROWS)
        heads = r.mixed[rows, :] + skip_row * r.act[rows, :].astype(f32)
        gate = r.gate_pre[rows, :]
        gated = heads * (gate * jax.nn.sigmoid(gate))
        r.gated[rows, :] = gated
        scaled = r.norm_grad[rows, :] * r.gain_row[...]
        squares = gated * gated
        products = scaled * gated

        def lane_sum(v):
            total = v[:, :LANES]
            for g in range(1, NP):
                total = total + v[:, g * LANES : g * LANES + LANES]
            return total

        r.squares[rows, :] = lane_sum(squares)
        r.products[rows, :] = lane_sum(products)
        return 0

    lax.fori_loop(0, T // ROWS, gated_rows, 0)
    square_row = jnp.sum(r.squares[...].T, axis=0, keepdims=True)
    product_row = jnp.sum(r.products[...].T, axis=0, keepdims=True)
    spans = T // LANES
    tile_row = iota((2 * spans, LANES), 0)
    packed_sums = jnp.zeros((2 * spans, LANES), f32)
    for k in range(spans):
        lanes = slice(k * LANES, k * LANES + LANES)
        for at, row in ((k, square_row), (spans + k, product_row)):
            packed_sums = jnp.where(
                tile_row == at, jnp.broadcast_to(row[:, lanes], (2 * spans, LANES)), packed_sums
            )
    r.sums_send[...] = packed_sums
    r.sums_recv[tp] = r.sums_send[...]
    sums_wait = spread(
        "tp", lambda t: r.sums_send, lambda t: r.sums_recv.at[t], r.sums_ss, r.sums_rs
    )
    stage("sums_wait")
    sums_wait()
    stage("sums")
    sums = r.sums_recv[0]
    for t in range(1, n_tp):
        sums = sums + r.sums_recv[t]
    count = HI * n_tp
    squares = jnp.concatenate([sums[k : k + 1] for k in range(spans)], axis=1)
    products = jnp.concatenate([sums[spans + k : spans + k + 1] for k in range(spans)], axis=1)
    norm_row = lax.rsqrt(squares / count + epsilon)
    back_row = norm_row * norm_row * norm_row * (products / count)
    r.norm_col[...] = jnp.broadcast_to(norm_row, (LANES, T)).T
    r.back_col[...] = jnp.broadcast_to(back_row, (LANES, T)).T

    stage("back_gated")
    r.head_sum[...] = (iota((HI, LANES), 0) // P_ == iota((HI, LANES), 1)).astype(f32).astype(bf)
    r.sum_acc[...] = jnp.zeros_like(r.sum_acc)

    def tile4(v):
        return jnp.concatenate([v] * NP, axis=1)

    def summed(v, which):
        high, lowv = halves(v)
        return dg(high, which, 1, 0) + dg(lowv, which, 1, 0)

    def gated_norm_rows(i, _):
        rows = pl.ds(pl.multiple_of(i * ROWS, ROWS), ROWS)
        unit = r.gated[rows, :] * tile4(r.norm_col[rows, :])
        r.gated_norm[rows, :] = (unit * r.gain_row[...]).astype(bf)
        return 0

    lax.fori_loop(0, T // ROWS, gated_norm_rows, 0)
    stage("out_projection")
    for j in range(D // 256):
        value = dg(r.gated_norm[...], r.out_weight[:, 256 * j : 256 * j + 256], 1, 0).astype(bf)
        for k in range(256 // fold_width[0]):
            at = j * (256 // fold_width[0]) + k
            r.branch[at] = value[:, k * fold_width[0] : (k + 1) * fold_width[0]]
            fold_start(0, at)
    stage("back_rows")

    def back_rows(i, _):
        rows = pl.ds(pl.multiple_of(i * ROWS, ROWS), ROWS)
        norm = tile4(r.norm_col[rows, :])
        back = tile4(r.back_col[rows, :])
        gated = r.gated[rows, :]
        grad = r.norm_grad[rows, :]
        gain = r.gain_row[...]
        gate = r.gate_pre[rows, :]
        sigma = jax.nn.sigmoid(gate)
        unit = gated * norm
        r.sum_acc[0] = r.sum_acc[0] + fold8(grad * unit)
        gated_grad = norm * (grad * gain) - gated * back
        heads_grad = gated_grad * (gate * sigma)
        heads = r.mixed[rows, :] + skip_row * r.act[rows, :].astype(f32)
        r.gate_grad[rows, :] = (
            gated_grad * heads * (sigma * (1.0 + gate * (1.0 - sigma)))
        ).astype(bf)
        r.heads_grad[rows, :] = heads_grad
        x = r.act[rows, :].astype(f32)
        r.sum_acc[1] = r.sum_acc[1] + fold8(heads_grad * x)
        r.dy[rows, :], r.dy_rest[rows, :] = halves(heads_grad)
        r.dy_enter[rows, :], r.dy_enter_rest[rows, :] = halves(heads_grad * r.enter_wide[rows, :])
        r.sum_y[rows, :] = summed(heads_grad * r.mixed[rows, :], r.head_sum[...])
        return 0

    lax.fori_loop(0, T // ROWS, back_rows, 0)

    stage("grad_states")
    grad_in = None
    for c in reversed(range(NC)):
        rows = slice(c * Q, c * Q + Q)
        queries = r.queries[rows, :]
        local = dg(r.dy_enter[rows, :], queries, 0, 0) + dg(r.dy_enter_rest[rows, :], queries, 0, 0)
        r.grad_local[c] = local
        grad_in = local if grad_in is None else r.decay_wide[c] * grad_in + local
    r.grad_send[...] = grad_in
    r.grad_recv[seq] = r.grad_send[own_rows, :]
    grad_wait = spread(
        "seq", lambda d: block(r.grad_send, d), lambda d: r.grad_recv.at[d], r.grad_ss, r.grad_rs
    )
    stage("inside_back")
    r.score_grad[...] = jnp.zeros_like(r.score_grad)

    def inside_back(i, _):
        c = i // NP
        p = i % NP
        rows = pl.ds(pl.multiple_of(c * Q, Q), Q)
        lanes = pl.ds(pl.multiple_of(p * LANES, LANES), LANES)
        x = r.act[rows, lanes]
        dy = r.dy[rows, lanes]
        dy_rest = r.dy_rest[rows, lanes]
        zero = jnp.zeros_like(dy)
        x_turned, dy_turned = pltpu.roll(x, P_, 1), pltpu.roll(dy_rest, P_, 1)
        result = None
        for s in range(2):
            h = 2 * p + s
            ours = low if s == 0 else jnp.logical_not(low)
            pairs = dg(jnp.where(ours, dy, dy_turned), jnp.where(ours, x, x_turned), 1, 1)
            r.score_grad[c] = r.score_grad[c] + pairs * (r.decays[c, h] * r.step_rows[pl.ds(h, 1), rows])
            term = dg(r.turned[c, h], jnp.where(ours, dy, zero), 1, 0)
            result = term if s == 0 else result + term
        r.x_inside[rows, lanes] = result
        return 0

    lax.fori_loop(0, 4, inside_back, 0)
    fold_in(0, 0)
    lax.fori_loop(4, 7, inside_back, 0)
    fold_in(0, 1)
    lax.fori_loop(7, NC * NP, inside_back, 0)

    stage("poll_at_grad_wait")
    stage("grad_wait")
    grad_wait()
    stage("leave_scan")
    running = jnp.zeros((R, N), f32)
    for d in reversed(range(n_seq)):
        r.leave_send[d] = running
        running = decay_of(d) * running + r.grad_recv[d]
    r.leave_grad[own_rows, :] = r.leave_send[seq]
    leave_wait = spread(
        "seq", lambda d: r.leave_send.at[d], lambda d: block(r.leave_grad, d), r.leave_ss, r.leave_rs
    )

    stage("query_grad")
    for c in range(NC):
        rows = slice(c * Q, c * Q + Q)
        score_low, score_rest = halves(r.score_grad[c])
        r.query_grad[rows, :] = (
            dg(score_low, r.keys[rows, :], 1, 0)
            + dg(score_rest, r.keys[rows, :], 1, 0)
            + dg(r.dy_enter[rows, :], r.state_in_low[c], 1, 0)
            + dg(r.dy_enter_rest[rows, :], r.state_in_low[c], 1, 0)
            + dg(r.dy_enter[rows, :], r.state_in_rest[c], 1, 0)
        )

    def shared_copy(d, arriving=False):
        target = (tp + d) % n_tp
        slot = (tp + n_tp - d) % n_tp if arriving else tp
        sems = (r.shared_ss.at[d - 1], r.shared_rs.at[d - 1])
        return remote(r.shared_send.at[target], r.shared_recv.at[slot], *sems, (seq, target))

    def pack_shared(ref, group):
        top, bottom = ref[0 : T // 2, :], ref[T // 2 : T, :]
        at = group * shards
        r.shared_send[at] = jnp.where(half_low, top, pltpu.roll(bottom, NS, 1)).astype(bf)
        r.shared_send[at + 1] = jnp.where(half_low, pltpu.roll(top, NS, 1), bottom).astype(bf)

        @pl.when(tp // shards == group)
        def _():
            r.shared_recv[tp] = r.shared_send[tp]

        for d in range(1, n_tp):
            pl.when((tp + d) % n_tp // shards == group)(shared_copy(d).start)

    pack_shared(r.query_grad, 1)
    stage("poll_at_weights_one")
    fold_in(0, 2)
    stage("weights_one")
    def weight_rows(i, _):
        cols = pl.ds(pl.multiple_of(i * LANES, LANES), LANES)
        r.wg_one[cols, 0:HI] = dg(r.normed[:, cols], r.gate_grad[...], 0, 0).astype(bf)
        r.wg_one[cols, HI : 2 * HI] = dg(r.out_cotangent[:, cols], r.gated_norm[...], 0, 0).astype(bf)
        return 0

    lax.fori_loop(0, D // LANES, weight_rows, 0)

    chips = n_seq // 2
    core = seq % 2
    chip = seq // 2
    sibling = seq + 1 - 2 * core

    def pair_copy(k, q):
        rows = pl.ds(pl.multiple_of((2 * q + 1 - core) * R2, R2), R2)
        source, target = ((r.wg_one, r.pair_one), (r.wg_two, r.pair_two))[k]
        return remote(
            source.at[rows], target.at[q], r.pair_ss.at[k, q], r.pair_rs.at[k, q], (sibling, tp)
        )

    def chip_copy(k, d, arriving=False):
        to = (chip + d) % chips
        slot = (chip + chips - d) % chips if arriving else chip
        source, target = ((r.chip_one_send, r.chip_one), (r.chip_two_send, r.chip_two))[k]
        return remote(
            source.at[to],
            target.at[slot],
            r.chip_ss.at[k, d - 1],
            r.chip_rs.at[k, d - 1],
            (2 * to + core, tp),
        )

    def pair_start(k):
        for q in range(chips):
            pair_copy(k, q).start()

    def chip_start(k):
        own, pair, send, kept = (
            (r.wg_one, r.pair_one, r.chip_one_send, r.chip_one),
            (r.wg_two, r.pair_two, r.chip_two_send, r.chip_two),
        )[k]
        for q in range(chips):
            rows = pl.ds(pl.multiple_of((2 * q + core) * R2, R2), R2)
            pair_copy(k, q).wait_recv()
            send[q] = (own[rows, :].astype(f32) + pair[q].astype(f32)).astype(bf)
        for d in range(1, chips):
            chip_copy(k, d).start()
        kept[chip] = send[chip]

    def chip_sum(k):
        kept = (r.chip_one, r.chip_two)[k]
        for d in range(1, chips):
            chip_copy(k, d, True).wait_recv()
        value = kept[0].astype(f32)
        for q in range(1, chips):
            value = value + kept[q].astype(f32)
        for q in range(chips):
            pair_copy(k, q).wait_send()
        for d in range(1, chips):
            chip_copy(k, d).wait_send()
        return value

    pair_start(0)
    stage("poll_at_leave_wait")
    fold_middle(0, 0)
    fold_in(0, 3)
    stage("leave_wait")
    leave_wait()
    stage("leave")
    carry_terms = [None] * NC
    for c in reversed(range(NC)):
        rows = slice(c * Q, c * Q + Q)
        if c == NC - 1:
            grad = r.leave_grad[...]
        else:
            grad = r.decay_wide[c + 1] * grad + r.grad_local[c + 1]
        grad_low, grad_rest = halves(grad)
        keys, queries = r.keys[rows, :], r.queries[rows, :]
        for j in range(HI // 256):
            cols = slice(256 * j, 256 * j + 256)
            read = dg(keys, grad_low[cols, :], 1, 1) + dg(keys, grad_rest[cols, :], 1, 1)
            r.x_carry[rows, cols] = r.tail_wide[rows, cols] * read
        high, lowv = halves(grad * r.state_in[c])
        pair = dg(expand[0:H], high, 1, 0) + dg(expand[0:H], lowv, 1, 0)
        carry_terms[c] = chunk_decay[c] * jnp.sum(pair, axis=1, keepdims=True)
        score_low, score_rest = halves(r.score_grad[c])
        r.key_grad[rows, :] = (
            dg(score_low, queries, 0, 0)
            + dg(score_rest, queries, 0, 0)
            + dg(r.xt[rows, :], grad_low, 1, 0)
            + dg(r.xt_rest[rows, :], grad_low, 1, 0)
            + dg(r.xt[rows, :], grad_rest, 1, 0)
        )

    pack_shared(r.key_grad, 0)
    stage("poll_at_chip_one")
    fold_middle(0, 1)
    stage("after_keys")
    stage("poll_at_x_grads")
    fold_in(0, 4)
    fold_middle(0, 2)
    stage("x_grads")
    r.head_sum_two[...] = (
        iota((HI, LANES), 0) // P_ + H == iota((HI, LANES), 1)
    ).astype(f32).astype(bf)
    r.head_sum_three[...] = (
        iota((HI, LANES), 0) // P_ + 2 * H == iota((HI, LANES), 1)
    ).astype(f32).astype(bf)

    def x_rows(i, _):
        rows = pl.ds(pl.multiple_of(i * ROWS, ROWS), ROWS)
        x = r.act[rows, :].astype(f32)
        z = r.x_inside[rows, :]
        carried = r.x_carry[rows, :]
        both = z + carried
        step_rows = r.step_wide[rows, :]
        xs = x * step_rows
        x_grad = step_rows * both + skip_row * r.heads_grad[rows, :]
        conv_grad = x_grad * slope(r.inner_conv[rows, :])
        for g in range(NP):
            r.grad_ext[g, rows, :] = conv_grad[:, g * LANES : g * LANES + LANES]
        r.sum_x[rows, :] = (
            summed(x * both, r.head_sum[...])
            + summed(xs * carried, r.head_sum_two[...])
            + summed(xs * z, r.head_sum_three[...])
        )
        return 0

    lax.fori_loop(0, T // ROWS, x_rows, 0)
    halo_one = remote(
        r.grad_ext.at[:, pl.ds(0, PAD)],
        r.grad_ext.at[:, pl.ds(T, PAD)],
        r.halo_send.at[0],
        r.halo_recv.at[0],
        left,
    )
    halo_one.start()
    waits.append(halo_one)

    sums_y = r.sum_y[...].T
    sums_x = r.sum_x[...].T
    step_grad = sums_x[0:H]
    tail_part = sums_x[H : 2 * H]
    pair_part = sums_y[0:H] - sums_x[2 * H : 3 * H]
    decay_grads = []
    for c in range(NC):
        cols = slice(c * Q, c * Q + Q)
        suffix = fold3(dg(split3(pair_part[:, cols]), r.upto[...], 1, 1))
        before = fold3(dg(split3(tail_part[:, cols]), r.upto[...], 1, 0)) - tail_part[:, cols]
        decay_grads.append(suffix + before + carry_terms[c])
    decay_grad = jnp.concatenate(decay_grads, axis=1)
    step_total = step_grad - rate * decay_grad
    step_pre_grad = step_total * r.sigmoid_step[...]
    rate_sum = jnp.sum(r.log_decay[...] * decay_grad, axis=1, keepdims=True)
    bias_sum = jnp.sum(step_pre_grad, axis=1, keepdims=True)
    step_cols = jnp.concatenate(
        [jnp.zeros((NS, T), f32), step_pre_grad, jnp.zeros((LANES - NS - H, T), f32)], axis=0
    ).T

    stage("poll_at_conv_back")
    fold_in(0, 5)
    fold_middle(0, 3)
    stage("conv_back")
    def after_masks(base):
        position = first_token + base + iota((ROWS, LANES), 0)
        now = segment(position)
        masks = []
        for k in range(CONV - 1):
            later = position + (CONV - 1) - k
            masks.append((segment(later) == now) & (later < total_tokens))
        return masks

    def conv_back(ext, taps, base, lanes, masks):
        value = None
        for k in range(CONV):
            term = taps[k : k + 1, lanes] * ext[pl.ds(base + CONV - 1 - k, ROWS), :]
            if k < CONV - 1:
                term = jnp.where(masks[k], term, 0.0)
            value = term if value is None else value + term
        return value

    def tap_sums(ext, grad, base, masks):
        sums = []
        for k in range(CONV):
            term = grad * ext[pl.ds(base + PAD - CONV + 1 + k, ROWS), :]
            sums.append(fold8(term if k == CONV - 1 else jnp.where(masks[k], term, 0.0)))
        return sums + [fold8(grad)]

    stage("inner_back")

    def inner_back_rows(i, _):
        base = pl.multiple_of(i * ROWS, ROWS)
        rows = pl.ds(base, ROWS)
        masks = after_masks(base)
        before = agreements(base, ROWS)
        taps = r.inner_kernel[...]
        for g in range(NP):
            lanes = slice(g * LANES, g * LANES + LANES)
            r.inner_grad[rows, lanes] = conv_back(r.grad_ext.at[g], taps, base, lanes, masks).astype(bf)
            found = tap_sums(r.inner_ext.at[g], r.grad_ext[g, rows, :], base, before)
            for k, v in enumerate(found):
                r.sum_acc[2 + k, :, lanes] = r.sum_acc[2 + k, :, lanes] + v
        return 0

    lax.fori_loop(0, T // ROWS - 1, inner_back_rows, 0)
    stage("poll_at_halo_one_wait")
    fold_in(0, 6)
    fold_middle(0, 4)
    stage("halo_one_wait")
    halo_one.wait_recv()
    stage("inner_back_last")
    inner_back_rows(T // ROWS - 1, 0)

    stage("poll_at_shared_wait")
    fold_middle(0, 5)
    fold_in(0, 7)
    stage("shared_wait")
    for d in range(1, n_tp):
        shared_copy(d, True).wait_recv()
    stage("shared_use")
    packed = r.shared_recv[0].astype(f32)
    for t in range(1, n_tp):
        packed = packed + r.shared_recv[t].astype(f32)
    r.state_grad_ext[0 : T // 2, :] = packed * slope(r.misc_conv[0 : T // 2, :])
    r.state_grad_ext[T // 2 : T, :] = pltpu.roll(packed, NS, 1) * slope(r.misc_conv[T // 2 : T, :])
    halo_two = remote(
        r.state_grad_ext.at[pl.ds(0, PAD)],
        r.state_grad_ext.at[pl.ds(T, PAD)],
        r.halo_send.at[1],
        r.halo_recv.at[1],
        left,
    )
    halo_two.start()
    waits.append(halo_two)
    stage("chip_one")
    chip_start(0)
    stage("poll_at_misc_back")
    fold_middle(0, 6)
    stage("misc_back")
    r.misc_acc[...] = jnp.zeros_like(r.misc_acc)
    r.step_cols[...] = step_cols

    def misc_back_rows(i, _):
        base = pl.multiple_of(i * ROWS, ROWS)
        rows = pl.ds(base, ROWS)
        masks = after_masks(base)
        before = agreements(base, ROWS)
        taps = r.misc_taps[...]
        lanes = slice(0, LANES)
        value = conv_back(r.state_grad_ext, taps, base, lanes, masks)
        value = jnp.where(iota((ROWS, LANES), 1) < NS, value, r.step_cols[rows, :])
        r.misc_grad[rows, :] = value.astype(bf)
        found = tap_sums(r.misc_ext.at[0], r.state_grad_ext[rows, :], base, before)
        for k, v in enumerate(found):
            r.misc_acc[k] = r.misc_acc[k] + v
        return 0

    lax.fori_loop(0, T // ROWS - 1, misc_back_rows, 0)
    stage("halo_two_wait")
    halo_two.wait_recv()
    stage("misc_back_last")
    misc_back_rows(T // ROWS - 1, 0)

    stage("poll_at_normed_grad")
    stage("normed_grad")
    width, tall = fold_width[1], fold_rows[1]
    for j in range(D // 256):
        cols = slice(256 * j, 256 * (j + 1))
        value = (
            dg(r.gate_grad[...], r.gate_weight[cols, :], 1, 1)
            + dg(r.inner_grad[...], r.inner_weight[cols, :], 1, 1)
            + dg(r.misc_grad[...], r.misc_weight[:, cols], 1, 0)
        )
        value_low = value.astype(bf)
        for k in range(256 // width):
            for m in range(T // tall):
                at = (j * (256 // width) + k) * (T // tall) + m
                r.normed_part[at] = value_low[m * tall : m * tall + tall, k * width : k * width + width]
                fold_start(1, at)
        hats = r.block_input[:, cols].astype(f32) * jnp.concatenate([r.inverse[...]] * 2, axis=1)
        r.gain_part[:, cols] = fold8(value * hats)

    stage("poll_at_small_sums")
    fold_middle(0, 7)
    stage("small_sums")

    def row_of(v):
        return jnp.sum(v, axis=0, keepdims=True)

    eye_wide = iota((H, LANES), 0) == iota((H, LANES), 1)

    def lanes_of(v):
        return row_of(jnp.where(eye_wide, jnp.broadcast_to(v, (H, LANES)), 0.0))

    r.small_send[...] = jnp.zeros_like(r.small_send)
    for k in range(CONV + 1):
        r.small_send[k : k + 1, :] = row_of(r.sum_acc[2 + k])
    r.small_send[5:6, :] = row_of(r.sum_acc[0])
    r.small_send[6:7, :] = row_of(r.sum_acc[1])
    for k in range(CONV):
        r.small_send[7:8, k * LANES : k * LANES + LANES] = row_of(r.misc_acc[k])
    r.small_send[8:9, 0:LANES] = row_of(r.misc_acc[CONV])
    r.small_send[8:9, LANES : 2 * LANES] = lanes_of(bias_sum)
    r.small_send[8:9, 2 * LANES : 3 * LANES] = lanes_of(rate_sum)
    gain_rows = row_of(r.gain_part[...])
    for k in range(D // HI):
        r.small_send[9 + k : 10 + k, :] = gain_rows[:, k * HI : k * HI + HI]
    r.small_recv[seq] = r.small_send[...]
    small_wait = spread(
        "seq", lambda d: r.small_send, lambda d: r.small_recv.at[d], r.small_ss, r.small_rs
    )
    stage("weights_two")

    def weight_rows_two(i, _):
        cols = pl.ds(pl.multiple_of(i * LANES, LANES), LANES)
        r.wg_two[cols, 0:HI] = dg(r.normed[:, cols], r.inner_grad[...], 0, 0).astype(bf)
        r.wg_two[cols, HI : HI + LANES] = dg(r.normed[:, cols], r.misc_grad[...], 0, 0).astype(bf)
        return 0

    lax.fori_loop(0, D // LANES // 2, weight_rows_two, 0)
    fold_in(1, 0)
    lax.fori_loop(D // LANES // 2, D // LANES, weight_rows_two, 0)
    pair_start(1)
    stage("folds")
    last = fold_pieces[1]
    for j in range(last + 2):
        if 0 < j < last:
            fold_in(1, j)
        if j > 1:
            fold_middle(1, j - 2)
        if j == 2:
            chip_start(1)
        if j == 10:
            small_wait()
            total = r.small_recv[0]
            for d in range(1, n_seq):
                total = total + r.small_recv[d]
            r.small_total[...] = total
            r.gain_recv[tp] = r.small_total[8:16, :]
            gain_wait = spread(
                "tp",
                lambda t: r.small_total.at[pl.ds(8, 8)],
                lambda t: r.gain_recv.at[t],
                r.gain_ss,
                r.gain_rs,
            )
    for j in range(fold_pieces[0]):
        fold_end(0, j)
    stage("weight_sums")
    r.sum_one[...] = chip_sum(0)
    r.sum_two[...] = chip_sum(1)
    gain_wait()
    gains = r.gain_recv[0]
    for t in range(1, n_tp):
        gains = gains + r.gain_recv[t]
    r.gain_total[...] = gains
    stage("folds_last")
    for j in range(fold_pieces[1]):
        fold_end(1, j)
    stage("drain")
    for d in range(1, n_tp):
        shared_copy(d).wait_send()
    for copy in waits:
        copy.wait_send()
    marks.close()


def finish(sizes, names, *refs):
    r = types.SimpleNamespace(**dict(zip(names, refs)))
    T, D, HI, H, NS = sizes
    P_ = HI // H
    T = r.block_input.shape[0]

    def final_rows(i, _):
        rows = pl.ds(pl.multiple_of(i * ROWS, ROWS), ROWS)
        x = r.block_input[rows, :].astype(f32)
        r.block_output[rows, :] = (x + r.branch_sum[rows, :].astype(f32)).astype(bf)
        inverse = lax.rsqrt(jnp.mean(x * x, axis=1, keepdims=True) + epsilon)
        hat = x * inverse
        hat_grad = r.normed_sum[rows, :].astype(f32) * r.input_gain[...].reshape(1, D)
        mean = jnp.mean(hat_grad * hat, axis=1, keepdims=True)
        r.input_grad[rows, :] = r.out_cotangent[rows, :].astype(f32) + inverse * (
            hat_grad - hat * mean
        )
        return 0

    lax.fori_loop(0, T // ROWS, final_rows, 0)
    @pl.when(pl.program_id(0) == 0)
    def _():
        r.gate_weight_grad[...] = r.sum_one[:, 0:HI]
        r.out_weight_grad[...] = r.sum_one[:, HI : 2 * HI].T
        r.inner_weight_grad[...] = r.sum_two[:, 0:HI]
        narrow = r.sum_two[:, HI : HI + LANES].T
        r.state_weight_grad[...] = narrow[0:NS]
        r.step_weight_grad[...] = narrow[NS : NS + H]
        small = r.small_total
        r.inner_kernel_grad[...] = small[0:CONV, :]
        r.inner_conv_bias_grad[...] = small[CONV : CONV + 1, :].reshape(HI)
        r.gate_gain_grad[...] = small[5:6, :].reshape(HI)
        head_sum = (iota((HI, LANES), 0) // P_ == iota((HI, LANES), 1)).astype(f32).astype(bf)
        skip_sums = fold3(dg(split3(jnp.broadcast_to(small[6:7, :], (8, HI))), head_sum, 1, 0))
        r.skip_scale_grad[...] = skip_sums[0:1, 0:H].reshape(H)
        for k in range(CONV):
            r.state_kernel_grad[k : k + 1, :] = small[7:8, k * LANES : k * LANES + NS]
        r.state_conv_bias_grad[...] = small[8:9, 0:NS].reshape(NS)
        r.step_bias_grad[...] = small[8:9, LANES : LANES + H].reshape(H)
        r.rate_log_grad[...] = small[8:9, 2 * LANES : 2 * LANES + H].reshape(H)
        for k in range(D // HI):
            r.input_gain_grad[k * HI : k * HI + HI] = r.gain_total[1 + k : 2 + k, :].reshape(HI)


INPUTS = (
    "block_input",
    "scene_lengths",
    "input_gain",
    "gate_weight",
    "inner_weight",
    "state_weight",
    "step_weight",
    "step_bias",
    "rate_log",
    "inner_kernel",
    "inner_conv_bias",
    "state_kernel",
    "state_conv_bias",
    "skip_scale",
    "gate_gain",
    "out_weight",
    "out_cotangent",
)
OUTPUTS = (
    "block_output",
    "input_grad",
    "input_gain_grad",
    "gate_weight_grad",
    "inner_weight_grad",
    "state_weight_grad",
    "step_weight_grad",
    "step_bias_grad",
    "rate_log_grad",
    "inner_kernel_grad",
    "inner_conv_bias_grad",
    "state_kernel_grad",
    "state_conv_bias_grad",
    "skip_scale_grad",
    "gate_gain_grad",
    "out_weight_grad",
)


SUMS = ("branch_sum", "normed_sum", "sum_one", "sum_two", "small_total", "gain_total")


def local(*args):
    given = dict(zip(INPUTS, args))
    given["state_weight"] = given["state_weight"].T
    given["step_weight"] = given["step_weight"].T
    n_seq = lax.axis_size("seq")
    n_tp = lax.axis_size("tp")
    T, D = given["block_input"].shape
    HI = given["gate_weight"].shape[1]
    H = given["step_bias"].shape[0]
    NS = given["state_weight"].shape[0]
    N = STATE
    Q = CHUNK
    NC = T // Q
    NP = HI // LANES
    R = HI // n_seq
    R2 = D // n_seq
    outs = (
        ((T, D), bf),
        ((T, D), f32),
        ((D,), f32),
        ((R2, HI), f32),
        ((R2, HI), f32),
        ((NS, R2), f32),
        ((H, R2), f32),
        ((H,), f32),
        ((H,), f32),
        ((CONV, HI), f32),
        ((HI,), f32),
        ((CONV, NS), f32),
        ((NS,), f32),
        ((H,), f32),
        ((HI,), f32),
        ((HI, R2), f32),
    )
    sums = (
        ((T, D), bf),
        ((T, D), bf),
        ((R2, 2 * HI), f32),
        ((R2, HI + LANES), f32),
        ((16, HI), f32),
        ((8, HI), f32),
    )
    scratch = dict(
        inverse=((T, LANES), f32),
        normed=((T, D), bf),
        misc_weight=((LANES, D), bf),
        inner_ext=((NP, T + PAD, LANES), f32),
        misc_ext=((1, T + PAD, LANES), f32),
        gate_pre=((T, HI), f32),
        misc_taps=((8, LANES), f32),
        inner_bias=((1, HI), f32),
        gain_row=((1, HI), f32),
        misc_conv=((T, LANES), f32),
        inner_conv=((T, HI), f32),
        act=((T, HI), bf),
        state_send=((T // 2, LANES), bf),
        state_recv=((n_tp, T // 2, LANES), bf),
        keys=((T, N), bf),
        queries=((T, N), bf),
        sigmoid_step=((H, T), f32),
        step_rows=((H, T), f32),
        log_decay=((H, T), f32),
        upto=((Q, Q), bf),
        expand=((3 * H, HI), bf),
        mask=((NC, Q, Q), f32),
        cum_left=((H, 16, T), bf),
        cum_right=((H, 16, T), bf),
        step_wide=((T, HI), f32),
        enter_wide=((T, HI), f32),
        tail_wide=((T, HI), f32),
        decay_wide=((NC, HI, LANES), f32),
        skip_wide=((8, HI), f32),
        xt=((T, HI), bf),
        xt_rest=((T, HI), bf),
        fresh=((NC, HI, N), f32),
        end_send=((HI, N), f32),
        end_recv=((n_seq, R, N), f32),
        decay_send=((H, LANES), f32),
        decay_recv=((n_seq, H, LANES), f32),
        enter_send=((n_seq, R, N), f32),
        enter_state=((HI, N), f32),
        state_in=((NC, HI, N), f32),
        state_in_low=((NC, HI, N), bf),
        state_in_rest=((NC, HI, N), bf),
        scores=((NC, Q, Q), f32),
        score_grad=((NC, Q, Q), f32),
        decays=((NC, H, Q, Q), f32),
        turned=((NC, H, Q, Q), bf),
        mixed=((T, HI), f32),
        norm_grad=((T, HI), f32),
        gated=((T, HI), f32),
        squares=((T, LANES), f32),
        products=((T, LANES), f32),
        sums_send=((2 * T // LANES, LANES), f32),
        sums_recv=((n_tp, 2 * T // LANES, LANES), f32),
        norm_col=((T, LANES), f32),
        back_col=((T, LANES), f32),
        head_sum=((HI, LANES), bf),
        head_sum_two=((HI, LANES), bf),
        head_sum_three=((HI, LANES), bf),
        sum_acc=((7, 8, HI), f32),
        gated_norm=((T, HI), bf),
        gate_grad=((T, HI), bf),
        heads_grad=((T, HI), f32),
        dy=((T, HI), bf),
        dy_rest=((T, HI), bf),
        dy_enter=((T, HI), bf),
        dy_enter_rest=((T, HI), bf),
        sum_y=((T, LANES), f32),
        sum_x=((T, LANES), f32),
        grad_local=((NC, HI, N), f32),
        grad_send=((HI, N), f32),
        grad_recv=((n_seq, R, N), f32),
        leave_send=((n_seq, R, N), f32),
        leave_grad=((HI, N), f32),
        x_inside=((T, HI), f32),
        x_carry=((T, HI), f32),
        wg_one=((D, 2 * HI), bf),
        pair_one=((n_seq // 2, R2, 2 * HI), bf),
        chip_one_send=((n_seq // 2, R2, 2 * HI), bf),
        chip_one=((n_seq // 2, R2, 2 * HI), bf),
        wg_two=((D, HI + LANES), bf),
        pair_two=((n_seq // 2, R2, HI + LANES), bf),
        chip_two_send=((n_seq // 2, R2, HI + LANES), bf),
        chip_two=((n_seq // 2, R2, HI + LANES), bf),
        query_grad=((T, N), f32),
        key_grad=((T, N), f32),
        shared_send=((n_tp, T // 2, LANES), bf),
        shared_recv=((n_tp, T // 2, LANES), bf),
        grad_ext=((NP, T + PAD, LANES), f32),
        state_grad_ext=((T + PAD, LANES), f32),
        inner_grad=((T, HI), bf),
        step_cols=((T, LANES), f32),
        misc_grad=((T, LANES), bf),
        misc_acc=((CONV + 1, 8, LANES), f32),
        normed_part=((16, T // 2, D // 8), bf),
        normed_in=((16, T // 2, D // 8), bf),
        normed_across=((16, T // 2, D // 8), bf),
        branch=((8, T, D // 8), bf),
        branch_in=((8, T, D // 8), bf),
        branch_across=((8, T, D // 8), bf),
        gain_part=((8, D), f32),
        small_send=((16, HI), f32),
        small_recv=((n_seq, 16, HI), f32),
        gain_recv=((n_tp, 8, HI), f32),
    )
    semaphores = dict(
        rim_send=(2,),
        rim_recv=(2,),
        halo_send=(2,),
        halo_recv=(2,),
        pair_ss=(2, n_seq // 2),
        pair_rs=(2, n_seq // 2),
        chip_ss=(2, n_seq // 2 - 1),
        chip_rs=(2, n_seq // 2 - 1),
        fold_ss=(3, 24),
        fold_rs=(3, 24),
    )
    for name in ("state", "sums", "shared", "gain"):
        semaphores[name + "_ss"] = (n_tp - 1,)
        semaphores[name + "_rs"] = (n_tp - 1,)
    for name in ("decay", "end", "enter", "grad", "leave", "small"):
        semaphores[name + "_ss"] = (n_seq - 1,)
        semaphores[name + "_rs"] = (n_seq - 1,)
    scratch.update({n: (given[n].shape, bf) for n in LOADED})
    semaphores["load_sems"] = (len(LOADED),)
    names = tuple(n + "_hbm" if n in LOADED else n for n in INPUTS) + SUMS + tuple(scratch) + tuple(semaphores)
    vmem = pl.BlockSpec(memory_space=pltpu.VMEM)
    smem = pl.BlockSpec(memory_space=pltpu.SMEM)
    totals = pl.pallas_call(
        functools.partial(kernel, (n_seq, n_tp, T, D, HI, H, NS), names),
        out_shape=tuple(jax.ShapeDtypeStruct(s, t) for s, t in sums),
        in_specs=[
            smem if n == "scene_lengths" else pl.BlockSpec(memory_space=pl.ANY) if n in LOADED else vmem
            for n in INPUTS
        ],
        out_specs=tuple(vmem for _ in sums),
        scratch_shapes=[pltpu.VMEM(s, t) for s, t in scratch.values()]
        + [pltpu.SemaphoreType.DMA(s) for s in semaphores.values()],
        compiler_params=pltpu.CompilerParams(
            collective_id=0, has_side_effects=True, vmem_limit_bytes=61 * 2**20
        ),
    )(*given.values())
    tall = ("block_input", "out_cotangent", "branch_sum", "normed_sum", "block_output", "input_grad")
    steps = 2
    by_rows = pl.BlockSpec((T // steps, D), lambda i: (i, 0))

    def whole(shape):
        return pl.BlockSpec(shape, lambda i: (0,) * len(shape))

    needed = ("block_input", "input_gain", "out_cotangent")
    results = pl.pallas_call(
        functools.partial(finish, (T, D, HI, H, NS), needed + SUMS + OUTPUTS),
        out_shape=tuple(jax.ShapeDtypeStruct(s, t) for s, t in outs),
        grid=(steps,),
        in_specs=[by_rows if n in tall else whole(given[n].shape) for n in needed]
        + [by_rows if n in tall else whole(s) for n, (s, _) in zip(SUMS, sums)],
        out_specs=tuple(by_rows if n in tall else whole(s) for n, (s, _) in zip(OUTPUTS, outs)),
        compiler_params=pltpu.CompilerParams(vmem_limit_bytes=60 * 2**20),
    )(*(given[n] for n in needed), *totals)
    results = dict(zip(OUTPUTS, results))
    results["state_weight_grad"] = results["state_weight_grad"].T
    results["step_weight_grad"] = results["step_weight_grad"].T
    return tuple(results.values())


def solution(mesh):
    rows = P("seq", None)
    cols = P(None, "tp")
    heads = P("tp")
    return jax.shard_map(
        local,
        mesh=mesh,
        in_specs=(
            rows,
            P(),
            P(),
            cols,
            cols,
            cols,
            cols,
            heads,
            heads,
            cols,
            heads,
            cols,
            heads,
            heads,
            heads,
            P("tp", None),
            rows,
        ),
        out_specs=(
            rows,
            rows,
            P(),
            P("seq", "tp"),
            P("seq", "tp"),
            P("seq", "tp"),
            P("seq", "tp"),
            heads,
            heads,
            cols,
            heads,
            cols,
            heads,
            heads,
            heads,
            P("tp", "seq"),
        ),
        check_vma=False,
    )
```
